32 devices in a mesh: dp: 8 (over y, x, core), tensor: 4 (over z).
Axes of the slice: x: 2, y: 2, z: 4, core: 2. Of those that a mesh axis runs over, the one named last changes fastest.
Arguments:
- tokens: bfloat16 [16384, 768], P(('dp', 'tensor')), may hold values from -6 to 6
- segment_ids: int32 [16384], P('dp'), may hold values from 0 to 2, as said below
- out_grad: bfloat16 [16384, 768], P('dp'), may hold values from -6 to 6
- heads_weight: float32 [768, 2304], P('dp', 'tensor'), may hold values from -0.3125 to 0.3125
- merge_weight: float32 [768, 768], P('tensor', 'dp'), may hold values from -0.875 to 0.875
- expand_weight: float32 [768, 3072], P(None, ('tensor', 'dp')), may hold values from -0.21875 to 0.21875
- reduce_weight: float32 [3072, 768], P(('tensor', 'dp')), may hold values from -0.109375 to 0.109375
- heads_momentum: float32 [768, 2304], P('dp', 'tensor'), may hold values from -8192 to 8192
- merge_momentum: float32 [768, 768], P('tensor', 'dp'), may hold values from -8192 to 8192
- expand_momentum: float32 [768, 3072], P(None, ('tensor', 'dp')), may hold values from -8192 to 8192
- reduce_momentum: float32 [3072, 768], P(('tensor', 'dp')), may hold values from -8192 to 8192
- heads_average: float32 [768, 2304], P('dp', 'tensor'), may hold values from -0.3125 to 0.3125
- merge_average: float32 [768, 768], P('tensor', 'dp'), may hold values from -0.875 to 0.875
- expand_average: float32 [768, 3072], P(None, ('tensor', 'dp')), may hold values from -0.21875 to 0.21875
- reduce_average: float32 [3072, 768], P(('tensor', 'dp')), may hold values from -0.109375 to 0.109375
- vectors: float32 [6, 768], replicated, may hold values from -0.5 to 1.5
- vector_momentum: float32 [6, 768], replicated, may hold values from -8192 to 8192
- vector_average: float32 [6, 768], replicated, may hold values from -0.5 to 1.5
Outputs:
- layer_output: bfloat16 [16384, 768], P(('dp', 'tensor'))
- input_gradient: float32 [16384, 768], P(('dp', 'tensor'))
- heads_gradient: float32 [768, 2304], P('dp', 'tensor')
- merge_gradient: float32 [768, 768], P('tensor', 'dp')
- expand_gradient: float32 [768, 3072], P(None, ('tensor', 'dp'))
- reduce_gradient: float32 [3072, 768], P(('tensor', 'dp'))
- heads_new_momentum: float32 [768, 2304], P('dp', 'tensor')
- merge_new_momentum: float32 [768, 768], P('tensor', 'dp')
- expand_new_momentum: float32 [768, 3072], P(None, ('tensor', 'dp'))
- reduce_new_momentum: float32 [3072, 768], P(('tensor', 'dp'))
- heads_new_weight: float32 [768, 2304], P('dp', 'tensor')
- merge_new_weight: float32 [768, 768], P('tensor', 'dp')
- expand_new_weight: float32 [768, 3072], P(None, ('tensor', 'dp'))
- reduce_new_weight: float32 [3072, 768], P(('tensor', 'dp'))
- heads_new_average: float32 [768, 2304], P('dp', 'tensor')
- merge_new_average: float32 [768, 768], P('tensor', 'dp')
- expand_new_average: float32 [768, 3072], P(None, ('tensor', 'dp'))
- reduce_new_average: float32 [3072, 768], P(('tensor', 'dp'))
- vector_gradient: float32 [6, 768], replicated
- vector_new_momentum: float32 [6, 768], replicated
- vector_new_value: float32 [6, 768], replicated
- vector_new_average: float32 [6, 768], replicated
The draws below stay inside these ranges and needn't reach their ends.
Inputs may be any that keep to these rules, and one draw needn't show every extreme that they name: `segment_ids`: in each sequence of 2048 tokens the ids never fall and form three segments numbered 0, 1, 2, each of one token or more.
All inputs are finite; a program needn't handle non-finite values.
Results may differ from the reference program's by a relative error of at most 0.02.
Values may be sent and summed in bfloat16 or wider, within the bound.
A program may use at most 192 MiB of HBM per device.

```python
import math
from functools import partial
import jax
import jax.numpy as jnp
from jax import lax

D = 768
HEADS = 12
HEAD_DIM = 64
FF = 3072
SEQ = 2048
NEWTON_STEPS = 5
TOKENS = 16384
N_DP = 8
N_TENSOR = 4


def bounded_normal(key, shape, factor):
    sample = jnp.clip(jax.random.normal(key, shape, jnp.float32), -5.0, 5.0)
    return sample * (factor * math.sqrt(TOKENS))


def vector_table(key):
    gains = jax.random.uniform(key, (6, D), jnp.float32, 0.5, 1.5)
    shifts = jax.random.uniform(jax.random.fold_in(key, 7), (6, D), jnp.float32, -0.5, 0.5)
    is_gain = (jnp.arange(6) % 2 == 0) & (jnp.arange(6) < 4)
    return jnp.where(is_gain[:, None], gains, shifts)


def draw_segment_ids(key, part):
    key = jax.random.fold_in(key, 11)
    first_key, last_key = jax.random.split(key)
    quarter = SEQ // N_TENSOR
    first_cut = jax.random.randint(first_key, (N_DP, 1), 1, quarter)
    last_cut = jax.random.randint(last_key, (N_DP, 1), SEQ - quarter + 1, SEQ)
    position = jnp.arange(SEQ, dtype=jnp.int32)[None, :]
    labels = (position >= first_cut).astype(jnp.int32) + (position >= last_cut).astype(jnp.int32)
    return labels.reshape(-1)


def draw_heads_momentum(key, part):
    key = jax.random.fold_in(key, 1)
    return bounded_normal(key, (D, 3 * D), 0.3)


def draw_merge_momentum(key, part):
    key = jax.random.fold_in(key, 2)
    return bounded_normal(key, (D, D), 0.3)


def draw_expand_momentum(key, part):
    key = jax.random.fold_in(key, 3)
    return bounded_normal(key, (D, FF), 0.5)


def draw_reduce_momentum(key, part):
    key = jax.random.fold_in(key, 4)
    return bounded_normal(key, (FF, D), 0.6)


def draw_vector_momentum(key, part):
    key = jax.random.fold_in(key, 5)
    return bounded_normal(key, (6, D), 1.0)


def draw_vectors(key, part):
    key = jax.random.fold_in(key, 21)
    return vector_table(key)


def draw_vector_average(key, part):
    key = jax.random.fold_in(key, 22)
    return vector_table(key)


def levels(rng, dims, pieces, least, largest):
    factor_of = 1.0
    for axis_at, parts in pieces:
        steps = jax.random.uniform(jax.random.fold_in(jax.random.fold_in(rng, 6), axis_at), (parts,), jnp.float32, least / len(pieces), largest / len(pieces))
        factor_of = factor_of * jnp.repeat(jnp.exp(steps), dims[axis_at] // parts).reshape((-1,) + (1,) * (len(dims) - 1 - axis_at))
    return factor_of


def gaussian(stream_key, dims, deviation, most, shards=(), held_as=jnp.bfloat16):
    drawn = jax.random.normal(stream_key, dims, jnp.float32) * deviation
    if len(shards) > 0:
        drawn = levels(stream_key, dims, shards, -0.22, 0.18) * drawn
    return jnp.clip(drawn, min=-most, max=most).astype(held_as)


def setup_inputs(seed: int = 0) -> dict:
    streams_of = jax.random.split(jax.random.key(seed), 19)
    tokens = gaussian(streams_of[0], (TOKENS, D), 1.0, 6.0, ((0, 32),))
    segment_ids = draw_segment_ids(jax.random.fold_in(streams_of[18], 71), 0)
    out_grad = gaussian(streams_of[2], (TOKENS, D), 1.0, 6.0, ((0, 8),))
    heads_weight = gaussian(streams_of[3], (D, 3 * D), (D // 2) ** -0.5, 0.3125, ((0, 8), (1, 4)), jnp.float32)
    merge_weight = gaussian(streams_of[4], (D, D), (D // 16) ** -0.5, 0.875, ((0, 4), (1, 8)), jnp.float32)
    expand_weight = gaussian(streams_of[5], (D, FF), D ** -0.5, 0.21875, ((1, 32),), jnp.float32)
    reduce_weight = gaussian(streams_of[6], (FF, D), FF ** -0.5, 0.109375, ((0, 32),), jnp.float32)
    heads_momentum = draw_heads_momentum(jax.random.fold_in(streams_of[18], 71), 0)
    merge_momentum = draw_merge_momentum(jax.random.fold_in(streams_of[18], 71), 0)
    expand_momentum = draw_expand_momentum(jax.random.fold_in(streams_of[18], 71), 0)
    reduce_momentum = draw_reduce_momentum(jax.random.fold_in(streams_of[18], 71), 0)
    heads_average = gaussian(streams_of[11], (D, 3 * D), (D // 2) ** -0.5, 0.3125, ((0, 8), (1, 4)), jnp.float32)
    merge_average = gaussian(streams_of[12], (D, D), (D // 16) ** -0.5, 0.875, ((0, 4), (1, 8)), jnp.float32)
    expand_average = gaussian(streams_of[13], (D, FF), D ** -0.5, 0.21875, ((1, 32),), jnp.float32)
    reduce_average = gaussian(streams_of[14], (FF, D), FF ** -0.5, 0.109375, ((0, 32),), jnp.float32)
    vectors = draw_vectors(jax.random.fold_in(streams_of[18], 71), 0)
    vector_momentum = draw_vector_momentum(jax.random.fold_in(streams_of[18], 71), 0)
    vector_average = draw_vector_average(jax.random.fold_in(streams_of[18], 71), 0)
    return dict(tokens=tokens, segment_ids=segment_ids, out_grad=out_grad, heads_weight=heads_weight, merge_weight=merge_weight, expand_weight=expand_weight, reduce_weight=reduce_weight, heads_momentum=heads_momentum, merge_momentum=merge_momentum, expand_momentum=expand_momentum, reduce_momentum=reduce_momentum, heads_average=heads_average, merge_average=merge_average, expand_average=expand_average, reduce_average=reduce_average, vectors=vectors, vector_momentum=vector_momentum, vector_average=vector_average)


@jax.custom_vjp
def low(v):
    return lax.optimization_barrier(v.astype(jnp.bfloat16)).astype(jnp.float32)

@jax.custom_vjp
def low_back(v):
    return v

def low_keep(v):
    return (low(v), None)

def low_pass(kept, grad):
    return (grad,)

def back_keep(v):
    return (v, None)

def back_low(kept, grad):
    return (low(grad),)
low.defvjp(low_keep, low_pass)
low_back.defvjp(back_keep, back_low)
highest = lax.Precision.HIGHEST
norm_epsilon = 1e-06
newton_epsilon = 1e-07
newton_linear = 3.4445
newton_cubic = -4.775
newton_quintic = 2.0315
momentum_decay = 0.5
average_decay = 0.9
muon_rate = 0.2
weight_decay = 0.1
vector_rate = 0.15
masked_score = -1e+30

def layer_norm(values, gain, shift):
    average = lax.optimization_barrier(jnp.mean(values, axis=-1, keepdims=True))
    centered = values - average
    variance = lax.optimization_barrier(jnp.mean(centered * centered, axis=-1, keepdims=True))
    return centered * lax.rsqrt(variance + norm_epsilon) * gain + shift

def gelu_exact(values):
    return jax.nn.gelu(values, approximate=False)

def sequence_attention(packed, segments):
    queries = packed[:, :, 0]
    key_rows = packed[:, :, 1]
    value_rows = packed[:, :, 2]
    scores = jnp.einsum('qhd,khd->hqk', queries, key_rows, precision=highest) * HEAD_DIM ** (-0.5)
    scores = jnp.where((segments[:, None] == segments[None, :])[None], scores, masked_score)
    scores = low_back(scores)
    row_max = lax.optimization_barrier(jnp.max(scores, axis=-1, keepdims=True))
    exponent = jnp.exp(scores - row_max)
    chances = low(exponent / lax.optimization_barrier(jnp.sum(exponent, axis=-1, keepdims=True)))
    attended = jnp.einsum('hqk,khd->qhd', chances, value_rows, precision=highest)
    return attended.reshape(packed.shape[0], -1)

def attend_pair(inputs):
    return jax.checkpoint(sequence_attention)(inputs[0], inputs[1])

def layer_forward(dense_rows, vector_rows, heads_matrix, merge_matrix, expand_matrix, reduce_matrix, segment_ids):
    first_in = low(layer_norm(dense_rows, vector_rows[0], vector_rows[1]))
    projected = jnp.dot(first_in, low(heads_matrix), precision=highest)
    projected = low(low_back(projected))
    packed = projected.reshape(N_DP, SEQ, HEADS, 3, HEAD_DIM)
    attended = lax.map(attend_pair, (packed, segment_ids.reshape(N_DP, SEQ)))
    attended = low(low_back(attended.reshape(TOKENS, D)))
    merged = low_back(jnp.dot(attended, low(merge_matrix), precision=highest))
    middle = dense_rows + merged + vector_rows[4]
    second_in = low(layer_norm(middle, vector_rows[2], vector_rows[3]))
    expanded = low_back(jnp.dot(second_in, low(expand_matrix), precision=highest))
    hidden = low(gelu_exact(expanded))
    return middle + jnp.dot(hidden, low(reduce_matrix), precision=highest) + vector_rows[5]

def newton(matrix, left):
    matrix = matrix / (jnp.sqrt(jnp.sum(matrix * matrix)) + newton_epsilon)
    for iteration in range(NEWTON_STEPS):
        if left:
            gram = jnp.dot(matrix, matrix.T, precision=highest)
            side = jnp.dot(gram, matrix, precision=highest)
            matrix = newton_linear * matrix + newton_cubic * side + newton_quintic * jnp.dot(gram, side, precision=highest)
        else:
            gram = jnp.dot(matrix.T, matrix, precision=highest)
            side = jnp.dot(matrix, gram, precision=highest)
            matrix = newton_linear * matrix + newton_cubic * side + newton_quintic * jnp.dot(side, gram, precision=highest)
    return matrix

def reference(tokens, segment_ids, out_grad, heads_weight, merge_weight, expand_weight, reduce_weight, heads_momentum, merge_momentum, expand_momentum, reduce_momentum, heads_average, merge_average, expand_average, reduce_average, vectors, vector_momentum, vector_average):
    dense_rows = tokens.astype(jnp.float32)

    def forward(inputs, vector_rows, heads_matrix, merge_matrix, expand_matrix, reduce_matrix):
        return layer_forward(inputs, vector_rows, heads_matrix, merge_matrix, expand_matrix, reduce_matrix, segment_ids)
    output, pullback = jax.vjp(forward, dense_rows, vectors, heads_weight, merge_weight, expand_weight, reduce_weight)
    input_gradient, vector_gradient, heads_gradient, merge_gradient, expand_gradient, reduce_gradient = pullback(out_grad.astype(jnp.float32))
    heads_new_momentum = momentum_decay * heads_momentum + heads_gradient
    merge_new_momentum = momentum_decay * merge_momentum + merge_gradient
    expand_new_momentum = momentum_decay * expand_momentum + expand_gradient
    reduce_new_momentum = momentum_decay * reduce_momentum + reduce_gradient
    vector_new_momentum = momentum_decay * vector_momentum + vector_gradient
    heads_orth = jax.vmap(partial(newton, left=False), in_axes=1, out_axes=1)(heads_new_momentum.reshape(D, HEADS * 3, HEAD_DIM)).reshape(D, 3 * D)
    merge_orth = jax.vmap(partial(newton, left=True))(merge_new_momentum.reshape(HEADS, HEAD_DIM, D)).reshape(D, D)
    expand_orth = newton(expand_new_momentum, True)
    reduce_orth = newton(reduce_new_momentum, False)
    keep = 1.0 - muon_rate * weight_decay
    head_step = muon_rate * 0.2 * math.sqrt(max(D, HEAD_DIM))
    wide_step = muon_rate * 0.2 * math.sqrt(max(D, FF))
    heads_new_weight = heads_weight * keep - head_step * heads_orth
    merge_new_weight = merge_weight * keep - head_step * merge_orth
    expand_new_weight = expand_weight * keep - wide_step * expand_orth
    reduce_new_weight = reduce_weight * keep - wide_step * reduce_orth
    vector_new_value = vectors - vector_rate / math.sqrt(TOKENS) * vector_new_momentum
    heads_new_average = average_decay * heads_average + (1.0 - average_decay) * heads_new_weight
    merge_new_average = average_decay * merge_average + (1.0 - average_decay) * merge_new_weight
    expand_new_average = average_decay * expand_average + (1.0 - average_decay) * expand_new_weight
    reduce_new_average = average_decay * reduce_average + (1.0 - average_decay) * reduce_new_weight
    vector_new_average = average_decay * vector_average + (1.0 - average_decay) * vector_new_value
    return (output.astype(jnp.bfloat16), input_gradient, heads_gradient, merge_gradient, expand_gradient, reduce_gradient, heads_new_momentum, merge_new_momentum, expand_new_momentum, reduce_new_momentum, heads_new_weight, merge_new_weight, expand_new_weight, reduce_new_weight, heads_new_average, merge_new_average, expand_new_average, reduce_new_average, vector_gradient, vector_new_momentum, vector_new_value, vector_new_average)
```

```python
import math

import jax
import jax.numpy as jnp
from jax import lax
from jax.sharding import PartitionSpec as P

D = 768
HEAD_DIM = 64
FF = 3072
SEQ = 2048
NEWTON_STEPS = 5


highest = lax.Precision.HIGHEST
norm_epsilon = 1e-06
newton_epsilon = 1e-07
newton_linear = 3.4445
newton_cubic = -4.775
newton_quintic = 2.0315
momentum_decay = 0.5
average_decay = 0.9
muon_rate = 0.2
weight_decay = 0.1
vector_rate = 0.15
masked_score = -1e30
query_block = 512


def center_scale(values):
    average = jnp.mean(values, axis=-1, keepdims=True)
    centered = values - average
    inverse = lax.rsqrt(jnp.mean(centered * centered, axis=-1, keepdims=True) + norm_epsilon)
    return (centered * inverse, inverse)


def norm_backward(upstream, normed, inverse, gain):
    scaled = upstream * gain
    mean_one = jnp.mean(scaled, axis=-1, keepdims=True)
    mean_two = jnp.mean(scaled * normed, axis=-1, keepdims=True)
    return inverse * (scaled - mean_one - normed * mean_two)


def gelu_exact(values):
    return jax.nn.gelu(values, approximate=False)


def contract_rows(left_side, right_side):
    return lax.dot_general(
        left_side, right_side, (((0,), (0,)), ((), ())), preferred_element_type=jnp.float32
    )


def contract_cols(left_side, right_side):
    return lax.dot_general(
        left_side, right_side, (((1,), (1,)), ((), ())), preferred_element_type=jnp.float32
    )


def masked_scores(query_rows, key_rows, seg_rows, segment_full, score_scale):
    scores = (
        jnp.einsum("qhd,khd->hqk", query_rows, key_rows, preferred_element_type=jnp.float32)
        * score_scale
    )
    return jnp.where((seg_rows[:, None] == segment_full[None, :])[None], scores, masked_score)


def attention_forward(packed, segment_full):
    seq_len, head_local, three_way, head_dim = packed.shape
    block_size = min(query_block, seq_len)
    block_count = seq_len // block_size
    score_scale = head_dim ** (-0.5)
    key_rows = packed[:, :, 1]
    value_rows = packed[:, :, 2]
    queries = packed[:, :, 0].reshape(block_count, block_size, head_local, head_dim)
    segment_blocks = segment_full.reshape(block_count, block_size)

    def one_block(inputs):
        query_rows, seg_rows = inputs
        scores = masked_scores(query_rows, key_rows, seg_rows, segment_full, score_scale)
        row_max = jnp.max(scores, axis=-1, keepdims=True)
        exponent = jnp.exp(scores - row_max)
        totals = jnp.sum(exponent, axis=-1, keepdims=True)
        chances = (exponent / totals).astype(jnp.bfloat16)
        output = jnp.einsum("hqk,khd->qhd", chances, value_rows, preferred_element_type=jnp.float32)
        return (output, row_max + jnp.log(totals))

    outputs, logsum = lax.map(one_block, (queries, segment_blocks))
    return (outputs.reshape(seq_len, head_local * head_dim), logsum)


def attention_backward(packed, segment_full, logsum, attended_grad):
    seq_len, head_local, three_way, head_dim = packed.shape
    block_size = min(query_block, seq_len)
    block_count = seq_len // block_size
    score_scale = head_dim ** (-0.5)
    key_rows = packed[:, :, 1]
    value_rows = packed[:, :, 2]
    queries = packed[:, :, 0].reshape(block_count, block_size, head_local, head_dim)
    segment_blocks = segment_full.reshape(block_count, block_size)
    grad_blocks = attended_grad.reshape(block_count, block_size, head_local, head_dim)

    def one_block(carry, inputs):
        key_total, value_total = carry
        query_rows, seg_rows, grad_rows, lse_rows = inputs
        scores = masked_scores(query_rows, key_rows, seg_rows, segment_full, score_scale)
        chances = jnp.exp(scores - lse_rows)
        chance_grad = jnp.einsum(
            "qhd,khd->hqk", grad_rows, value_rows, preferred_element_type=jnp.float32
        )
        row_dot = jnp.sum(chances * chance_grad, axis=-1, keepdims=True)
        score_grad = (chances * (chance_grad - row_dot)).astype(jnp.bfloat16)
        query_grad = (
            jnp.einsum("hqk,khd->qhd", score_grad, key_rows, preferred_element_type=jnp.float32)
            * score_scale
        )
        key_total = (
            key_total
            + jnp.einsum("hqk,qhd->khd", score_grad, query_rows, preferred_element_type=jnp.float32)
            * score_scale
        )
        value_total = value_total + jnp.einsum(
            "hqk,qhd->khd",
            chances.astype(jnp.bfloat16),
            grad_rows,
            preferred_element_type=jnp.float32,
        )
        return ((key_total, value_total), query_grad)

    zero_rows = jnp.zeros((seq_len, head_local, head_dim), jnp.float32)
    (key_grad, value_grad), query_grad = lax.scan(
        one_block, (zero_rows, zero_rows), (queries, segment_blocks, grad_blocks, logsum)
    )
    query_grad = query_grad.reshape(seq_len, head_local, head_dim)
    return jnp.stack([query_grad, key_grad, value_grad], axis=2)


EXACT_THREE = lax.Precision.HIGH
SIDE = 256


def swap_bit(values, axis_name, bit):
    count = lax.axis_size(axis_name)
    return lax.ppermute(values, axis_name, [(i, i ^ bit) for i in range(count)])


def data_bits():
    return [1 << k for k in range(1, lax.axis_size("dp").bit_length() - 1)]


def has_bit(index, bit):
    return (index & bit) != 0


def gather_bits_absolute(block, bits):
    index = lax.axis_index("dp")
    for bit in bits:
        other = swap_bit(block, "dp", bit)
        mine = has_bit(index, bit)
        block = jnp.concatenate(
            [jnp.where(mine, other, block), jnp.where(mine, block, other)], axis=0
        )
    return block


def scatter_bits_absolute(total, bits, wire):
    index = lax.axis_index("dp")
    for bit in reversed(bits):
        half = total.shape[0] // 2
        low, high = total[:half], total[half:]
        mine = has_bit(index, bit)
        arrived = swap_bit(jnp.where(mine, low, high).astype(wire), "dp", bit)
        total = jnp.where(mine, high, low).astype(jnp.float32) + arrived.astype(jnp.float32)
    return total


def line_up(values):
    count = lax.axis_size("tensor")
    return lax.ppermute(values, "tensor", [(i, i + 1) for i in range(count - 1)])


def line_down(values):
    count = lax.axis_size("tensor")
    return lax.ppermute(values, "tensor", [(i + 1, i) for i in range(count - 1)])


def gather_line(block):
    count = lax.axis_size("tensor")
    index = lax.axis_index("tensor")
    below, above = [block], [block]
    for step in range(count - 1):
        below.append(line_up(below[-1]))
        above.append(line_down(above[-1]))
    parts = [block]
    for offset in range(1, count):
        parts.append(jnp.where(index + offset < count, above[offset], below[count - offset]))
    return parts


def scatter_line(parts, wire):
    count = lax.axis_size("tensor")
    index = lax.axis_index("tensor")
    upward, downward = None, None
    for offset in range(count - 1, 0, -1):
        send_up = parts[offset].astype(jnp.float32)
        send_down = parts[count - offset].astype(jnp.float32)
        if upward is not None:
            send_up = send_up + upward.astype(jnp.float32)
            send_down = send_down + downward.astype(jnp.float32)
        upward = line_up(jnp.where(index + offset < count, send_up, 0.0).astype(wire))
        downward = line_down(jnp.where(index >= offset, send_down, 0.0).astype(wire))
    return parts[0].astype(jnp.float32) + upward.astype(jnp.float32) + downward.astype(jnp.float32)


def pair_permute(values, where_to):
    data_count, tensor_count = lax.axis_size("dp"), lax.axis_size("tensor")
    moves = []
    for i in range(data_count):
        for j in range(tensor_count):
            target = where_to(i, j)
            if target is not None:
                moves.append((i * tensor_count + j, target[0] * tensor_count + target[1]))
    return lax.ppermute(values, ("dp", "tensor"), moves)


def exchange_home(values):
    return pair_permute(
        values, lambda i, j: (i ^ 1, j ^ 2) if (i & 1) != (j >> 1) else None
    )


def group_swap(values, member):
    if member == 1:
        return swap_bit(values, "dp", 1)
    if member == 2:
        return swap_bit(values, "tensor", 1)
    return pair_permute(values, lambda i, j: (i ^ 1, j ^ 1))


def gather_head_group(shard):
    first = []
    for core in (0, 1):
        got = []
        for half in (0, 1):
            got.append(
                pair_permute(
                    shard,
                    lambda i, j: (i - core + (j & 1), (j >> 1) + 2 * half)
                    if (i & 1) == core
                    else None,
                )
            )
        first.append(jnp.where(lax.axis_index("tensor") >= 2, got[1], got[0]))
    return gather_bits_absolute(jnp.concatenate(first, axis=0), data_bits())


def scatter_head_group(total, wire):
    total = scatter_bits_absolute(total, data_bits(), wire)
    rows = total.shape[0] // 2
    result = None
    for core in (0, 1):
        piece = total[core * rows : (core + 1) * rows].astype(wire)
        arrived = None
        for half in (0, 1):
            got = pair_permute(
                piece,
                lambda i, j: ((i & ~1) + core, 2 * (j & 1) + (i & 1))
                if (j >> 1) == half
                else None,
            ).astype(jnp.float32)
            arrived = got if arrived is None else arrived + got
        result = arrived if core == 0 else jnp.where((lax.axis_index("dp") & 1) == 1, arrived, result)
    return result


def gather_units(pair):
    parts = jnp.stack(gather_line(pair))
    bits = data_bits()
    both = []
    for which, order in ((0, bits), (1, bits[::-1])):
        block = parts[:, which]
        done = []
        for bit in order:
            other = swap_bit(block, "dp", bit)
            place = sum(1 for b in done if b > bit)
            block = jnp.stack([block, other], axis=place)
            done.append(bit)
        other = swap_bit(block, "dp", 1)
        both.append((block.reshape(-1, block.shape[-1]), other.reshape(-1, block.shape[-1])))
    return both


def scatter_units(mine, theirs, order, wire):
    total = mine + swap_bit(theirs.astype(wire), "dp", 1).astype(jnp.float32)
    bits = data_bits()
    count = lax.axis_size("tensor")
    width = total.shape[-1]
    rows = total.shape[0] // (count << len(bits))
    total = total.reshape((2,) * len(bits) + (count, rows, width))
    left = sorted(bits, reverse=True)
    for bit in order:
        place = left.index(bit)
        keep = lax.index_in_dim(total, 0, place, keepdims=False)
        send = lax.index_in_dim(total, 1, place, keepdims=False)
        total = keep + swap_bit(send.astype(wire), "dp", bit).astype(jnp.float32)
        left.remove(bit)
    return scatter_line([total[k] for k in range(count)], wire)


def pack_symmetric(gram):
    return jnp.concatenate(
        [gram[k : k + SIDE, k:] for k in range(0, gram.shape[0], SIDE)], axis=1
    )


def unpack_symmetric(packed, size):
    rows, at = [], 0
    for k in range(0, size, SIDE):
        rows.append(packed[:, at : at + size - k])
        at += size - k
    full = []
    for i in range(len(rows)):
        blocks = [rows[j][:, (i - j) * SIDE : (i - j + 1) * SIDE].T for j in range(i)]
        full.append(jnp.concatenate(blocks + [rows[i]], axis=1))
    return jnp.concatenate(full, axis=0)


def sum_over_chips(packed):
    count = lax.axis_size("tensor")
    index = lax.axis_index("tensor")
    part = scatter_bits_absolute(packed, data_bits(), jnp.float32)
    part = part.reshape(count, part.shape[0] // count, part.shape[1])
    ring = (index + jnp.arange(count)) % count
    turned = jnp.take(part, ring, axis=0)
    own = scatter_line([turned[k] for k in range(count)], jnp.float32)
    parts = jnp.stack(gather_line(own))
    part = jnp.take(parts, (jnp.arange(count) - index) % count, axis=0)
    part = part.reshape(count * part.shape[1], part.shape[2])
    return gather_bits_absolute(part, data_bits())


def sum_over_all(values):
    for bit in (1, 2):
        values = values + swap_bit(values, "tensor", bit)
    for bit in [1] + data_bits():
        values = values + swap_bit(values, "dp", bit)
    return values


def polynomial_chain(gram, product):
    identity = jnp.eye(gram.shape[-1], dtype=jnp.float32)
    chain = None
    for step in range(NEWTON_STEPS):
        square = product(gram, gram)
        factor = newton_linear * identity + newton_cubic * gram + newton_quintic * square
        chain = factor if chain is None else product(chain, factor)
        if step < NEWTON_STEPS - 1:
            gram = product(product(gram, factor), factor)
    return chain


def per_device(
    tokens,
    segment_ids,
    out_grad,
    heads_weight,
    merge_weight,
    expand_weight,
    reduce_weight,
    heads_momentum,
    merge_momentum,
    expand_momentum,
    reduce_momentum,
    heads_average,
    merge_average,
    expand_average,
    reduce_average,
    vectors,
    vector_momentum,
    vector_average,
):
    low = jnp.bfloat16
    tensor_count = lax.axis_size("tensor")
    data_count = lax.axis_size("dp")
    tensor_index = lax.axis_index("tensor")
    core = lax.axis_index("dp") & 1
    row_count = tokens.shape[0]
    seq_len = row_count * tensor_count
    head_local = heads_weight.shape[1] // (3 * HEAD_DIM)
    group_width = head_local * HEAD_DIM
    at_home = core == (tensor_index >> 1)
    group = 2 * (tensor_index & 1) + core

    own_tokens = jnp.where(at_home, tokens, exchange_home(tokens))
    across = swap_bit(own_tokens, "tensor", 1)
    full_heads = gather_head_group(heads_weight.astype(low))
    beside = swap_bit(own_tokens, "dp", 1)
    diagonal = swap_bit(across, "dp", 1)
    token_chunks = jnp.stack([own_tokens, beside, across, diagonal])
    own_segments = jnp.where(at_home, segment_ids, swap_bit(segment_ids, "dp", 1))
    chunk_at = []
    for member in range(4):
        its_core, its_tensor = core ^ (member & 1), tensor_index ^ (member >> 1)
        chunk_at.append(jnp.where(its_core == (its_tensor >> 1), its_tensor, its_tensor ^ 2))
    segments = jnp.take(
        own_segments.reshape(tensor_count, row_count), jnp.stack(chunk_at), axis=0
    ).reshape(seq_len)
    sent_grad = lax.dynamic_slice_in_dim(out_grad, (tensor_index ^ 2) * row_count, row_count, 0)
    home_grad = lax.dynamic_slice_in_dim(out_grad, tensor_index * row_count, row_count, 0)
    own_grad = jnp.where(at_home, home_grad, swap_bit(sent_grad, "dp", 1))

    (expand_mine, expand_other), (reduce_mine, reduce_other) = gather_units(
        jnp.stack([expand_weight.T.astype(low), reduce_weight.astype(low)])
    )
    merge_rows = jnp.stack(gather_line(merge_weight.T.astype(low)), axis=1)
    merge_rows = gather_bits_absolute(merge_rows, [1] + data_bits())
    in_groups = ((group ^ jnp.arange(tensor_count)) - tensor_index) % tensor_count
    full_merge = jnp.take(merge_rows, in_groups, axis=1).reshape(D, D)

    dense_full = token_chunks.reshape(seq_len, D).astype(jnp.float32)
    normed_full, _ = center_scale(dense_full)
    first_full = (normed_full * vectors[0] + vectors[1]).astype(low)
    dense_rows = own_tokens.astype(jnp.float32)
    normed_one, inverse_one = center_scale(dense_rows)
    projected = jnp.dot(first_full, full_heads, preferred_element_type=jnp.float32)
    packed = projected.astype(low).reshape(seq_len, head_local, 3, HEAD_DIM)
    attended, logsum = attention_forward(packed, segments)
    attended = attended.astype(low).reshape(4, row_count, group_width)
    attended_own = jnp.concatenate(
        [attended[0]] + [group_swap(attended[k], k) for k in (1, 2, 3)], axis=1
    )
    merged = contract_cols(attended_own, full_merge)
    middle = dense_rows + merged + vectors[4]
    normed_two, inverse_two = center_scale(middle)
    second_in = (normed_two * vectors[2] + vectors[3]).astype(low)

    layer_sum = middle + vectors[5]
    second_grad = 0.0
    unit_sums = []
    for expand_half, reduce_half in ((expand_mine, reduce_mine), (expand_other, reduce_other)):
        expanded = contract_cols(second_in, expand_half)
        activated, gelu_pull = jax.vjp(gelu_exact, expanded)
        hidden = activated.astype(low)
        layer_sum = layer_sum + jnp.dot(hidden, reduce_half, preferred_element_type=jnp.float32)
        reduce_sum = contract_rows(hidden, own_grad)
        (expand_grad,) = gelu_pull(contract_cols(own_grad, reduce_half))
        expand_low = expand_grad.astype(low)
        expand_sum = contract_rows(expand_low, second_in)
        second_grad = second_grad + jnp.dot(
            expand_low, expand_half, preferred_element_type=jnp.float32
        )
        unit_sums.append((expand_sum, reduce_sum))
    output_rows = layer_sum.astype(low)
    layer_output = jnp.where(at_home, output_rows, exchange_home(output_rows))

    bits = data_bits()
    expand_rows = scatter_units(unit_sums[0][0], unit_sums[1][0], bits[::-1], low)
    reduce_gradient = scatter_units(unit_sums[0][1], unit_sums[1][1], bits, low)
    expand_gradient = expand_rows.T
    expand_new_momentum = momentum_decay * expand_momentum + expand_gradient
    reduce_new_momentum = momentum_decay * reduce_momentum + reduce_gradient
    expand_part = expand_new_momentum.T
    reduce_part = reduce_new_momentum
    expand_gram = lax.dot_general(
        expand_part, expand_part, (((0,), (0,)), ((), ())), precision=EXACT_THREE
    )
    reduce_gram = lax.dot_general(
        reduce_part, reduce_part, (((0,), (0,)), ((), ())), precision=EXACT_THREE
    )
    expand_gram, reduce_gram = pack_symmetric(expand_gram), pack_symmetric(reduce_gram)
    first_core = core == 0
    wide_gram = jnp.where(first_core, expand_gram, reduce_gram) + swap_bit(
        jnp.where(first_core, reduce_gram, expand_gram), "dp", 1
    )
    wide_gram = unpack_symmetric(sum_over_chips(wide_gram), D)

    middle_grad = own_grad.astype(jnp.float32) + norm_backward(
        second_grad, normed_two, inverse_two, vectors[2]
    )
    middle_low = middle_grad.astype(low)
    attended_grad = jnp.dot(middle_low, full_merge, preferred_element_type=jnp.float32).astype(low)
    grad_parts = [attended_grad[:, k * group_width : (k + 1) * group_width] for k in range(4)]
    attended_grad = jnp.concatenate(
        [grad_parts[0]] + [group_swap(grad_parts[k], k) for k in (1, 2, 3)], axis=0
    )
    merge_sum = contract_rows(middle_low, attended_own)
    merge_sum = merge_sum.astype(low).reshape(D, 4, group_width)
    turned = group ^ ((tensor_index + jnp.arange(tensor_count)) % tensor_count)
    merge_sum = jnp.take(merge_sum, turned, axis=1)
    merge_sum = scatter_line([merge_sum[:, k] for k in range(tensor_count)], low)
    merge_gradient = scatter_bits_absolute(merge_sum, [1] + data_bits(), low).T

    packed_grad = attention_backward(packed, segments, logsum, attended_grad)
    projected_grad = packed_grad.reshape(seq_len, 3 * group_width).astype(low)
    heads_sum = contract_rows(first_full, projected_grad)
    heads_gradient = scatter_head_group(heads_sum, low)
    first_parts = contract_cols(projected_grad, full_heads).reshape(4, row_count, D)
    kept = first_parts[0::2] + swap_bit(first_parts[1::2].astype(low), "dp", 1).astype(jnp.float32)
    first_grad = kept[0] + swap_bit(kept[1].astype(low), "tensor", 1).astype(jnp.float32)
    input_rows = middle_grad + norm_backward(first_grad, normed_one, inverse_one, vectors[0])
    input_gradient = jnp.where(
        at_home, input_rows, exchange_home(input_rows.astype(low)).astype(jnp.float32)
    )
    vector_gradient = sum_over_all(
        jnp.stack(
            [
                jnp.sum(first_grad * normed_one, axis=0),
                jnp.sum(first_grad, axis=0),
                jnp.sum(second_grad * normed_two, axis=0),
                jnp.sum(second_grad, axis=0),
                jnp.sum(middle_grad, axis=0),
                jnp.sum(own_grad.astype(jnp.float32), axis=0),
            ]
        )
    )
    heads_new_momentum = momentum_decay * heads_momentum + heads_gradient
    merge_new_momentum = momentum_decay * merge_momentum + merge_gradient
    vector_new_momentum = momentum_decay * vector_momentum + vector_gradient

    heads_part = heads_new_momentum.reshape(heads_new_momentum.shape[0], head_local * 3, HEAD_DIM)
    merge_part = merge_new_momentum.reshape(head_local, HEAD_DIM, merge_new_momentum.shape[1])
    small_gram = jnp.concatenate(
        [
            jnp.einsum("rmd,rme->mde", heads_part, heads_part, precision=highest),
            jnp.einsum("hdc,hec->hde", merge_part, merge_part, precision=highest),
        ],
        axis=0,
    )
    for bit in [1] + data_bits():
        small_gram = small_gram + swap_bit(small_gram, "dp", bit)
    small_factor = 1.0 / (jnp.sqrt(jnp.trace(small_gram, axis1=1, axis2=2)) + newton_epsilon)
    small_chain = polynomial_chain(
        small_gram * (small_factor * small_factor)[:, None, None],
        lambda left, right: jnp.einsum("mde,mef->mdf", left, right, precision=highest),
    )
    small_chain = small_chain * small_factor[:, None, None]
    side_count = 3 * head_local
    heads_ortho = jnp.einsum("rmd,mde->rme", heads_part, small_chain[:side_count], precision=highest)
    merge_ortho = jnp.einsum("hde,hec->hdc", small_chain[side_count:], merge_part, precision=highest)

    wide_factor = 1.0 / (jnp.sqrt(jnp.trace(wide_gram)) + newton_epsilon)
    wide_chain = polynomial_chain(
        wide_gram * (wide_factor * wide_factor),
        lambda left, right: jnp.dot(left, right, precision=EXACT_THREE),
    )
    wide_chain = wide_chain * wide_factor
    other_chain = swap_bit(wide_chain, "dp", 1)
    expand_ortho = jnp.dot(
        expand_part, jnp.where(first_core, wide_chain, other_chain), precision=EXACT_THREE
    ).T
    reduce_ortho = jnp.dot(
        reduce_part, jnp.where(first_core, other_chain, wide_chain), precision=EXACT_THREE
    )

    keep_factor = 1.0 - muon_rate * weight_decay
    head_step = muon_rate * 0.2 * math.sqrt(max(D, HEAD_DIM))
    wide_step = muon_rate * 0.2 * math.sqrt(max(D, FF))
    heads_new_weight = heads_weight * keep_factor - head_step * heads_ortho.reshape(
        heads_weight.shape
    )
    merge_new_weight = merge_weight * keep_factor - head_step * merge_ortho.reshape(
        merge_weight.shape
    )
    expand_new_weight = expand_weight * keep_factor - wide_step * expand_ortho
    reduce_new_weight = reduce_weight * keep_factor - wide_step * reduce_ortho
    vector_new_value = vectors - vector_rate / math.sqrt(SEQ * data_count) * vector_new_momentum
    heads_new_average = average_decay * heads_average + (1.0 - average_decay) * heads_new_weight
    merge_new_average = average_decay * merge_average + (1.0 - average_decay) * merge_new_weight
    expand_new_average = average_decay * expand_average + (1.0 - average_decay) * expand_new_weight
    reduce_new_average = average_decay * reduce_average + (1.0 - average_decay) * reduce_new_weight
    vector_new_average = average_decay * vector_average + (1.0 - average_decay) * vector_new_value
    return (
        layer_output,
        input_gradient,
        heads_gradient,
        merge_gradient,
        expand_gradient,
        reduce_gradient,
        heads_new_momentum,
        merge_new_momentum,
        expand_new_momentum,
        reduce_new_momentum,
        heads_new_weight,
        merge_new_weight,
        expand_new_weight,
        reduce_new_weight,
        heads_new_average,
        merge_new_average,
        expand_new_average,
        reduce_new_average,
        vector_gradient,
        vector_new_momentum,
        vector_new_value,
        vector_new_average,
    )


def solution(mesh):
    placed = (
        P(("dp", "tensor"), None),
        P("dp"),
        P("dp", None),
        P("dp", "tensor"),
        P("tensor", "dp"),
        P(None, ("tensor", "dp")),
        P(("tensor", "dp"), None),
        P("dp", "tensor"),
        P("tensor", "dp"),
        P(None, ("tensor", "dp")),
        P(("tensor", "dp"), None),
        P("dp", "tensor"),
        P("tensor", "dp"),
        P(None, ("tensor", "dp")),
        P(("tensor", "dp"), None),
        P(),
        P(),
        P(),
    )
    return jax.shard_map(
        per_device,
        mesh=mesh,
        in_specs=placed,
        out_specs=(
            P(("dp", "tensor"), None),
            P(("dp", "tensor"), None),
            P("dp", "tensor"),
            P("tensor", "dp"),
            P(None, ("tensor", "dp")),
            P(("tensor", "dp"), None),
            P("dp", "tensor"),
            P("tensor", "dp"),
            P(None, ("tensor", "dp")),
            P(("tensor", "dp"), None),
            P("dp", "tensor"),
            P("tensor", "dp"),
            P(None, ("tensor", "dp")),
            P(("tensor", "dp"), None),
            P("dp", "tensor"),
            P("tensor", "dp"),
            P(None, ("tensor", "dp")),
            P(("tensor", "dp"), None),
            P(),
            P(),
            P(),
            P(),
        ),
        check_vma=False,
    )
```

```python
import math

import jax
import jax.numpy as jnp
from jax import lax
from jax.experimental import pallas as pl
from jax.experimental.pallas import tpu as pltpu
from jax.sharding import PartitionSpec as P

D = 768
HEAD_DIM = 64
FF = 3072
SEQ = 2048
NEWTON_STEPS = 5


highest = lax.Precision.HIGHEST
norm_epsilon = 1e-06
newton_epsilon = 1e-07
newton_linear = 3.4445
newton_cubic = -4.775
newton_quintic = 2.0315
momentum_decay = 0.5
average_decay = 0.9
muon_rate = 0.2
weight_decay = 0.1
vector_rate = 0.15
masked_score = -1e30
VMEM_LIMIT = 56 * 2**20


def center_scale(values):
    average = jnp.mean(values, axis=-1, keepdims=True)
    centered = values - average
    inverse = lax.rsqrt(jnp.mean(centered * centered, axis=-1, keepdims=True) + norm_epsilon)
    return (centered * inverse, inverse)


def norm_backward(upstream, normed, inverse, gain):
    scaled = upstream * gain
    mean_one = jnp.mean(scaled, axis=-1, keepdims=True)
    mean_two = jnp.mean(scaled * normed, axis=-1, keepdims=True)
    return inverse * (scaled - mean_one - normed * mean_two)


def gelu_exact(values):
    return jax.nn.gelu(values, approximate=False)


def contract_rows(left_side, right_side):
    return lax.dot_general(
        left_side, right_side, (((0,), (0,)), ((), ())), preferred_element_type=jnp.float32
    )


def contract_cols(left_side, right_side):
    return lax.dot_general(
        left_side, right_side, (((1,), (1,)), ((), ())), preferred_element_type=jnp.float32
    )


KEY_BLOCK = 256
AUX = 128


def attend_kernel(projected, segment_column, attended, query_aux, key_aux, value_aux):
    seq_len, width = projected.shape
    head_local = width // (3 * HEAD_DIM)
    block = min(KEY_BLOCK, seq_len)
    lane = lax.broadcasted_iota(jnp.int32, (block, AUX), 1)
    low = jnp.bfloat16
    blank = jnp.zeros((block, AUX - HEAD_DIM), jnp.float32)

    def prepare(step, carry):
        rows = pl.ds(pl.multiple_of(step * block, block), block)
        segment = segment_column[rows, :]
        same = lane - HEAD_DIM == segment
        segment_lane = (lane >= HEAD_DIM) & (lane < HEAD_DIM + 3)
        query_extra = jnp.where(same & segment_lane, 1.0, 0.0)
        key_extra = jnp.where(
            segment_lane,
            jnp.where(same, 0.0, masked_score),
            jnp.where((lane >= HEAD_DIM + 3) & (lane < HEAD_DIM + 6), -1.0, 0.0),
        )
        value_extra = jnp.where(
            lane == HEAD_DIM,
            1.0,
            jnp.where((lane == HEAD_DIM + 1) | (lane == HEAD_DIM + 2), -1.0, 0.0),
        )
        all_columns = projected[rows, :].astype(jnp.float32)
        for head in range(head_local):
            for which, (ref, extra, factor) in enumerate(
                (
                    (query_aux, query_extra, HEAD_DIM**-0.5),
                    (key_aux, key_extra, 1.0),
                    (value_aux, value_extra, 1.0),
                )
            ):
                at = (3 * head + which) * HEAD_DIM
                part = jnp.concatenate([all_columns[:, at : at + HEAD_DIM] * factor, blank], axis=1)
                ref[head, rows, :] = jnp.where(lane < HEAD_DIM, part, extra).astype(low)
        return carry

    lax.fori_loop(0, seq_len // block, prepare, 0)

    def attend(step, carry):
        rows = pl.ds(pl.multiple_of(step * block, block), block)
        done = []
        for head in range(head_local):
            query = query_aux[head, rows, :]
            scores = contract_cols(query, key_aux[head])
            row_max = jnp.max(scores, axis=1, keepdims=True)
            exponent = jnp.exp(scores - row_max).astype(low)
            output = jnp.dot(exponent, value_aux[head], preferred_element_type=jnp.float32)
            totals = output[:, HEAD_DIM : HEAD_DIM + 1]
            done.append(output[:, :HEAD_DIM] / totals)
            logsum = row_max + jnp.log(totals)
            first = logsum.astype(low).astype(jnp.float32)
            second = (logsum - first).astype(low).astype(jnp.float32)
            third = logsum - first - second
            wide = query.astype(jnp.float32)
            wide = jnp.where(lane == HEAD_DIM + 3, first, wide)
            wide = jnp.where(lane == HEAD_DIM + 4, second, wide)
            wide = jnp.where(lane == HEAD_DIM + 5, third, wide)
            query_aux[head, rows, :] = wide.astype(low)
        attended[rows, :] = jnp.concatenate(done, axis=1).astype(low)
        return carry

    lax.fori_loop(0, seq_len // block, attend, 0)


def attend_pallas(projected, segments):
    seq_len, width = projected.shape
    head_local = width // (3 * HEAD_DIM)
    aux = jax.ShapeDtypeStruct((head_local, seq_len, AUX), jnp.bfloat16)
    whole = pl.BlockSpec(memory_space=pltpu.VMEM)
    return pl.pallas_call(
        attend_kernel,
        out_shape=(
            jax.ShapeDtypeStruct((seq_len, head_local * HEAD_DIM), jnp.bfloat16),
            aux,
            aux,
            aux,
        ),
        in_specs=[whole, whole],
        out_specs=(whole,) * 4,
        compiler_params=pltpu.CompilerParams(vmem_limit_bytes=VMEM_LIMIT),
        cost_estimate=pl.CostEstimate(
            flops=4 * head_local * seq_len * seq_len * AUX,
            bytes_accessed=8 * seq_len * width,
            transcendentals=head_local * seq_len * seq_len,
        ),
        name="attend",
    )(projected, segments.reshape(seq_len, 1))


def attend_back_kernel(
    attended, attended_grad, query_aux, key_aux, value_aux, projected_grad, grad_aux, key_turned, query_total
):
    seq_len, width = attended.shape
    head_local = width // HEAD_DIM
    block = min(KEY_BLOCK, seq_len)
    lane = lax.broadcasted_iota(jnp.int32, (block, AUX), 1)
    low = jnp.bfloat16
    blank = jnp.zeros((block, AUX - HEAD_DIM), jnp.float32)

    def prepare(step, carry):
        rows = pl.ds(pl.multiple_of(step * block, block), block)
        upstream = attended_grad[rows, :].astype(jnp.float32)
        product = upstream * attended[rows, :].astype(jnp.float32)
        for head in range(head_local):
            columns = slice(head * HEAD_DIM, (head + 1) * HEAD_DIM)
            row_dot = jnp.sum(product[:, columns], axis=1, keepdims=True)
            first = row_dot.astype(low).astype(jnp.float32)
            wide = jnp.concatenate([upstream[:, columns], blank], axis=1)
            wide = jnp.where(lane == HEAD_DIM + 1, first, wide)
            wide = jnp.where(lane == HEAD_DIM + 2, row_dot - first, wide)
            grad_aux[head, rows, :] = wide.astype(low)
            key_turned[head, :, rows] = key_aux[head, rows, :].T[:HEAD_DIM]
        return carry

    lax.fori_loop(0, seq_len // block, prepare, 0)
    query_total[...] = jnp.zeros_like(query_total)

    def back(step, carry):
        rows = pl.ds(pl.multiple_of(step * block, block), block)
        for head in range(head_local):
            scores = contract_cols(key_aux[head, rows, :], query_aux[head])
            chances = jnp.exp(scores)
            chance_grad = contract_cols(value_aux[head, rows, :], grad_aux[head])
            score_grad = (chances * chance_grad).astype(low)
            value_grad = jnp.dot(
                chances.astype(low), grad_aux[head], preferred_element_type=jnp.float32
            )
            key_grad = jnp.dot(score_grad, query_aux[head], preferred_element_type=jnp.float32)
            query_total[head] += jnp.dot(
                key_turned[head, :, rows], score_grad, preferred_element_type=jnp.float32
            )
            at = 3 * head * HEAD_DIM
            pair = jnp.concatenate([key_grad[:, :HEAD_DIM], value_grad[:, :HEAD_DIM]], axis=1)
            projected_grad[rows, at + HEAD_DIM : at + 3 * HEAD_DIM] = pair.astype(low)
        return carry

    lax.fori_loop(0, seq_len // block, back, 0)

    def finish(step, carry):
        rows = pl.ds(pl.multiple_of(step * block, block), block)
        for head in range(head_local):
            query_grad = query_total[head, :, rows].T * HEAD_DIM**-0.5
            at = 3 * head * HEAD_DIM
            projected_grad[rows, at : at + HEAD_DIM] = query_grad.astype(low)
        return carry

    lax.fori_loop(0, seq_len // block, finish, 0)


def attend_back_pallas(attended, attended_grad, query_aux, key_aux, value_aux):
    seq_len, width = attended.shape
    head_local = width // HEAD_DIM
    whole = pl.BlockSpec(memory_space=pltpu.VMEM)
    return pl.pallas_call(
        attend_back_kernel,
        out_shape=jax.ShapeDtypeStruct((seq_len, 3 * width), jnp.bfloat16),
        in_specs=[whole] * 5,
        out_specs=whole,
        scratch_shapes=[
            pltpu.VMEM((head_local, seq_len, AUX), jnp.bfloat16),
            pltpu.VMEM((head_local, HEAD_DIM, seq_len), jnp.bfloat16),
            pltpu.VMEM((head_local, HEAD_DIM, seq_len), jnp.float32),
        ],
        compiler_params=pltpu.CompilerParams(vmem_limit_bytes=VMEM_LIMIT),
        cost_estimate=pl.CostEstimate(
            flops=10 * head_local * seq_len * seq_len * AUX,
            bytes_accessed=10 * seq_len * width,
            transcendentals=head_local * seq_len * seq_len,
        ),
        name="attend_back",
    )(attended, attended_grad, query_aux, key_aux, value_aux)


EXACT_THREE = lax.Precision.HIGH
SIDE = 256


def swap_bit(values, axis_name, bit):
    count = lax.axis_size(axis_name)
    return lax.ppermute(values, axis_name, [(i, i ^ bit) for i in range(count)])


def data_bits():
    return [1 << k for k in range(1, lax.axis_size("dp").bit_length() - 1)]


def has_bit(index, bit):
    return (index & bit) != 0


def gather_bits_absolute(block, bits):
    index = lax.axis_index("dp")
    for bit in bits:
        other = swap_bit(block, "dp", bit)
        mine = has_bit(index, bit)
        block = jnp.concatenate(
            [jnp.where(mine, other, block), jnp.where(mine, block, other)], axis=0
        )
    return block


def scatter_bits_absolute(total, bits, wire):
    index = lax.axis_index("dp")
    for bit in reversed(bits):
        half = total.shape[0] // 2
        low, high = total[:half], total[half:]
        mine = has_bit(index, bit)
        arrived = swap_bit(jnp.where(mine, low, high).astype(wire), "dp", bit)
        total = jnp.where(mine, high, low).astype(jnp.float32) + arrived.astype(jnp.float32)
    return total


def line_up(values):
    count = lax.axis_size("tensor")
    return lax.ppermute(values, "tensor", [(i, i + 1) for i in range(count - 1)])


def line_down(values):
    count = lax.axis_size("tensor")
    return lax.ppermute(values, "tensor", [(i + 1, i) for i in range(count - 1)])


def gather_line(block):
    count = lax.axis_size("tensor")
    index = lax.axis_index("tensor")
    below, above = [block], [block]
    for step in range(count - 1):
        below.append(line_up(below[-1]))
        above.append(line_down(above[-1]))
    parts = [block]
    for offset in range(1, count):
        parts.append(jnp.where(index + offset < count, above[offset], below[count - offset]))
    return parts


def scatter_line(parts, wire):
    count = lax.axis_size("tensor")
    index = lax.axis_index("tensor")
    upward, downward = None, None
    for offset in range(count - 1, 0, -1):
        send_up = parts[offset].astype(jnp.float32)
        send_down = parts[count - offset].astype(jnp.float32)
        if upward is not None:
            send_up = send_up + upward.astype(jnp.float32)
            send_down = send_down + downward.astype(jnp.float32)
        upward = line_up(jnp.where(index + offset < count, send_up, 0.0).astype(wire))
        downward = line_down(jnp.where(index >= offset, send_down, 0.0).astype(wire))
    return parts[0].astype(jnp.float32) + upward.astype(jnp.float32) + downward.astype(jnp.float32)


def pair_permute(values, where_to):
    data_count, tensor_count = lax.axis_size("dp"), lax.axis_size("tensor")
    moves = []
    for i in range(data_count):
        for j in range(tensor_count):
            target = where_to(i, j)
            if target is not None:
                moves.append((i * tensor_count + j, target[0] * tensor_count + target[1]))
    return lax.ppermute(values, ("dp", "tensor"), moves)


def exchange_home(values):
    return pair_permute(
        values, lambda i, j: (i ^ 1, j ^ 2) if (i & 1) != (j >> 1) else None
    )


def group_swap(values, member):
    if member == 1:
        return swap_bit(values, "dp", 1)
    if member == 2:
        return swap_bit(values, "tensor", 1)
    return pair_permute(values, lambda i, j: (i ^ 1, j ^ 1))


def gather_head_group(shard):
    first = []
    for core in (0, 1):
        got = []
        for half in (0, 1):
            got.append(
                pair_permute(
                    shard,
                    lambda i, j: (i - core + (j & 1), (j >> 1) + 2 * half)
                    if (i & 1) == core
                    else None,
                )
            )
        first.append(jnp.where(lax.axis_index("tensor") >= 2, got[1], got[0]))
    return gather_bits_absolute(jnp.concatenate(first, axis=0), data_bits())


def scatter_head_group(total, wire):
    total = scatter_bits_absolute(total, data_bits(), wire)
    rows = total.shape[0] // 2
    result = None
    for core in (0, 1):
        piece = total[core * rows : (core + 1) * rows].astype(wire)
        arrived = None
        for half in (0, 1):
            got = pair_permute(
                piece,
                lambda i, j: ((i & ~1) + core, 2 * (j & 1) + (i & 1))
                if (j >> 1) == half
                else None,
            ).astype(jnp.float32)
            arrived = got if arrived is None else arrived + got
        result = arrived if core == 0 else jnp.where((lax.axis_index("dp") & 1) == 1, arrived, result)
    return result


def gather_units(pair):
    parts = jnp.stack(gather_line(pair))
    bits = data_bits()
    both = []
    for which, order in ((0, bits), (1, bits[::-1])):
        block = parts[:, which]
        done = []
        for bit in order:
            other = swap_bit(block, "dp", bit)
            place = sum(1 for b in done if b > bit)
            block = jnp.stack([block, other], axis=place)
            done.append(bit)
        other = swap_bit(block, "dp", 1)
        both.append((block.reshape(-1, block.shape[-1]), other.reshape(-1, block.shape[-1])))
    return both


def scatter_units(mine, theirs, order, wire):
    total = mine + swap_bit(theirs.astype(wire), "dp", 1).astype(jnp.float32)
    bits = data_bits()
    count = lax.axis_size("tensor")
    width = total.shape[-1]
    rows = total.shape[0] // (count << len(bits))
    total = total.reshape((2,) * len(bits) + (count, rows, width))
    left = sorted(bits, reverse=True)
    for bit in order:
        place = left.index(bit)
        keep = lax.index_in_dim(total, 0, place, keepdims=False)
        send = lax.index_in_dim(total, 1, place, keepdims=False)
        total = keep + swap_bit(send.astype(wire), "dp", bit).astype(jnp.float32)
        left.remove(bit)
    return scatter_line([total[k] for k in range(count)], wire)


def pack_symmetric(gram):
    return jnp.concatenate(
        [gram[k : k + SIDE, k:] for k in range(0, gram.shape[0], SIDE)], axis=1
    )


def unpack_symmetric(packed, size):
    rows, at = [], 0
    for k in range(0, size, SIDE):
        rows.append(packed[:, at : at + size - k])
        at += size - k
    full = []
    for i in range(len(rows)):
        blocks = [rows[j][:, (i - j) * SIDE : (i - j + 1) * SIDE].T for j in range(i)]
        full.append(jnp.concatenate(blocks + [rows[i]], axis=1))
    return jnp.concatenate(full, axis=0)


def sum_over_chips(packed):
    count = lax.axis_size("tensor")
    index = lax.axis_index("tensor")
    part = scatter_bits_absolute(packed, data_bits(), jnp.float32)
    part = part.reshape(count, part.shape[0] // count, part.shape[1])
    ring = (index + jnp.arange(count)) % count
    turned = jnp.take(part, ring, axis=0)
    own = scatter_line([turned[k] for k in range(count)], jnp.float32)
    parts = jnp.stack(gather_line(own))
    part = jnp.take(parts, (jnp.arange(count) - index) % count, axis=0)
    part = part.reshape(count * part.shape[1], part.shape[2])
    return gather_bits_absolute(part, data_bits())


def sum_over_all(values):
    for bit in (1, 2):
        values = values + swap_bit(values, "tensor", bit)
    for bit in [1] + data_bits():
        values = values + swap_bit(values, "dp", bit)
    return values


def polynomial_chain(gram, product):
    identity = jnp.eye(gram.shape[-1], dtype=jnp.float32)
    chain = None
    for step in range(NEWTON_STEPS):
        square = product(gram, gram)
        factor = newton_linear * identity + newton_cubic * gram + newton_quintic * square
        chain = factor if chain is None else product(chain, factor)
        if step < NEWTON_STEPS - 1:
            gram = product(product(gram, factor), factor)
    return chain


def per_device(
    tokens,
    segment_ids,
    out_grad,
    heads_weight,
    merge_weight,
    expand_weight,
    reduce_weight,
    heads_momentum,
    merge_momentum,
    expand_momentum,
    reduce_momentum,
    heads_average,
    merge_average,
    expand_average,
    reduce_average,
    vectors,
    vector_momentum,
    vector_average,
):
    low = jnp.bfloat16
    tensor_count = lax.axis_size("tensor")
    data_count = lax.axis_size("dp")
    tensor_index = lax.axis_index("tensor")
    core = lax.axis_index("dp") & 1
    row_count = tokens.shape[0]
    seq_len = row_count * tensor_count
    head_local = heads_weight.shape[1] // (3 * HEAD_DIM)
    group_width = head_local * HEAD_DIM
    at_home = core == (tensor_index >> 1)
    group = 2 * (tensor_index & 1) + core

    own_tokens = jnp.where(at_home, tokens, exchange_home(tokens))
    across = swap_bit(own_tokens, "tensor", 1)
    full_heads = gather_head_group(heads_weight.astype(low))
    beside = swap_bit(own_tokens, "dp", 1)
    diagonal = swap_bit(across, "dp", 1)
    token_chunks = jnp.stack([own_tokens, beside, across, diagonal])
    own_segments = jnp.where(at_home, segment_ids, swap_bit(segment_ids, "dp", 1))
    chunk_at = []
    for member in range(4):
        its_core, its_tensor = core ^ (member & 1), tensor_index ^ (member >> 1)
        chunk_at.append(jnp.where(its_core == (its_tensor >> 1), its_tensor, its_tensor ^ 2))
    segments = jnp.take(
        own_segments.reshape(tensor_count, row_count), jnp.stack(chunk_at), axis=0
    ).reshape(seq_len)
    sent_grad = lax.dynamic_slice_in_dim(out_grad, (tensor_index ^ 2) * row_count, row_count, 0)
    home_grad = lax.dynamic_slice_in_dim(out_grad, tensor_index * row_count, row_count, 0)
    own_grad = jnp.where(at_home, home_grad, swap_bit(sent_grad, "dp", 1))

    (expand_mine, expand_other), (reduce_mine, reduce_other) = gather_units(
        jnp.stack([expand_weight.T.astype(low), reduce_weight.astype(low)])
    )
    merge_rows = jnp.stack(gather_line(merge_weight.T.astype(low)), axis=1)
    merge_rows = gather_bits_absolute(merge_rows, [1] + data_bits())
    in_groups = ((group ^ jnp.arange(tensor_count)) - tensor_index) % tensor_count
    full_merge = jnp.take(merge_rows, in_groups, axis=1).reshape(D, D)

    dense_full = token_chunks.reshape(seq_len, D).astype(jnp.float32)
    normed_full, _ = center_scale(dense_full)
    first_full = (normed_full * vectors[0] + vectors[1]).astype(low)
    dense_rows = own_tokens.astype(jnp.float32)
    normed_one, inverse_one = center_scale(dense_rows)
    projected = jnp.dot(first_full, full_heads, preferred_element_type=jnp.float32)
    attended_full, query_aux, key_aux, value_aux = attend_pallas(projected.astype(low), segments)
    attended = attended_full.reshape(4, row_count, group_width)
    attended_own = jnp.concatenate(
        [attended[0]] + [group_swap(attended[k], k) for k in (1, 2, 3)], axis=1
    )
    merged = contract_cols(attended_own, full_merge)
    middle = dense_rows + merged + vectors[4]
    normed_two, inverse_two = center_scale(middle)
    second_in = (normed_two * vectors[2] + vectors[3]).astype(low)

    layer_sum = middle + vectors[5]
    second_grad = 0.0
    unit_sums = []
    for expand_half, reduce_half in ((expand_mine, reduce_mine), (expand_other, reduce_other)):
        expanded = contract_cols(second_in, expand_half)
        activated, gelu_pull = jax.vjp(gelu_exact, expanded)
        hidden = activated.astype(low)
        layer_sum = layer_sum + jnp.dot(hidden, reduce_half, preferred_element_type=jnp.float32)
        reduce_sum = contract_rows(hidden, own_grad)
        (expand_grad,) = gelu_pull(contract_cols(own_grad, reduce_half))
        expand_low = expand_grad.astype(low)
        expand_sum = contract_rows(expand_low, second_in)
        second_grad = second_grad + jnp.dot(
            expand_low, expand_half, preferred_element_type=jnp.float32
        )
        unit_sums.append((expand_sum, reduce_sum))
    output_rows = layer_sum.astype(low)
    layer_output = jnp.where(at_home, output_rows, exchange_home(output_rows))

    bits = data_bits()
    expand_rows = scatter_units(unit_sums[0][0], unit_sums[1][0], bits[::-1], low)
    reduce_gradient = scatter_units(unit_sums[0][1], unit_sums[1][1], bits, low)
    expand_gradient = expand_rows.T
    expand_new_momentum = momentum_decay * expand_momentum + expand_gradient
    reduce_new_momentum = momentum_decay * reduce_momentum + reduce_gradient
    expand_part = expand_new_momentum.T
    reduce_part = reduce_new_momentum
    expand_gram = lax.dot_general(
        expand_part, expand_part, (((0,), (0,)), ((), ())), precision=EXACT_THREE
    )
    reduce_gram = lax.dot_general(
        reduce_part, reduce_part, (((0,), (0,)), ((), ())), precision=EXACT_THREE
    )
    expand_gram, reduce_gram = pack_symmetric(expand_gram), pack_symmetric(reduce_gram)
    first_core = core == 0
    wide_gram = jnp.where(first_core, expand_gram, reduce_gram) + swap_bit(
        jnp.where(first_core, reduce_gram, expand_gram), "dp", 1
    )
    wide_gram = unpack_symmetric(sum_over_chips(wide_gram), D)

    middle_grad = own_grad.astype(jnp.float32) + norm_backward(
        second_grad, normed_two, inverse_two, vectors[2]
    )
    middle_low = middle_grad.astype(low)
    attended_grad = jnp.dot(middle_low, full_merge, preferred_element_type=jnp.float32).astype(low)
    grad_parts = [attended_grad[:, k * group_width : (k + 1) * group_width] for k in range(4)]
    attended_grad = jnp.concatenate(
        [grad_parts[0]] + [group_swap(grad_parts[k], k) for k in (1, 2, 3)], axis=0
    )
    merge_sum = contract_rows(middle_low, attended_own)
    merge_sum = merge_sum.astype(low).reshape(D, 4, group_width)
    turned = group ^ ((tensor_index + jnp.arange(tensor_count)) % tensor_count)
    merge_sum = jnp.take(merge_sum, turned, axis=1)
    merge_sum = scatter_line([merge_sum[:, k] for k in range(tensor_count)], low)
    merge_gradient = scatter_bits_absolute(merge_sum, [1] + data_bits(), low).T

    projected_grad = attend_back_pallas(
        attended_full, attended_grad, query_aux, key_aux, value_aux
    )
    heads_sum = contract_rows(first_full, projected_grad)
    heads_gradient = scatter_head_group(heads_sum, low)
    first_parts = contract_cols(projected_grad, full_heads).reshape(4, row_count, D)
    kept = first_parts[0::2] + swap_bit(first_parts[1::2].astype(low), "dp", 1).astype(jnp.float32)
    first_grad = kept[0] + swap_bit(kept[1].astype(low), "tensor", 1).astype(jnp.float32)
    input_rows = middle_grad + norm_backward(first_grad, normed_one, inverse_one, vectors[0])
    input_gradient = jnp.where(
        at_home, input_rows, exchange_home(input_rows.astype(low)).astype(jnp.float32)
    )
    vector_gradient = sum_over_all(
        jnp.stack(
            [
                jnp.sum(first_grad * normed_one, axis=0),
                jnp.sum(first_grad, axis=0),
                jnp.sum(second_grad * normed_two, axis=0),
                jnp.sum(second_grad, axis=0),
                jnp.sum(middle_grad, axis=0),
                jnp.sum(own_grad.astype(jnp.float32), axis=0),
            ]
        )
    )
    heads_new_momentum = momentum_decay * heads_momentum + heads_gradient
    merge_new_momentum = momentum_decay * merge_momentum + merge_gradient
    vector_new_momentum = momentum_decay * vector_momentum + vector_gradient

    heads_part = heads_new_momentum.reshape(heads_new_momentum.shape[0], head_local * 3, HEAD_DIM)
    merge_part = merge_new_momentum.reshape(head_local, HEAD_DIM, merge_new_momentum.shape[1])
    small_gram = jnp.concatenate(
        [
            jnp.einsum("rmd,rme->mde", heads_part, heads_part, precision=highest),
            jnp.einsum("hdc,hec->hde", merge_part, merge_part, precision=highest),
        ],
        axis=0,
    )
    for bit in [1] + data_bits():
        small_gram = small_gram + swap_bit(small_gram, "dp", bit)
    small_factor = 1.0 / (jnp.sqrt(jnp.trace(small_gram, axis1=1, axis2=2)) + newton_epsilon)
    small_chain = polynomial_chain(
        small_gram * (small_factor * small_factor)[:, None, None],
        lambda left, right: jnp.einsum("mde,mef->mdf", left, right, precision=highest),
    )
    small_chain = small_chain * small_factor[:, None, None]
    side_count = 3 * head_local
    heads_ortho = jnp.einsum("rmd,mde->rme", heads_part, small_chain[:side_count], precision=highest)
    merge_ortho = jnp.einsum("hde,hec->hdc", small_chain[side_count:], merge_part, precision=highest)

    wide_factor = 1.0 / (jnp.sqrt(jnp.trace(wide_gram)) + newton_epsilon)
    wide_chain = polynomial_chain(
        wide_gram * (wide_factor * wide_factor),
        lambda left, right: jnp.dot(left, right, precision=EXACT_THREE),
    )
    wide_chain = wide_chain * wide_factor
    other_chain = swap_bit(wide_chain, "dp", 1)
    expand_ortho = jnp.dot(
        expand_part, jnp.where(first_core, wide_chain, other_chain), precision=EXACT_THREE
    ).T
    reduce_ortho = jnp.dot(
        reduce_part, jnp.where(first_core, other_chain, wide_chain), precision=EXACT_THREE
    )

    keep_factor = 1.0 - muon_rate * weight_decay
    head_step = muon_rate * 0.2 * math.sqrt(max(D, HEAD_DIM))
    wide_step = muon_rate * 0.2 * math.sqrt(max(D, FF))
    heads_new_weight = heads_weight * keep_factor - head_step * heads_ortho.reshape(
        heads_weight.shape
    )
    merge_new_weight = merge_weight * keep_factor - head_step * merge_ortho.reshape(
        merge_weight.shape
    )
    expand_new_weight = expand_weight * keep_factor - wide_step * expand_ortho
    reduce_new_weight = reduce_weight * keep_factor - wide_step * reduce_ortho
    vector_new_value = vectors - vector_rate / math.sqrt(SEQ * data_count) * vector_new_momentum
    heads_new_average = average_decay * heads_average + (1.0 - average_decay) * heads_new_weight
    merge_new_average = average_decay * merge_average + (1.0 - average_decay) * merge_new_weight
    expand_new_average = average_decay * expand_average + (1.0 - average_decay) * expand_new_weight
    reduce_new_average = average_decay * reduce_average + (1.0 - average_decay) * reduce_new_weight
    vector_new_average = average_decay * vector_average + (1.0 - average_decay) * vector_new_value
    return (
        layer_output,
        input_gradient,
        heads_gradient,
        merge_gradient,
        expand_gradient,
        reduce_gradient,
        heads_new_momentum,
        merge_new_momentum,
        expand_new_momentum,
        reduce_new_momentum,
        heads_new_weight,
        merge_new_weight,
        expand_new_weight,
        reduce_new_weight,
        heads_new_average,
        merge_new_average,
        expand_new_average,
        reduce_new_average,
        vector_gradient,
        vector_new_momentum,
        vector_new_value,
        vector_new_average,
    )


def solution(mesh):
    placed = (
        P(("dp", "tensor"), None),
        P("dp"),
        P("dp", None),
        P("dp", "tensor"),
        P("tensor", "dp"),
        P(None, ("tensor", "dp")),
        P(("tensor", "dp"), None),
        P("dp", "tensor"),
        P("tensor", "dp"),
        P(None, ("tensor", "dp")),
        P(("tensor", "dp"), None),
        P("dp", "tensor"),
        P("tensor", "dp"),
        P(None, ("tensor", "dp")),
        P(("tensor", "dp"), None),
        P(),
        P(),
        P(),
    )
    return jax.shard_map(
        per_device,
        mesh=mesh,
        in_specs=placed,
        out_specs=(
            P(("dp", "tensor"), None),
            P(("dp", "tensor"), None),
            P("dp", "tensor"),
            P("tensor", "dp"),
            P(None, ("tensor", "dp")),
            P(("tensor", "dp"), None),
            P("dp", "tensor"),
            P("tensor", "dp"),
            P(None, ("tensor", "dp")),
            P(("tensor", "dp"), None),
            P("dp", "tensor"),
            P("tensor", "dp"),
            P(None, ("tensor", "dp")),
            P(("tensor", "dp"), None),
            P("dp", "tensor"),
            P("tensor", "dp"),
            P(None, ("tensor", "dp")),
            P(("tensor", "dp"), None),
            P(),
            P(),
            P(),
            P(),
        ),
        check_vma=False,
    )
```

```python
import math

import jax
import jax.numpy as jnp
from jax import lax
from jax.experimental import pallas as pl
from jax.experimental.pallas import tpu as pltpu
from jax.sharding import PartitionSpec as P

D = 768
HEAD_DIM = 64
FF = 3072
SEQ = 2048
NEWTON_STEPS = 5


highest = lax.Precision.HIGHEST
norm_epsilon = 1e-06
newton_epsilon = 1e-07
newton_linear = 3.4445
newton_cubic = -4.775
newton_quintic = 2.0315
momentum_decay = 0.5
average_decay = 0.9
muon_rate = 0.2
weight_decay = 0.1
vector_rate = 0.15
masked_score = -1e30
VMEM_LIMIT = 56 * 2**20


def center_scale(values):
    average = jnp.mean(values, axis=-1, keepdims=True)
    centered = values - average
    inverse = lax.rsqrt(jnp.mean(centered * centered, axis=-1, keepdims=True) + norm_epsilon)
    return (centered * inverse, inverse)


def norm_backward(upstream, normed, inverse, gain):
    scaled = upstream * gain
    mean_one = jnp.mean(scaled, axis=-1, keepdims=True)
    mean_two = jnp.mean(scaled * normed, axis=-1, keepdims=True)
    return inverse * (scaled - mean_one - normed * mean_two)


def gelu_exact(values):
    return jax.nn.gelu(values, approximate=False)


def contract_rows(left_side, right_side):
    return lax.dot_general(
        left_side, right_side, (((0,), (0,)), ((), ())), preferred_element_type=jnp.float32
    )


def contract_cols(left_side, right_side):
    return lax.dot_general(
        left_side, right_side, (((1,), (1,)), ((), ())), preferred_element_type=jnp.float32
    )


KEY_BLOCK = 256
AUX = 128


MESH = pl.DeviceIdType.MESH


def low_rank_bits(data_count):
    return [1 << k for k in range(1, data_count.bit_length() - 1)]


class Wires:
    def __init__(self, send, receive):
        self.send, self.receive, self.used = send, receive, 0

    def number(self):
        self.used += 1
        return self.used - 1

    def start(self, k, source, target, device):
        copy = pltpu.make_async_remote_copy(
            source, target, self.send.at[k], self.receive.at[k], device_id=device, device_id_type=MESH
        )
        copy.start()

    def sent(self, k, source, device):
        pltpu.make_async_remote_copy(
            source, source, self.send.at[k], self.receive.at[k], device_id=device, device_id_type=MESH
        ).wait_send()

    def arrived(self, k, target, device):
        pltpu.make_async_remote_copy(
            target, target, self.send.at[k], self.receive.at[k], device_id=device, device_id_type=MESH
        ).wait_recv()


def greet(devices):
    barrier = pltpu.get_barrier_semaphore()
    for device in devices:
        pl.semaphore_signal(barrier, inc=1, device_id=device, device_id_type=MESH)
    pl.semaphore_wait(barrier, len(devices))


def column_and_plane(data, tensor, data_count, tensor_count):
    found = []
    for core in (0, 1):
        for step in range(tensor_count):
            if core or step:
                found.append((data ^ core, lax.rem(tensor + step, tensor_count)))
    for k in range(1, data_count // 2):
        found.append((data ^ (2 * k), tensor))
    return found


def front_kernel(
    data_count,
    tensor_count,
    gather_heads,
    tokens,
    heads,
    expand,
    reduce,
    merge,
    vectors,
    segment_column,
    attended,
    attended_rows,
    query_aux,
    key_aux,
    value_aux,
    first_full,
    chunks,
    all_heads,
    all_expand,
    all_reduce,
    all_merge,
    arrivals,
    send,
    receive,
    local,
):
    low = jnp.bfloat16
    rows, width = tokens.shape
    head_local = query_aux.shape[0]
    group_width = head_local * HEAD_DIM
    data, tensor = lax.axis_index("dp"), lax.axis_index("tensor")
    core, half = data & 1, tensor >> 1
    home = core == half
    group = 2 * (tensor & 1) + core
    wires = Wires(send, receive)
    beside, across, diagonal = (data ^ 1, tensor), (data, tensor ^ 1), (data ^ 1, tensor ^ 1)
    members = [None, beside, across, diagonal]
    away = (data ^ 1, tensor ^ 2)
    pieces = [pl.ds(p * (rows // 2), rows // 2) for p in range(2)]
    pending = []

    def begin(k, source, target, device, when=None):
        if when is None:
            wires.start(k, source, target, device)
        else:

            @pl.when(when)
            def _():
                wires.start(k, source, target, device)

        pending.append((k, source, device, when))

    def await_arrival(k, target, device, when=None):
        if when is None:
            wires.arrived(k, target, device)
        else:

            @pl.when(when)
            def _():
                wires.arrived(k, target, device)

    mats = [all_expand, all_reduce, all_merge]
    own = []
    for k, (source, target) in enumerate(zip((expand, reduce, merge), mats)):
        copy = pltpu.make_async_copy(source, target.at[data, tensor], local.at[k])
        copy.start()
        own.append(copy)
    greet(column_and_plane(data, tensor, data_count, tensor_count))

    pair = (data >> 1) * 2
    if gather_heads:
        head_numbers = [wires.number() for _ in range(4)]
        for k in (0, 1):
            target = (pair + (tensor & 1), (tensor >> 1) + 2 * k)
            itself = (target[0] == data) & (target[1] == tensor)
            for c in (0, 1):
                begin(
                    head_numbers[2 * k + c],
                    heads,
                    all_heads.at[data],
                    target,
                    jnp.logical_not(itself) & (core == c),
                )

            @pl.when(itself)
            def _():
                all_heads[data] = heads[...]

    numbers = [wires.number() for _ in range(12)]
    for p, piece in enumerate(pieces):
        begin(numbers[p], tokens.at[piece], chunks.at[2, piece], across, home)
        begin(numbers[2 + p], tokens.at[piece], chunks.at[0, piece], away, jnp.logical_not(home))
        begin(numbers[4 + p], tokens.at[piece], chunks.at[1, piece], beside, home)

    @pl.when(home)
    def _():
        chunks[0] = tokens[...]

    if gather_heads:
        for k in (0, 1):
            for c in (0, 1):
                source = (pair + c, group)
                itself = (source[0] == data) & (source[1] == tensor)
                await_arrival(
                    head_numbers[2 * k + c],
                    all_heads.at[pair + c],
                    source,
                    jnp.logical_not(itself) & (half == k),
                )
        plane = []
        for k in range(1, data_count // 2):
            number = wires.number()
            plane.append((number, k))
            begin(number, all_heads.at[pl.ds(pair, 2)], all_heads.at[pl.ds(pair, 2)], (data ^ (2 * k), tensor))

    for p, piece in enumerate(pieces):
        await_arrival(numbers[2 + p], chunks.at[0, piece], away, jnp.logical_not(home))
        begin(numbers[6 + p], chunks.at[0, piece], chunks.at[2, piece], across, jnp.logical_not(home))
        begin(numbers[8 + p], chunks.at[0, piece], chunks.at[1, piece], beside, jnp.logical_not(home))

    if gather_heads:
        for number, k in plane:
            there = pl.ds(pair ^ (2 * k), 2)
            await_arrival(number, all_heads.at[there], (data ^ (2 * k), tensor))

    block = min(KEY_BLOCK, rows)
    lane = lax.broadcasted_iota(jnp.int32, (block, AUX), 1)
    blank = jnp.zeros((block, AUX - HEAD_DIM), jnp.float32)
    steps = rows // block

    def prepare(member):
        def one(step, carry):
            inside = pl.ds(pl.multiple_of(step * block, block), block)
            at_rows = pl.ds(pl.multiple_of(member * rows + step * block, block), block)
            normed, _ = center_scale(chunks[member, inside, :].astype(jnp.float32))
            first_in = (normed * vectors[0:1, :] + vectors[1:2, :]).astype(low)
            first_full[at_rows, :] = first_in
            weight = all_heads[...].reshape(width, 3 * group_width)
            projected = jnp.dot(first_in, weight, preferred_element_type=jnp.float32)
            projected = projected.astype(low).astype(jnp.float32)
            same = lane - HEAD_DIM == segment_column[at_rows, :]
            segment_lane = (lane >= HEAD_DIM) & (lane < HEAD_DIM + 3)
            query_extra = jnp.where(same & segment_lane, 1.0, 0.0)
            key_extra = jnp.where(
                segment_lane,
                jnp.where(same, 0.0, masked_score),
                jnp.where((lane >= HEAD_DIM + 3) & (lane < HEAD_DIM + 6), -1.0, 0.0),
            )
            value_extra = jnp.where(
                lane == HEAD_DIM,
                1.0,
                jnp.where((lane == HEAD_DIM + 1) | (lane == HEAD_DIM + 2), -1.0, 0.0),
            )
            for head in range(head_local):
                for which, (ref, extra, factor) in enumerate(
                    (
                        (query_aux, query_extra, HEAD_DIM**-0.5),
                        (key_aux, key_extra, 1.0),
                        (value_aux, value_extra, 1.0),
                    )
                ):
                    at = (3 * head + which) * HEAD_DIM
                    part = jnp.concatenate([projected[:, at : at + HEAD_DIM] * factor, blank], axis=1)
                    ref[head, at_rows, :] = jnp.where(lane < HEAD_DIM, part, extra).astype(low)
            return carry

        lax.fori_loop(0, steps, one, 0)

    def attend(member):
        def one(step, carry):
            inside = pl.ds(pl.multiple_of(step * block, block), block)
            at_rows = pl.ds(pl.multiple_of(member * rows + step * block, block), block)
            done = []
            for head in range(head_local):
                query = query_aux[head, at_rows, :]
                scores = contract_cols(query, key_aux[head])
                row_max = jnp.max(scores, axis=1, keepdims=True)
                exponent = jnp.exp(scores - row_max).astype(low)
                output = jnp.dot(exponent, value_aux[head], preferred_element_type=jnp.float32)
                totals = output[:, HEAD_DIM : HEAD_DIM + 1]
                done.append(output[:, :HEAD_DIM] / totals)
                logsum = row_max + jnp.log(totals)
                first = logsum.astype(low).astype(jnp.float32)
                second = (logsum - first).astype(low).astype(jnp.float32)
                third = logsum - first - second
                wide = query.astype(jnp.float32)
                wide = jnp.where(lane == HEAD_DIM + 3, first, wide)
                wide = jnp.where(lane == HEAD_DIM + 4, second, wide)
                wide = jnp.where(lane == HEAD_DIM + 5, third, wide)
                query_aux[head, at_rows, :] = wide.astype(low)
            attended[member, inside, :] = jnp.concatenate(done, axis=1).astype(low)
            return carry

        lax.fori_loop(0, steps, one, 0)

    prepare(0)
    for p, piece in enumerate(pieces):
        await_arrival(numbers[p], chunks.at[2, piece], across, home)
        await_arrival(numbers[6 + p], chunks.at[2, piece], across, jnp.logical_not(home))
        begin(numbers[10 + p], chunks.at[2, piece], chunks.at[3, piece], beside)

    def z_hop(hop):
        made = []
        for mat, single in zip(mats, (expand, reduce, merge)):
            for way in (1, -1):
                number = wires.number()
                slot = tensor - way * (hop - 1)
                going = (tensor + way >= 0) & (tensor + way < tensor_count)
                going = going & (slot >= 0) & (slot < tensor_count)
                source = single if hop == 1 else mat.at[data, slot]
                begin(number, source, mat.at[data, slot], (data, tensor + way), going)
                made.append((number, mat, tensor - way * hop, tensor - way))
        return made

    def z_wait(made):
        for number, mat, slot, source in made:
            valid = (slot >= 0) & (slot < tensor_count)
            await_arrival(number, mat.at[data, slot], (data, source), valid)

    def bit_step(plan):
        made = []
        for mat, bit, held in plan:
            for offset in held:
                number = wires.number()
                place = data ^ offset
                begin(number, mat.at[place], mat.at[place], (data ^ bit, tensor))
                made.append((number, mat, place ^ bit, bit))
        return made

    def bit_wait(made):
        for number, mat, place, bit in made:
            await_arrival(number, mat.at[place], (data ^ bit, tensor))

    made = z_hop(1)
    for p, piece in enumerate(pieces):
        await_arrival(numbers[4 + p], chunks.at[1, piece], beside, jnp.logical_not(home))
        await_arrival(numbers[8 + p], chunks.at[1, piece], beside, home)
    prepare(1)
    prepare(2)
    for p, piece in enumerate(pieces):
        await_arrival(numbers[10 + p], chunks.at[3, piece], beside)
    prepare(3)

    bits = low_rank_bits(data_count)
    schedule, held = [], [[0], [0], [0]]
    for k in range(len(bits)):
        plan = []
        for m, mat in enumerate(mats):
            bit = bits[k] if m == 0 else bits[-1 - k]
            plan.append((mat, bit, list(held[m])))
            held[m] = held[m] + [offset ^ bit for offset in held[m]]
        schedule.append(plan)
    schedule.append([(mat, 1, list(held[m])) for m, mat in enumerate(mats)])

    exchange = {}
    z_wait(made)
    made = z_hop(2)
    for member in (3, 2, 1, 0):
        attend(member)
        if member:
            number = wires.number()
            begin(number, attended.at[member], arrivals.at[group], members[member])
            exchange[member] = number
        else:
            arrivals[group] = attended[0]
        if member == 3:
            z_wait(made)
            made = z_hop(3)
        elif member == 2:
            z_wait(made)
            for copy in own:
                copy.wait()
            made = bit_step(schedule[0])
        elif member == 1:
            bit_wait(made)
            made = bit_step(schedule[1])
    for plan in schedule[2:]:
        bit_wait(made)
        made = bit_step(plan)
    for member, number in exchange.items():
        await_arrival(number, arrivals.at[group ^ member], members[member])
    attended_rows[...] = jnp.concatenate([arrivals[k] for k in range(4)], axis=1)
    bit_wait(made)
    for k, source, device, when in pending:
        if when is None:
            wires.sent(k, source, device)
        else:

            @pl.when(when)
            def _():
                wires.sent(k, source, device)


def front_pallas(tokens, heads, expand, reduce, merge, vectors, segments, gather_heads):
    data_count, tensor_count = lax.axis_size("dp"), lax.axis_size("tensor")
    rows, width = tokens.shape
    low = jnp.bfloat16
    head_columns = heads.shape[-1]
    head_local = head_columns // (3 * HEAD_DIM)
    seq_len = segments.shape[0]
    group_width = head_local * HEAD_DIM
    aux = jax.ShapeDtypeStruct((head_local, seq_len, AUX), low)
    inside = pl.BlockSpec(memory_space=pltpu.VMEM)
    anywhere = pl.BlockSpec(memory_space=pl.ANY)
    gathered = [
        jax.ShapeDtypeStruct((data_count, tensor_count) + block.shape, low)
        for block in (expand, reduce, merge)
    ]
    hops = 6 * (tensor_count - 1) + 3 * (data_count - 1)
    copies = 4 + data_count // 2 + 12 + hops + 3
    if gather_heads:
        heads_out = jax.ShapeDtypeStruct((data_count,) + heads.shape, low)
    else:
        heads_out = jax.ShapeDtypeStruct(heads.shape, low)

    def kernel(*refs):
        if not gather_heads:
            refs = list(refs)
            refs[14] = refs[1]
        front_kernel(data_count, tensor_count, gather_heads, *refs)

    return pl.pallas_call(
        kernel,
        out_shape=(
            jax.ShapeDtypeStruct((4, rows, group_width), low),
            jax.ShapeDtypeStruct((rows, 4 * group_width), low),
            aux,
            aux,
            aux,
            jax.ShapeDtypeStruct((seq_len, width), low),
            jax.ShapeDtypeStruct((4, rows, width), low),
            heads_out,
            *gathered,
        ),
        in_specs=[inside] * 7,
        out_specs=(inside,) * 8 + (anywhere,) * 3,
        scratch_shapes=[
            pltpu.VMEM((4, rows, group_width), low),
            pltpu.SemaphoreType.DMA((copies,)),
            pltpu.SemaphoreType.DMA((copies,)),
            pltpu.SemaphoreType.DMA((3,)),
        ],
        compiler_params=pltpu.CompilerParams(
            vmem_limit_bytes=VMEM_LIMIT, collective_id=1, has_side_effects=True
        ),
        cost_estimate=pl.CostEstimate(
            flops=4 * head_local * seq_len * seq_len * AUX,
            bytes_accessed=8 * seq_len * width,
            transcendentals=head_local * seq_len * seq_len,
        ),
        name="front",
    )(tokens, heads, expand, reduce, merge, vectors, segments.reshape(seq_len, 1))


def attend_back_kernel(
    attended, attended_grad, query_aux, key_aux, value_aux, projected_grad, grad_aux, key_turned, query_total
):
    seq_len, width = attended.shape
    head_local = width // HEAD_DIM
    block = min(KEY_BLOCK, seq_len)
    lane = lax.broadcasted_iota(jnp.int32, (block, AUX), 1)
    low = jnp.bfloat16
    blank = jnp.zeros((block, AUX - HEAD_DIM), jnp.float32)

    def prepare(step, carry):
        rows = pl.ds(pl.multiple_of(step * block, block), block)
        upstream = attended_grad[rows, :].astype(jnp.float32)
        product = upstream * attended[rows, :].astype(jnp.float32)
        for head in range(head_local):
            columns = slice(head * HEAD_DIM, (head + 1) * HEAD_DIM)
            row_dot = jnp.sum(product[:, columns], axis=1, keepdims=True)
            first = row_dot.astype(low).astype(jnp.float32)
            wide = jnp.concatenate([upstream[:, columns], blank], axis=1)
            wide = jnp.where(lane == HEAD_DIM + 1, first, wide)
            wide = jnp.where(lane == HEAD_DIM + 2, row_dot - first, wide)
            grad_aux[head, rows, :] = wide.astype(low)
            key_turned[head, :, rows] = key_aux[head, rows, :].T[:HEAD_DIM]
        return carry

    lax.fori_loop(0, seq_len // block, prepare, 0)
    query_total[...] = jnp.zeros_like(query_total)

    def back(step, carry):
        rows = pl.ds(pl.multiple_of(step * block, block), block)
        for head in range(head_local):
            scores = contract_cols(key_aux[head, rows, :], query_aux[head])
            chances = jnp.exp(scores)
            chance_grad = contract_cols(value_aux[head, rows, :], grad_aux[head])
            score_grad = (chances * chance_grad).astype(low)
            value_grad = jnp.dot(
                chances.astype(low), grad_aux[head], preferred_element_type=jnp.float32
            )
            key_grad = jnp.dot(score_grad, query_aux[head], preferred_element_type=jnp.float32)
            query_total[head] += jnp.dot(
                key_turned[head, :, rows], score_grad, preferred_element_type=jnp.float32
            )
            at = 3 * head * HEAD_DIM
            pair = jnp.concatenate([key_grad[:, :HEAD_DIM], value_grad[:, :HEAD_DIM]], axis=1)
            projected_grad[rows, at + HEAD_DIM : at + 3 * HEAD_DIM] = pair.astype(low)
        return carry

    lax.fori_loop(0, seq_len // block, back, 0)

    def finish(step, carry):
        rows = pl.ds(pl.multiple_of(step * block, block), block)
        for head in range(head_local):
            query_grad = query_total[head, :, rows].T * HEAD_DIM**-0.5
            at = 3 * head * HEAD_DIM
            projected_grad[rows, at : at + HEAD_DIM] = query_grad.astype(low)
        return carry

    lax.fori_loop(0, seq_len // block, finish, 0)


def attend_back_pallas(attended, attended_grad, query_aux, key_aux, value_aux):
    seq_len, width = attended.shape
    head_local = width // HEAD_DIM
    whole = pl.BlockSpec(memory_space=pltpu.VMEM)
    return pl.pallas_call(
        attend_back_kernel,
        out_shape=jax.ShapeDtypeStruct((seq_len, 3 * width), jnp.bfloat16),
        in_specs=[whole] * 5,
        out_specs=whole,
        scratch_shapes=[
            pltpu.VMEM((head_local, seq_len, AUX), jnp.bfloat16),
            pltpu.VMEM((head_local, HEAD_DIM, seq_len), jnp.bfloat16),
            pltpu.VMEM((head_local, HEAD_DIM, seq_len), jnp.float32),
        ],
        compiler_params=pltpu.CompilerParams(vmem_limit_bytes=VMEM_LIMIT),
        cost_estimate=pl.CostEstimate(
            flops=10 * head_local * seq_len * seq_len * AUX,
            bytes_accessed=10 * seq_len * width,
            transcendentals=head_local * seq_len * seq_len,
        ),
        name="attend_back",
    )(attended, attended_grad, query_aux, key_aux, value_aux)


EXACT_THREE = lax.Precision.HIGH
SIDE = 256


def swap_bit(values, axis_name, bit):
    count = lax.axis_size(axis_name)
    return lax.ppermute(values, axis_name, [(i, i ^ bit) for i in range(count)])


def data_bits():
    return [1 << k for k in range(1, lax.axis_size("dp").bit_length() - 1)]


def has_bit(index, bit):
    return (index & bit) != 0


def gather_bits_absolute(block, bits):
    index = lax.axis_index("dp")
    for bit in bits:
        other = swap_bit(block, "dp", bit)
        mine = has_bit(index, bit)
        block = jnp.concatenate(
            [jnp.where(mine, other, block), jnp.where(mine, block, other)], axis=0
        )
    return block


def scatter_bits_absolute(total, bits, wire):
    index = lax.axis_index("dp")
    for bit in reversed(bits):
        half = total.shape[0] // 2
        low, high = total[:half], total[half:]
        mine = has_bit(index, bit)
        arrived = swap_bit(jnp.where(mine, low, high).astype(wire), "dp", bit)
        total = jnp.where(mine, high, low).astype(jnp.float32) + arrived.astype(jnp.float32)
    return total


def line_up(values):
    count = lax.axis_size("tensor")
    return lax.ppermute(values, "tensor", [(i, i + 1) for i in range(count - 1)])


def line_down(values):
    count = lax.axis_size("tensor")
    return lax.ppermute(values, "tensor", [(i + 1, i) for i in range(count - 1)])


def gather_line(block):
    count = lax.axis_size("tensor")
    index = lax.axis_index("tensor")
    below, above = [block], [block]
    for step in range(count - 1):
        below.append(line_up(below[-1]))
        above.append(line_down(above[-1]))
    parts = [block]
    for offset in range(1, count):
        parts.append(jnp.where(index + offset < count, above[offset], below[count - offset]))
    return parts


def scatter_line(parts, wire):
    count = lax.axis_size("tensor")
    index = lax.axis_index("tensor")
    upward, downward = None, None
    for offset in range(count - 1, 0, -1):
        send_up = parts[offset].astype(jnp.float32)
        send_down = parts[count - offset].astype(jnp.float32)
        if upward is not None:
            send_up = send_up + upward.astype(jnp.float32)
            send_down = send_down + downward.astype(jnp.float32)
        upward = line_up(jnp.where(index + offset < count, send_up, 0.0).astype(wire))
        downward = line_down(jnp.where(index >= offset, send_down, 0.0).astype(wire))
    return parts[0].astype(jnp.float32) + upward.astype(jnp.float32) + downward.astype(jnp.float32)


def pair_permute(values, where_to):
    data_count, tensor_count = lax.axis_size("dp"), lax.axis_size("tensor")
    moves = []
    for i in range(data_count):
        for j in range(tensor_count):
            target = where_to(i, j)
            if target is not None:
                moves.append((i * tensor_count + j, target[0] * tensor_count + target[1]))
    return lax.ppermute(values, ("dp", "tensor"), moves)


def exchange_home(values):
    return pair_permute(
        values, lambda i, j: (i ^ 1, j ^ 2) if (i & 1) != (j >> 1) else None
    )


def group_swap(values, member):
    if member == 1:
        return swap_bit(values, "dp", 1)
    if member == 2:
        return swap_bit(values, "tensor", 1)
    return pair_permute(values, lambda i, j: (i ^ 1, j ^ 1))


def gather_head_group(shard):
    first = []
    for core in (0, 1):
        got = []
        for half in (0, 1):
            got.append(
                pair_permute(
                    shard,
                    lambda i, j: (i - core + (j & 1), (j >> 1) + 2 * half)
                    if (i & 1) == core
                    else None,
                )
            )
        first.append(jnp.where(lax.axis_index("tensor") >= 2, got[1], got[0]))
    return gather_bits_absolute(jnp.concatenate(first, axis=0), data_bits())


def scatter_head_group(total, wire):
    total = scatter_bits_absolute(total, data_bits(), wire)
    rows = total.shape[0] // 2
    result = None
    for core in (0, 1):
        piece = total[core * rows : (core + 1) * rows].astype(wire)
        arrived = None
        for half in (0, 1):
            got = pair_permute(
                piece,
                lambda i, j: ((i & ~1) + core, 2 * (j & 1) + (i & 1))
                if (j >> 1) == half
                else None,
            ).astype(jnp.float32)
            arrived = got if arrived is None else arrived + got
        result = arrived if core == 0 else jnp.where((lax.axis_index("dp") & 1) == 1, arrived, result)
    return result


def scatter_units(sums, order, wire):
    count, data_count = lax.axis_size("tensor"), lax.axis_size("dp")
    width = sums.shape[-1]
    rows = sums.shape[0] // (count * data_count)
    bits = data_bits()
    offsets = jnp.zeros((1,), jnp.int32)
    for bit in bits + [1]:
        offsets = jnp.concatenate([offsets, offsets ^ bit])
    ring = (lax.axis_index("tensor") + jnp.arange(count)) % count
    places = (lax.axis_index("dp") ^ offsets)[:, None] * count + ring[None, :]
    total = jnp.take(
        sums.astype(wire).reshape(-1, rows, width), places.reshape(-1), axis=0
    ).reshape((2,) * (1 + len(bits)) + (count, rows, width))
    total = total[0].astype(jnp.float32) + swap_bit(total[1], "dp", 1).astype(jnp.float32)
    left = sorted(bits, reverse=True)
    for bit in order:
        place = left.index(bit)
        keep = lax.index_in_dim(total, 0, place, keepdims=False)
        send = lax.index_in_dim(total, 1, place, keepdims=False)
        total = keep + swap_bit(send.astype(wire), "dp", bit).astype(jnp.float32)
        left.remove(bit)
    return scatter_line([total[k] for k in range(count)], wire)


def pack_symmetric(gram):
    return jnp.concatenate(
        [gram[k : k + SIDE, k:] for k in range(0, gram.shape[0], SIDE)], axis=1
    )


def unpack_symmetric(packed, size):
    rows, at = [], 0
    for k in range(0, size, SIDE):
        rows.append(packed[:, at : at + size - k])
        at += size - k
    full = []
    for i in range(len(rows)):
        blocks = [rows[j][:, (i - j) * SIDE : (i - j + 1) * SIDE].T for j in range(i)]
        full.append(jnp.concatenate(blocks + [rows[i]], axis=1))
    return jnp.concatenate(full, axis=0)


def sum_over_chips(packed):
    count = lax.axis_size("tensor")
    index = lax.axis_index("tensor")
    part = scatter_bits_absolute(packed, data_bits(), jnp.float32)
    part = part.reshape(count, part.shape[0] // count, part.shape[1])
    ring = (index + jnp.arange(count)) % count
    turned = jnp.take(part, ring, axis=0)
    own = scatter_line([turned[k] for k in range(count)], jnp.float32)
    parts = jnp.stack(gather_line(own))
    part = jnp.take(parts, (jnp.arange(count) - index) % count, axis=0)
    part = part.reshape(count * part.shape[1], part.shape[2])
    return gather_bits_absolute(part, data_bits())


def sum_over_all(values):
    for bit in (1, 2):
        values = values + swap_bit(values, "tensor", bit)
    for bit in [1] + data_bits():
        values = values + swap_bit(values, "dp", bit)
    return values


def polynomial_chain(gram, product):
    identity = jnp.eye(gram.shape[-1], dtype=jnp.float32)
    chain = None
    for step in range(NEWTON_STEPS):
        square = product(gram, gram)
        factor = newton_linear * identity + newton_cubic * gram + newton_quintic * square
        chain = factor if chain is None else product(chain, factor)
        if step < NEWTON_STEPS - 1:
            gram = product(product(gram, factor), factor)
    return chain


def per_device(
    tokens,
    segment_ids,
    out_grad,
    heads_weight,
    merge_weight,
    expand_weight,
    reduce_weight,
    heads_momentum,
    merge_momentum,
    expand_momentum,
    reduce_momentum,
    heads_average,
    merge_average,
    expand_average,
    reduce_average,
    vectors,
    vector_momentum,
    vector_average,
):
    low = jnp.bfloat16
    tensor_count = lax.axis_size("tensor")
    data_count = lax.axis_size("dp")
    tensor_index = lax.axis_index("tensor")
    core = lax.axis_index("dp") & 1
    row_count = tokens.shape[0]
    seq_len = row_count * tensor_count
    head_local = heads_weight.shape[1] // (3 * HEAD_DIM)
    group_width = head_local * HEAD_DIM
    at_home = core == (tensor_index >> 1)
    group = 2 * (tensor_index & 1) + core

    own_segments = jnp.where(at_home, segment_ids, swap_bit(segment_ids, "dp", 1))
    chunk_at = []
    for member in range(4):
        its_core, its_tensor = core ^ (member & 1), tensor_index ^ (member >> 1)
        chunk_at.append(jnp.where(its_core == (its_tensor >> 1), its_tensor, its_tensor ^ 2))
    segments = jnp.take(
        own_segments.reshape(tensor_count, row_count), jnp.stack(chunk_at), axis=0
    ).reshape(seq_len)
    sent_grad = lax.dynamic_slice_in_dim(out_grad, (tensor_index ^ 2) * row_count, row_count, 0)
    home_grad = lax.dynamic_slice_in_dim(out_grad, tensor_index * row_count, row_count, 0)
    own_grad = jnp.where(at_home, home_grad, swap_bit(sent_grad, "dp", 1))

    gather_heads = heads_weight.shape[0] % 16 == 0
    heads_low = heads_weight.astype(low)
    if not gather_heads:
        heads_low = gather_head_group(heads_low)
    (
        attended_full,
        attended_own,
        query_aux,
        key_aux,
        value_aux,
        first_full,
        token_chunks,
        full_heads,
        full_expand,
        full_reduce,
        full_merge,
    ) = front_pallas(
        tokens,
        heads_low,
        expand_weight.T.astype(low),
        reduce_weight.astype(low),
        merge_weight.T.astype(low),
        vectors,
        segments,
        gather_heads,
    )
    full_heads = full_heads.reshape(D, 3 * group_width) if gather_heads else heads_low
    attended_full = attended_full.reshape(seq_len, group_width)
    full_merge = jnp.transpose(full_merge, (0, 2, 1, 3)).reshape(D, D)
    full_expand = full_expand.reshape(FF, D)
    full_reduce = full_reduce.reshape(FF, D)

    dense_rows = token_chunks[0].astype(jnp.float32)
    normed_one, inverse_one = center_scale(dense_rows)
    merged = contract_cols(attended_own, full_merge)
    middle = dense_rows + merged + vectors[4]
    normed_two, inverse_two = center_scale(middle)
    second_in = (normed_two * vectors[2] + vectors[3]).astype(low)

    expanded = contract_cols(second_in, full_expand)
    activated, gelu_pull = jax.vjp(gelu_exact, expanded)
    hidden = activated.astype(low)
    reduce_sum = contract_rows(hidden, own_grad)
    (expand_grad,) = gelu_pull(contract_cols(own_grad, full_reduce))
    expand_low = expand_grad.astype(low)
    expand_sum = contract_rows(expand_low, second_in)
    second_grad = jnp.dot(expand_low, full_expand, preferred_element_type=jnp.float32)
    layer_sum = middle + vectors[5] + jnp.dot(hidden, full_reduce, preferred_element_type=jnp.float32)
    output_rows = layer_sum.astype(low)
    layer_output = jnp.where(at_home, output_rows, exchange_home(output_rows))

    bits = data_bits()
    expand_rows = scatter_units(expand_sum, bits[::-1], low)
    reduce_gradient = scatter_units(reduce_sum, bits, low)
    expand_gradient = expand_rows.T
    expand_new_momentum = momentum_decay * expand_momentum + expand_gradient
    reduce_new_momentum = momentum_decay * reduce_momentum + reduce_gradient
    expand_part = expand_new_momentum.T
    reduce_part = reduce_new_momentum
    expand_gram = lax.dot_general(
        expand_part, expand_part, (((0,), (0,)), ((), ())), precision=EXACT_THREE
    )
    reduce_gram = lax.dot_general(
        reduce_part, reduce_part, (((0,), (0,)), ((), ())), precision=EXACT_THREE
    )
    expand_gram, reduce_gram = pack_symmetric(expand_gram), pack_symmetric(reduce_gram)
    first_core = core == 0
    wide_gram = jnp.where(first_core, expand_gram, reduce_gram) + swap_bit(
        jnp.where(first_core, reduce_gram, expand_gram), "dp", 1
    )
    wide_gram = unpack_symmetric(sum_over_chips(wide_gram), D)

    middle_grad = own_grad.astype(jnp.float32) + norm_backward(
        second_grad, normed_two, inverse_two, vectors[2]
    )
    middle_low = middle_grad.astype(low)
    attended_grad = jnp.dot(middle_low, full_merge, preferred_element_type=jnp.float32).astype(low)
    grad_parts = [
        lax.dynamic_slice_in_dim(attended_grad, (group ^ k) * group_width, group_width, 1)
        for k in range(4)
    ]
    attended_grad = jnp.concatenate(
        [grad_parts[0]] + [group_swap(grad_parts[k], k) for k in (1, 2, 3)], axis=0
    )
    merge_sum = contract_rows(middle_low, attended_own)
    merge_sum = merge_sum.astype(low).reshape(D, 4, group_width)
    turned = (tensor_index + jnp.arange(tensor_count)) % tensor_count
    merge_sum = jnp.take(merge_sum, turned, axis=1)
    merge_sum = scatter_line([merge_sum[:, k] for k in range(tensor_count)], low)
    merge_gradient = scatter_bits_absolute(merge_sum, [1] + data_bits(), low).T

    projected_grad = attend_back_pallas(
        attended_full, attended_grad, query_aux, key_aux, value_aux
    )
    heads_sum = contract_rows(first_full, projected_grad)
    heads_gradient = scatter_head_group(heads_sum, low)
    first_parts = contract_cols(projected_grad, full_heads).reshape(4, row_count, D)
    kept = first_parts[0::2] + swap_bit(first_parts[1::2].astype(low), "dp", 1).astype(jnp.float32)
    first_grad = kept[0] + swap_bit(kept[1].astype(low), "tensor", 1).astype(jnp.float32)
    input_rows = middle_grad + norm_backward(first_grad, normed_one, inverse_one, vectors[0])
    input_gradient = jnp.where(
        at_home, input_rows, exchange_home(input_rows.astype(low)).astype(jnp.float32)
    )
    vector_gradient = sum_over_all(
        jnp.stack(
            [
                jnp.sum(first_grad * normed_one, axis=0),
                jnp.sum(first_grad, axis=0),
                jnp.sum(second_grad * normed_two, axis=0),
                jnp.sum(second_grad, axis=0),
                jnp.sum(middle_grad, axis=0),
                jnp.sum(own_grad.astype(jnp.float32), axis=0),
            ]
        )
    )
    heads_new_momentum = momentum_decay * heads_momentum + heads_gradient
    merge_new_momentum = momentum_decay * merge_momentum + merge_gradient
    vector_new_momentum = momentum_decay * vector_momentum + vector_gradient

    heads_part = heads_new_momentum.reshape(heads_new_momentum.shape[0], head_local * 3, HEAD_DIM)
    merge_part = merge_new_momentum.reshape(head_local, HEAD_DIM, merge_new_momentum.shape[1])
    small_gram = jnp.concatenate(
        [
            jnp.einsum("rmd,rme->mde", heads_part, heads_part, precision=highest),
            jnp.einsum("hdc,hec->hde", merge_part, merge_part, precision=highest),
        ],
        axis=0,
    )
    for bit in [1] + data_bits():
        small_gram = small_gram + swap_bit(small_gram, "dp", bit)
    small_factor = 1.0 / (jnp.sqrt(jnp.trace(small_gram, axis1=1, axis2=2)) + newton_epsilon)
    small_chain = polynomial_chain(
        small_gram * (small_factor * small_factor)[:, None, None],
        lambda left, right: jnp.einsum("mde,mef->mdf", left, right, precision=highest),
    )
    small_chain = small_chain * small_factor[:, None, None]
    side_count = 3 * head_local
    heads_ortho = jnp.einsum("rmd,mde->rme", heads_part, small_chain[:side_count], precision=highest)
    merge_ortho = jnp.einsum("hde,hec->hdc", small_chain[side_count:], merge_part, precision=highest)

    wide_factor = 1.0 / (jnp.sqrt(jnp.trace(wide_gram)) + newton_epsilon)
    wide_chain = polynomial_chain(
        wide_gram * (wide_factor * wide_factor),
        lambda left, right: jnp.dot(left, right, precision=EXACT_THREE),
    )
    wide_chain = wide_chain * wide_factor
    other_chain = swap_bit(wide_chain, "dp", 1)
    expand_ortho = jnp.dot(
        expand_part, jnp.where(first_core, wide_chain, other_chain), precision=EXACT_THREE
    ).T
    reduce_ortho = jnp.dot(
        reduce_part, jnp.where(first_core, other_chain, wide_chain), precision=EXACT_THREE
    )

    keep_factor = 1.0 - muon_rate * weight_decay
    head_step = muon_rate * 0.2 * math.sqrt(max(D, HEAD_DIM))
    wide_step = muon_rate * 0.2 * math.sqrt(max(D, FF))
    heads_new_weight = heads_weight * keep_factor - head_step * heads_ortho.reshape(
        heads_weight.shape
    )
    merge_new_weight = merge_weight * keep_factor - head_step * merge_ortho.reshape(
        merge_weight.shape
    )
    expand_new_weight = expand_weight * keep_factor - wide_step * expand_ortho
    reduce_new_weight = reduce_weight * keep_factor - wide_step * reduce_ortho
    vector_new_value = vectors - vector_rate / math.sqrt(SEQ * data_count) * vector_new_momentum
    heads_new_average = average_decay * heads_average + (1.0 - average_decay) * heads_new_weight
    merge_new_average = average_decay * merge_average + (1.0 - average_decay) * merge_new_weight
    expand_new_average = average_decay * expand_average + (1.0 - average_decay) * expand_new_weight
    reduce_new_average = average_decay * reduce_average + (1.0 - average_decay) * reduce_new_weight
    vector_new_average = average_decay * vector_average + (1.0 - average_decay) * vector_new_value
    return (
        layer_output,
        input_gradient,
        heads_gradient,
        merge_gradient,
        expand_gradient,
        reduce_gradient,
        heads_new_momentum,
        merge_new_momentum,
        expand_new_momentum,
        reduce_new_momentum,
        heads_new_weight,
        merge_new_weight,
        expand_new_weight,
        reduce_new_weight,
        heads_new_average,
        merge_new_average,
        expand_new_average,
        reduce_new_average,
        vector_gradient,
        vector_new_momentum,
        vector_new_value,
        vector_new_average,
    )


def solution(mesh):
    placed = (
        P(("dp", "tensor"), None),
        P("dp"),
        P("dp", None),
        P("dp", "tensor"),
        P("tensor", "dp"),
        P(None, ("tensor", "dp")),
        P(("tensor", "dp"), None),
        P("dp", "tensor"),
        P("tensor", "dp"),
        P(None, ("tensor", "dp")),
        P(("tensor", "dp"), None),
        P("dp", "tensor"),
        P("tensor", "dp"),
        P(None, ("tensor", "dp")),
        P(("tensor", "dp"), None),
        P(),
        P(),
        P(),
    )
    return jax.shard_map(
        per_device,
        mesh=mesh,
        in_specs=placed,
        out_specs=(
            P(("dp", "tensor"), None),
            P(("dp", "tensor"), None),
            P("dp", "tensor"),
            P("tensor", "dp"),
            P(None, ("tensor", "dp")),
            P(("tensor", "dp"), None),
            P("dp", "tensor"),
            P("tensor", "dp"),
            P(None, ("tensor", "dp")),
            P(("tensor", "dp"), None),
            P("dp", "tensor"),
            P("tensor", "dp"),
            P(None, ("tensor", "dp")),
            P(("tensor", "dp"), None),
            P("dp", "tensor"),
            P("tensor", "dp"),
            P(None, ("tensor", "dp")),
            P(("tensor", "dp"), None),
            P(),
            P(),
            P(),
            P(),
        ),
        check_vma=False,
    )
```

```python
import functools
import math

import jax
import jax.numpy as jnp
from jax import lax
from jax.experimental import pallas as pl
from jax.experimental.pallas import tpu as pltpu
from jax.sharding import PartitionSpec as P

D = 768
HEAD_DIM = 64
FF = 3072
SEQ = 2048
NEWTON_STEPS = 5


highest = lax.Precision.HIGHEST
norm_epsilon = 1e-06
newton_epsilon = 1e-07
newton_linear = 3.4445
newton_cubic = -4.775
newton_quintic = 2.0315
momentum_decay = 0.5
average_decay = 0.9
muon_rate = 0.2
weight_decay = 0.1
vector_rate = 0.15
masked_score = -1e30
VMEM_LIMIT = 56 * 2**20


def center_scale(values):
    average = jnp.mean(values, axis=-1, keepdims=True)
    centered = values - average
    inverse = lax.rsqrt(jnp.mean(centered * centered, axis=-1, keepdims=True) + norm_epsilon)
    return (centered * inverse, inverse)


def norm_backward(upstream, normed, inverse, gain):
    scaled = upstream * gain
    mean_one = jnp.mean(scaled, axis=-1, keepdims=True)
    mean_two = jnp.mean(scaled * normed, axis=-1, keepdims=True)
    return inverse * (scaled - mean_one - normed * mean_two)


def gelu_exact(values):
    return jax.nn.gelu(values, approximate=False)


def contract_rows(left_side, right_side):
    return lax.dot_general(
        left_side, right_side, (((0,), (0,)), ((), ())), preferred_element_type=jnp.float32
    )


def contract_cols(left_side, right_side):
    return lax.dot_general(
        left_side, right_side, (((1,), (1,)), ((), ())), preferred_element_type=jnp.float32
    )


KEY_BLOCK = 256
AUX = 128


MESH = pl.DeviceIdType.MESH


def low_rank_bits(data_count):
    return [1 << k for k in range(1, data_count.bit_length() - 1)]


class Wires:
    def __init__(self, send, receive):
        self.send, self.receive, self.used = send, receive, 0

    def number(self):
        self.used += 1
        return self.used - 1

    def start(self, k, source, target, device):
        copy = pltpu.make_async_remote_copy(
            source, target, self.send.at[k], self.receive.at[k], device_id=device, device_id_type=MESH
        )
        copy.start()

    def sent(self, k, source, device):
        pltpu.make_async_remote_copy(
            source, source, self.send.at[k], self.receive.at[k], device_id=device, device_id_type=MESH
        ).wait_send()

    def arrived(self, k, target, device):
        pltpu.make_async_remote_copy(
            target, target, self.send.at[k], self.receive.at[k], device_id=device, device_id_type=MESH
        ).wait_recv()


def greet(devices):
    barrier = pltpu.get_barrier_semaphore()
    for device in devices:
        pl.semaphore_signal(barrier, inc=1, device_id=device, device_id_type=MESH)
    pl.semaphore_wait(barrier, len(devices))


def column_and_plane(data, tensor, data_count, tensor_count):
    found = []
    for core in (0, 1):
        for step in range(tensor_count):
            if core or step:
                found.append((data ^ core, lax.rem(tensor + step, tensor_count)))
    for k in range(1, data_count // 2):
        found.append((data ^ (2 * k), tensor))
    return found


def front_kernel(
    data_count,
    tensor_count,
    gather_heads,
    tokens,
    heads,
    expand,
    reduce,
    merge,
    vectors,
    segment_column,
    out_grad,
    attended,
    attended_rows,
    query_aux,
    key_aux,
    value_aux,
    first_full,
    chunks,
    all_heads,
    all_expand,
    all_reduce,
    all_merge,
    sequence_grad,
    arrivals,
    send,
    receive,
    local,
):
    low = jnp.bfloat16
    rows, width = tokens.shape
    head_local = query_aux.shape[0]
    group_width = head_local * HEAD_DIM
    data, tensor = lax.axis_index("dp"), lax.axis_index("tensor")
    core, half = data & 1, tensor >> 1
    home = core == half
    group = 2 * (tensor & 1) + core
    wires = Wires(send, receive)
    beside, across, diagonal = (data ^ 1, tensor), (data, tensor ^ 1), (data ^ 1, tensor ^ 1)
    members = [None, beside, across, diagonal]
    away = (data ^ 1, tensor ^ 2)
    pieces = [pl.ds(p * (rows // 2), rows // 2) for p in range(2)]
    pending = []

    def begin(k, source, target, device, when=None):
        if when is None:
            wires.start(k, source, target, device)
        else:

            @pl.when(when)
            def _():
                wires.start(k, source, target, device)

        pending.append((k, source, device, when))

    def await_arrival(k, target, device, when=None):
        if when is None:
            wires.arrived(k, target, device)
        else:

            @pl.when(when)
            def _():
                wires.arrived(k, target, device)

    own = pltpu.make_async_copy(merge, all_merge.at[data, tensor], local.at[0])
    own.start()
    greet(column_and_plane(data, tensor, data_count, tensor_count))

    def z_hop(hop):
        made = []
        for mat, single in ((all_merge, merge),):
            for way in (1, -1):
                number = wires.number()
                slot = tensor - way * (hop - 1)
                going = (tensor + way >= 0) & (tensor + way < tensor_count)
                going = going & (slot >= 0) & (slot < tensor_count)
                source = single if hop == 1 else mat.at[data, slot]
                begin(number, source, mat.at[data, slot], (data, tensor + way), going)
                made.append((number, mat, tensor - way * hop, tensor - way))
        return made

    def z_wait(made):
        for number, mat, slot, source in made:
            valid = (slot >= 0) & (slot < tensor_count)
            await_arrival(number, mat.at[data, slot], (data, source), valid)

    pair = (data >> 1) * 2

    def group_send(block, whole):
        numbers = [wires.number() for _ in range(4)]
        for k in (0, 1):
            target = (pair + (tensor & 1), (tensor >> 1) + 2 * k)
            itself = (target[0] == data) & (target[1] == tensor)
            for c in (0, 1):
                begin(
                    numbers[2 * k + c],
                    block,
                    whole.at[data],
                    target,
                    jnp.logical_not(itself) & (core == c),
                )

            @pl.when(itself)
            def _():
                copy = pltpu.make_async_copy(block, whole.at[data], local.at[1])
                copy.start()
                copy.wait()

        return numbers

    def group_wait(numbers, whole):
        for k in (0, 1):
            for c in (0, 1):
                source = (pair + c, group)
                itself = (source[0] == data) & (source[1] == tensor)
                await_arrival(
                    numbers[2 * k + c],
                    whole.at[pair + c],
                    source,
                    jnp.logical_not(itself) & (half == k),
                )

    merge_first = z_hop(1)
    if gather_heads:
        head_numbers = group_send(heads, all_heads)

    numbers = [wires.number() for _ in range(12)]
    for p, piece in enumerate(pieces):
        begin(numbers[p], tokens.at[piece], chunks.at[2, piece], across, home)
        begin(numbers[2 + p], tokens.at[piece], chunks.at[0, piece], away, jnp.logical_not(home))
        begin(numbers[4 + p], tokens.at[piece], chunks.at[1, piece], beside, home)

    @pl.when(home)
    def _():
        chunks[0] = tokens[...]

    if gather_heads:
        group_wait(head_numbers, all_heads)
        plane = []
        for k in range(1, data_count // 2):
            number = wires.number()
            plane.append((number, k))
            begin(number, all_heads.at[pl.ds(pair, 2)], all_heads.at[pl.ds(pair, 2)], (data ^ (2 * k), tensor))

    for p, piece in enumerate(pieces):
        await_arrival(numbers[2 + p], chunks.at[0, piece], away, jnp.logical_not(home))
        begin(numbers[6 + p], chunks.at[0, piece], chunks.at[2, piece], across, jnp.logical_not(home))
        begin(numbers[8 + p], chunks.at[0, piece], chunks.at[1, piece], beside, jnp.logical_not(home))

    expand_numbers = group_send(expand, all_expand)
    reduce_numbers = group_send(reduce, all_reduce)

    if gather_heads:
        for number, k in plane:
            there = pl.ds(pair ^ (2 * k), 2)
            await_arrival(number, all_heads.at[there], (data ^ (2 * k), tensor))

    block = min(KEY_BLOCK, rows)
    lane = lax.broadcasted_iota(jnp.int32, (block, AUX), 1)
    blank = jnp.zeros((block, AUX - HEAD_DIM), jnp.float32)
    steps = rows // block

    def prepare(member):
        def one(step, carry):
            inside = pl.ds(pl.multiple_of(step * block, block), block)
            at_rows = pl.ds(pl.multiple_of(member * rows + step * block, block), block)
            normed, _ = center_scale(chunks[member, inside, :].astype(jnp.float32))
            first_in = (normed * vectors[0:1, :] + vectors[1:2, :]).astype(low)
            first_full[at_rows, :] = first_in
            weight = all_heads[...].reshape(width, 3 * group_width)
            projected = jnp.dot(first_in, weight, preferred_element_type=jnp.float32)
            projected = projected.astype(low).astype(jnp.float32)
            same = lane - HEAD_DIM == segment_column[at_rows, :]
            segment_lane = (lane >= HEAD_DIM) & (lane < HEAD_DIM + 3)
            query_extra = jnp.where(same & segment_lane, 1.0, 0.0)
            key_extra = jnp.where(
                segment_lane,
                jnp.where(same, 0.0, masked_score),
                jnp.where((lane >= HEAD_DIM + 3) & (lane < HEAD_DIM + 6), -1.0, 0.0),
            )
            value_extra = jnp.where(
                lane == HEAD_DIM,
                1.0,
                jnp.where((lane == HEAD_DIM + 1) | (lane == HEAD_DIM + 2), -1.0, 0.0),
            )
            for head in range(head_local):
                for which, (ref, extra, factor) in enumerate(
                    (
                        (query_aux, query_extra, HEAD_DIM**-0.5),
                        (key_aux, key_extra, 1.0),
                        (value_aux, value_extra, 1.0),
                    )
                ):
                    at = (3 * head + which) * HEAD_DIM
                    part = jnp.concatenate([projected[:, at : at + HEAD_DIM] * factor, blank], axis=1)
                    ref[head, at_rows, :] = jnp.where(lane < HEAD_DIM, part, extra).astype(low)
            return carry

        lax.fori_loop(0, steps, one, 0)

    def attend(member, steps_here):
        def one(step, carry):
            inside = pl.ds(pl.multiple_of(step * block, block), block)
            at_rows = pl.ds(pl.multiple_of(member * rows + step * block, block), block)
            done = []
            for head in range(head_local):
                query = query_aux[head, at_rows, :]
                scores = contract_cols(query, key_aux[head])
                row_max = jnp.max(scores, axis=1, keepdims=True)
                exponent = jnp.exp(scores - row_max).astype(low)
                output = jnp.dot(exponent, value_aux[head], preferred_element_type=jnp.float32)
                totals = output[:, HEAD_DIM : HEAD_DIM + 1]
                done.append(output[:, :HEAD_DIM] / totals)
                logsum = row_max + jnp.log(totals)
                first = logsum.astype(low).astype(jnp.float32)
                second = (logsum - first).astype(low).astype(jnp.float32)
                third = logsum - first - second
                wide = query.astype(jnp.float32)
                wide = jnp.where(lane == HEAD_DIM + 3, first, wide)
                wide = jnp.where(lane == HEAD_DIM + 4, second, wide)
                wide = jnp.where(lane == HEAD_DIM + 5, third, wide)
                query_aux[head, at_rows, :] = wide.astype(low)
            attended[member, inside, :] = jnp.concatenate(done, axis=1).astype(low)
            return carry

        lax.fori_loop(*steps_here, one, 0)

    bits = low_rank_bits(data_count)
    schedule = []
    held = [[0], [0], [0]]
    for k in range(len(bits)):
        plan = []
        for m, mat in enumerate((all_expand, all_reduce, all_merge)):
            bit = bits[-1 - k] if m == 1 else bits[k]
            plan.append((mat, bit, list(held[m]), m < 2))
            held[m] = held[m] + [offset ^ bit for offset in held[m]]
        schedule.append(plan)
    schedule.append([(all_merge, 1, list(held[2]), False)])

    prepare(0)
    for p, piece in enumerate(pieces):
        await_arrival(numbers[p], chunks.at[2, piece], across, home)
        await_arrival(numbers[6 + p], chunks.at[2, piece], across, jnp.logical_not(home))
        begin(numbers[10 + p], chunks.at[2, piece], chunks.at[3, piece], beside)

    def bit_step(plan):
        made = []
        for mat, bit, held, wide in plan:
            for offset in held:
                number = wires.number()
                place = (pair if wide else data) ^ offset
                there = pl.ds(place ^ bit, 2) if wide else place ^ bit
                place = pl.ds(place, 2) if wide else place
                begin(number, mat.at[place], mat.at[place], (data ^ bit, tensor))
                made.append((number, mat, there, bit))
        return made

    def bit_wait(made):
        for number, mat, there, bit in made:
            await_arrival(number, mat.at[there], (data ^ bit, tensor))


    grad_numbers = [wires.number() for _ in range(4)]
    grad_copies = []
    for member in range(4):
        its_core, its_tensor = core ^ (member & 1), tensor ^ (member >> 1)
        chunk = its_tensor ^ (2 * (its_core ^ (its_tensor >> 1)))
        source = out_grad.at[pl.ds(pl.multiple_of(chunk * rows, rows), rows)]
        copy = pltpu.make_async_copy(source, sequence_grad.at[member], local.at[2 + member])
        grad_copies.append(copy)
        pl.when(home)(copy.start)
        begin(grad_numbers[member], source, sequence_grad.at[member ^ 1], beside, home)
    for p, piece in enumerate(pieces):
        await_arrival(numbers[4 + p], chunks.at[1, piece], beside, jnp.logical_not(home))
        await_arrival(numbers[8 + p], chunks.at[1, piece], beside, home)
    z_wait(merge_first)
    merge_made = z_hop(2)
    prepare(1)
    prepare(2)
    for p, piece in enumerate(pieces):
        await_arrival(numbers[10 + p], chunks.at[3, piece], beside)
    prepare(3)
    z_wait(merge_made)
    merge_made = z_hop(3)
    group_wait(expand_numbers, all_expand)
    group_wait(reduce_numbers, all_reduce)
    made = bit_step(schedule[0][:2])

    exchange = {}
    for member in (3, 2, 1, 0):
        attend(member, (0, steps // 2))
        if member == 3:
            z_wait(merge_made)
            own.wait()
            merge_made = bit_step(schedule[0][2:])
        elif member == 2:
            bit_wait(made)
            made = bit_step(schedule[1][:2])
        attend(member, (steps // 2, steps))
        if member:
            number = wires.number()
            begin(number, attended.at[member], arrivals.at[group], members[member])
            exchange[member] = number
        else:
            arrivals[group] = attended[0]
        if member == 2:
            bit_wait(merge_made)
            merge_made = bit_step(schedule[1][2:])
        elif member == 1:
            bit_wait(merge_made)
            merge_made = bit_step(schedule[2])
    made = made + merge_made
    for plan in schedule[3:]:
        bit_wait(made)
        made = bit_step(plan)
    for member, number in exchange.items():
        await_arrival(number, arrivals.at[group ^ member], members[member])
    attended_rows[...] = jnp.concatenate([arrivals[k] for k in range(4)], axis=1)
    bit_wait(made)
    for member in range(4):
        pl.when(home)(grad_copies[member].wait)
        await_arrival(
            grad_numbers[member], sequence_grad.at[member ^ 1], beside, jnp.logical_not(home)
        )
    for k, source, device, when in pending:
        if when is None:
            wires.sent(k, source, device)
        else:

            @pl.when(when)
            def _():
                wires.sent(k, source, device)


def front_pallas(tokens, heads, expand, reduce, merge, vectors, segments, out_grad, gather_heads):
    data_count, tensor_count = lax.axis_size("dp"), lax.axis_size("tensor")
    rows, width = tokens.shape
    low = jnp.bfloat16
    head_columns = heads.shape[-1]
    head_local = head_columns // (3 * HEAD_DIM)
    seq_len = segments.shape[0]
    group_width = head_local * HEAD_DIM
    aux = jax.ShapeDtypeStruct((head_local, seq_len, AUX), low)
    inside = pl.BlockSpec(memory_space=pltpu.VMEM)
    anywhere = pl.BlockSpec(memory_space=pl.ANY)
    gathered = [
        jax.ShapeDtypeStruct((data_count,) + expand.shape, low),
        jax.ShapeDtypeStruct((data_count,) + reduce.shape, low),
        jax.ShapeDtypeStruct((data_count, tensor_count) + merge.shape, low),
        jax.ShapeDtypeStruct((4, rows, width), low),
    ]
    hops = 2 * (tensor_count - 1) + 2 * (data_count // 2 - 1) + data_count - 1
    copies = 12 + data_count // 2 + 12 + hops + 4 + 3
    if gather_heads:
        heads_out = jax.ShapeDtypeStruct((data_count,) + heads.shape, low)
    else:
        heads_out = jax.ShapeDtypeStruct(heads.shape, low)

    def kernel(*refs):
        if not gather_heads:
            refs = list(refs)
            refs[15] = refs[1]
        front_kernel(data_count, tensor_count, gather_heads, *refs)

    return pl.pallas_call(
        kernel,
        out_shape=(
            jax.ShapeDtypeStruct((4, rows, group_width), low),
            jax.ShapeDtypeStruct((rows, 4 * group_width), low),
            aux,
            aux,
            aux,
            jax.ShapeDtypeStruct((seq_len, width), low),
            jax.ShapeDtypeStruct((4, rows, width), low),
            heads_out,
            *gathered,
        ),
        in_specs=[inside] * 7 + [anywhere],
        out_specs=(inside,) * 8 + (anywhere,) * 3 + (inside,),
        scratch_shapes=[
            pltpu.VMEM((4, rows, group_width), low),
            pltpu.SemaphoreType.DMA((copies,)),
            pltpu.SemaphoreType.DMA((copies,)),
            pltpu.SemaphoreType.DMA((6,)),
        ],
        compiler_params=pltpu.CompilerParams(
            vmem_limit_bytes=VMEM_LIMIT, collective_id=1, has_side_effects=True
        ),
        cost_estimate=pl.CostEstimate(
            flops=4 * head_local * seq_len * seq_len * AUX,
            bytes_accessed=8 * seq_len * width,
            transcendentals=head_local * seq_len * seq_len,
        ),
        name="front",
    )(tokens, heads, expand, reduce, merge, vectors, segments.reshape(seq_len, 1), out_grad)


def dot_rows(left_side, right_side):
    return jnp.dot(left_side, right_side, preferred_element_type=jnp.float32)


def middle_kernel(
    attended_rows,
    merge,
    tokens,
    vectors,
    expand,
    reduce,
    sequence_grad,
    layer_base,
    layer_across,
    middle_grad,
    attended_grad,
    expand_sum,
    reduce_sum,
    merge_sum,
    vector_sums,
    second_in,
    middle,
    hidden,
    expand_grad,
    partial,
    reduced,
    from_beside,
    reduced_beside,
    from_across,
    send,
    receive,
):
    low = jnp.bfloat16
    rows, width = tokens.shape
    group_width = width // 4
    data, tensor = lax.axis_index("dp"), lax.axis_index("tensor")
    wires = Wires(send, receive)
    beside, across = (data ^ 1, tensor), (data, tensor ^ 1)
    part = rows // 2
    pieces = [pl.ds(p * part, part) for p in range(2)]
    pending = []

    def begin(k, source, target, device):
        wires.start(k, source, target, device)
        pending.append((k, source, device))

    greet([beside, across])
    numbers = [[wires.number() for _ in range(2)] for _ in range(3)]
    for p, piece in enumerate(pieces):
        merged = contract_cols(attended_rows[piece, :], merge[...])
        here = tokens[piece, :].astype(jnp.float32) + merged + vectors[4:5, :]
        middle[piece, :] = here
        normed, _ = center_scale(here)
        second_in[0, piece, :] = (normed * vectors[2:3, :] + vectors[3:4, :]).astype(low)
        begin(numbers[0][p], second_in.at[0, piece], second_in.at[2, piece], across)
        begin(numbers[1][p], second_in.at[0, piece], second_in.at[1, piece], beside)

    def unit(member, p):
        piece = pieces[p]
        expanded = contract_cols(second_in[member, piece, :], expand[...])
        cdf = 0.5 + 0.5 * lax.erf(expanded * math.sqrt(0.5))
        activated = (expanded * cdf).astype(low)
        hidden[member, piece, :] = activated
        reduced[member, piece, :] = dot_rows(activated, reduce[...]).astype(low)
        slope = cdf + expanded * (jnp.exp(-0.5 * expanded * expanded) * (1.0 / math.sqrt(2.0 * math.pi)))
        upstream = contract_cols(sequence_grad[member, piece, :], reduce[...])
        grad = (upstream * slope).astype(low)
        expand_grad[member, piece, :] = grad
        partial[member, piece, :] = dot_rows(grad, expand[...]).astype(low)

    unit(0, 0)
    unit(0, 1)
    back = [[wires.number() for _ in range(2)] for _ in range(5)]
    for p, piece in enumerate(pieces):
        wires.arrived(numbers[1][p], second_in.at[1, piece], beside)
        unit(1, p)
        begin(back[0][p], partial.at[1, piece], from_beside.at[0, piece], beside)
        begin(back[3][p], reduced.at[1, piece], reduced_beside.at[0, piece], beside)
    for p, piece in enumerate(pieces):
        wires.arrived(numbers[0][p], second_in.at[2, piece], across)
        begin(numbers[2][p], second_in.at[2, piece], second_in.at[3, piece], beside)
    for p, piece in enumerate(pieces):
        wires.arrived(numbers[2][p], second_in.at[3, piece], beside)
        unit(3, p)
        begin(back[1][p], partial.at[3, piece], from_beside.at[1, piece], beside)
        begin(back[4][p], reduced.at[3, piece], reduced_beside.at[1, piece], beside)
        unit(2, p)
        wires.arrived(back[1][p], from_beside.at[1, piece], beside)
        both = partial[2, piece, :].astype(jnp.float32) + from_beside[1, piece, :].astype(jnp.float32)
        partial[2, piece, :] = both.astype(low)
        begin(back[2][p], partial.at[2, piece], from_across.at[piece], across)

    def sum_rows(target, left, right):
        total = None
        for member in range(4):
            term = contract_rows(left[member], right[member])
            total = term if total is None else total + term
        target[...] = total.astype(low)

    sum_rows(reduce_sum, hidden, sequence_grad)
    sum_rows(expand_sum, expand_grad, second_in)
    for p, piece in enumerate(pieces):
        wires.arrived(back[3][p], reduced_beside.at[0, piece], beside)
        wires.arrived(back[4][p], reduced_beside.at[1, piece], beside)
        base = reduced[0, piece, :].astype(jnp.float32) + reduced_beside[0, piece, :].astype(jnp.float32)
        layer_base[piece, :] = base + middle[piece, :] + vectors[5:6, :]
        layer_across[piece, :] = (
            reduced[2, piece, :].astype(jnp.float32)
            + reduced_beside[1, piece, :].astype(jnp.float32)
        ).astype(low)
    sums = [0.0] * 4
    for p, piece in enumerate(pieces):
        wires.arrived(back[0][p], from_beside.at[0, piece], beside)
        wires.arrived(back[2][p], from_across.at[piece], across)
        second_grad = (
            partial[0, piece, :].astype(jnp.float32)
            + from_beside[0, piece, :].astype(jnp.float32)
            + from_across[piece, :].astype(jnp.float32)
        )
        normed, inverse = center_scale(middle[piece, :])
        own = sequence_grad[0, piece, :].astype(jnp.float32)
        total = own + norm_backward(second_grad, normed, inverse, vectors[2:3, :])
        middle_grad[piece, :] = total
        for k, term in enumerate((second_grad * normed, second_grad, total, own)):
            sums[k] = sums[k] + jnp.sum(term, axis=0, keepdims=True)
        into_attended = dot_rows(total.astype(low), merge[...]).astype(low)
        for k in range(4):
            attended_grad[k, piece, :] = into_attended[:, k * group_width : (k + 1) * group_width]
    vector_sums[...] = jnp.concatenate(sums, axis=0)
    into_merge = contract_rows(middle_grad[...].astype(low), attended_rows[...]).astype(low)
    for k in range(4):
        merge_sum[k] = into_merge[:, k * group_width : (k + 1) * group_width]
    for k, source, device in pending:
        wires.sent(k, source, device)


def middle_pallas(attended_rows, merge, tokens, vectors, expand, reduce, sequence_grad):
    rows, width = tokens.shape
    units = expand.shape[0]
    low, wide = jnp.bfloat16, jnp.float32
    inside = pl.BlockSpec(memory_space=pltpu.VMEM)
    shapes = (
        ((rows, width), wide),
        ((rows, width), low),
        ((rows, width), wide),
        ((4, rows, width // 4), low),
        ((units, width), low),
        ((units, width), low),
        ((4, width, width // 4), low),
        ((4, width), wide),
    )
    return pl.pallas_call(
        middle_kernel,
        out_shape=tuple(jax.ShapeDtypeStruct(*shape) for shape in shapes),
        in_specs=[inside] * 7,
        out_specs=(inside,) * 8,
        scratch_shapes=[
            pltpu.VMEM((4, rows, width), low),
            pltpu.VMEM((rows, width), wide),
            pltpu.VMEM((4, rows, units), low),
            pltpu.VMEM((4, rows, units), low),
            pltpu.VMEM((4, rows, width), low),
            pltpu.VMEM((4, rows, width), low),
            pltpu.VMEM((2, rows, width), low),
            pltpu.VMEM((2, rows, width), low),
            pltpu.VMEM((rows, width), low),
            pltpu.SemaphoreType.DMA((16,)),
            pltpu.SemaphoreType.DMA((16,)),
        ],
        compiler_params=pltpu.CompilerParams(
            vmem_limit_bytes=VMEM_LIMIT, collective_id=2, has_side_effects=True
        ),
        cost_estimate=pl.CostEstimate(
            flops=52 * rows * width * units, bytes_accessed=20 * rows * width, transcendentals=rows * units * 8
        ),
        name="middle",
    )(attended_rows, merge, tokens, vectors, expand, reduce, sequence_grad)


class Group:
    def __init__(self, work, arrived, last, order, place, wires, begin):
        self.work, self.got, self.last, self.order = work, arrived, last, order
        self.data, self.tensor = place
        self.pair = (self.data >> 1) * 2
        self.core, self.half = self.data & 1, self.tensor >> 1
        self.wires, self.begin = wires, begin
        self.left = list(range(0, work.shape[0], 2))
        self.slot, self.flight, self.step = 0, [], 0

    def bit_send(self):
        bit = self.order[self.step]
        self.flight = []
        for offset in [o for o in self.left if o & bit]:
            number = self.wires.number()
            target = (self.data ^ bit, self.tensor)
            self.begin(number, self.work.at[pl.ds(self.pair ^ offset, 2)], self.got.at[self.slot], target)
            self.flight.append((number, self.slot, offset ^ bit, target))
            self.slot += 1
        self.left = [o for o in self.left if not o & bit]
        self.step += 1

    def bit_add(self):
        for number, slot, offset, target in self.flight:
            self.wires.arrived(number, self.got.at[slot], target)
            here = pl.ds(self.pair ^ offset, 2)
            total = self.work[here].astype(jnp.float32) + self.got[slot].astype(jnp.float32)
            self.work[here] = total.astype(self.work.dtype)

    def own_send(self):
        group = 2 * (self.tensor & 1) + self.core
        self.numbers = [self.wires.number() for _ in range(4)]
        for c in (0, 1):
            owner = (self.pair + c, group)
            itself = (owner[0] == self.data) & (owner[1] == self.tensor)
            for b in (0, 1):
                self.begin(
                    self.numbers[2 * c + b],
                    self.work.at[self.pair + c],
                    self.last.at[b],
                    owner,
                    jnp.logical_not(itself) & (self.half == b),
                )

    def own_sum(self):
        for b in (0, 1):
            source = (self.pair + (self.tensor & 1), (self.tensor >> 1) + 2 * b)
            itself = (source[0] == self.data) & (source[1] == self.tensor)
            for c in (0, 1):

                @pl.when(jnp.logical_not(itself) & (self.core == c))
                def _():
                    self.wires.arrived(self.numbers[2 * c + b], self.last.at[b], source)

            @pl.when(itself)
            def _():
                self.last[b] = self.work[self.data]

        return self.last[0].astype(jnp.float32) + self.last[1].astype(jnp.float32)


class ChipSum:
    def __init__(
        self, array, result, arrived, last, base, size, order, place, tensor_count, wires, begin
    ):
        self.array, self.result, self.got, self.last = array, result, arrived, last
        self.start, self.size, self.order = base, size, order
        self.data, self.tensor = place
        self.count, self.wires, self.begin = tensor_count, wires, begin
        self.slot, self.step, self.trail = 0, 0, []

    def bit_send(self):
        bit = self.order[self.step]
        self.step += 1
        half = self.size // 2
        mine = (self.data & bit) // bit
        keep, give = self.start + mine * half, self.start + (1 - mine) * half
        number = self.wires.number()
        target = (self.data ^ bit, self.tensor)
        there = self.got.at[pl.ds(self.slot, half)]
        self.begin(number, self.array.at[pl.ds(give, half)], there, target)
        self.trail.append((bit, keep, give, half))
        self.flight = (number, self.slot, half, target)
        self.start, self.size = keep, half
        self.slot += half

    def bit_add(self):
        number, slot, half, target = self.flight
        self.wires.arrived(number, self.got.at[pl.ds(slot, half)], target)
        here = pl.ds(self.start, half)
        self.array[here] = self.array[here] + self.got[pl.ds(slot, half)]

    def line_send(self):
        self.spread = self.size % self.count == 0
        self.portion = self.size // self.count if self.spread else self.size
        self.flight = []
        for k in range(1, self.count):
            number = self.wires.number()
            peer = lax.rem(self.tensor + k, self.count)
            at = self.start + peer * self.portion if self.spread else self.start
            source = self.array.at[pl.ds(at, self.portion)]
            self.begin(number, source, self.last.at[k - 1], (self.data, peer))
            origin = lax.rem(self.tensor + self.count - k, self.count)
            self.flight.append((number, k - 1, (self.data, origin)))

    def line_add(self):
        at = self.start + self.tensor * self.portion if self.spread else self.start
        here = pl.ds(at, self.portion)
        for number, slot, origin in self.flight:
            self.wires.arrived(number, self.last.at[slot], origin)
        total = self.array[here]
        for number, slot, origin in self.flight:
            total = total + self.last[slot]
        self.result[here] = total

    def line_back(self):
        self.flight = []
        if self.spread:
            here = pl.ds(self.start + self.tensor * self.portion, self.portion)
            for k in range(1, self.count):
                number = self.wires.number()
                peer = lax.rem(self.tensor + k, self.count)
                self.begin(number, self.result.at[here], self.result.at[here], (self.data, peer))
                origin = lax.rem(self.tensor + self.count - k, self.count)
                there = pl.ds(self.start + origin * self.portion, self.portion)
                self.flight.append((number, there, (self.data, origin)))

    def bit_back(self):
        bit, keep, give, half = self.trail.pop()
        number = self.wires.number()
        target = (self.data ^ bit, self.tensor)
        here = pl.ds(keep, half)
        self.begin(number, self.result.at[here], self.result.at[here], target)
        self.flight = [(number, pl.ds(give, half), target)]
        self.start = jnp.minimum(keep, give)
        self.size = 2 * half

    def back_wait(self):
        for number, there, target in self.flight:
            self.wires.arrived(number, self.result.at[there], target)


def split_low(values):
    high = values.astype(jnp.bfloat16)
    return high, (values - high.astype(jnp.float32)).astype(jnp.bfloat16)


def back_kernel(
    data_count,
    tensor_count,
    attended,
    attended_grad,
    query_aux,
    key_aux,
    value_aux,
    first_full,
    heads_weight,
    expand_sum,
    reduce_sum,
    merge_sum,
    layer_base,
    layer_across,
    expand_momentum,
    reduce_momentum,
    expand_out,
    reduce_out,
    merge_out,
    heads_out,
    first_grad,
    output_rows,
    gram,
    upstream,
    grad_aux,
    key_turned,
    query_total,
    projected_grad,
    first_parts,
    first_beside,
    first_across,
    layer_got,
    expand_work,
    expand_got,
    expand_last,
    reduce_work,
    reduce_got,
    reduce_last,
    merge_work,
    merge_core,
    merge_line,
    merge_got,
    merge_last,
    heads_work,
    heads_got,
    heads_last,
    side,
    side_got,
    gram_work,
    gram_got,
    gram_last,
    send,
    receive,
    local,
):
    low = jnp.bfloat16
    members, rows, group_width = attended.shape
    head_local = group_width // HEAD_DIM
    seq_len = members * rows
    data, tensor = lax.axis_index("dp"), lax.axis_index("tensor")
    place = (data, tensor)
    core = data & 1
    group = 2 * (tensor & 1) + core
    wires = Wires(send, receive)
    beside, across, diagonal = (data ^ 1, tensor), (data, tensor ^ 1), (data ^ 1, tensor ^ 1)
    peers = [None, beside, across, diagonal]
    pending = []

    def begin(k, source, target, device, when=None):
        if when is None:
            wires.start(k, source, target, device)
        else:

            @pl.when(when)
            def _():
                wires.start(k, source, target, device)

        pending.append((k, source, device, when))

    def finish_sends():
        for k, source, device, when in pending:
            if when is None:
                wires.sent(k, source, device)
            else:

                @pl.when(when)
                def _():
                    wires.sent(k, source, device)

        pending.clear()

    copies = []
    for k, (source, target) in enumerate(
        ((expand_sum, expand_work), (reduce_sum, reduce_work), (merge_sum, merge_work))
    ):
        copies.append(pltpu.make_async_copy(source, target, local.at[k]))
        copies[-1].start()
    greet(column_and_plane(data, tensor, data_count, tensor_count))

    grad_numbers = {}
    for member in (2, 3, 1):
        grad_numbers[member] = wires.number()
        begin(
            grad_numbers[member],
            attended_grad.at[group ^ member],
            upstream.at[member],
            peers[member],
        )
    for copy in copies:
        copy.wait()
    bits = low_rank_bits(data_count)
    own_merge = merge_work.at[group]
    expand_group = Group(expand_work, expand_got, expand_last, bits[::-1], place, wires, begin)
    reduce_group = Group(reduce_work, reduce_got, reduce_last, bits, place, wires, begin)
    merge_group = Group(own_merge, merge_got, merge_last, bits[::-1], place, wires, begin)
    heads_group = Group(heads_work, heads_got, heads_last, bits, place, wires, begin)
    merge_numbers = [wires.number() for _ in range(3)]
    begin(merge_numbers[0], merge_work.at[group ^ 1], merge_core.at[0], beside)
    begin(merge_numbers[1], merge_work.at[group ^ 3], merge_core.at[1], beside)
    expand_group.bit_send()
    reduce_group.bit_send()
    layer_number = wires.number()
    upstream[0] = attended_grad[group]

    block = min(KEY_BLOCK, rows)
    lane = lax.broadcasted_iota(jnp.int32, (block, AUX), 1)
    blank = jnp.zeros((block, AUX - HEAD_DIM), jnp.float32)
    steps = rows // block

    def prepare(member):
        def one(step, carry):
            inside = pl.ds(pl.multiple_of(step * block, block), block)
            at_rows = pl.ds(pl.multiple_of(member * rows + step * block, block), block)
            gradient = upstream[member, inside, :].astype(jnp.float32)
            product = gradient * attended[member, inside, :].astype(jnp.float32)
            for head in range(head_local):
                columns = slice(head * HEAD_DIM, (head + 1) * HEAD_DIM)
                row_dot = jnp.sum(product[:, columns], axis=1, keepdims=True)
                first = row_dot.astype(low).astype(jnp.float32)
                wide = jnp.concatenate([gradient[:, columns], blank], axis=1)
                wide = jnp.where(lane == HEAD_DIM + 1, first, wide)
                wide = jnp.where(lane == HEAD_DIM + 2, row_dot - first, wide)
                grad_aux[head, at_rows, :] = wide.astype(low)
                key_turned[head, :, at_rows] = key_aux[head, at_rows, :].T[:HEAD_DIM]
            return carry

        lax.fori_loop(0, steps, one, 0)

    prepare(0)
    for member in (1, 2, 3):
        wires.arrived(grad_numbers[member], upstream.at[member], peers[member])
        prepare(member)
    begin(layer_number, layer_across, layer_got, across)
    query_total[...] = jnp.zeros_like(query_total)

    def back(step, carry):
        at_rows = pl.ds(pl.multiple_of(step * block, block), block)
        for head in range(head_local):
            scores = contract_cols(key_aux[head, at_rows, :], query_aux[head])
            chances = jnp.exp(scores)
            chance_grad = contract_cols(value_aux[head, at_rows, :], grad_aux[head])
            score_grad = (chances * chance_grad).astype(low)
            value_grad = dot_rows(chances.astype(low), grad_aux[head])
            key_grad = dot_rows(score_grad, query_aux[head])
            query_total[head] += dot_rows(key_turned[head, :, at_rows], score_grad)
            at = 3 * head * HEAD_DIM
            two = jnp.concatenate([key_grad[:, :HEAD_DIM], value_grad[:, :HEAD_DIM]], axis=1)
            projected_grad[at_rows, at + HEAD_DIM : at + 3 * HEAD_DIM] = two.astype(low)
        return carry

    quarter = seq_len // block // 4

    lax.fori_loop(0, quarter, back, 0)
    wires.arrived(merge_numbers[0], merge_core.at[0], beside)
    wires.arrived(merge_numbers[1], merge_core.at[1], beside)
    for k in (0, 1):
        here = group ^ (2 * k)
        total = merge_work[here].astype(jnp.float32) + merge_core[k].astype(jnp.float32)
        merge_work[here] = total.astype(low)
    begin(merge_numbers[2], merge_work.at[group ^ 2], merge_line, across)

    lax.fori_loop(quarter, 2 * quarter, back, 0)
    expand_group.bit_add()
    reduce_group.bit_add()
    expand_group.bit_send()
    reduce_group.bit_send()
    wires.arrived(merge_numbers[2], merge_line, across)
    total = merge_work[group].astype(jnp.float32) + merge_line[...].astype(jnp.float32)
    merge_work[group] = total.astype(low)
    merge_group.bit_send()

    lax.fori_loop(2 * quarter, 3 * quarter, back, 0)
    for which in (expand_group, reduce_group):
        which.bit_add()
        for _ in range(2, len(bits)):
            which.bit_send()
            which.bit_add()
        which.own_send()
    merge_group.bit_add()
    merge_group.bit_send()

    lax.fori_loop(3 * quarter, 4 * quarter, back, 0)
    merge_group.bit_add()
    for _ in range(2, len(bits)):
        merge_group.bit_send()
        merge_group.bit_add()
    expand_out[...] = expand_group.own_sum()
    reduce_out[...] = reduce_group.own_sum()
    merge_group.own_send()

    expand_part = momentum_decay * expand_momentum[...] + expand_out[...]
    reduce_part = momentum_decay * reduce_momentum[...] + reduce_out[...]
    first_core = core == 0
    side[0] = jnp.where(first_core, expand_part, reduce_part)
    side[1] = jnp.where(first_core, reduce_part, expand_part)
    side_number = wires.number()
    begin(side_number, side.at[1], side_got, beside)

    def finish(step, carry):
        at_rows = pl.ds(pl.multiple_of(step * block, block), block)
        for head in range(head_local):
            query_grad = query_total[head, :, at_rows].T * HEAD_DIM**-0.5
            at = 3 * head * HEAD_DIM
            projected_grad[at_rows, at : at + HEAD_DIM] = query_grad.astype(low)
        return carry

    lax.fori_loop(0, seq_len // block, finish, 0)

    wires.arrived(side_number, side_got, beside)
    both = jnp.concatenate([side[0], side_got[...]], axis=0)
    width = both.shape[1]
    high, rest = split_low(both)
    at = 0
    for k in range(0, width, SIDE):
        span = width - k
        part = contract_rows(high[:, k : k + SIDE], high[:, k:])
        part = part + contract_rows(high[:, k : k + SIDE], rest[:, k:])
        part = part + contract_rows(rest[:, k : k + SIDE], high[:, k:])
        gram_work[:, :, at : at + span] = part.reshape(SIDE // 8, 8, span)
        at += span
    slots = SIDE // 16
    halves = [
        ChipSum(gram_work, gram, gram_got.at[h], gram_last.at[h], h * slots, slots, order, place, tensor_count, wires, begin)
        for h, order in enumerate((bits, bits[::-1]))
    ]
    for half in halves:
        half.bit_send()

    heads_work[...] = (
        contract_rows(first_full[...], projected_grad[...]).reshape(heads_work.shape).astype(low)
    )
    heads_group.bit_send()
    first_numbers = [wires.number() for _ in range(3)]

    def first_part(member):
        at_rows = pl.ds(member * rows, rows)
        part = contract_cols(projected_grad[at_rows, :], heads_weight[...])
        first_parts[member] = part.astype(low)

    for k, member in enumerate((3, 1)):
        first_part(member)
        begin(first_numbers[k], first_parts.at[member], first_beside.at[k], beside)
    for half in halves:
        half.bit_add()
        for _ in range(2, len(bits)):
            half.bit_send()
            half.bit_add()
        half.bit_send()
    first_part(2)
    wires.arrived(first_numbers[0], first_beside.at[0], beside)
    total = first_parts[2].astype(jnp.float32) + first_beside[0].astype(jnp.float32)
    first_parts[2] = total.astype(low)
    heads_group.bit_add()
    for _ in range(2, len(bits)):
        heads_group.bit_send()
        heads_group.bit_add()
    heads_group.bit_send()
    for half in halves:
        half.bit_add()
        half.line_send()
    heads_group.bit_add()
    heads_group.own_send()
    begin(first_numbers[2], first_parts.at[2], first_across, across)
    first_part(0)
    for half in halves:
        half.line_add()
        half.line_back()
    merge_out[...] = merge_group.own_sum()
    wires.arrived(layer_number, layer_got, across)
    output_rows[...] = (layer_base[...] + layer_got[...].astype(jnp.float32)).astype(low)
    for _ in bits:
        for half in halves:
            half.back_wait()
            half.bit_back()
    heads_out[...] = heads_group.own_sum()
    wires.arrived(first_numbers[1], first_beside.at[1], beside)
    wires.arrived(first_numbers[2], first_across, across)
    first_grad[...] = (
        first_parts[0].astype(jnp.float32)
        + first_beside[1].astype(jnp.float32)
        + first_across[...].astype(jnp.float32)
    )
    for half in halves:
        half.back_wait()
    finish_sends()


def back_pallas(
    attended,
    attended_grad,
    query_aux,
    key_aux,
    value_aux,
    first_full,
    heads_weight,
    expand_sum,
    reduce_sum,
    merge_sum,
    layer_base,
    layer_across,
    expand_momentum,
    reduce_momentum,
):
    data_count, tensor_count = lax.axis_size("dp"), lax.axis_size("tensor")
    members, rows, group_width = attended.shape
    head_local = group_width // HEAD_DIM
    seq_len = members * rows
    low, wide = jnp.bfloat16, jnp.float32
    width, columns = heads_weight.shape
    unit_block = expand_sum.shape[1:]
    merge_block = merge_sum.shape[2:]
    heads_block = (width // data_count, columns)
    packed = sum(width - k for k in range(0, width, SIDE))
    inside = pl.BlockSpec(memory_space=pltpu.VMEM)
    outs = (
        (unit_block, wide),
        (unit_block, wide),
        (merge_block, wide),
        (heads_block, wide),
        ((rows, width), wide),
        ((rows, width), low),
        ((SIDE // 8, 8, packed), wide),
    )
    steps = data_count // 2 - 1
    slots = SIDE // 16
    left = slots // (data_count // 2)
    portion = left // tensor_count if left % tensor_count == 0 else left
    scratch = []
    for shape, kind in (
        ((members, rows, group_width), low),
        ((head_local, seq_len, AUX), low),
        ((head_local, HEAD_DIM, seq_len), low),
        ((head_local, HEAD_DIM, seq_len), wide),
        ((seq_len, columns), low),
        ((members, rows, width), low),
        ((2, rows, width), low),
        ((rows, width), low),
        ((rows, width), low),
        ((data_count,) + unit_block, low),
        ((steps, 2) + unit_block, low),
        ((2,) + unit_block, low),
        ((data_count,) + unit_block, low),
        ((steps, 2) + unit_block, low),
        ((2,) + unit_block, low),
        (merge_sum.shape, low),
        ((2, data_count) + merge_block, low),
        ((data_count,) + merge_block, low),
        ((steps, 2) + merge_block, low),
        ((2,) + merge_block, low),
        ((data_count,) + heads_block, low),
        ((steps, 2) + heads_block, low),
        ((2,) + heads_block, low),
        ((2,) + unit_block, wide),
        (unit_block, wide),
        ((SIDE // 8, 8, packed), wide),
        ((2, slots, 8, packed), wide),
        ((2, tensor_count - 1, portion, 8, packed), wide),
    ):
        scratch.append(pltpu.VMEM(shape, kind))
    copies = 3 + 3 + 1 + 4 * (steps + 4) + 1 + 3
    copies += 2 * (2 * (data_count // 2).bit_length() + 2 * tensor_count)
    return pl.pallas_call(
        functools.partial(back_kernel, data_count, tensor_count),
        out_shape=tuple(jax.ShapeDtypeStruct(*out) for out in outs),
        in_specs=[inside] * 14,
        out_specs=(inside,) * len(outs),
        scratch_shapes=scratch
        + [
            pltpu.SemaphoreType.DMA((copies,)),
            pltpu.SemaphoreType.DMA((copies,)),
            pltpu.SemaphoreType.DMA((3,)),
        ],
        compiler_params=pltpu.CompilerParams(
            vmem_limit_bytes=VMEM_LIMIT, collective_id=3, has_side_effects=True
        ),
        cost_estimate=pl.CostEstimate(
            flops=10 * head_local * seq_len * seq_len * AUX,
            bytes_accessed=10 * seq_len * width,
            transcendentals=head_local * seq_len * seq_len,
        ),
        name="back",
    )(
        attended,
        attended_grad,
        query_aux,
        key_aux,
        value_aux,
        first_full,
        heads_weight,
        expand_sum,
        reduce_sum,
        merge_sum,
        layer_base,
        layer_across,
        expand_momentum,
        reduce_momentum,
    )


EXACT_THREE = lax.Precision.HIGH
SIDE = 256


def swap_bit(values, axis_name, bit):
    count = lax.axis_size(axis_name)
    return lax.ppermute(values, axis_name, [(i, i ^ bit) for i in range(count)])


def data_bits():
    return [1 << k for k in range(1, lax.axis_size("dp").bit_length() - 1)]


def has_bit(index, bit):
    return (index & bit) != 0


def gather_bits_absolute(block, bits):
    index = lax.axis_index("dp")
    for bit in bits:
        other = swap_bit(block, "dp", bit)
        mine = has_bit(index, bit)
        block = jnp.concatenate(
            [jnp.where(mine, other, block), jnp.where(mine, block, other)], axis=0
        )
    return block


def pair_permute(values, where_to):
    data_count, tensor_count = lax.axis_size("dp"), lax.axis_size("tensor")
    moves = []
    for i in range(data_count):
        for j in range(tensor_count):
            target = where_to(i, j)
            if target is not None:
                moves.append((i * tensor_count + j, target[0] * tensor_count + target[1]))
    return lax.ppermute(values, ("dp", "tensor"), moves)


def exchange_home(values):
    return pair_permute(
        values, lambda i, j: (i ^ 1, j ^ 2) if (i & 1) != (j >> 1) else None
    )


def gather_head_group(shard):
    first = []
    for core in (0, 1):
        got = []
        for half in (0, 1):
            got.append(
                pair_permute(
                    shard,
                    lambda i, j: (i - core + (j & 1), (j >> 1) + 2 * half)
                    if (i & 1) == core
                    else None,
                )
            )
        first.append(jnp.where(lax.axis_index("tensor") >= 2, got[1], got[0]))
    return gather_bits_absolute(jnp.concatenate(first, axis=0), data_bits())


def unpack_symmetric(packed, size):
    rows, at = [], 0
    for k in range(0, size, SIDE):
        rows.append(packed[:, at : at + size - k])
        at += size - k
    full = []
    for i in range(len(rows)):
        blocks = [rows[j][:, (i - j) * SIDE : (i - j + 1) * SIDE].T for j in range(i)]
        full.append(jnp.concatenate(blocks + [rows[i]], axis=1))
    return jnp.concatenate(full, axis=0)


def sum_over_all(values):
    for bit in (1, 2):
        values = values + swap_bit(values, "tensor", bit)
    for bit in [1] + data_bits():
        values = values + swap_bit(values, "dp", bit)
    return values


def polynomial_chain(gram, product):
    identity = jnp.eye(gram.shape[-1], dtype=jnp.float32)
    chain = None
    for step in range(NEWTON_STEPS):
        square = product(gram, gram)
        factor = newton_linear * identity + newton_cubic * gram + newton_quintic * square
        chain = factor if chain is None else product(chain, factor)
        if step < NEWTON_STEPS - 1:
            gram = product(product(gram, factor), factor)
    return chain


def per_device(
    tokens,
    segment_ids,
    out_grad,
    heads_weight,
    merge_weight,
    expand_weight,
    reduce_weight,
    heads_momentum,
    merge_momentum,
    expand_momentum,
    reduce_momentum,
    heads_average,
    merge_average,
    expand_average,
    reduce_average,
    vectors,
    vector_momentum,
    vector_average,
):
    low = jnp.bfloat16
    tensor_count = lax.axis_size("tensor")
    data_count = lax.axis_size("dp")
    tensor_index = lax.axis_index("tensor")
    core = lax.axis_index("dp") & 1
    row_count = tokens.shape[0]
    seq_len = row_count * tensor_count
    head_local = heads_weight.shape[1] // (3 * HEAD_DIM)
    group_width = head_local * HEAD_DIM
    at_home = core == (tensor_index >> 1)
    group = 2 * (tensor_index & 1) + core

    own_segments = jnp.where(at_home, segment_ids, swap_bit(segment_ids, "dp", 1))
    chunk_at = []
    for member in range(4):
        its_core, its_tensor = core ^ (member & 1), tensor_index ^ (member >> 1)
        chunk_at.append(jnp.where(its_core == (its_tensor >> 1), its_tensor, its_tensor ^ 2))
    segments = jnp.take(
        own_segments.reshape(tensor_count, row_count), jnp.stack(chunk_at), axis=0
    ).reshape(seq_len)
    gather_heads = heads_weight.shape[0] % 16 == 0
    heads_low = heads_weight.astype(low)
    if not gather_heads:
        heads_low = gather_head_group(heads_low)
    (
        attended_full,
        attended_own,
        query_aux,
        key_aux,
        value_aux,
        first_full,
        token_chunks,
        full_heads,
        full_expand,
        full_reduce,
        full_merge,
        sequence_grad,
    ) = front_pallas(
        tokens,
        heads_low,
        expand_weight.T.astype(low),
        reduce_weight.astype(low),
        merge_weight.T.astype(low),
        vectors,
        segments,
        out_grad,
        gather_heads,
    )
    full_heads = full_heads.reshape(D, 3 * group_width) if gather_heads else heads_low
    full_merge = jnp.transpose(full_merge, (0, 2, 1, 3)).reshape(D, D)
    full_expand = full_expand.reshape(-1, D)
    full_reduce = full_reduce.reshape(-1, D)
    (
        layer_base,
        layer_across,
        middle_grad,
        attended_grad,
        expand_sum,
        reduce_sum,
        merge_sum,
        vector_sums,
    ) = middle_pallas(
        attended_own, full_merge, token_chunks[0], vectors, full_expand, full_reduce, sequence_grad
    )
    unit_shape = (data_count,) + reduce_weight.shape
    (
        expand_rows,
        reduce_gradient,
        merge_rows,
        heads_gradient,
        first_grad,
        output_rows,
        wide_gram,
    ) = back_pallas(
        attended_full,
        attended_grad,
        query_aux,
        key_aux,
        value_aux,
        first_full,
        full_heads,
        expand_sum.reshape(unit_shape),
        reduce_sum.reshape(unit_shape),
        merge_sum.reshape(4, data_count, merge_weight.shape[1], group_width),
        layer_base,
        layer_across,
        expand_momentum.T,
        reduce_momentum,
    )
    layer_output = jnp.where(at_home, output_rows, exchange_home(output_rows))
    expand_gradient, merge_gradient = expand_rows.T, merge_rows.T
    expand_new_momentum = momentum_decay * expand_momentum + expand_gradient
    reduce_new_momentum = momentum_decay * reduce_momentum + reduce_gradient
    expand_part = expand_new_momentum.T
    reduce_part = reduce_new_momentum
    first_core = core == 0
    wide_gram = unpack_symmetric(wide_gram.reshape(SIDE, -1), D)

    normed_one, inverse_one = center_scale(token_chunks[0].astype(jnp.float32))
    input_rows = middle_grad + norm_backward(first_grad, normed_one, inverse_one, vectors[0])
    input_gradient = jnp.where(
        at_home, input_rows, exchange_home(input_rows.astype(low)).astype(jnp.float32)
    )
    vector_local = jnp.stack(
        [jnp.sum(first_grad * normed_one, axis=0), jnp.sum(first_grad, axis=0)]
    )
    vector_gradient = sum_over_all(jnp.concatenate([vector_local, vector_sums], axis=0))
    heads_new_momentum = momentum_decay * heads_momentum + heads_gradient
    merge_new_momentum = momentum_decay * merge_momentum + merge_gradient
    vector_new_momentum = momentum_decay * vector_momentum + vector_gradient

    heads_part = heads_new_momentum.reshape(heads_new_momentum.shape[0], head_local * 3, HEAD_DIM)
    merge_part = merge_new_momentum.reshape(head_local, HEAD_DIM, merge_new_momentum.shape[1])
    small_gram = jnp.concatenate(
        [
            jnp.einsum("rmd,rme->mde", heads_part, heads_part, precision=highest),
            jnp.einsum("hdc,hec->hde", merge_part, merge_part, precision=highest),
        ],
        axis=0,
    )
    for bit in [1] + data_bits():
        small_gram = small_gram + swap_bit(small_gram, "dp", bit)
    small_factor = 1.0 / (jnp.sqrt(jnp.trace(small_gram, axis1=1, axis2=2)) + newton_epsilon)
    small_chain = polynomial_chain(
        small_gram * (small_factor * small_factor)[:, None, None],
        lambda left, right: jnp.einsum("mde,mef->mdf", left, right, precision=highest),
    )
    small_chain = small_chain * small_factor[:, None, None]
    side_count = 3 * head_local
    heads_ortho = jnp.einsum("rmd,mde->rme", heads_part, small_chain[:side_count], precision=highest)
    merge_ortho = jnp.einsum("hde,hec->hdc", small_chain[side_count:], merge_part, precision=highest)

    wide_factor = 1.0 / (jnp.sqrt(jnp.trace(wide_gram)) + newton_epsilon)
    wide_chain = polynomial_chain(
        wide_gram * (wide_factor * wide_factor),
        lambda left, right: jnp.dot(left, right, precision=EXACT_THREE),
    )
    wide_chain = wide_chain * wide_factor
    other_chain = swap_bit(wide_chain, "dp", 1)
    expand_ortho = jnp.dot(
        expand_part, jnp.where(first_core, wide_chain, other_chain), precision=EXACT_THREE
    ).T
    reduce_ortho = jnp.dot(
        reduce_part, jnp.where(first_core, other_chain, wide_chain), precision=EXACT_THREE
    )

    keep_factor = 1.0 - muon_rate * weight_decay
    head_step = muon_rate * 0.2 * math.sqrt(max(D, HEAD_DIM))
    wide_step = muon_rate * 0.2 * math.sqrt(max(D, FF))
    heads_new_weight = heads_weight * keep_factor - head_step * heads_ortho.reshape(
        heads_weight.shape
    )
    merge_new_weight = merge_weight * keep_factor - head_step * merge_ortho.reshape(
        merge_weight.shape
    )
    expand_new_weight = expand_weight * keep_factor - wide_step * expand_ortho
    reduce_new_weight = reduce_weight * keep_factor - wide_step * reduce_ortho
    vector_new_value = vectors - vector_rate / math.sqrt(SEQ * data_count) * vector_new_momentum
    heads_new_average = average_decay * heads_average + (1.0 - average_decay) * heads_new_weight
    merge_new_average = average_decay * merge_average + (1.0 - average_decay) * merge_new_weight
    expand_new_average = average_decay * expand_average + (1.0 - average_decay) * expand_new_weight
    reduce_new_average = average_decay * reduce_average + (1.0 - average_decay) * reduce_new_weight
    vector_new_average = average_decay * vector_average + (1.0 - average_decay) * vector_new_value
    return (
        layer_output,
        input_gradient,
        heads_gradient,
        merge_gradient,
        expand_gradient,
        reduce_gradient,
        heads_new_momentum,
        merge_new_momentum,
        expand_new_momentum,
        reduce_new_momentum,
        heads_new_weight,
        merge_new_weight,
        expand_new_weight,
        reduce_new_weight,
        heads_new_average,
        merge_new_average,
        expand_new_average,
        reduce_new_average,
        vector_gradient,
        vector_new_momentum,
        vector_new_value,
        vector_new_average,
    )


def solution(mesh):
    placed = (
        P(("dp", "tensor"), None),
        P("dp"),
        P("dp", None),
        P("dp", "tensor"),
        P("tensor", "dp"),
        P(None, ("tensor", "dp")),
        P(("tensor", "dp"), None),
        P("dp", "tensor"),
        P("tensor", "dp"),
        P(None, ("tensor", "dp")),
        P(("tensor", "dp"), None),
        P("dp", "tensor"),
        P("tensor", "dp"),
        P(None, ("tensor", "dp")),
        P(("tensor", "dp"), None),
        P(),
        P(),
        P(),
    )
    return jax.shard_map(
        per_device,
        mesh=mesh,
        in_specs=placed,
        out_specs=(
            P(("dp", "tensor"), None),
            P(("dp", "tensor"), None),
            P("dp", "tensor"),
            P("tensor", "dp"),
            P(None, ("tensor", "dp")),
            P(("tensor", "dp"), None),
            P("dp", "tensor"),
            P("tensor", "dp"),
            P(None, ("tensor", "dp")),
            P(("tensor", "dp"), None),
            P("dp", "tensor"),
            P("tensor", "dp"),
            P(None, ("tensor", "dp")),
            P(("tensor", "dp"), None),
            P("dp", "tensor"),
            P("tensor", "dp"),
            P(None, ("tensor", "dp")),
            P(("tensor", "dp"), None),
            P(),
            P(),
            P(),
            P(),
        ),
        check_vma=False,
    )
```

```python
import functools
import math

import jax
import jax.numpy as jnp
from jax import lax
from jax.experimental import pallas as pl
from jax.experimental.pallas import tpu as pltpu
from jax.sharding import PartitionSpec as P

D = 768
HEAD_DIM = 64
FF = 3072
SEQ = 2048
NEWTON_STEPS = 5


highest = lax.Precision.HIGHEST
norm_epsilon = 1e-06
newton_epsilon = 1e-07
newton_linear = 3.4445
newton_cubic = -4.775
newton_quintic = 2.0315
momentum_decay = 0.5
average_decay = 0.9
muon_rate = 0.2
weight_decay = 0.1
vector_rate = 0.15
masked_score = -1e30
VMEM_LIMIT = 56 * 2**20


def center_scale(values):
    average = jnp.mean(values, axis=-1, keepdims=True)
    centered = values - average
    inverse = lax.rsqrt(jnp.mean(centered * centered, axis=-1, keepdims=True) + norm_epsilon)
    return (centered * inverse, inverse)


def norm_backward(upstream, normed, inverse, gain):
    scaled = upstream * gain
    mean_one = jnp.mean(scaled, axis=-1, keepdims=True)
    mean_two = jnp.mean(scaled * normed, axis=-1, keepdims=True)
    return inverse * (scaled - mean_one - normed * mean_two)


def gelu_exact(values):
    return jax.nn.gelu(values, approximate=False)


def contract_rows(left_side, right_side):
    return lax.dot_general(
        left_side, right_side, (((0,), (0,)), ((), ())), preferred_element_type=jnp.float32
    )


def contract_cols(left_side, right_side):
    return lax.dot_general(
        left_side, right_side, (((1,), (1,)), ((), ())), preferred_element_type=jnp.float32
    )


KEY_BLOCK = 256
AUX = 128


MESH = pl.DeviceIdType.MESH


def low_rank_bits(data_count):
    return [1 << k for k in range(1, data_count.bit_length() - 1)]


class Wires:
    def __init__(self, send, receive):
        self.send, self.receive, self.used = send, receive, 0

    def number(self):
        self.used += 1
        return self.used - 1

    def start(self, k, source, target, device):
        copy = pltpu.make_async_remote_copy(
            source, target, self.send.at[k], self.receive.at[k], device_id=device, device_id_type=MESH
        )
        copy.start()

    def sent(self, k, source, device):
        pltpu.make_async_remote_copy(
            source, source, self.send.at[k], self.receive.at[k], device_id=device, device_id_type=MESH
        ).wait_send()

    def arrived(self, k, target, device):
        pltpu.make_async_remote_copy(
            target, target, self.send.at[k], self.receive.at[k], device_id=device, device_id_type=MESH
        ).wait_recv()


def greet(devices):
    barrier = pltpu.get_barrier_semaphore()
    for device in devices:
        pl.semaphore_signal(barrier, inc=1, device_id=device, device_id_type=MESH)
    pl.semaphore_wait(barrier, len(devices))


def column_and_plane(data, tensor, data_count, tensor_count):
    found = []
    for core in (0, 1):
        for step in range(tensor_count):
            if core or step:
                found.append((data ^ core, lax.rem(tensor + step, tensor_count)))
    for k in range(1, data_count // 2):
        found.append((data ^ (2 * k), tensor))
    return found


def front_kernel(
    data_count,
    tensor_count,
    gather_heads,
    tokens,
    heads,
    expand,
    reduce,
    merge,
    vectors,
    segment_column,
    out_grad,
    attended,
    attended_rows,
    query_aux,
    key_aux,
    value_aux,
    first_full,
    chunks,
    all_heads,
    all_expand,
    all_reduce,
    all_merge,
    sequence_grad,
    arrivals,
    send,
    receive,
    local,
):
    low = jnp.bfloat16
    rows, width = tokens.shape
    head_local = query_aux.shape[0]
    group_width = head_local * HEAD_DIM
    data, tensor = lax.axis_index("dp"), lax.axis_index("tensor")
    core, half = data & 1, tensor >> 1
    home = core == half
    group = 2 * (tensor & 1) + core
    wires = Wires(send, receive)
    beside, across, diagonal = (data ^ 1, tensor), (data, tensor ^ 1), (data ^ 1, tensor ^ 1)
    members = [None, beside, across, diagonal]
    away = (data ^ 1, tensor ^ 2)
    pieces = [pl.ds(p * (rows // 2), rows // 2) for p in range(2)]
    pending = []

    def begin(k, source, target, device, when=None):
        if when is None:
            wires.start(k, source, target, device)
        else:

            @pl.when(when)
            def _():
                wires.start(k, source, target, device)

        pending.append((k, source, device, when))

    def await_arrival(k, target, device, when=None):
        if when is None:
            wires.arrived(k, target, device)
        else:

            @pl.when(when)
            def _():
                wires.arrived(k, target, device)

    own = pltpu.make_async_copy(merge, all_merge.at[data, tensor], local.at[0])
    own.start()
    greet(column_and_plane(data, tensor, data_count, tensor_count))

    def z_hop(hop):
        made = []
        for mat, single in ((all_merge, merge),):
            for way in (1, -1):
                number = wires.number()
                slot = tensor - way * (hop - 1)
                going = (tensor + way >= 0) & (tensor + way < tensor_count)
                going = going & (slot >= 0) & (slot < tensor_count)
                source = single if hop == 1 else mat.at[data, slot]
                begin(number, source, mat.at[data, slot], (data, tensor + way), going)
                made.append((number, mat, tensor - way * hop, tensor - way))
        return made

    def z_wait(made):
        for number, mat, slot, source in made:
            valid = (slot >= 0) & (slot < tensor_count)
            await_arrival(number, mat.at[data, slot], (data, source), valid)

    pair = (data >> 1) * 2

    def group_send(block, whole):
        numbers = [wires.number() for _ in range(4)]
        for k in (0, 1):
            target = (pair + (tensor & 1), (tensor >> 1) + 2 * k)
            itself = (target[0] == data) & (target[1] == tensor)
            for c in (0, 1):
                begin(
                    numbers[2 * k + c],
                    block,
                    whole.at[data],
                    target,
                    jnp.logical_not(itself) & (core == c),
                )

            @pl.when(itself)
            def _():
                copy = pltpu.make_async_copy(block, whole.at[data], local.at[1])
                copy.start()
                copy.wait()

        return numbers

    def group_wait(numbers, whole):
        for k in (0, 1):
            for c in (0, 1):
                source = (pair + c, group)
                itself = (source[0] == data) & (source[1] == tensor)
                await_arrival(
                    numbers[2 * k + c],
                    whole.at[pair + c],
                    source,
                    jnp.logical_not(itself) & (half == k),
                )

    merge_first = z_hop(1)
    if gather_heads:
        head_numbers = group_send(heads, all_heads)

    numbers = [wires.number() for _ in range(12)]
    for p, piece in enumerate(pieces):
        begin(numbers[p], tokens.at[piece], chunks.at[2, piece], across, home)
        begin(numbers[2 + p], tokens.at[piece], chunks.at[0, piece], away, jnp.logical_not(home))
        begin(numbers[4 + p], tokens.at[piece], chunks.at[1, piece], beside, home)

    @pl.when(home)
    def _():
        chunks[0] = tokens[...]

    if gather_heads:
        group_wait(head_numbers, all_heads)
        plane = []
        for k in range(1, data_count // 2):
            number = wires.number()
            plane.append((number, k))
            begin(number, all_heads.at[pl.ds(pair, 2)], all_heads.at[pl.ds(pair, 2)], (data ^ (2 * k), tensor))

    for p, piece in enumerate(pieces):
        await_arrival(numbers[2 + p], chunks.at[0, piece], away, jnp.logical_not(home))
        begin(numbers[6 + p], chunks.at[0, piece], chunks.at[2, piece], across, jnp.logical_not(home))
        begin(numbers[8 + p], chunks.at[0, piece], chunks.at[1, piece], beside, jnp.logical_not(home))

    expand_numbers = group_send(expand, all_expand)
    reduce_numbers = group_send(reduce, all_reduce)

    if gather_heads:
        for number, k in plane:
            there = pl.ds(pair ^ (2 * k), 2)
            await_arrival(number, all_heads.at[there], (data ^ (2 * k), tensor))

    block = min(KEY_BLOCK, rows)
    lane = lax.broadcasted_iota(jnp.int32, (block, AUX), 1)
    blank = jnp.zeros((block, AUX - HEAD_DIM), jnp.float32)
    steps = rows // block

    def prepare(member):
        def one(step, carry):
            inside = pl.ds(pl.multiple_of(step * block, block), block)
            at_rows = pl.ds(pl.multiple_of(member * rows + step * block, block), block)
            normed, _ = center_scale(chunks[member, inside, :].astype(jnp.float32))
            first_in = (normed * vectors[0:1, :] + vectors[1:2, :]).astype(low)
            first_full[at_rows, :] = first_in
            weight = all_heads[...].reshape(width, 3 * group_width)
            projected = jnp.dot(first_in, weight, preferred_element_type=jnp.float32)
            projected = projected.astype(low).astype(jnp.float32)
            same = lane - HEAD_DIM == segment_column[at_rows, :]
            segment_lane = (lane >= HEAD_DIM) & (lane < HEAD_DIM + 3)
            query_extra = jnp.where(same & segment_lane, 1.0, 0.0)
            key_extra = jnp.where(
                segment_lane,
                jnp.where(same, 0.0, masked_score),
                jnp.where((lane >= HEAD_DIM + 3) & (lane < HEAD_DIM + 6), -1.0, 0.0),
            )
            value_extra = jnp.where(
                lane == HEAD_DIM,
                1.0,
                jnp.where((lane == HEAD_DIM + 1) | (lane == HEAD_DIM + 2), -1.0, 0.0),
            )
            for head in range(head_local):
                for which, (ref, extra, factor) in enumerate(
                    (
                        (query_aux, query_extra, HEAD_DIM**-0.5),
                        (key_aux, key_extra, 1.0),
                        (value_aux, value_extra, 1.0),
                    )
                ):
                    at = (3 * head + which) * HEAD_DIM
                    part = jnp.concatenate([projected[:, at : at + HEAD_DIM] * factor, blank], axis=1)
                    ref[head, at_rows, :] = jnp.where(lane < HEAD_DIM, part, extra).astype(low)
            return carry

        lax.fori_loop(0, steps, one, 0)

    def attend(member, steps_here):
        def one(step, carry):
            inside = pl.ds(pl.multiple_of(step * block, block), block)
            at_rows = pl.ds(pl.multiple_of(member * rows + step * block, block), block)
            done = []
            for head in range(head_local):
                query = query_aux[head, at_rows, :]
                scores = contract_cols(query, key_aux[head])
                row_max = jnp.max(scores, axis=1, keepdims=True)
                exponent = jnp.exp(scores - row_max).astype(low)
                output = jnp.dot(exponent, value_aux[head], preferred_element_type=jnp.float32)
                totals = output[:, HEAD_DIM : HEAD_DIM + 1]
                done.append(output[:, :HEAD_DIM] / totals)
                logsum = row_max + jnp.log(totals)
                first = logsum.astype(low).astype(jnp.float32)
                second = (logsum - first).astype(low).astype(jnp.float32)
                third = logsum - first - second
                wide = query.astype(jnp.float32)
                wide = jnp.where(lane == HEAD_DIM + 3, first, wide)
                wide = jnp.where(lane == HEAD_DIM + 4, second, wide)
                wide = jnp.where(lane == HEAD_DIM + 5, third, wide)
                query_aux[head, at_rows, :] = wide.astype(low)
            attended[member, inside, :] = jnp.concatenate(done, axis=1).astype(low)
            return carry

        lax.fori_loop(*steps_here, one, 0)

    bits = low_rank_bits(data_count)
    schedule = []
    held = [[0], [0], [0]]
    for k in range(len(bits)):
        plan = []
        for m, mat in enumerate((all_expand, all_reduce, all_merge)):
            bit = bits[-1 - k] if m == 1 else bits[k]
            plan.append((mat, bit, list(held[m]), m < 2))
            held[m] = held[m] + [offset ^ bit for offset in held[m]]
        schedule.append(plan)
    schedule.append([(all_merge, 1, list(held[2]), False)])

    prepare(0)
    for p, piece in enumerate(pieces):
        await_arrival(numbers[p], chunks.at[2, piece], across, home)
        await_arrival(numbers[6 + p], chunks.at[2, piece], across, jnp.logical_not(home))
        begin(numbers[10 + p], chunks.at[2, piece], chunks.at[3, piece], beside)

    def bit_step(plan):
        made = []
        for mat, bit, held, wide in plan:
            for offset in held:
                number = wires.number()
                place = (pair if wide else data) ^ offset
                there = pl.ds(place ^ bit, 2) if wide else place ^ bit
                place = pl.ds(place, 2) if wide else place
                begin(number, mat.at[place], mat.at[place], (data ^ bit, tensor))
                made.append((number, mat, there, bit))
        return made

    def bit_wait(made):
        for number, mat, there, bit in made:
            await_arrival(number, mat.at[there], (data ^ bit, tensor))


    grad_numbers = [wires.number() for _ in range(4)]
    grad_copies = []
    for member in range(4):
        its_core, its_tensor = core ^ (member & 1), tensor ^ (member >> 1)
        chunk = its_tensor ^ (2 * (its_core ^ (its_tensor >> 1)))
        source = out_grad.at[pl.ds(pl.multiple_of(chunk * rows, rows), rows)]
        copy = pltpu.make_async_copy(source, sequence_grad.at[member], local.at[2 + member])
        grad_copies.append(copy)
        pl.when(home)(copy.start)
        begin(grad_numbers[member], source, sequence_grad.at[member ^ 1], beside, home)
    for p, piece in enumerate(pieces):
        await_arrival(numbers[4 + p], chunks.at[1, piece], beside, jnp.logical_not(home))
        await_arrival(numbers[8 + p], chunks.at[1, piece], beside, home)
    z_wait(merge_first)
    merge_made = z_hop(2)
    prepare(1)
    prepare(2)
    for p, piece in enumerate(pieces):
        await_arrival(numbers[10 + p], chunks.at[3, piece], beside)
    prepare(3)
    z_wait(merge_made)
    merge_made = z_hop(3)
    group_wait(expand_numbers, all_expand)
    group_wait(reduce_numbers, all_reduce)
    made = bit_step(schedule[0][:2])

    exchange = {}
    for member in (3, 2, 1, 0):
        attend(member, (0, steps // 2))
        if member == 3:
            z_wait(merge_made)
            own.wait()
            merge_made = bit_step(schedule[0][2:])
        elif member == 2:
            bit_wait(made)
            made = bit_step(schedule[1][:2])
        attend(member, (steps // 2, steps))
        if member:
            number = wires.number()
            begin(number, attended.at[member], arrivals.at[group], members[member])
            exchange[member] = number
        else:
            arrivals[group] = attended[0]
        if member == 2:
            bit_wait(merge_made)
            merge_made = bit_step(schedule[1][2:])
        elif member == 1:
            bit_wait(merge_made)
            merge_made = bit_step(schedule[2])
    made = made + merge_made
    for plan in schedule[3:]:
        bit_wait(made)
        made = bit_step(plan)
    for member, number in exchange.items():
        await_arrival(number, arrivals.at[group ^ member], members[member])
    attended_rows[...] = jnp.concatenate([arrivals[k] for k in range(4)], axis=1)
    bit_wait(made)
    for member in range(4):
        pl.when(home)(grad_copies[member].wait)
        await_arrival(
            grad_numbers[member], sequence_grad.at[member ^ 1], beside, jnp.logical_not(home)
        )
    for k, source, device, when in pending:
        if when is None:
            wires.sent(k, source, device)
        else:

            @pl.when(when)
            def _():
                wires.sent(k, source, device)


def front_pallas(tokens, heads, expand, reduce, merge, vectors, segments, out_grad, gather_heads):
    data_count, tensor_count = lax.axis_size("dp"), lax.axis_size("tensor")
    rows, width = tokens.shape
    low = jnp.bfloat16
    head_columns = heads.shape[-1]
    head_local = head_columns // (3 * HEAD_DIM)
    seq_len = segments.shape[0]
    group_width = head_local * HEAD_DIM
    aux = jax.ShapeDtypeStruct((head_local, seq_len, AUX), low)
    inside = pl.BlockSpec(memory_space=pltpu.VMEM)
    anywhere = pl.BlockSpec(memory_space=pl.ANY)
    gathered = [
        jax.ShapeDtypeStruct((data_count,) + expand.shape, low),
        jax.ShapeDtypeStruct((data_count,) + reduce.shape, low),
        jax.ShapeDtypeStruct((data_count, tensor_count) + merge.shape, low),
        jax.ShapeDtypeStruct((4, rows, width), low),
    ]
    hops = 2 * (tensor_count - 1) + 2 * (data_count // 2 - 1) + data_count - 1
    copies = 12 + data_count // 2 + 12 + hops + 4 + 3
    if gather_heads:
        heads_out = jax.ShapeDtypeStruct((data_count,) + heads.shape, low)
    else:
        heads_out = jax.ShapeDtypeStruct(heads.shape, low)

    def kernel(*refs):
        if not gather_heads:
            refs = list(refs)
            refs[15] = refs[1]
        front_kernel(data_count, tensor_count, gather_heads, *refs)

    return pl.pallas_call(
        kernel,
        out_shape=(
            jax.ShapeDtypeStruct((4, rows, group_width), low),
            jax.ShapeDtypeStruct((rows, 4 * group_width), low),
            aux,
            aux,
            aux,
            jax.ShapeDtypeStruct((seq_len, width), low),
            jax.ShapeDtypeStruct((4, rows, width), low),
            heads_out,
            *gathered,
        ),
        in_specs=[inside] * 7 + [anywhere],
        out_specs=(inside,) * 8 + (anywhere,) * 3 + (inside,),
        scratch_shapes=[
            pltpu.VMEM((4, rows, group_width), low),
            pltpu.SemaphoreType.DMA((copies,)),
            pltpu.SemaphoreType.DMA((copies,)),
            pltpu.SemaphoreType.DMA((6,)),
        ],
        compiler_params=pltpu.CompilerParams(
            vmem_limit_bytes=VMEM_LIMIT, collective_id=1, has_side_effects=True
        ),
        cost_estimate=pl.CostEstimate(
            flops=4 * head_local * seq_len * seq_len * AUX,
            bytes_accessed=8 * seq_len * width,
            transcendentals=head_local * seq_len * seq_len,
        ),
        name="front",
    )(tokens, heads, expand, reduce, merge, vectors, segments.reshape(seq_len, 1), out_grad)


def dot_rows(left_side, right_side):
    return jnp.dot(left_side, right_side, preferred_element_type=jnp.float32)


def middle_kernel(
    data_count,
    attended_rows,
    merge,
    tokens,
    vectors,
    expand,
    reduce,
    sequence_grad,
    layer_base,
    layer_across,
    middle_grad,
    attended_grad,
    expand_sum,
    reduce_sum,
    merge_sum,
    vector_sums,
    second_in,
    middle,
    hidden,
    expand_grad,
    partial,
    reduced,
    from_beside,
    reduced_beside,
    from_across,
    expand_got,
    reduce_got,
    send,
    receive,
):
    low = jnp.bfloat16
    rows, width = tokens.shape
    group_width = width // 4
    data, tensor = lax.axis_index("dp"), lax.axis_index("tensor")
    wires = Wires(send, receive)
    beside, across = (data ^ 1, tensor), (data, tensor ^ 1)
    part = rows // 2
    pieces = [pl.ds(p * part, part) for p in range(2)]
    pending = []

    def begin(k, source, target, device):
        wires.start(k, source, target, device)
        pending.append((k, source, device))

    bits = low_rank_bits(data_count)
    greet([beside, across] + [(data ^ bit, tensor) for bit in sorted({bits[0], bits[-1]})])
    groups = [
        Group(work, got, None, order, (data, tensor), wires, begin)
        for work, got, order in (
            (expand_sum, expand_got, bits[::-1]),
            (reduce_sum, reduce_got, bits),
        )
    ]
    numbers = [[wires.number() for _ in range(2)] for _ in range(3)]
    for p, piece in enumerate(pieces):
        merged = contract_cols(attended_rows[piece, :], merge[...])
        here = tokens[piece, :].astype(jnp.float32) + merged + vectors[4:5, :]
        middle[piece, :] = here
        normed, _ = center_scale(here)
        second_in[0, piece, :] = (normed * vectors[2:3, :] + vectors[3:4, :]).astype(low)
        begin(numbers[0][p], second_in.at[0, piece], second_in.at[2, piece], across)
        begin(numbers[1][p], second_in.at[0, piece], second_in.at[1, piece], beside)

    def unit(member, p):
        piece = pieces[p]
        expanded = contract_cols(second_in[member, piece, :], expand[...])
        cdf = 0.5 + 0.5 * lax.erf(expanded * math.sqrt(0.5))
        activated = (expanded * cdf).astype(low)
        hidden[member, piece, :] = activated
        reduced[member, piece, :] = dot_rows(activated, reduce[...]).astype(low)
        slope = cdf + expanded * (jnp.exp(-0.5 * expanded * expanded) * (1.0 / math.sqrt(2.0 * math.pi)))
        upstream = contract_cols(sequence_grad[member, piece, :], reduce[...])
        grad = (upstream * slope).astype(low)
        expand_grad[member, piece, :] = grad
        partial[member, piece, :] = dot_rows(grad, expand[...]).astype(low)

    unit(0, 0)
    unit(0, 1)
    back = [[wires.number() for _ in range(2)] for _ in range(5)]
    for p, piece in enumerate(pieces):
        wires.arrived(numbers[1][p], second_in.at[1, piece], beside)
        unit(1, p)
        begin(back[0][p], partial.at[1, piece], from_beside.at[0, piece], beside)
        begin(back[3][p], reduced.at[1, piece], reduced_beside.at[0, piece], beside)
    for p, piece in enumerate(pieces):
        wires.arrived(numbers[0][p], second_in.at[2, piece], across)
        begin(numbers[2][p], second_in.at[2, piece], second_in.at[3, piece], beside)
    for p, piece in enumerate(pieces):
        wires.arrived(numbers[2][p], second_in.at[3, piece], beside)
        unit(3, p)
        begin(back[1][p], partial.at[3, piece], from_beside.at[1, piece], beside)
        begin(back[4][p], reduced.at[3, piece], reduced_beside.at[1, piece], beside)
        unit(2, p)
        wires.arrived(back[1][p], from_beside.at[1, piece], beside)
        both = partial[2, piece, :].astype(jnp.float32) + from_beside[1, piece, :].astype(jnp.float32)
        partial[2, piece, :] = both.astype(low)
        begin(back[2][p], partial.at[2, piece], from_across.at[piece], across)

    def sum_rows(target, left, right):
        total = None
        for member in range(4):
            term = contract_rows(left[member], right[member])
            total = term if total is None else total + term
        target[...] = total.reshape(target.shape).astype(low)

    sum_rows(reduce_sum, hidden, sequence_grad)
    groups[1].bit_send()
    sum_rows(expand_sum, expand_grad, second_in)
    groups[0].bit_send()
    for p, piece in enumerate(pieces):
        wires.arrived(back[3][p], reduced_beside.at[0, piece], beside)
        wires.arrived(back[4][p], reduced_beside.at[1, piece], beside)
        base = reduced[0, piece, :].astype(jnp.float32) + reduced_beside[0, piece, :].astype(jnp.float32)
        layer_base[piece, :] = base + middle[piece, :] + vectors[5:6, :]
        layer_across[piece, :] = (
            reduced[2, piece, :].astype(jnp.float32)
            + reduced_beside[1, piece, :].astype(jnp.float32)
        ).astype(low)
    sums = [0.0] * 4
    for p, piece in enumerate(pieces):
        wires.arrived(back[0][p], from_beside.at[0, piece], beside)
        wires.arrived(back[2][p], from_across.at[piece], across)
        second_grad = (
            partial[0, piece, :].astype(jnp.float32)
            + from_beside[0, piece, :].astype(jnp.float32)
            + from_across[piece, :].astype(jnp.float32)
        )
        normed, inverse = center_scale(middle[piece, :])
        own = sequence_grad[0, piece, :].astype(jnp.float32)
        total = own + norm_backward(second_grad, normed, inverse, vectors[2:3, :])
        middle_grad[piece, :] = total
        for k, term in enumerate((second_grad * normed, second_grad, total, own)):
            sums[k] = sums[k] + jnp.sum(term, axis=0, keepdims=True)
        into_attended = dot_rows(total.astype(low), merge[...]).astype(low)
        for k in range(4):
            attended_grad[k, piece, :] = into_attended[:, k * group_width : (k + 1) * group_width]
    vector_sums[...] = jnp.concatenate(sums, axis=0)
    into_merge = contract_rows(middle_grad[...].astype(low), attended_rows[...]).astype(low)
    for k in range(4):
        merge_sum[k] = into_merge[:, k * group_width : (k + 1) * group_width]
    for which in groups:
        which.bit_add()
    for k, source, device in pending:
        wires.sent(k, source, device)


def middle_pallas(attended_rows, merge, tokens, vectors, expand, reduce, sequence_grad):
    rows, width = tokens.shape
    units = expand.shape[0]
    data_count = lax.axis_size("dp")
    unit_block = (units // data_count, width)
    first_slots = data_count // 4
    low, wide = jnp.bfloat16, jnp.float32
    inside = pl.BlockSpec(memory_space=pltpu.VMEM)
    shapes = (
        ((rows, width), wide),
        ((rows, width), low),
        ((rows, width), wide),
        ((4, rows, width // 4), low),
        ((data_count,) + unit_block, low),
        ((data_count,) + unit_block, low),
        ((4, width, width // 4), low),
        ((4, width), wide),
    )
    copies = 16 + 2 * first_slots
    return pl.pallas_call(
        functools.partial(middle_kernel, data_count),
        out_shape=tuple(jax.ShapeDtypeStruct(*shape) for shape in shapes),
        in_specs=[inside] * 7,
        out_specs=(inside,) * 8,
        scratch_shapes=[
            pltpu.VMEM((4, rows, width), low),
            pltpu.VMEM((rows, width), wide),
            pltpu.VMEM((4, rows, units), low),
            pltpu.VMEM((4, rows, units), low),
            pltpu.VMEM((4, rows, width), low),
            pltpu.VMEM((4, rows, width), low),
            pltpu.VMEM((2, rows, width), low),
            pltpu.VMEM((2, rows, width), low),
            pltpu.VMEM((rows, width), low),
            pltpu.VMEM((first_slots, 2) + unit_block, low),
            pltpu.VMEM((first_slots, 2) + unit_block, low),
            pltpu.SemaphoreType.DMA((copies,)),
            pltpu.SemaphoreType.DMA((copies,)),
        ],
        compiler_params=pltpu.CompilerParams(
            vmem_limit_bytes=VMEM_LIMIT, collective_id=2, has_side_effects=True
        ),
        cost_estimate=pl.CostEstimate(
            flops=52 * rows * width * units, bytes_accessed=20 * rows * width, transcendentals=rows * units * 8
        ),
        name="middle",
    )(attended_rows, merge, tokens, vectors, expand, reduce, sequence_grad)


class Group:
    def __init__(self, work, arrived, last, order, place, wires, begin, first=0):
        self.work, self.got, self.last, self.order = work, arrived, last, order
        self.data, self.tensor = place
        self.pair = (self.data >> 1) * 2
        self.core, self.half = self.data & 1, self.tensor >> 1
        self.wires, self.begin = wires, begin
        self.left = [
            o for o in range(0, work.shape[0], 2) if not any(o & bit for bit in order[:first])
        ]
        self.slot, self.flight, self.step = 0, [], first

    def bit_send(self):
        bit = self.order[self.step]
        self.flight = []
        for offset in [o for o in self.left if o & bit]:
            number = self.wires.number()
            target = (self.data ^ bit, self.tensor)
            self.begin(number, self.work.at[pl.ds(self.pair ^ offset, 2)], self.got.at[self.slot], target)
            self.flight.append((number, self.slot, offset ^ bit, target))
            self.slot += 1
        self.left = [o for o in self.left if not o & bit]
        self.step += 1

    def bit_add(self):
        for number, slot, offset, target in self.flight:
            self.wires.arrived(number, self.got.at[slot], target)
            here = pl.ds(self.pair ^ offset, 2)
            total = self.work[here].astype(jnp.float32) + self.got[slot].astype(jnp.float32)
            self.work[here] = total.astype(self.work.dtype)

    def own_send(self):
        group = 2 * (self.tensor & 1) + self.core
        self.numbers = [self.wires.number() for _ in range(4)]
        for c in (0, 1):
            owner = (self.pair + c, group)
            itself = (owner[0] == self.data) & (owner[1] == self.tensor)
            for b in (0, 1):
                self.begin(
                    self.numbers[2 * c + b],
                    self.work.at[self.pair + c],
                    self.last.at[b],
                    owner,
                    jnp.logical_not(itself) & (self.half == b),
                )

    def own_sum(self):
        for b in (0, 1):
            source = (self.pair + (self.tensor & 1), (self.tensor >> 1) + 2 * b)
            itself = (source[0] == self.data) & (source[1] == self.tensor)
            for c in (0, 1):

                @pl.when(jnp.logical_not(itself) & (self.core == c))
                def _():
                    self.wires.arrived(self.numbers[2 * c + b], self.last.at[b], source)

            @pl.when(itself)
            def _():
                self.last[b] = self.work[self.data]

        return self.last[0].astype(jnp.float32) + self.last[1].astype(jnp.float32)


class ChipSum:
    def __init__(
        self, array, result, arrived, last, base, size, order, place, tensor_count, wires, begin
    ):
        self.array, self.result, self.got, self.last = array, result, arrived, last
        self.start, self.size, self.order = base, size, order
        self.data, self.tensor = place
        self.count, self.wires, self.begin = tensor_count, wires, begin
        self.slot, self.step, self.trail = 0, 0, []

    def bit_send(self):
        bit = self.order[self.step]
        self.step += 1
        half = self.size // 2
        mine = (self.data & bit) // bit
        keep, give = self.start + mine * half, self.start + (1 - mine) * half
        number = self.wires.number()
        target = (self.data ^ bit, self.tensor)
        there = self.got.at[pl.ds(self.slot, half)]
        self.begin(number, self.array.at[pl.ds(give, half)], there, target)
        self.trail.append((bit, keep, give, half))
        self.flight = (number, self.slot, half, target)
        self.start, self.size = keep, half
        self.slot += half

    def bit_add(self):
        number, slot, half, target = self.flight
        self.wires.arrived(number, self.got.at[pl.ds(slot, half)], target)
        here = pl.ds(self.start, half)
        self.array[here] = self.array[here] + self.got[pl.ds(slot, half)]

    def line_send(self):
        self.spread = self.size % self.count == 0
        self.portion = self.size // self.count if self.spread else self.size
        self.flight = []
        for k in range(1, self.count):
            number = self.wires.number()
            peer = lax.rem(self.tensor + k, self.count)
            at = self.start + peer * self.portion if self.spread else self.start
            source = self.array.at[pl.ds(at, self.portion)]
            self.begin(number, source, self.last.at[k - 1], (self.data, peer))
            origin = lax.rem(self.tensor + self.count - k, self.count)
            self.flight.append((number, k - 1, (self.data, origin)))

    def line_add(self):
        at = self.start + self.tensor * self.portion if self.spread else self.start
        here = pl.ds(at, self.portion)
        for number, slot, origin in self.flight:
            self.wires.arrived(number, self.last.at[slot], origin)
        total = self.array[here]
        for number, slot, origin in self.flight:
            total = total + self.last[slot]
        self.result[here] = total

    def line_back(self):
        self.flight = []
        if self.spread:
            here = pl.ds(self.start + self.tensor * self.portion, self.portion)
            for k in range(1, self.count):
                number = self.wires.number()
                peer = lax.rem(self.tensor + k, self.count)
                self.begin(number, self.result.at[here], self.result.at[here], (self.data, peer))
                origin = lax.rem(self.tensor + self.count - k, self.count)
                there = pl.ds(self.start + origin * self.portion, self.portion)
                self.flight.append((number, there, (self.data, origin)))

    def bit_back(self):
        bit, keep, give, half = self.trail.pop()
        number = self.wires.number()
        target = (self.data ^ bit, self.tensor)
        here = pl.ds(keep, half)
        self.begin(number, self.result.at[here], self.result.at[here], target)
        self.flight = [(number, pl.ds(give, half), target)]
        self.start = jnp.minimum(keep, give)
        self.size = 2 * half

    def back_wait(self):
        for number, there, target in self.flight:
            self.wires.arrived(number, self.result.at[there], target)


def split_low(values):
    high = values.astype(jnp.bfloat16)
    return high, (values - high.astype(jnp.float32)).astype(jnp.bfloat16)


def back_kernel(
    data_count,
    tensor_count,
    attended,
    attended_grad,
    query_aux,
    key_aux,
    value_aux,
    first_full,
    heads_weight,
    expand_sum,
    reduce_sum,
    merge_sum,
    layer_base,
    layer_across,
    expand_momentum,
    reduce_momentum,
    tokens,
    middle_grad,
    vectors,
    vector_sums,
    expand_out,
    reduce_out,
    merge_out,
    heads_out,
    input_rows,
    vector_part,
    output_rows,
    gram,
    both,
    upstream,
    grad_aux,
    key_turned,
    query_total,
    projected_grad,
    first_parts,
    first_beside,
    first_across,
    layer_got,
    expand_work,
    expand_got,
    expand_last,
    reduce_work,
    reduce_got,
    reduce_last,
    merge_work,
    merge_core,
    merge_line,
    merge_got,
    merge_last,
    heads_work,
    heads_got,
    heads_last,
    side,
    side_got,
    gram_work,
    gram_got,
    gram_last,
    send,
    receive,
    local,
):
    low = jnp.bfloat16
    members, rows, group_width = attended.shape
    head_local = group_width // HEAD_DIM
    seq_len = members * rows
    data, tensor = lax.axis_index("dp"), lax.axis_index("tensor")
    place = (data, tensor)
    core = data & 1
    group = 2 * (tensor & 1) + core
    wires = Wires(send, receive)
    beside, across, diagonal = (data ^ 1, tensor), (data, tensor ^ 1), (data ^ 1, tensor ^ 1)
    peers = [None, beside, across, diagonal]
    pending = []

    def begin(k, source, target, device, when=None):
        if when is None:
            wires.start(k, source, target, device)
        else:

            @pl.when(when)
            def _():
                wires.start(k, source, target, device)

        pending.append((k, source, device, when))

    def finish_sends():
        for k, source, device, when in pending:
            if when is None:
                wires.sent(k, source, device)
            else:

                @pl.when(when)
                def _():
                    wires.sent(k, source, device)

        pending.clear()

    copies = []
    for k, (source, target) in enumerate(
        ((expand_sum, expand_work), (reduce_sum, reduce_work), (merge_sum, merge_work))
    ):
        copies.append(pltpu.make_async_copy(source, target, local.at[k]))
        copies[-1].start()
    greet(column_and_plane(data, tensor, data_count, tensor_count))

    grad_numbers = {}
    for member in (2, 3, 1):
        grad_numbers[member] = wires.number()
        begin(
            grad_numbers[member],
            attended_grad.at[group ^ member],
            upstream.at[member],
            peers[member],
        )
    for copy in copies:
        copy.wait()
    bits = low_rank_bits(data_count)
    own_merge = merge_work.at[group]
    expand_group = Group(expand_work, expand_got, expand_last, bits[::-1], place, wires, begin, 1)
    reduce_group = Group(reduce_work, reduce_got, reduce_last, bits, place, wires, begin, 1)
    merge_group = Group(own_merge, merge_got, merge_last, bits[::-1], place, wires, begin)
    heads_group = Group(heads_work, heads_got, heads_last, bits, place, wires, begin)
    merge_numbers = [wires.number() for _ in range(3)]
    begin(merge_numbers[0], merge_work.at[group ^ 1], merge_core.at[0], beside)
    begin(merge_numbers[1], merge_work.at[group ^ 3], merge_core.at[1], beside)
    if len(bits) > 1:
        expand_group.bit_send()
        reduce_group.bit_send()
    layer_number = wires.number()
    upstream[0] = attended_grad[group]

    block = min(KEY_BLOCK, rows)
    lane = lax.broadcasted_iota(jnp.int32, (block, AUX), 1)
    blank = jnp.zeros((block, AUX - HEAD_DIM), jnp.float32)
    steps = rows // block

    def prepare(member):
        def one(step, carry):
            inside = pl.ds(pl.multiple_of(step * block, block), block)
            at_rows = pl.ds(pl.multiple_of(member * rows + step * block, block), block)
            gradient = upstream[member, inside, :].astype(jnp.float32)
            product = gradient * attended[member, inside, :].astype(jnp.float32)
            for head in range(head_local):
                columns = slice(head * HEAD_DIM, (head + 1) * HEAD_DIM)
                row_dot = jnp.sum(product[:, columns], axis=1, keepdims=True)
                first = row_dot.astype(low).astype(jnp.float32)
                wide = jnp.concatenate([gradient[:, columns], blank], axis=1)
                wide = jnp.where(lane == HEAD_DIM + 1, first, wide)
                wide = jnp.where(lane == HEAD_DIM + 2, row_dot - first, wide)
                grad_aux[head, at_rows, :] = wide.astype(low)
                key_turned[head, :, at_rows] = key_aux[head, at_rows, :].T[:HEAD_DIM]
            return carry

        lax.fori_loop(0, steps, one, 0)

    prepare(0)
    for member in (1, 2, 3):
        wires.arrived(grad_numbers[member], upstream.at[member], peers[member])
        prepare(member)
    query_total[...] = jnp.zeros_like(query_total)

    def back(step, carry):
        at_rows = pl.ds(pl.multiple_of(step * block, block), block)
        for head in range(head_local):
            scores = contract_cols(key_aux[head, at_rows, :], query_aux[head])
            chances = jnp.exp(scores)
            chance_grad = contract_cols(value_aux[head, at_rows, :], grad_aux[head])
            score_grad = (chances * chance_grad).astype(low)
            value_grad = dot_rows(chances.astype(low), grad_aux[head])
            key_grad = dot_rows(score_grad, query_aux[head])
            query_total[head] += dot_rows(key_turned[head, :, at_rows], score_grad)
            at = 3 * head * HEAD_DIM
            two = jnp.concatenate([key_grad[:, :HEAD_DIM], value_grad[:, :HEAD_DIM]], axis=1)
            projected_grad[at_rows, at + HEAD_DIM : at + 3 * HEAD_DIM] = two.astype(low)
        return carry

    eighth = seq_len // block // 8

    def back_eighths(start, stop):
        lax.fori_loop(start * eighth, stop * eighth, back, 0)

    for which in (expand_group, reduce_group):
        for k in range(1, len(bits)):
            which.bit_add()
            if k + 1 < len(bits):
                which.bit_send()
        which.own_send()
    wires.arrived(merge_numbers[0], merge_core.at[0], beside)
    wires.arrived(merge_numbers[1], merge_core.at[1], beside)
    for k in (0, 1):
        here = group ^ (2 * k)
        total = merge_work[here].astype(jnp.float32) + merge_core[k].astype(jnp.float32)
        merge_work[here] = total.astype(low)
    begin(merge_numbers[2], merge_work.at[group ^ 2], merge_line, across)

    back_eighths(0, 3)
    expand_out[...] = expand_group.own_sum()
    reduce_out[...] = reduce_group.own_sum()
    expand_part = momentum_decay * expand_momentum[...] + expand_out[...]
    reduce_part = momentum_decay * reduce_momentum[...] + reduce_out[...]
    first_core = core == 0
    side[0] = jnp.where(first_core, expand_part, reduce_part)
    side[1] = jnp.where(first_core, reduce_part, expand_part)
    side_number = wires.number()
    begin(side_number, side.at[1], side_got, beside)
    wires.arrived(merge_numbers[2], merge_line, across)
    total = merge_work[group].astype(jnp.float32) + merge_line[...].astype(jnp.float32)
    merge_work[group] = total.astype(low)
    merge_group.bit_send()

    back_eighths(3, 4)
    begin(layer_number, layer_across, layer_got, across)
    wires.arrived(side_number, side_got, beside)
    part_rows = side_got.shape[0]
    both[:part_rows, :] = side[0]
    both[part_rows:, :] = side_got[...]
    width = both.shape[1]
    high, rest = split_low(both[...])
    at = 0
    for k in range(0, width, SIDE):
        span = width - k
        part = contract_rows(high[:, k : k + SIDE], high[:, k:])
        part = part + contract_rows(high[:, k : k + SIDE], rest[:, k:])
        part = part + contract_rows(rest[:, k : k + SIDE], high[:, k:])
        gram_work[:, :, at : at + span] = part.reshape(SIDE // 8, 8, span)
        at += span
    slots = SIDE // 16
    halves = [
        ChipSum(
            gram_work,
            gram,
            gram_got.at[h],
            gram_last.at[h],
            h * slots,
            slots,
            order,
            place,
            tensor_count,
            wires,
            begin,
        )
        for h, order in enumerate((bits, bits[::-1]))
    ]
    for half in halves:
        half.bit_send()

    back_eighths(4, 6)
    for half in halves:
        half.bit_add()
        for _ in range(2, len(bits)):
            half.bit_send()
            half.bit_add()
        half.bit_send()
    merge_group.bit_add()
    merge_group.bit_send()

    back_eighths(6, 7)
    for half in halves:
        half.bit_add()
        half.line_send()
    merge_group.bit_add()
    for _ in range(2, len(bits)):
        merge_group.bit_send()
        merge_group.bit_add()
    merge_group.own_send()

    back_eighths(7, 8)

    def finish(step, carry):
        at_rows = pl.ds(pl.multiple_of(step * block, block), block)
        for head in range(head_local):
            query_grad = query_total[head, :, at_rows].T * HEAD_DIM**-0.5
            at = 3 * head * HEAD_DIM
            projected_grad[at_rows, at : at + HEAD_DIM] = query_grad.astype(low)
        return carry

    lax.fori_loop(0, seq_len // block, finish, 0)
    first_numbers = [wires.number() for _ in range(3)]

    def first_part(member):
        at_rows = pl.ds(member * rows, rows)
        part = contract_cols(projected_grad[at_rows, :], heads_weight[...])
        first_parts[member] = part.astype(low)

    heads_work[...] = (
        contract_rows(first_full[...], projected_grad[...]).reshape(heads_work.shape).astype(low)
    )
    heads_group.bit_send()
    for half in halves:
        half.line_add()
        half.line_back()
    for k, member in enumerate((3, 1)):
        first_part(member)
        begin(first_numbers[k], first_parts.at[member], first_beside.at[k], beside)
    first_part(2)
    wires.arrived(first_numbers[0], first_beside.at[0], beside)
    total = first_parts[2].astype(jnp.float32) + first_beside[0].astype(jnp.float32)
    first_parts[2] = total.astype(low)
    for half in halves:
        half.back_wait()
        half.bit_back()
    begin(first_numbers[2], first_parts.at[2], first_across, across)
    heads_group.bit_add()
    for _ in range(2, len(bits)):
        heads_group.bit_send()
        heads_group.bit_add()
    heads_group.bit_send()
    first_part(0)
    for _ in range(1, len(bits)):
        for half in halves:
            half.back_wait()
            half.bit_back()
    heads_group.bit_add()
    heads_group.own_send()
    merge_out[...] = merge_group.own_sum()
    wires.arrived(layer_number, layer_got, across)
    output_rows[...] = (layer_base[...] + layer_got[...].astype(jnp.float32)).astype(low)
    wires.arrived(first_numbers[1], first_beside.at[1], beside)
    wires.arrived(first_numbers[2], first_across, across)
    sums = [0.0, 0.0]
    for p in range(2):
        piece = pl.ds(p * (rows // 2), rows // 2)
        first_grad = (
            first_parts[0, piece, :].astype(jnp.float32)
            + first_beside[1, piece, :].astype(jnp.float32)
            + first_across[piece, :].astype(jnp.float32)
        )
        normed, inverse = center_scale(tokens[piece, :].astype(jnp.float32))
        input_rows[piece, :] = middle_grad[piece, :] + norm_backward(
            first_grad, normed, inverse, vectors[0:1, :]
        )
        sums[0] = sums[0] + jnp.sum(first_grad * normed, axis=0, keepdims=True)
        sums[1] = sums[1] + jnp.sum(first_grad, axis=0, keepdims=True)
    vector_part[...] = jnp.concatenate(sums + [vector_sums[...]], axis=0)
    heads_out[...] = heads_group.own_sum()
    for half in halves:
        half.back_wait()
    finish_sends()


def back_pallas(
    attended,
    attended_grad,
    query_aux,
    key_aux,
    value_aux,
    first_full,
    heads_weight,
    expand_sum,
    reduce_sum,
    merge_sum,
    layer_base,
    layer_across,
    expand_momentum,
    reduce_momentum,
    tokens,
    middle_grad,
    vectors,
    vector_sums,
):
    data_count, tensor_count = lax.axis_size("dp"), lax.axis_size("tensor")
    members, rows, group_width = attended.shape
    head_local = group_width // HEAD_DIM
    seq_len = members * rows
    low, wide = jnp.bfloat16, jnp.float32
    width, columns = heads_weight.shape
    unit_block = expand_sum.shape[1:]
    merge_block = merge_sum.shape[2:]
    heads_block = (width // data_count, columns)
    packed = sum(width - k for k in range(0, width, SIDE))
    inside = pl.BlockSpec(memory_space=pltpu.VMEM)
    outs = (
        (unit_block, wide),
        (unit_block, wide),
        (merge_block, wide),
        (heads_block, wide),
        ((rows, width), wide),
        (vectors.shape, wide),
        ((rows, width), low),
        ((SIDE // 8, 8, packed), wide),
        ((2 * unit_block[0], unit_block[1]), wide),
    )
    steps = data_count // 2 - 1
    later = max(data_count // 4 - 1, 1)
    slots = SIDE // 16
    left = slots // (data_count // 2)
    portion = left // tensor_count if left % tensor_count == 0 else left
    scratch = []
    for shape, kind in (
        ((members, rows, group_width), low),
        ((head_local, seq_len, AUX), low),
        ((head_local, HEAD_DIM, seq_len), low),
        ((head_local, HEAD_DIM, seq_len), wide),
        ((seq_len, columns), low),
        ((members, rows, width), low),
        ((2, rows, width), low),
        ((rows, width), low),
        ((rows, width), low),
        ((data_count,) + unit_block, low),
        ((later, 2) + unit_block, low),
        ((2,) + unit_block, low),
        ((data_count,) + unit_block, low),
        ((later, 2) + unit_block, low),
        ((2,) + unit_block, low),
        (merge_sum.shape, low),
        ((2, data_count) + merge_block, low),
        ((data_count,) + merge_block, low),
        ((steps, 2) + merge_block, low),
        ((2,) + merge_block, low),
        ((data_count,) + heads_block, low),
        ((steps, 2) + heads_block, low),
        ((2,) + heads_block, low),
        ((2,) + unit_block, wide),
        (unit_block, wide),
        ((SIDE // 8, 8, packed), wide),
        ((2, slots, 8, packed), wide),
        ((2, tensor_count - 1, portion, 8, packed), wide),
    ):
        scratch.append(pltpu.VMEM(shape, kind))
    copies = 3 + 3 + 1 + 4 * (steps + 4) + 1 + 3
    copies += 2 * (2 * (data_count // 2).bit_length() + 2 * tensor_count)
    return pl.pallas_call(
        functools.partial(back_kernel, data_count, tensor_count),
        out_shape=tuple(jax.ShapeDtypeStruct(*out) for out in outs),
        in_specs=[inside] * 7 + [pl.BlockSpec(memory_space=pl.ANY)] * 3 + [inside] * 8,
        out_specs=(inside,) * len(outs),
        scratch_shapes=scratch
        + [
            pltpu.SemaphoreType.DMA((copies,)),
            pltpu.SemaphoreType.DMA((copies,)),
            pltpu.SemaphoreType.DMA((3,)),
        ],
        compiler_params=pltpu.CompilerParams(
            vmem_limit_bytes=VMEM_LIMIT, collective_id=3, has_side_effects=True
        ),
        cost_estimate=pl.CostEstimate(
            flops=10 * head_local * seq_len * seq_len * AUX,
            bytes_accessed=10 * seq_len * width,
            transcendentals=head_local * seq_len * seq_len,
        ),
        name="back",
    )(
        attended,
        attended_grad,
        query_aux,
        key_aux,
        value_aux,
        first_full,
        heads_weight,
        expand_sum,
        reduce_sum,
        merge_sum,
        layer_base,
        layer_across,
        expand_momentum,
        reduce_momentum,
        tokens,
        middle_grad,
        vectors,
        vector_sums,
    )


def everyone_near(data, tensor, data_count, tensor_count):
    found = []
    for core in (0, 1):
        for step in range(tensor_count):
            if core or step:
                found.append((data ^ core, lax.rem(tensor + step, tensor_count)))
    for k in range(2, data_count):
        found.append((data ^ k, tensor))
    return found


def three_pass(left, right):
    return dot_rows(left[0], right[0]) + (dot_rows(left[0], right[1]) + dot_rows(left[1], right[0]))


def last_kernel(
    data_count,
    tensor_count,
    gram,
    both,
    small_gram,
    vector_part,
    output_rows,
    input_rows,
    ortho_mine,
    ortho_other,
    small_chain,
    vector_sum,
    moved_output,
    moved_input,
    square,
    gram_high,
    gram_low,
    factor_high,
    factor_low,
    part,
    theirs,
    small_got,
    vector_got,
    vector_line,
    vector_half,
    send,
    receive,
):
    size = part.shape[1]
    rows = part.shape[0] // 2
    data, tensor = lax.axis_index("dp"), lax.axis_index("tensor")
    beside, away = (data ^ 1, tensor), (data ^ 1, tensor ^ 2)
    moved = jnp.logical_not((data & 1) == (tensor >> 1))
    wires = Wires(send, receive)
    pending = []

    def begin(k, source, target, device, when=None):
        if when is None:
            wires.start(k, source, target, device)
        else:

            @pl.when(when)
            def _():
                wires.start(k, source, target, device)

        pending.append((k, source, device, when))

    greet(everyone_near(data, tensor, data_count, tensor_count))
    small_numbers, vector_numbers = [], []
    for k in range(1, data_count):
        small_numbers.append(wires.number())
        vector_numbers.append(wires.number())
        peer = (data ^ k, tensor)
        begin(vector_numbers[-1], vector_part, vector_got.at[k - 1], peer)
        begin(small_numbers[-1], small_gram, small_got.at[k - 1], peer)
    input_number, output_number = wires.number(), wires.number()
    begin(input_number, input_rows, moved_input, away, moved)
    begin(output_number, output_rows, moved_output, away, moved)

    identity = (
        lax.broadcasted_iota(jnp.int32, (SIDE, SIDE), 0)
        == lax.broadcasted_iota(jnp.int32, (SIDE, SIDE), 1)
    ).astype(jnp.float32)
    blocks = size // SIDE
    trace = 0.0
    at = 0
    for i in range(blocks):
        span = size - i * SIDE
        strip = gram[:, :, at : at + span].reshape(SIDE, span)
        trace = trace + jnp.sum(strip[:, :SIDE] * identity)
        at += span
    factor = 1.0 / (jnp.sqrt(trace) + newton_epsilon)

    def keep(strip, i, high, low):
        top, rest = split_low(strip)
        high[i * SIDE : (i + 1) * SIDE, i * SIDE :] = top
        low[i * SIDE : (i + 1) * SIDE, i * SIDE :] = rest
        for j in range(i + 1, blocks):
            turned = strip[:, (j - i) * SIDE : (j - i + 1) * SIDE].T
            top, rest = split_low(turned)
            high[j * SIDE : (j + 1) * SIDE, i * SIDE : (i + 1) * SIDE] = top
            low[j * SIDE : (j + 1) * SIDE, i * SIDE : (i + 1) * SIDE] = rest

    at = 0
    for i in range(blocks):
        span = size - i * SIDE
        strip = gram[:, :, at : at + span].reshape(SIDE, span) * (factor * factor)
        square[i * SIDE : (i + 1) * SIDE, i * SIDE :] = strip
        keep(strip, i, gram_high, gram_low)
        at += span
    part[...] = both[...] * factor

    def strip_of(left, right, i):
        here = slice(i * SIDE, (i + 1) * SIDE)
        return three_pass(
            (left[0][here, :], left[1][here, :]), (right[0][:, i * SIDE :], right[1][:, i * SIDE :])
        )

    gram_pair, factor_pair = (gram_high, gram_low), (factor_high, factor_low)

    def wide_factor():
        for i in range(blocks):
            here = slice(i * SIDE, (i + 1) * SIDE)
            strip = newton_cubic * square[here, i * SIDE :] + newton_quintic * strip_of(
                gram_pair, gram_pair, i
            )
            first = strip[:, :SIDE] + newton_linear * identity
            strip = first if i == blocks - 1 else jnp.concatenate([first, strip[:, SIDE:]], axis=1)
            keep(strip, i, factor_high, factor_low)

    def wide_part():
        part[...] = three_pass(split_low(part[...]), (factor_high[...], factor_low[...]))

    def wide_gram():
        strips = [strip_of(gram_pair, factor_pair, i) for i in range(blocks)]
        for i in range(blocks):
            keep(strips[i], i, gram_high, gram_low)
        strips = [strip_of(gram_pair, factor_pair, i) for i in range(blocks)]
        for i in range(blocks):
            square[i * SIDE : (i + 1) * SIDE, i * SIDE :] = strips[i]
            keep(strips[i], i, gram_high, gram_low)

    count, head_size = small_gram.shape[0], small_gram.shape[1]
    per = SIDE // head_size
    row_block = lax.broadcasted_iota(jnp.int32, (SIDE, SIDE), 0) // head_size
    column_block = lax.broadcasted_iota(jnp.int32, (SIDE, SIDE), 1) // head_size
    small = {}

    def small_start():
        for number, k in zip(small_numbers, range(1, data_count)):
            wires.arrived(number, small_got.at[k - 1], (data ^ k, tensor))
        total = small_gram[...]
        for k in range(data_count - 1):
            total = total + small_got[k]
        small["gram"], small["chain"], small["scale"] = [], [], []
        for b in range(count // per):
            tall = total[b * per : (b + 1) * per].reshape(SIDE, head_size)
            full = jnp.concatenate([tall] * per, axis=1)
            full = jnp.where(row_block == column_block, full, 0.0)
            diagonal = jnp.sum(full * identity, axis=1, keepdims=True)
            scale = jnp.zeros((SIDE, 1), jnp.float32)
            column = row_block[:, :1]
            for k in range(per):
                inside = column == k
                norm = jnp.sqrt(jnp.sum(jnp.where(inside, diagonal, 0.0)))
                scale = jnp.where(inside, 1.0 / (norm + newton_epsilon), scale)
            small["gram"].append(full * (scale * scale))
            small["scale"].append(scale)
            small["chain"].append(None)

    def small_step(last):
        for b in range(count // per):
            here = split_low(small["gram"][b])
            step = newton_linear * identity + newton_cubic * small["gram"][b]
            step = step + newton_quintic * three_pass(here, here)
            step_pair = split_low(step)
            before = small["chain"][b]
            small["chain"][b] = step if before is None else three_pass(split_low(before), step_pair)
            if not last:
                next_gram = three_pass(here, step_pair)
                small["gram"][b] = three_pass(split_low(next_gram), step_pair)

    def small_end():
        for b in range(count // per):
            chain = small["chain"][b] * small["scale"][b]
            for k in range(per):
                here = slice(k * head_size, (k + 1) * head_size)
                small_chain[b * per + k] = chain[here, here]

    line_numbers = [wires.number() for _ in range(tensor_count - 1)]
    side_number = wires.number()
    small_at = NEWTON_STEPS // 2
    for step in range(NEWTON_STEPS):
        wide_factor()
        if step == small_at:
            small_start()
            for number, k in zip(vector_numbers, range(1, data_count)):
                wires.arrived(number, vector_got.at[k - 1], (data ^ k, tensor))
            total = vector_part[...]
            for k in range(data_count - 1):
                total = total + vector_got[k]
            vector_half[...] = total
            for k in range(1, tensor_count):
                peer = lax.rem(tensor + k, tensor_count)
                begin(line_numbers[k - 1], vector_half, vector_line.at[k - 1], (data, peer))
            small_step(False)
        elif step > small_at:
            small_step(False)
            if step < NEWTON_STEPS - 1:
                small_step(False)
        wide_part()
        if step < NEWTON_STEPS - 1:
            wide_gram()
    ortho_mine[...] = part[:rows, :]
    theirs[...] = part[rows:, :]
    begin(side_number, theirs, ortho_other, beside)
    small_step(True)
    small_end()
    total = vector_half[...]
    for k in range(1, tensor_count):
        origin = lax.rem(tensor + tensor_count - k, tensor_count)
        wires.arrived(line_numbers[k - 1], vector_line.at[k - 1], (data, origin))
        total = total + vector_line[k - 1]
    vector_sum[...] = total

    @pl.when(moved)
    def _():
        wires.arrived(input_number, moved_input, away)
        wires.arrived(output_number, moved_output, away)

    wires.arrived(side_number, ortho_other, beside)
    for k, source, device, when in pending:
        if when is None:
            wires.sent(k, source, device)
        else:

            @pl.when(when)
            def _():
                wires.sent(k, source, device)


def last_pallas(gram, both, small_gram, vector_part, output_rows, input_rows):
    data_count, tensor_count = lax.axis_size("dp"), lax.axis_size("tensor")
    low, wide = jnp.bfloat16, jnp.float32
    size = both.shape[1]
    rows = both.shape[0] // 2
    inside = pl.BlockSpec(memory_space=pltpu.VMEM)
    outs = (
        ((rows, size), wide),
        ((rows, size), wide),
        (small_gram.shape, wide),
        (vector_part.shape, wide),
        (output_rows.shape, low),
        (input_rows.shape, low),
    )
    scratch = [
        pltpu.VMEM(shape, kind)
        for shape, kind in (
            ((size, size), wide),
            ((size, size), low),
            ((size, size), low),
            ((size, size), low),
            ((size, size), low),
            (both.shape, wide),
            ((rows, size), wide),
            ((data_count - 1,) + small_gram.shape, wide),
            ((data_count - 1,) + vector_part.shape, wide),
            ((tensor_count - 1,) + vector_part.shape, wide),
            (vector_part.shape, wide),
        )
    ]
    copies = 2 * (data_count - 1) + 2 + tensor_count
    return pl.pallas_call(
        functools.partial(last_kernel, data_count, tensor_count),
        out_shape=tuple(jax.ShapeDtypeStruct(*out) for out in outs),
        in_specs=[inside] * 6,
        out_specs=(inside,) * len(outs),
        scratch_shapes=scratch
        + [pltpu.SemaphoreType.DMA((copies,)), pltpu.SemaphoreType.DMA((copies,))],
        compiler_params=pltpu.CompilerParams(
            vmem_limit_bytes=VMEM_LIMIT, collective_id=4, has_side_effects=True
        ),
        cost_estimate=pl.CostEstimate(
            flops=90 * size * size * size, bytes_accessed=20 * size * size, transcendentals=0
        ),
        name="last",
    )(gram, both, small_gram, vector_part, output_rows, input_rows)


SIDE = 256


def swap_bit(values, axis_name, bit):
    count = lax.axis_size(axis_name)
    return lax.ppermute(values, axis_name, [(i, i ^ bit) for i in range(count)])


def data_bits():
    return [1 << k for k in range(1, lax.axis_size("dp").bit_length() - 1)]


def has_bit(index, bit):
    return (index & bit) != 0


def gather_bits_absolute(block, bits):
    index = lax.axis_index("dp")
    for bit in bits:
        other = swap_bit(block, "dp", bit)
        mine = has_bit(index, bit)
        block = jnp.concatenate(
            [jnp.where(mine, other, block), jnp.where(mine, block, other)], axis=0
        )
    return block


def pair_permute(values, where_to):
    data_count, tensor_count = lax.axis_size("dp"), lax.axis_size("tensor")
    moves = []
    for i in range(data_count):
        for j in range(tensor_count):
            target = where_to(i, j)
            if target is not None:
                moves.append((i * tensor_count + j, target[0] * tensor_count + target[1]))
    return lax.ppermute(values, ("dp", "tensor"), moves)


def exchange_home(values):
    return pair_permute(
        values, lambda i, j: (i ^ 1, j ^ 2) if (i & 1) != (j >> 1) else None
    )


def gather_head_group(shard):
    first = []
    for core in (0, 1):
        got = []
        for half in (0, 1):
            got.append(
                pair_permute(
                    shard,
                    lambda i, j: (i - core + (j & 1), (j >> 1) + 2 * half)
                    if (i & 1) == core
                    else None,
                )
            )
        first.append(jnp.where(lax.axis_index("tensor") >= 2, got[1], got[0]))
    return gather_bits_absolute(jnp.concatenate(first, axis=0), data_bits())


def per_device(
    tokens,
    segment_ids,
    out_grad,
    heads_weight,
    merge_weight,
    expand_weight,
    reduce_weight,
    heads_momentum,
    merge_momentum,
    expand_momentum,
    reduce_momentum,
    heads_average,
    merge_average,
    expand_average,
    reduce_average,
    vectors,
    vector_momentum,
    vector_average,
):
    low = jnp.bfloat16
    tensor_count = lax.axis_size("tensor")
    data_count = lax.axis_size("dp")
    tensor_index = lax.axis_index("tensor")
    core = lax.axis_index("dp") & 1
    row_count = tokens.shape[0]
    seq_len = row_count * tensor_count
    head_local = heads_weight.shape[1] // (3 * HEAD_DIM)
    group_width = head_local * HEAD_DIM
    at_home = core == (tensor_index >> 1)
    group = 2 * (tensor_index & 1) + core

    own_segments = jnp.where(at_home, segment_ids, swap_bit(segment_ids, "dp", 1))
    chunk_at = []
    for member in range(4):
        its_core, its_tensor = core ^ (member & 1), tensor_index ^ (member >> 1)
        chunk_at.append(jnp.where(its_core == (its_tensor >> 1), its_tensor, its_tensor ^ 2))
    segments = jnp.take(
        own_segments.reshape(tensor_count, row_count), jnp.stack(chunk_at), axis=0
    ).reshape(seq_len)
    gather_heads = heads_weight.shape[0] % 16 == 0
    heads_low = heads_weight.astype(low)
    if not gather_heads:
        heads_low = gather_head_group(heads_low)
    (
        attended_full,
        attended_own,
        query_aux,
        key_aux,
        value_aux,
        first_full,
        token_chunks,
        full_heads,
        full_expand,
        full_reduce,
        full_merge,
        sequence_grad,
    ) = front_pallas(
        tokens,
        heads_low,
        expand_weight.T.astype(low),
        reduce_weight.astype(low),
        merge_weight.T.astype(low),
        vectors,
        segments,
        out_grad,
        gather_heads,
    )
    full_heads = full_heads.reshape(D, 3 * group_width) if gather_heads else heads_low
    full_merge = jnp.transpose(full_merge, (0, 2, 1, 3)).reshape(D, D)
    full_expand = full_expand.reshape(-1, D)
    full_reduce = full_reduce.reshape(-1, D)
    (
        layer_base,
        layer_across,
        middle_grad,
        attended_grad,
        expand_sum,
        reduce_sum,
        merge_sum,
        vector_sums,
    ) = middle_pallas(
        attended_own, full_merge, token_chunks[0], vectors, full_expand, full_reduce, sequence_grad
    )
    (
        expand_rows,
        reduce_gradient,
        merge_rows,
        heads_gradient,
        input_rows,
        vector_part,
        output_rows,
        wide_gram,
        wide_rows,
    ) = back_pallas(
        attended_full,
        attended_grad,
        query_aux,
        key_aux,
        value_aux,
        first_full,
        full_heads,
        expand_sum,
        reduce_sum,
        merge_sum.reshape(4, data_count, merge_weight.shape[1], group_width),
        layer_base,
        layer_across,
        expand_momentum.T,
        reduce_momentum,
        token_chunks[0],
        middle_grad,
        vectors,
        vector_sums,
    )
    expand_gradient, merge_gradient = expand_rows.T, merge_rows.T
    expand_new_momentum = momentum_decay * expand_momentum + expand_gradient
    reduce_new_momentum = momentum_decay * reduce_momentum + reduce_gradient
    heads_new_momentum = momentum_decay * heads_momentum + heads_gradient
    merge_new_momentum = momentum_decay * merge_momentum + merge_gradient

    heads_part = heads_new_momentum.reshape(heads_new_momentum.shape[0], head_local * 3, HEAD_DIM)
    merge_part = merge_new_momentum.reshape(head_local, HEAD_DIM, merge_new_momentum.shape[1])
    small_gram = jnp.concatenate(
        [
            jnp.einsum("rmd,rme->mde", heads_part, heads_part, precision=highest),
            jnp.einsum("hdc,hec->hde", merge_part, merge_part, precision=highest),
        ],
        axis=0,
    )
    ortho_mine, ortho_other, small_chain, vector_gradient, moved_output, moved_input = last_pallas(
        wide_gram, wide_rows, small_gram, vector_part, output_rows, input_rows.astype(low)
    )
    layer_output = jnp.where(at_home, output_rows, moved_output)
    input_gradient = jnp.where(at_home, input_rows, moved_input.astype(jnp.float32))
    vector_new_momentum = momentum_decay * vector_momentum + vector_gradient
    side_count = 3 * head_local
    heads_ortho = jnp.einsum("rmd,mde->rme", heads_part, small_chain[:side_count], precision=highest)
    merge_ortho = jnp.einsum("hde,hec->hdc", small_chain[side_count:], merge_part, precision=highest)

    first_core = core == 0
    expand_ortho = jnp.where(first_core, ortho_mine, ortho_other).T
    reduce_ortho = jnp.where(first_core, ortho_other, ortho_mine)

    keep_factor = 1.0 - muon_rate * weight_decay
    head_step = muon_rate * 0.2 * math.sqrt(max(D, HEAD_DIM))
    wide_step = muon_rate * 0.2 * math.sqrt(max(D, FF))
    heads_new_weight = heads_weight * keep_factor - head_step * heads_ortho.reshape(
        heads_weight.shape
    )
    merge_new_weight = merge_weight * keep_factor - head_step * merge_ortho.reshape(
        merge_weight.shape
    )
    expand_new_weight = expand_weight * keep_factor - wide_step * expand_ortho
    reduce_new_weight = reduce_weight * keep_factor - wide_step * reduce_ortho
    vector_new_value = vectors - vector_rate / math.sqrt(SEQ * data_count) * vector_new_momentum
    heads_new_average = average_decay * heads_average + (1.0 - average_decay) * heads_new_weight
    merge_new_average = average_decay * merge_average + (1.0 - average_decay) * merge_new_weight
    expand_new_average = average_decay * expand_average + (1.0 - average_decay) * expand_new_weight
    reduce_new_average = average_decay * reduce_average + (1.0 - average_decay) * reduce_new_weight
    vector_new_average = average_decay * vector_average + (1.0 - average_decay) * vector_new_value
    return (
        layer_output,
        input_gradient,
        heads_gradient,
        merge_gradient,
        expand_gradient,
        reduce_gradient,
        heads_new_momentum,
        merge_new_momentum,
        expand_new_momentum,
        reduce_new_momentum,
        heads_new_weight,
        merge_new_weight,
        expand_new_weight,
        reduce_new_weight,
        heads_new_average,
        merge_new_average,
        expand_new_average,
        reduce_new_average,
        vector_gradient,
        vector_new_momentum,
        vector_new_value,
        vector_new_average,
    )


def solution(mesh):
    placed = (
        P(("dp", "tensor"), None),
        P("dp"),
        P("dp", None),
        P("dp", "tensor"),
        P("tensor", "dp"),
        P(None, ("tensor", "dp")),
        P(("tensor", "dp"), None),
        P("dp", "tensor"),
        P("tensor", "dp"),
        P(None, ("tensor", "dp")),
        P(("tensor", "dp"), None),
        P("dp", "tensor"),
        P("tensor", "dp"),
        P(None, ("tensor", "dp")),
        P(("tensor", "dp"), None),
        P(),
        P(),
        P(),
    )
    return jax.shard_map(
        per_device,
        mesh=mesh,
        in_specs=placed,
        out_specs=(
            P(("dp", "tensor"), None),
            P(("dp", "tensor"), None),
            P("dp", "tensor"),
            P("tensor", "dp"),
            P(None, ("tensor", "dp")),
            P(("tensor", "dp"), None),
            P("dp", "tensor"),
            P("tensor", "dp"),
            P(None, ("tensor", "dp")),
            P(("tensor", "dp"), None),
            P("dp", "tensor"),
            P("tensor", "dp"),
            P(None, ("tensor", "dp")),
            P(("tensor", "dp"), None),
            P("dp", "tensor"),
            P("tensor", "dp"),
            P(None, ("tensor", "dp")),
            P(("tensor", "dp"), None),
            P(),
            P(),
            P(),
            P(),
        ),
        check_vma=False,
    )
```

```python
import functools
import math

import jax
import jax.numpy as jnp
from jax import lax
from jax.experimental import pallas as pl
from jax.experimental.pallas import tpu as pltpu
from jax.sharding import PartitionSpec as P

D = 768
HEAD_DIM = 64
FF = 3072
SEQ = 2048
NEWTON_STEPS = 5


highest = lax.Precision.HIGHEST
norm_epsilon = 1e-06
newton_epsilon = 1e-07
newton_linear = 3.4445
newton_cubic = -4.775
newton_quintic = 2.0315
momentum_decay = 0.5
average_decay = 0.9
muon_rate = 0.2
weight_decay = 0.1
vector_rate = 0.15
masked_score = -1e30
VMEM_LIMIT = 56 * 2**20


def center_scale(values):
    average = jnp.mean(values, axis=-1, keepdims=True)
    centered = values - average
    inverse = lax.rsqrt(jnp.mean(centered * centered, axis=-1, keepdims=True) + norm_epsilon)
    return (centered * inverse, inverse)


def norm_backward(upstream, normed, inverse, gain):
    scaled = upstream * gain
    mean_one = jnp.mean(scaled, axis=-1, keepdims=True)
    mean_two = jnp.mean(scaled * normed, axis=-1, keepdims=True)
    return inverse * (scaled - mean_one - normed * mean_two)


def gelu_exact(values):
    return jax.nn.gelu(values, approximate=False)


def contract_rows(left_side, right_side):
    return lax.dot_general(
        left_side, right_side, (((0,), (0,)), ((), ())), preferred_element_type=jnp.float32
    )


def contract_cols(left_side, right_side):
    return lax.dot_general(
        left_side, right_side, (((1,), (1,)), ((), ())), preferred_element_type=jnp.float32
    )


KEY_BLOCK = 256
AUX = 128


MESH = pl.DeviceIdType.MESH


def low_rank_bits(data_count):
    return [1 << k for k in range(1, data_count.bit_length() - 1)]


class Wires:
    def __init__(self, send, receive):
        self.send, self.receive, self.used = send, receive, 0

    def number(self):
        self.used += 1
        return self.used - 1

    def start(self, k, source, target, device):
        copy = pltpu.make_async_remote_copy(
            source, target, self.send.at[k], self.receive.at[k], device_id=device, device_id_type=MESH
        )
        copy.start()

    def sent(self, k, source, device):
        pltpu.make_async_remote_copy(
            source, source, self.send.at[k], self.receive.at[k], device_id=device, device_id_type=MESH
        ).wait_send()

    def arrived(self, k, target, device):
        pltpu.make_async_remote_copy(
            target, target, self.send.at[k], self.receive.at[k], device_id=device, device_id_type=MESH
        ).wait_recv()


def greet(devices):
    barrier = pltpu.get_barrier_semaphore()
    for device in devices:
        pl.semaphore_signal(barrier, inc=1, device_id=device, device_id_type=MESH)
    pl.semaphore_wait(barrier, len(devices))


def column_and_plane(data, tensor, data_count, tensor_count):
    found = []
    for core in (0, 1):
        for step in range(tensor_count):
            if core or step:
                found.append((data ^ core, lax.rem(tensor + step, tensor_count)))
    for k in range(1, data_count // 2):
        found.append((data ^ (2 * k), tensor))
    return found


def front_kernel(
    data_count,
    tensor_count,
    gather_heads,
    late,
    tokens,
    heads,
    expand,
    reduce,
    merge,
    vectors,
    segment_column,
    out_grad,
    attended,
    attended_rows,
    query_aux,
    key_aux,
    value_aux,
    first_full,
    own_tokens,
    all_heads,
    all_expand,
    all_reduce,
    merge_full,
    sequence_grad,
    all_merge,
    chunks,
    arrivals,
    send,
    receive,
    local,
):
    low = jnp.bfloat16
    rows, width = tokens.shape
    head_local = query_aux.shape[0]
    group_width = head_local * HEAD_DIM
    data, tensor = lax.axis_index("dp"), lax.axis_index("tensor")
    core, half = data & 1, tensor >> 1
    home = core == half
    group = 2 * (tensor & 1) + core
    wires = Wires(send, receive)
    beside, across, diagonal = (data ^ 1, tensor), (data, tensor ^ 1), (data ^ 1, tensor ^ 1)
    members = [None, beside, across, diagonal]
    away = (data ^ 1, tensor ^ 2)
    pieces = [pl.ds(p * (rows // 2), rows // 2) for p in range(2)]
    pending = []

    def begin(k, source, target, device, when=None):
        if when is None:
            wires.start(k, source, target, device)
        else:

            @pl.when(when)
            def _():
                wires.start(k, source, target, device)

        pending.append((k, source, device, when))

    def await_arrival(k, target, device, when=None):
        if when is None:
            wires.arrived(k, target, device)
        else:

            @pl.when(when)
            def _():
                wires.arrived(k, target, device)

    all_merge[data, tensor] = merge[...]
    greet(column_and_plane(data, tensor, data_count, tensor_count))

    pair = (data >> 1) * 2

    def group_send(block, whole):
        numbers = [wires.number() for _ in range(4)]
        for k in (0, 1):
            target = (pair + (tensor & 1), (tensor >> 1) + 2 * k)
            itself = (target[0] == data) & (target[1] == tensor)
            for c in (0, 1):
                begin(
                    numbers[2 * k + c],
                    block,
                    whole.at[data],
                    target,
                    jnp.logical_not(itself) & (core == c),
                )

            @pl.when(itself)
            def _():
                copy = pltpu.make_async_copy(block, whole.at[data], local.at[1])
                copy.start()
                copy.wait()

        return numbers

    def group_wait(numbers, whole):
        for k in (0, 1):
            for c in (0, 1):
                source = (pair + c, group)
                itself = (source[0] == data) & (source[1] == tensor)
                await_arrival(
                    numbers[2 * k + c],
                    whole.at[pair + c],
                    source,
                    jnp.logical_not(itself) & (half == k),
                )

    if gather_heads:
        head_numbers = group_send(heads, all_heads)

    numbers = [wires.number() for _ in range(12)]
    for p, piece in enumerate(pieces):
        begin(numbers[p], tokens.at[piece], chunks.at[2, piece], across, home)
        begin(numbers[2 + p], tokens.at[piece], chunks.at[0, piece], away, jnp.logical_not(home))
        begin(numbers[4 + p], tokens.at[piece], chunks.at[1, piece], beside, home)

    @pl.when(home)
    def _():
        chunks[0] = tokens[...]

    if gather_heads:
        group_wait(head_numbers, all_heads)
        plane = []
        for k in range(1, data_count // 2):
            number = wires.number()
            plane.append((number, k))
            begin(number, all_heads.at[pl.ds(pair, 2)], all_heads.at[pl.ds(pair, 2)], (data ^ (2 * k), tensor))

    def bit_step(plan):
        made = []
        for mat, bit, held, wide in plan:
            for offset in held:
                number = wires.number()
                place = (pair if wide else data) ^ offset
                there = pl.ds(place ^ bit, 2) if wide else place ^ bit
                place = pl.ds(place, 2) if wide else place
                begin(number, mat.at[place], mat.at[place], (data ^ bit, tensor))
                made.append((number, mat, there, bit))
        return made

    def bit_wait(made):
        for number, mat, there, bit in made:
            await_arrival(number, mat.at[there], (data ^ bit, tensor))


    bits = low_rank_bits(data_count)
    schedule = []
    held = [[0], [0], [0]]
    for k in range(len(bits)):
        plan = []
        for m, mat in enumerate((all_expand, all_reduce, all_merge)):
            bit = bits[-1 - k] if m == 1 else bits[k]
            plan.append((mat, bit, list(held[m]), m < 2))
            held[m] = held[m] + [offset ^ bit for offset in held[m]]
        schedule.append(plan)
    schedule.append([(all_merge, 1, list(held[2]), False)])

    for p, piece in enumerate(pieces):
        await_arrival(numbers[2 + p], chunks.at[0, piece], away, jnp.logical_not(home))
        begin(numbers[6 + p], chunks.at[0, piece], chunks.at[2, piece], across, jnp.logical_not(home))
        begin(numbers[8 + p], chunks.at[0, piece], chunks.at[1, piece], beside, jnp.logical_not(home))

    merge_numbers = [wires.number() for _ in range(tensor_count - 1)]
    for k in range(1, tensor_count):
        peer = (data, lax.rem(tensor + k, tensor_count))
        begin(merge_numbers[k - 1], merge, all_merge.at[data, tensor], peer)

    if gather_heads:
        for number, k in plane:
            there = pl.ds(pair ^ (2 * k), 2)
            await_arrival(number, all_heads.at[there], (data ^ (2 * k), tensor))

    block = min(KEY_BLOCK, rows)
    lane = lax.broadcasted_iota(jnp.int32, (block, AUX), 1)
    blank = jnp.zeros((block, AUX - HEAD_DIM), jnp.float32)
    steps = rows // block

    def prepare(member):
        def one(step, carry):
            inside = pl.ds(pl.multiple_of(step * block, block), block)
            at_rows = pl.ds(pl.multiple_of(member * rows + step * block, block), block)
            normed, _ = center_scale(chunks[member, inside, :].astype(jnp.float32))
            first_in = (normed * vectors[0:1, :] + vectors[1:2, :]).astype(low)
            first_full[at_rows, :] = first_in
            weight = all_heads[...].reshape(width, 3 * group_width)
            projected = jnp.dot(first_in, weight, preferred_element_type=jnp.float32)
            projected = projected.astype(low).astype(jnp.float32)
            same = lane - HEAD_DIM == segment_column[at_rows, :]
            segment_lane = (lane >= HEAD_DIM) & (lane < HEAD_DIM + 3)
            query_extra = jnp.where(same & segment_lane, 1.0, 0.0)
            key_extra = jnp.where(
                segment_lane,
                jnp.where(same, 0.0, masked_score),
                jnp.where((lane >= HEAD_DIM + 3) & (lane < HEAD_DIM + 6), -1.0, 0.0),
            )
            value_extra = jnp.where(
                lane == HEAD_DIM,
                1.0,
                jnp.where((lane == HEAD_DIM + 1) | (lane == HEAD_DIM + 2), -1.0, 0.0),
            )
            for head in range(head_local):
                for which, (ref, extra, factor) in enumerate(
                    (
                        (query_aux, query_extra, HEAD_DIM**-0.5),
                        (key_aux, key_extra, 1.0),
                        (value_aux, value_extra, 1.0),
                    )
                ):
                    at = (3 * head + which) * HEAD_DIM
                    part = jnp.concatenate([projected[:, at : at + HEAD_DIM] * factor, blank], axis=1)
                    ref[head, at_rows, :] = jnp.where(lane < HEAD_DIM, part, extra).astype(low)
            return carry

        lax.fori_loop(0, steps, one, 0)

    def attend(member, steps_here):
        def one(step, carry):
            inside = pl.ds(pl.multiple_of(step * block, block), block)
            at_rows = pl.ds(pl.multiple_of(member * rows + step * block, block), block)
            done = []
            for head in range(head_local):
                query = query_aux[head, at_rows, :]
                scores = contract_cols(query, key_aux[head])
                row_max = jnp.max(scores, axis=1, keepdims=True)
                exponent = jnp.exp(scores - row_max).astype(low)
                output = jnp.dot(exponent, value_aux[head], preferred_element_type=jnp.float32)
                totals = output[:, HEAD_DIM : HEAD_DIM + 1]
                done.append(output[:, :HEAD_DIM] / totals)
                logsum = row_max + jnp.log(totals)
                first = logsum.astype(low).astype(jnp.float32)
                second = (logsum - first).astype(low).astype(jnp.float32)
                third = logsum - first - second
                wide = query.astype(jnp.float32)
                wide = jnp.where(lane == HEAD_DIM + 3, first, wide)
                wide = jnp.where(lane == HEAD_DIM + 4, second, wide)
                wide = jnp.where(lane == HEAD_DIM + 5, third, wide)
                query_aux[head, at_rows, :] = wide.astype(low)
            attended[member, inside, :] = jnp.concatenate(done, axis=1).astype(low)
            return carry

        lax.fori_loop(*steps_here, one, 0)

    prepare(0)
    for p, piece in enumerate(pieces):
        await_arrival(numbers[p], chunks.at[2, piece], across, home)
        await_arrival(numbers[6 + p], chunks.at[2, piece], across, jnp.logical_not(home))
        begin(numbers[10 + p], chunks.at[2, piece], chunks.at[3, piece], beside)

    grad_numbers = [wires.number() for _ in range(4)]
    grad_copies = []
    for member in range(4):
        its_core, its_tensor = core ^ (member & 1), tensor ^ (member >> 1)
        chunk = its_tensor ^ (2 * (its_core ^ (its_tensor >> 1)))
        source = out_grad.at[pl.ds(pl.multiple_of(chunk * rows, rows), rows)]
        copy = pltpu.make_async_copy(source, sequence_grad.at[member], local.at[2 + member])
        grad_copies.append(copy)
        pl.when(home)(copy.start)
        begin(grad_numbers[member], source, sequence_grad.at[member ^ 1], beside, home)
    for p, piece in enumerate(pieces):
        await_arrival(numbers[4 + p], chunks.at[1, piece], beside, jnp.logical_not(home))
        await_arrival(numbers[8 + p], chunks.at[1, piece], beside, home)
    expand_numbers = group_send(expand, all_expand)
    reduce_numbers = group_send(reduce, all_reduce)
    prepare(1)
    prepare(2)
    for k in range(1, tensor_count):
        origin = lax.rem(tensor + tensor_count - k, tensor_count)
        await_arrival(merge_numbers[k - 1], all_merge.at[data, origin], (data, origin))
    merge_made = bit_step(schedule[0][2:])
    for p, piece in enumerate(pieces):
        await_arrival(numbers[10 + p], chunks.at[3, piece], beside)
    prepare(3)
    exchange = {}
    for member in (3, 2, 1, 0):
        attend(member, (0, steps // 2))
        if member == 3:
            for plan in schedule[1:-1]:
                bit_wait(merge_made)
                merge_made = bit_step(plan[2:])
        elif member == 2:
            group_wait(expand_numbers, all_expand)
            group_wait(reduce_numbers, all_reduce)
            made = bit_step(schedule[0][:2])
        attend(member, (steps // 2, steps))
        if member:
            number = wires.number()
            begin(number, attended.at[member], arrivals.at[group], members[member])
            exchange[member] = number
        else:
            arrivals[group] = attended[0]
        if member == 2:
            bit_wait(merge_made)
            merge_made = bit_step(schedule[-1])
    for plan in schedule[1 : -2 if late else -1]:
        bit_wait(made)
        made = bit_step(plan[:2])
    bit_wait(merge_made)
    strips = []
    for k in range(tensor_count):
        strip = all_merge[:, k].astype(jnp.float32)
        strips.append(strip.reshape(width, group_width))
    merge_full[...] = jnp.concatenate(strips, axis=1).astype(low)
    own_tokens[...] = chunks[0]
    for member, number in exchange.items():
        await_arrival(number, arrivals.at[group ^ member], members[member])
    attended_rows[...] = jnp.concatenate([arrivals[k] for k in range(4)], axis=1)
    bit_wait(made)
    for member in range(4):
        pl.when(home)(grad_copies[member].wait)
        await_arrival(
            grad_numbers[member], sequence_grad.at[member ^ 1], beside, jnp.logical_not(home)
        )
    for k, source, device, when in pending:
        if when is None:
            wires.sent(k, source, device)
        else:

            @pl.when(when)
            def _():
                wires.sent(k, source, device)


def front_pallas(tokens, heads, expand, reduce, merge, vectors, segments, out_grad, gather_heads, late):
    data_count, tensor_count = lax.axis_size("dp"), lax.axis_size("tensor")
    rows, width = tokens.shape
    low = jnp.bfloat16
    head_columns = heads.shape[-1]
    head_local = head_columns // (3 * HEAD_DIM)
    seq_len = segments.shape[0]
    group_width = head_local * HEAD_DIM
    aux = jax.ShapeDtypeStruct((head_local, seq_len, AUX), low)
    inside = pl.BlockSpec(memory_space=pltpu.VMEM)
    anywhere = pl.BlockSpec(memory_space=pl.ANY)
    gathered = [
        jax.ShapeDtypeStruct((data_count,) + expand.shape, low),
        jax.ShapeDtypeStruct((data_count,) + reduce.shape, low),
        jax.ShapeDtypeStruct((width, width), low),
        jax.ShapeDtypeStruct((4, rows, width), low),
    ]
    hops = 2 * (tensor_count - 1) + 2 * (data_count // 2 - 1) + data_count - 1
    copies = 12 + data_count // 2 + 12 + hops + 4 + 3
    if gather_heads:
        heads_out = jax.ShapeDtypeStruct((data_count,) + heads.shape, low)
    else:
        heads_out = jax.ShapeDtypeStruct(heads.shape, low)

    def kernel(*refs):
        if not gather_heads:
            refs = list(refs)
            refs[15] = refs[1]
        front_kernel(data_count, tensor_count, gather_heads, late, *refs)

    return pl.pallas_call(
        kernel,
        out_shape=(
            jax.ShapeDtypeStruct((4, rows, group_width), low),
            jax.ShapeDtypeStruct((rows, 4 * group_width), low),
            aux,
            aux,
            aux,
            jax.ShapeDtypeStruct((seq_len, width), low),
            jax.ShapeDtypeStruct((rows, width), low),
            heads_out,
            *gathered,
        ),
        in_specs=[inside] * 7 + [anywhere],
        out_specs=(inside,) * 8 + (anywhere,) * 2 + (inside,) * 2,
        scratch_shapes=[
            pltpu.VMEM((data_count, tensor_count) + merge.shape, low),
            pltpu.VMEM((4, rows, width), low),
            pltpu.VMEM((4, rows, group_width), low),
            pltpu.SemaphoreType.DMA((copies,)),
            pltpu.SemaphoreType.DMA((copies,)),
            pltpu.SemaphoreType.DMA((6,)),
        ],
        compiler_params=pltpu.CompilerParams(
            vmem_limit_bytes=VMEM_LIMIT, collective_id=1, has_side_effects=True
        ),
        cost_estimate=pl.CostEstimate(
            flops=4 * head_local * seq_len * seq_len * AUX,
            bytes_accessed=8 * seq_len * width,
            transcendentals=head_local * seq_len * seq_len,
        ),
        name="front",
    )(tokens, heads, expand, reduce, merge, vectors, segments.reshape(seq_len, 1), out_grad)


def dot_rows(left_side, right_side):
    return jnp.dot(left_side, right_side, preferred_element_type=jnp.float32)


def middle_kernel(
    data_count,
    late,
    attended_rows,
    merge,
    tokens,
    vectors,
    expand_in,
    reduce_in,
    sequence_grad,
    layer_base,
    layer_across,
    middle_grad,
    attended_grad,
    expand_sum,
    reduce_sum,
    merge_sum,
    vector_sums,
    second_in,
    middle,
    hidden,
    expand_grad,
    partial,
    reduced,
    from_beside,
    reduced_beside,
    from_across,
    expand_got,
    reduce_got,
    expand_full,
    reduce_full,
    send,
    receive,
    local,
):
    low = jnp.bfloat16
    rows, width = tokens.shape
    group_width = width // 4
    data, tensor = lax.axis_index("dp"), lax.axis_index("tensor")
    wires = Wires(send, receive)
    beside, across = (data ^ 1, tensor), (data, tensor ^ 1)
    part = rows // 2
    pieces = [pl.ds(p * part, part) for p in range(2)]
    pending = []

    def begin(k, source, target, device):
        wires.start(k, source, target, device)
        pending.append((k, source, device))

    bits = low_rank_bits(data_count)
    greet([beside, across] + [(data ^ bit, tensor) for bit in sorted({bits[0], bits[-1]})])
    groups = [
        Group(work, got, None, order, (data, tensor), wires, begin)
        for work, got, order in (
            (expand_sum, expand_got, bits[::-1]),
            (reduce_sum, reduce_got, bits),
        )
    ]
    pair = (data >> 1) * 2
    if late:
        made, copies = [], []
        for m, (source, full, bit) in enumerate(
            ((expand_in, expand_full, bits[-1]), (reduce_in, reduce_full, bits[0]))
        ):
            for offset in [o for o in range(0, data_count, 2) if not o & bit]:
                here = pl.ds(pair ^ offset, 2)
                number = wires.number()
                begin(number, source.at[here], full.at[here], (data ^ bit, tensor))
                made.append((number, full.at[pl.ds(pair ^ offset ^ bit, 2)], (data ^ bit, tensor)))
                copies.append(
                    pltpu.make_async_copy(source.at[here], full.at[here], local.at[len(copies)])
                )
                copies[-1].start()
    units = data_count * expand_full.shape[1]

    def expand():
        return expand_full[...].reshape(units, width) if late else expand_in[...]

    def reduce():
        return reduce_full[...].reshape(units, width) if late else reduce_in[...]

    numbers = [[wires.number() for _ in range(2)] for _ in range(3)]
    for p, piece in enumerate(pieces):
        merged = contract_cols(attended_rows[piece, :], merge[...])
        here = tokens[piece, :].astype(jnp.float32) + merged + vectors[4:5, :]
        middle[piece, :] = here
        normed, _ = center_scale(here)
        second_in[0, piece, :] = (normed * vectors[2:3, :] + vectors[3:4, :]).astype(low)
        begin(numbers[0][p], second_in.at[0, piece], second_in.at[2, piece], across)
        begin(numbers[1][p], second_in.at[0, piece], second_in.at[1, piece], beside)

    def unit(member, p):
        piece = pieces[p]
        expanded = contract_cols(second_in[member, piece, :], expand())
        cdf = 0.5 + 0.5 * lax.erf(expanded * math.sqrt(0.5))
        activated = (expanded * cdf).astype(low)
        hidden[member, piece, :] = activated
        reduced[member, piece, :] = dot_rows(activated, reduce()).astype(low)
        slope = cdf + expanded * (jnp.exp(-0.5 * expanded * expanded) * (1.0 / math.sqrt(2.0 * math.pi)))
        upstream = contract_cols(sequence_grad[member, piece, :], reduce())
        grad = (upstream * slope).astype(low)
        expand_grad[member, piece, :] = grad
        partial[member, piece, :] = dot_rows(grad, expand()).astype(low)

    if late:
        for copy in copies:
            copy.wait()
        for number, there, device in made:
            wires.arrived(number, there, device)
    unit(0, 0)
    unit(0, 1)
    back = [[wires.number() for _ in range(2)] for _ in range(5)]
    for p, piece in enumerate(pieces):
        wires.arrived(numbers[1][p], second_in.at[1, piece], beside)
        unit(1, p)
        begin(back[0][p], partial.at[1, piece], from_beside.at[0, piece], beside)
        begin(back[3][p], reduced.at[1, piece], reduced_beside.at[0, piece], beside)
    for p, piece in enumerate(pieces):
        wires.arrived(numbers[0][p], second_in.at[2, piece], across)
        begin(numbers[2][p], second_in.at[2, piece], second_in.at[3, piece], beside)
    for p, piece in enumerate(pieces):
        wires.arrived(numbers[2][p], second_in.at[3, piece], beside)
        unit(3, p)
        begin(back[1][p], partial.at[3, piece], from_beside.at[1, piece], beside)
        begin(back[4][p], reduced.at[3, piece], reduced_beside.at[1, piece], beside)
        unit(2, p)
        wires.arrived(back[1][p], from_beside.at[1, piece], beside)
        both = partial[2, piece, :].astype(jnp.float32) + from_beside[1, piece, :].astype(jnp.float32)
        partial[2, piece, :] = both.astype(low)
        begin(back[2][p], partial.at[2, piece], from_across.at[piece], across)

    def sum_rows(target, left, right):
        total = None
        for member in range(4):
            term = contract_rows(left[member], right[member])
            total = term if total is None else total + term
        target[...] = total.reshape(target.shape).astype(low)

    sum_rows(reduce_sum, hidden, sequence_grad)
    groups[1].bit_send()
    sum_rows(expand_sum, expand_grad, second_in)
    groups[0].bit_send()
    for p, piece in enumerate(pieces):
        wires.arrived(back[3][p], reduced_beside.at[0, piece], beside)
        wires.arrived(back[4][p], reduced_beside.at[1, piece], beside)
        base = reduced[0, piece, :].astype(jnp.float32) + reduced_beside[0, piece, :].astype(jnp.float32)
        layer_base[piece, :] = base + middle[piece, :] + vectors[5:6, :]
        layer_across[piece, :] = (
            reduced[2, piece, :].astype(jnp.float32)
            + reduced_beside[1, piece, :].astype(jnp.float32)
        ).astype(low)
    sums = [0.0] * 4
    for p, piece in enumerate(pieces):
        wires.arrived(back[0][p], from_beside.at[0, piece], beside)
        wires.arrived(back[2][p], from_across.at[piece], across)
        second_grad = (
            partial[0, piece, :].astype(jnp.float32)
            + from_beside[0, piece, :].astype(jnp.float32)
            + from_across[piece, :].astype(jnp.float32)
        )
        normed, inverse = center_scale(middle[piece, :])
        own = sequence_grad[0, piece, :].astype(jnp.float32)
        total = own + norm_backward(second_grad, normed, inverse, vectors[2:3, :])
        middle_grad[piece, :] = total
        for k, term in enumerate((second_grad * normed, second_grad, total, own)):
            sums[k] = sums[k] + jnp.sum(term, axis=0, keepdims=True)
        into_attended = dot_rows(total.astype(low), merge[...]).astype(low)
        for k in range(4):
            attended_grad[k, piece, :] = into_attended[:, k * group_width : (k + 1) * group_width]
    vector_sums[...] = jnp.concatenate(sums, axis=0)
    into_merge = contract_rows(middle_grad[...].astype(low), attended_rows[...]).astype(low)
    for k in range(4):
        merge_sum[k] = into_merge[:, k * group_width : (k + 1) * group_width]
    for which in groups:
        which.bit_add()
    for k, source, device in pending:
        wires.sent(k, source, device)


def middle_pallas(attended_rows, merge, tokens, vectors, expand, reduce, sequence_grad, late):
    rows, width = tokens.shape
    units = expand.shape[0] * (expand.shape[1] if late else 1)
    data_count = lax.axis_size("dp")
    unit_block = (units // data_count, width)
    first_slots = data_count // 4
    low, wide = jnp.bfloat16, jnp.float32
    inside = pl.BlockSpec(memory_space=pltpu.VMEM)
    shapes = (
        ((rows, width), wide),
        ((rows, width), low),
        ((rows, width), wide),
        ((4, rows, width // 4), low),
        ((data_count,) + unit_block, low),
        ((data_count,) + unit_block, low),
        ((4, width, width // 4), low),
        ((4, width), wide),
    )
    copies = 16 + 4 * first_slots
    return pl.pallas_call(
        functools.partial(middle_kernel, data_count, late),
        out_shape=tuple(jax.ShapeDtypeStruct(*shape) for shape in shapes),
        in_specs=[inside] * 4 + [pl.BlockSpec(memory_space=pl.ANY) if late else inside] * 2 + [inside],
        out_specs=(inside,) * 8,
        scratch_shapes=[
            pltpu.VMEM((4, rows, width), low),
            pltpu.VMEM((rows, width), wide),
            pltpu.VMEM((4, rows, units), low),
            pltpu.VMEM((4, rows, units), low),
            pltpu.VMEM((4, rows, width), low),
            pltpu.VMEM((4, rows, width), low),
            pltpu.VMEM((2, rows, width), low),
            pltpu.VMEM((2, rows, width), low),
            pltpu.VMEM((rows, width), low),
            pltpu.VMEM((first_slots, 2) + unit_block, low),
            pltpu.VMEM((first_slots, 2) + unit_block, low),
            pltpu.VMEM((data_count,) + unit_block, low),
            pltpu.VMEM((data_count,) + unit_block, low),
            pltpu.SemaphoreType.DMA((copies,)),
            pltpu.SemaphoreType.DMA((copies,)),
            pltpu.SemaphoreType.DMA((2 * first_slots,)),
        ],
        compiler_params=pltpu.CompilerParams(
            vmem_limit_bytes=VMEM_LIMIT, collective_id=2, has_side_effects=True
        ),
        cost_estimate=pl.CostEstimate(
            flops=52 * rows * width * units, bytes_accessed=20 * rows * width, transcendentals=rows * units * 8
        ),
        name="middle",
    )(attended_rows, merge, tokens, vectors, expand, reduce, sequence_grad)


class Group:
    def __init__(self, work, arrived, last, order, place, wires, begin, first=0):
        self.work, self.got, self.last, self.order = work, arrived, last, order
        self.data, self.tensor = place
        self.pair = (self.data >> 1) * 2
        self.core, self.half = self.data & 1, self.tensor >> 1
        self.wires, self.begin = wires, begin
        self.left = [
            o for o in range(0, work.shape[0], 2) if not any(o & bit for bit in order[:first])
        ]
        self.slot, self.flight, self.step = 0, [], first

    def bit_send(self):
        bit = self.order[self.step]
        self.flight = []
        for offset in [o for o in self.left if o & bit]:
            number = self.wires.number()
            target = (self.data ^ bit, self.tensor)
            self.begin(number, self.work.at[pl.ds(self.pair ^ offset, 2)], self.got.at[self.slot], target)
            self.flight.append((number, self.slot, offset ^ bit, target))
            self.slot += 1
        self.left = [o for o in self.left if not o & bit]
        self.step += 1

    def bit_add(self):
        for number, slot, offset, target in self.flight:
            self.wires.arrived(number, self.got.at[slot], target)
            here = pl.ds(self.pair ^ offset, 2)
            total = self.work[here].astype(jnp.float32) + self.got[slot].astype(jnp.float32)
            self.work[here] = total.astype(self.work.dtype)

    def own_send(self):
        group = 2 * (self.tensor & 1) + self.core
        self.numbers = [self.wires.number() for _ in range(4)]
        for c in (0, 1):
            owner = (self.pair + c, group)
            itself = (owner[0] == self.data) & (owner[1] == self.tensor)
            for b in (0, 1):
                self.begin(
                    self.numbers[2 * c + b],
                    self.work.at[self.pair + c],
                    self.last.at[b],
                    owner,
                    jnp.logical_not(itself) & (self.half == b),
                )

    def own_sum(self):
        for b in (0, 1):
            source = (self.pair + (self.tensor & 1), (self.tensor >> 1) + 2 * b)
            itself = (source[0] == self.data) & (source[1] == self.tensor)
            for c in (0, 1):

                @pl.when(jnp.logical_not(itself) & (self.core == c))
                def _():
                    self.wires.arrived(self.numbers[2 * c + b], self.last.at[b], source)

            @pl.when(itself)
            def _():
                self.last[b] = self.work[self.data]

        return self.last[0].astype(jnp.float32) + self.last[1].astype(jnp.float32)


class ChipSum:
    def __init__(
        self, array, result, arrived, last, base, size, order, place, tensor_count, wires, begin
    ):
        self.array, self.result, self.got, self.last = array, result, arrived, last
        self.start, self.size, self.order = base, size, order
        self.data, self.tensor = place
        self.count, self.wires, self.begin = tensor_count, wires, begin
        self.slot, self.step, self.trail = 0, 0, []

    def bit_send(self):
        bit = self.order[self.step]
        self.step += 1
        half = self.size // 2
        mine = (self.data & bit) // bit
        keep, give = self.start + mine * half, self.start + (1 - mine) * half
        number = self.wires.number()
        target = (self.data ^ bit, self.tensor)
        there = self.got.at[pl.ds(self.slot, half)]
        self.begin(number, self.array.at[pl.ds(give, half)], there, target)
        self.trail.append((bit, keep, give, half))
        self.flight = (number, self.slot, half, target)
        self.start, self.size = keep, half
        self.slot += half

    def bit_add(self):
        number, slot, half, target = self.flight
        self.wires.arrived(number, self.got.at[pl.ds(slot, half)], target)
        here = pl.ds(self.start, half)
        self.array[here] = self.array[here] + self.got[pl.ds(slot, half)]

    def line_send(self):
        self.spread = self.size % self.count == 0
        self.portion = self.size // self.count if self.spread else self.size
        self.flight = []
        for k in range(1, self.count):
            number = self.wires.number()
            peer = lax.rem(self.tensor + k, self.count)
            at = self.start + peer * self.portion if self.spread else self.start
            source = self.array.at[pl.ds(at, self.portion)]
            self.begin(number, source, self.last.at[k - 1], (self.data, peer))
            origin = lax.rem(self.tensor + self.count - k, self.count)
            self.flight.append((number, k - 1, (self.data, origin)))

    def line_add(self):
        at = self.start + self.tensor * self.portion if self.spread else self.start
        here = pl.ds(at, self.portion)
        for number, slot, origin in self.flight:
            self.wires.arrived(number, self.last.at[slot], origin)
        total = self.array[here]
        for number, slot, origin in self.flight:
            total = total + self.last[slot]
        self.result[here] = total

    def line_back(self):
        self.flight = []
        if self.spread:
            here = pl.ds(self.start + self.tensor * self.portion, self.portion)
            for k in range(1, self.count):
                number = self.wires.number()
                peer = lax.rem(self.tensor + k, self.count)
                self.begin(number, self.result.at[here], self.result.at[here], (self.data, peer))
                origin = lax.rem(self.tensor + self.count - k, self.count)
                there = pl.ds(self.start + origin * self.portion, self.portion)
                self.flight.append((number, there, (self.data, origin)))

    def bit_back(self):
        bit, keep, give, half = self.trail.pop()
        number = self.wires.number()
        target = (self.data ^ bit, self.tensor)
        here = pl.ds(keep, half)
        self.begin(number, self.result.at[here], self.result.at[here], target)
        self.flight = [(number, pl.ds(give, half), target)]
        self.start = jnp.minimum(keep, give)
        self.size = 2 * half

    def back_wait(self):
        for number, there, target in self.flight:
            self.wires.arrived(number, self.result.at[there], target)


def split_low(values):
    high = values.astype(jnp.bfloat16)
    return high, (values - high.astype(jnp.float32)).astype(jnp.bfloat16)


def back_kernel(
    data_count,
    tensor_count,
    attended,
    attended_grad,
    query_aux,
    key_aux,
    value_aux,
    first_full,
    heads_weight,
    expand_sum,
    reduce_sum,
    merge_sum,
    layer_base,
    layer_across,
    expand_momentum,
    reduce_momentum,
    tokens,
    middle_grad,
    vectors,
    vector_sums,
    expand_out,
    reduce_out,
    merge_out,
    heads_out,
    input_rows,
    vector_part,
    output_rows,
    gram,
    both,
    upstream,
    grad_aux,
    key_turned,
    query_total,
    projected_grad,
    first_parts,
    first_beside,
    first_across,
    layer_got,
    expand_work,
    expand_got,
    expand_last,
    reduce_work,
    reduce_got,
    reduce_last,
    merge_work,
    merge_core,
    merge_line,
    merge_got,
    merge_last,
    heads_work,
    heads_got,
    heads_last,
    side,
    side_got,
    gram_work,
    gram_got,
    gram_last,
    send,
    receive,
    local,
):
    low = jnp.bfloat16
    members, rows, group_width = attended.shape
    head_local = group_width // HEAD_DIM
    seq_len = members * rows
    data, tensor = lax.axis_index("dp"), lax.axis_index("tensor")
    place = (data, tensor)
    core = data & 1
    group = 2 * (tensor & 1) + core
    wires = Wires(send, receive)
    beside, across, diagonal = (data ^ 1, tensor), (data, tensor ^ 1), (data ^ 1, tensor ^ 1)
    peers = [None, beside, across, diagonal]
    pending = []

    def begin(k, source, target, device, when=None):
        if when is None:
            wires.start(k, source, target, device)
        else:

            @pl.when(when)
            def _():
                wires.start(k, source, target, device)

        pending.append((k, source, device, when))

    def finish_sends():
        for k, source, device, when in pending:
            if when is None:
                wires.sent(k, source, device)
            else:

                @pl.when(when)
                def _():
                    wires.sent(k, source, device)

        pending.clear()

    copies = []
    for k, (source, target) in enumerate(
        ((expand_sum, expand_work), (reduce_sum, reduce_work), (merge_sum, merge_work))
    ):
        copies.append(pltpu.make_async_copy(source, target, local.at[k]))
        copies[-1].start()
    greet(column_and_plane(data, tensor, data_count, tensor_count))

    grad_numbers = {}
    for member in (2, 3, 1):
        grad_numbers[member] = wires.number()
        begin(
            grad_numbers[member],
            attended_grad.at[group ^ member],
            upstream.at[member],
            peers[member],
        )
    for copy in copies:
        copy.wait()
    bits = low_rank_bits(data_count)
    own_merge = merge_work.at[group]
    expand_group = Group(expand_work, expand_got, expand_last, bits[::-1], place, wires, begin, 1)
    reduce_group = Group(reduce_work, reduce_got, reduce_last, bits, place, wires, begin, 1)
    merge_group = Group(own_merge, merge_got, merge_last, bits[::-1], place, wires, begin)
    heads_group = Group(heads_work, heads_got, heads_last, bits, place, wires, begin)
    merge_numbers = [wires.number() for _ in range(3)]
    begin(merge_numbers[0], merge_work.at[group ^ 1], merge_core.at[0], beside)
    begin(merge_numbers[1], merge_work.at[group ^ 3], merge_core.at[1], beside)
    if len(bits) > 1:
        expand_group.bit_send()
        reduce_group.bit_send()
    layer_number = wires.number()
    upstream[0] = attended_grad[group]

    block = min(KEY_BLOCK, rows)
    lane = lax.broadcasted_iota(jnp.int32, (block, AUX), 1)
    blank = jnp.zeros((block, AUX - HEAD_DIM), jnp.float32)
    steps = rows // block

    def prepare(member):
        def one(step, carry):
            inside = pl.ds(pl.multiple_of(step * block, block), block)
            at_rows = pl.ds(pl.multiple_of(member * rows + step * block, block), block)
            gradient = upstream[member, inside, :].astype(jnp.float32)
            product = gradient * attended[member, inside, :].astype(jnp.float32)
            for head in range(head_local):
                columns = slice(head * HEAD_DIM, (head + 1) * HEAD_DIM)
                row_dot = jnp.sum(product[:, columns], axis=1, keepdims=True)
                first = row_dot.astype(low).astype(jnp.float32)
                wide = jnp.concatenate([gradient[:, columns], blank], axis=1)
                wide = jnp.where(lane == HEAD_DIM + 1, first, wide)
                wide = jnp.where(lane == HEAD_DIM + 2, row_dot - first, wide)
                grad_aux[head, at_rows, :] = wide.astype(low)
                key_turned[head, :, at_rows] = key_aux[head, at_rows, :].T[:HEAD_DIM]
            return carry

        lax.fori_loop(0, steps, one, 0)

    prepare(0)
    for member in (1, 2, 3):
        wires.arrived(grad_numbers[member], upstream.at[member], peers[member])
        prepare(member)
    query_total[...] = jnp.zeros_like(query_total)

    def back(step, carry):
        at_rows = pl.ds(pl.multiple_of(step * block, block), block)
        for head in range(head_local):
            scores = contract_cols(key_aux[head, at_rows, :], query_aux[head])
            chances = jnp.exp(scores)
            chance_grad = contract_cols(value_aux[head, at_rows, :], grad_aux[head])
            score_grad = (chances * chance_grad).astype(low)
            value_grad = dot_rows(chances.astype(low), grad_aux[head])
            key_grad = dot_rows(score_grad, query_aux[head])
            query_total[head] += dot_rows(key_turned[head, :, at_rows], score_grad)
            at = 3 * head * HEAD_DIM
            two = jnp.concatenate([key_grad[:, :HEAD_DIM], value_grad[:, :HEAD_DIM]], axis=1)
            projected_grad[at_rows, at + HEAD_DIM : at + 3 * HEAD_DIM] = two.astype(low)
        return carry

    eighth = seq_len // block // 8

    def back_eighths(start, stop):
        lax.fori_loop(start * eighth, stop * eighth, back, 0)

    for which in (expand_group, reduce_group):
        for k in range(1, len(bits)):
            which.bit_add()
            if k + 1 < len(bits):
                which.bit_send()
        which.own_send()
    wires.arrived(merge_numbers[0], merge_core.at[0], beside)
    wires.arrived(merge_numbers[1], merge_core.at[1], beside)
    for k in (0, 1):
        here = group ^ (2 * k)
        total = merge_work[here].astype(jnp.float32) + merge_core[k].astype(jnp.float32)
        merge_work[here] = total.astype(low)
    begin(merge_numbers[2], merge_work.at[group ^ 2], merge_line, across)

    back_eighths(0, 3)
    expand_out[...] = expand_group.own_sum()
    reduce_out[...] = reduce_group.own_sum()
    expand_part = momentum_decay * expand_momentum[...] + expand_out[...]
    reduce_part = momentum_decay * reduce_momentum[...] + reduce_out[...]
    first_core = core == 0
    side[0] = jnp.where(first_core, expand_part, reduce_part)
    side[1] = jnp.where(first_core, reduce_part, expand_part)
    side_number = wires.number()
    begin(side_number, side.at[1], side_got, beside)
    wires.arrived(merge_numbers[2], merge_line, across)
    total = merge_work[group].astype(jnp.float32) + merge_line[...].astype(jnp.float32)
    merge_work[group] = total.astype(low)
    merge_group.bit_send()

    back_eighths(3, 4)
    begin(layer_number, layer_across, layer_got, across)
    wires.arrived(side_number, side_got, beside)
    part_rows = side_got.shape[0]
    both[:part_rows, :] = side[0]
    both[part_rows:, :] = side_got[...]
    width = both.shape[1]
    high, rest = split_low(both[...])
    at = 0
    for k in range(0, width, SIDE):
        span = width - k
        part = contract_rows(high[:, k : k + SIDE], high[:, k:])
        part = part + contract_rows(high[:, k : k + SIDE], rest[:, k:])
        part = part + contract_rows(rest[:, k : k + SIDE], high[:, k:])
        gram_work[:, :, at : at + span] = part.reshape(SIDE // 8, 8, span)
        at += span
    slots = SIDE // 16
    halves = [
        ChipSum(
            gram_work,
            gram,
            gram_got.at[h],
            gram_last.at[h],
            h * slots,
            slots,
            order,
            place,
            tensor_count,
            wires,
            begin,
        )
        for h, order in enumerate((bits, bits[::-1]))
    ]
    for half in halves:
        half.bit_send()

    back_eighths(4, 6)
    for half in halves:
        half.bit_add()
        for _ in range(2, len(bits)):
            half.bit_send()
            half.bit_add()
        half.bit_send()
    merge_group.bit_add()
    merge_group.bit_send()

    back_eighths(6, 7)
    for half in halves:
        half.bit_add()
        half.line_send()
    merge_group.bit_add()
    for _ in range(2, len(bits)):
        merge_group.bit_send()
        merge_group.bit_add()
    merge_group.own_send()

    back_eighths(7, 8)

    def finish(step, carry):
        at_rows = pl.ds(pl.multiple_of(step * block, block), block)
        for head in range(head_local):
            query_grad = query_total[head, :, at_rows].T * HEAD_DIM**-0.5
            at = 3 * head * HEAD_DIM
            projected_grad[at_rows, at : at + HEAD_DIM] = query_grad.astype(low)
        return carry

    lax.fori_loop(0, seq_len // block, finish, 0)
    first_numbers = [wires.number() for _ in range(3)]

    def first_part(member):
        at_rows = pl.ds(member * rows, rows)
        part = contract_cols(projected_grad[at_rows, :], heads_weight[...])
        first_parts[member] = part.astype(low)

    heads_work[...] = (
        contract_rows(first_full[...], projected_grad[...]).reshape(heads_work.shape).astype(low)
    )
    heads_group.bit_send()
    for half in halves:
        half.line_add()
        half.line_back()
    for k, member in enumerate((3, 1)):
        first_part(member)
        begin(first_numbers[k], first_parts.at[member], first_beside.at[k], beside)
    first_part(2)
    wires.arrived(first_numbers[0], first_beside.at[0], beside)
    total = first_parts[2].astype(jnp.float32) + first_beside[0].astype(jnp.float32)
    first_parts[2] = total.astype(low)
    for half in halves:
        half.back_wait()
        half.bit_back()
    begin(first_numbers[2], first_parts.at[2], first_across, across)
    heads_group.bit_add()
    for _ in range(2, len(bits)):
        heads_group.bit_send()
        heads_group.bit_add()
    heads_group.bit_send()
    first_part(0)
    for _ in range(1, len(bits)):
        for half in halves:
            half.back_wait()
            half.bit_back()
    heads_group.bit_add()
    heads_group.own_send()
    merge_out[...] = merge_group.own_sum()
    wires.arrived(layer_number, layer_got, across)
    output_rows[...] = (layer_base[...] + layer_got[...].astype(jnp.float32)).astype(low)
    wires.arrived(first_numbers[1], first_beside.at[1], beside)
    wires.arrived(first_numbers[2], first_across, across)
    sums = [0.0, 0.0]
    for p in range(2):
        piece = pl.ds(p * (rows // 2), rows // 2)
        first_grad = (
            first_parts[0, piece, :].astype(jnp.float32)
            + first_beside[1, piece, :].astype(jnp.float32)
            + first_across[piece, :].astype(jnp.float32)
        )
        normed, inverse = center_scale(tokens[piece, :].astype(jnp.float32))
        input_rows[piece, :] = middle_grad[piece, :] + norm_backward(
            first_grad, normed, inverse, vectors[0:1, :]
        )
        sums[0] = sums[0] + jnp.sum(first_grad * normed, axis=0, keepdims=True)
        sums[1] = sums[1] + jnp.sum(first_grad, axis=0, keepdims=True)
    vector_part[...] = jnp.concatenate(sums + [vector_sums[...]], axis=0)
    heads_out[...] = heads_group.own_sum()
    for half in halves:
        half.back_wait()
    finish_sends()


def back_pallas(
    attended,
    attended_grad,
    query_aux,
    key_aux,
    value_aux,
    first_full,
    heads_weight,
    expand_sum,
    reduce_sum,
    merge_sum,
    layer_base,
    layer_across,
    expand_momentum,
    reduce_momentum,
    tokens,
    middle_grad,
    vectors,
    vector_sums,
):
    data_count, tensor_count = lax.axis_size("dp"), lax.axis_size("tensor")
    members, rows, group_width = attended.shape
    head_local = group_width // HEAD_DIM
    seq_len = members * rows
    low, wide = jnp.bfloat16, jnp.float32
    width, columns = heads_weight.shape
    unit_block = expand_sum.shape[1:]
    merge_block = merge_sum.shape[2:]
    heads_block = (width // data_count, columns)
    packed = sum(width - k for k in range(0, width, SIDE))
    inside = pl.BlockSpec(memory_space=pltpu.VMEM)
    outs = (
        (unit_block, wide),
        (unit_block, wide),
        (merge_block, wide),
        (heads_block, wide),
        ((rows, width), wide),
        (vectors.shape, wide),
        ((rows, width), low),
        ((SIDE // 8, 8, packed), wide),
        ((2 * unit_block[0], unit_block[1]), wide),
    )
    steps = data_count // 2 - 1
    later = max(data_count // 4 - 1, 1)
    slots = SIDE // 16
    left = slots // (data_count // 2)
    portion = left // tensor_count if left % tensor_count == 0 else left
    scratch = []
    for shape, kind in (
        ((members, rows, group_width), low),
        ((head_local, seq_len, AUX), low),
        ((head_local, HEAD_DIM, seq_len), low),
        ((head_local, HEAD_DIM, seq_len), wide),
        ((seq_len, columns), low),
        ((members, rows, width), low),
        ((2, rows, width), low),
        ((rows, width), low),
        ((rows, width), low),
        ((data_count,) + unit_block, low),
        ((later, 2) + unit_block, low),
        ((2,) + unit_block, low),
        ((data_count,) + unit_block, low),
        ((later, 2) + unit_block, low),
        ((2,) + unit_block, low),
        (merge_sum.shape, low),
        ((2, data_count) + merge_block, low),
        ((data_count,) + merge_block, low),
        ((steps, 2) + merge_block, low),
        ((2,) + merge_block, low),
        ((data_count,) + heads_block, low),
        ((steps, 2) + heads_block, low),
        ((2,) + heads_block, low),
        ((2,) + unit_block, wide),
        (unit_block, wide),
        ((SIDE // 8, 8, packed), wide),
        ((2, slots, 8, packed), wide),
        ((2, tensor_count - 1, portion, 8, packed), wide),
    ):
        scratch.append(pltpu.VMEM(shape, kind))
    copies = 3 + 3 + 1 + 4 * (steps + 4) + 1 + 3
    copies += 2 * (2 * (data_count // 2).bit_length() + 2 * tensor_count)
    return pl.pallas_call(
        functools.partial(back_kernel, data_count, tensor_count),
        out_shape=tuple(jax.ShapeDtypeStruct(*out) for out in outs),
        in_specs=[inside] * 7 + [pl.BlockSpec(memory_space=pl.ANY)] * 3 + [inside] * 8,
        out_specs=(inside,) * len(outs),
        scratch_shapes=scratch
        + [
            pltpu.SemaphoreType.DMA((copies,)),
            pltpu.SemaphoreType.DMA((copies,)),
            pltpu.SemaphoreType.DMA((3,)),
        ],
        compiler_params=pltpu.CompilerParams(
            vmem_limit_bytes=VMEM_LIMIT, collective_id=3, has_side_effects=True
        ),
        cost_estimate=pl.CostEstimate(
            flops=10 * head_local * seq_len * seq_len * AUX,
            bytes_accessed=10 * seq_len * width,
            transcendentals=head_local * seq_len * seq_len,
        ),
        name="back",
    )(
        attended,
        attended_grad,
        query_aux,
        key_aux,
        value_aux,
        first_full,
        heads_weight,
        expand_sum,
        reduce_sum,
        merge_sum,
        layer_base,
        layer_across,
        expand_momentum,
        reduce_momentum,
        tokens,
        middle_grad,
        vectors,
        vector_sums,
    )


def three_pass(left, right):
    return dot_rows(left[0], right[0]) + (dot_rows(left[0], right[1]) + dot_rows(left[1], right[0]))


def last_kernel(
    data_count,
    tensor_count,
    gram,
    both,
    small_gram,
    vector_part,
    output_rows,
    input_rows,
    ortho_mine,
    ortho_other,
    small_chain,
    vector_sum,
    moved_output,
    moved_input,
    square,
    gram_high,
    gram_low,
    factor_high,
    factor_low,
    part,
    theirs,
    small_got,
    small_sum,
    small_mine,
    vector_got,
    vector_half,
    vector_line,
    send,
    receive,
):
    size = part.shape[1]
    rows = part.shape[0] // 2
    data, tensor = lax.axis_index("dp"), lax.axis_index("tensor")
    beside, away = (data ^ 1, tensor), (data ^ 1, tensor ^ 2)
    moved = jnp.logical_not((data & 1) == (tensor >> 1))
    wires = Wires(send, receive)
    pending = []

    def begin(k, source, target, device, when=None):
        if when is None:
            wires.start(k, source, target, device)
        else:

            @pl.when(when)
            def _():
                wires.start(k, source, target, device)

        pending.append((k, source, device, when))

    greet(column_and_plane(data, tensor, data_count, tensor_count))
    bits = [1] + low_rank_bits(data_count)
    hops = [(wires.number(), wires.number()) for _ in bits]

    core = data & 1

    def hop_send(k):
        peer = (data ^ bits[k], tensor)
        begin(hops[k][0], vector_half.at[k], vector_got.at[k], peer)
        small = small_gram.at[1 - core] if k == 0 else small_sum.at[k]
        begin(hops[k][1], small, small_got.at[k], peer)

    def hop_add(k):
        peer = (data ^ bits[k], tensor)
        wires.arrived(hops[k][0], vector_got.at[k], peer)
        wires.arrived(hops[k][1], small_got.at[k], peer)
        vector_half[k + 1] = vector_half[k] + vector_got[k]
        small = small_gram[core] if k == 0 else small_sum[k]
        small_sum[k + 1] = small + small_got[k]

    vector_half[0] = vector_part[...]
    hop_send(0)
    input_number, output_number = wires.number(), wires.number()
    begin(input_number, input_rows, moved_input, away, moved)
    begin(output_number, output_rows, moved_output, away, moved)

    identity = (
        lax.broadcasted_iota(jnp.int32, (SIDE, SIDE), 0)
        == lax.broadcasted_iota(jnp.int32, (SIDE, SIDE), 1)
    ).astype(jnp.float32)
    blocks = size // SIDE
    trace = 0.0
    at = 0
    for i in range(blocks):
        span = size - i * SIDE
        strip = gram[:, :, at : at + span].reshape(SIDE, span)
        trace = trace + jnp.sum(strip[:, :SIDE] * identity)
        at += span
    factor = 1.0 / (jnp.sqrt(trace) + newton_epsilon)

    def keep(strip, i, high, low):
        top, rest = split_low(strip)
        high[i * SIDE : (i + 1) * SIDE, i * SIDE :] = top
        low[i * SIDE : (i + 1) * SIDE, i * SIDE :] = rest
        for j in range(i + 1, blocks):
            turned = strip[:, (j - i) * SIDE : (j - i + 1) * SIDE].T
            top, rest = split_low(turned)
            high[j * SIDE : (j + 1) * SIDE, i * SIDE : (i + 1) * SIDE] = top
            low[j * SIDE : (j + 1) * SIDE, i * SIDE : (i + 1) * SIDE] = rest

    at = 0
    for i in range(blocks):
        span = size - i * SIDE
        strip = gram[:, :, at : at + span].reshape(SIDE, span) * (factor * factor)
        square[i * SIDE : (i + 1) * SIDE, i * SIDE :] = strip
        keep(strip, i, gram_high, gram_low)
        at += span
    part[...] = both[...] * factor

    def strip_of(left, right, i):
        here = slice(i * SIDE, (i + 1) * SIDE)
        return three_pass(
            (left[0][here, :], left[1][here, :]), (right[0][:, i * SIDE :], right[1][:, i * SIDE :])
        )

    gram_pair, factor_pair = (gram_high, gram_low), (factor_high, factor_low)

    def wide_factor():
        for i in range(blocks):
            here = slice(i * SIDE, (i + 1) * SIDE)
            strip = newton_cubic * square[here, i * SIDE :] + newton_quintic * strip_of(
                gram_pair, gram_pair, i
            )
            first = strip[:, :SIDE] + newton_linear * identity
            strip = first if i == blocks - 1 else jnp.concatenate([first, strip[:, SIDE:]], axis=1)
            keep(strip, i, factor_high, factor_low)

    def wide_part():
        part[...] = three_pass(split_low(part[...]), (factor_high[...], factor_low[...]))

    def wide_gram():
        strips = [strip_of(gram_pair, factor_pair, i) for i in range(blocks)]
        for i in range(blocks):
            keep(strips[i], i, gram_high, gram_low)
        strips = [strip_of(gram_pair, factor_pair, i) for i in range(blocks)]
        for i in range(blocks):
            square[i * SIDE : (i + 1) * SIDE, i * SIDE :] = strips[i]
            keep(strips[i], i, gram_high, gram_low)

    groups, head_size = small_gram.shape[1] // HEAD_DIM, HEAD_DIM
    double = 2 * head_size
    diagonal = identity[:double, :double]
    left = lax.broadcasted_iota(jnp.int32, (head_size, double), 1) < head_size
    small = {}

    def small_start():
        total = small_sum[len(bits)]
        small["gram"], small["chain"], small["scale"] = [], [], []
        for b in range(groups):
            pair = total[b * head_size : (b + 1) * head_size]
            full = jnp.concatenate([jnp.where(left, pair, 0.0), jnp.where(left, 0.0, pair)], axis=0)
            column = jnp.sum(full * diagonal, axis=1, keepdims=True)
            scales = []
            for k in range(2):
                norm = jnp.sqrt(jnp.sum(column[k * head_size : (k + 1) * head_size]))
                scales.append(jnp.full((head_size, 1), 1.0 / (norm + newton_epsilon), jnp.float32))
            scale = jnp.concatenate(scales, axis=0)
            small["gram"].append(full * (scale * scale))
            small["scale"].append(scale)
            small["chain"].append(None)

    def small_step(last):
        for b in range(groups):
            here = split_low(small["gram"][b])
            step = newton_linear * diagonal + newton_cubic * small["gram"][b]
            step = step + newton_quintic * three_pass(here, here)
            step_pair = split_low(step)
            before = small["chain"][b]
            small["chain"][b] = step if before is None else three_pass(split_low(before), step_pair)
            if not last:
                next_gram = three_pass(here, step_pair)
                small["gram"][b] = three_pass(split_low(next_gram), step_pair)

    def small_end():
        for b in range(groups):
            chain = small["chain"][b] * small["scale"][b]
            here = slice(b * head_size, (b + 1) * head_size)
            small_mine[here, :] = jnp.where(left, chain[:head_size], chain[head_size:])
        begin(small_number, small_mine, small_chain.at[core], beside)
        small_chain[core] = small_mine[...]

    small_number = wires.number()
    line_numbers = [wires.number() for _ in range(tensor_count - 1)]
    side_number = wires.number()
    for step in range(NEWTON_STEPS):
        wide_factor()
        if step == 1:
            hop_add(0)
            hop_send(1)
        elif step == 3:
            hop_add(2)
            for k in range(3, len(bits)):
                hop_send(k)
                hop_add(k)
            for k in range(1, tensor_count):
                peer = lax.rem(tensor + k, tensor_count)
                begin(line_numbers[k - 1], vector_half.at[len(bits)], vector_line.at[k - 1], (data, peer))
            small_start()
            small_step(False)
        elif step == 4:
            small_step(False)
        wide_part()
        if step < NEWTON_STEPS - 1:
            wide_gram()
        if step == 1:
            hop_add(1)
            hop_send(2)
        elif step == 3:
            small_step(False)
    small_step(False)
    ortho_mine[...] = part[:rows, :]
    theirs[...] = part[rows:, :]
    begin(side_number, theirs, ortho_other, beside)
    small_step(True)
    small_end()
    total = vector_half[len(bits)]
    for k in range(1, tensor_count):
        origin = lax.rem(tensor + tensor_count - k, tensor_count)
        wires.arrived(line_numbers[k - 1], vector_line.at[k - 1], (data, origin))
        total = total + vector_line[k - 1]
    vector_sum[...] = total

    @pl.when(moved)
    def _():
        wires.arrived(input_number, moved_input, away)
        wires.arrived(output_number, moved_output, away)

    wires.arrived(side_number, ortho_other, beside)
    wires.arrived(small_number, small_chain.at[1 - core], beside)
    for k, source, device, when in pending:
        if when is None:
            wires.sent(k, source, device)
        else:

            @pl.when(when)
            def _():
                wires.sent(k, source, device)


def last_pallas(gram, both, small_gram, vector_part, output_rows, input_rows):
    data_count, tensor_count = lax.axis_size("dp"), lax.axis_size("tensor")
    low, wide = jnp.bfloat16, jnp.float32
    size = both.shape[1]
    rows = both.shape[0] // 2
    hops = data_count.bit_length() - 1
    inside = pl.BlockSpec(memory_space=pltpu.VMEM)
    outs = (
        ((rows, size), wide),
        ((rows, size), wide),
        (small_gram.shape, wide),
        (vector_part.shape, wide),
        (output_rows.shape, low),
        (input_rows.shape, low),
    )
    scratch = [
        pltpu.VMEM(shape, kind)
        for shape, kind in (
            ((size, size), wide),
            ((size, size), low),
            ((size, size), low),
            ((size, size), low),
            ((size, size), low),
            (both.shape, wide),
            ((rows, size), wide),
            ((hops,) + small_gram.shape[1:], wide),
            ((hops + 1,) + small_gram.shape[1:], wide),
            (small_gram.shape[1:], wide),
            ((hops,) + vector_part.shape, wide),
            ((hops + 1,) + vector_part.shape, wide),
            ((tensor_count - 1,) + vector_part.shape, wide),
        )
    ]
    copies = 2 * hops + 3 + tensor_count
    return pl.pallas_call(
        functools.partial(last_kernel, data_count, tensor_count),
        out_shape=tuple(jax.ShapeDtypeStruct(*out) for out in outs),
        in_specs=[inside] * 6,
        out_specs=(inside,) * len(outs),
        scratch_shapes=scratch
        + [pltpu.SemaphoreType.DMA((copies,)), pltpu.SemaphoreType.DMA((copies,))],
        compiler_params=pltpu.CompilerParams(
            vmem_limit_bytes=VMEM_LIMIT, collective_id=4, has_side_effects=True
        ),
        cost_estimate=pl.CostEstimate(
            flops=90 * size * size * size, bytes_accessed=20 * size * size, transcendentals=0
        ),
        name="last",
    )(gram, both, small_gram, vector_part, output_rows, input_rows)


SIDE = 256


def swap_bit(values, axis_name, bit):
    count = lax.axis_size(axis_name)
    return lax.ppermute(values, axis_name, [(i, i ^ bit) for i in range(count)])


def data_bits():
    return [1 << k for k in range(1, lax.axis_size("dp").bit_length() - 1)]


def has_bit(index, bit):
    return (index & bit) != 0


def gather_bits_absolute(block, bits):
    index = lax.axis_index("dp")
    for bit in bits:
        other = swap_bit(block, "dp", bit)
        mine = has_bit(index, bit)
        block = jnp.concatenate(
            [jnp.where(mine, other, block), jnp.where(mine, block, other)], axis=0
        )
    return block


def pair_permute(values, where_to):
    data_count, tensor_count = lax.axis_size("dp"), lax.axis_size("tensor")
    moves = []
    for i in range(data_count):
        for j in range(tensor_count):
            target = where_to(i, j)
            if target is not None:
                moves.append((i * tensor_count + j, target[0] * tensor_count + target[1]))
    return lax.ppermute(values, ("dp", "tensor"), moves)


def exchange_home(values):
    return pair_permute(
        values, lambda i, j: (i ^ 1, j ^ 2) if (i & 1) != (j >> 1) else None
    )


def gather_head_group(shard):
    first = []
    for core in (0, 1):
        got = []
        for half in (0, 1):
            got.append(
                pair_permute(
                    shard,
                    lambda i, j: (i - core + (j & 1), (j >> 1) + 2 * half)
                    if (i & 1) == core
                    else None,
                )
            )
        first.append(jnp.where(lax.axis_index("tensor") >= 2, got[1], got[0]))
    return gather_bits_absolute(jnp.concatenate(first, axis=0), data_bits())


def per_device(
    tokens,
    segment_ids,
    out_grad,
    heads_weight,
    merge_weight,
    expand_weight,
    reduce_weight,
    heads_momentum,
    merge_momentum,
    expand_momentum,
    reduce_momentum,
    heads_average,
    merge_average,
    expand_average,
    reduce_average,
    vectors,
    vector_momentum,
    vector_average,
):
    low = jnp.bfloat16
    tensor_count = lax.axis_size("tensor")
    data_count = lax.axis_size("dp")
    tensor_index = lax.axis_index("tensor")
    core = lax.axis_index("dp") & 1
    row_count = tokens.shape[0]
    seq_len = row_count * tensor_count
    head_local = heads_weight.shape[1] // (3 * HEAD_DIM)
    group_width = head_local * HEAD_DIM
    at_home = core == (tensor_index >> 1)
    group = 2 * (tensor_index & 1) + core

    own_segments = jnp.where(at_home, segment_ids, swap_bit(segment_ids, "dp", 1))
    chunk_at = []
    for member in range(4):
        its_core, its_tensor = core ^ (member & 1), tensor_index ^ (member >> 1)
        chunk_at.append(jnp.where(its_core == (its_tensor >> 1), its_tensor, its_tensor ^ 2))
    segments = jnp.take(
        own_segments.reshape(tensor_count, row_count), jnp.stack(chunk_at), axis=0
    ).reshape(seq_len)
    gather_heads = heads_weight.shape[0] % 16 == 0
    late = reduce_weight.shape[0] % 16 == 0
    heads_low = heads_weight.astype(low)
    if not gather_heads:
        heads_low = gather_head_group(heads_low)
    (
        attended_full,
        attended_own,
        query_aux,
        key_aux,
        value_aux,
        first_full,
        own_tokens,
        full_heads,
        full_expand,
        full_reduce,
        full_merge,
        sequence_grad,
    ) = front_pallas(
        tokens,
        heads_low,
        expand_weight.T.astype(low),
        reduce_weight.astype(low),
        merge_weight.T.astype(low),
        vectors,
        segments,
        out_grad,
        gather_heads,
        late,
    )
    full_heads = full_heads.reshape(D, 3 * group_width) if gather_heads else heads_low
    if not late:
        full_expand, full_reduce = full_expand.reshape(-1, D), full_reduce.reshape(-1, D)
    (
        layer_base,
        layer_across,
        middle_grad,
        attended_grad,
        expand_sum,
        reduce_sum,
        merge_sum,
        vector_sums,
    ) = middle_pallas(
        attended_own, full_merge, own_tokens, vectors, full_expand, full_reduce, sequence_grad, late
    )
    (
        expand_rows,
        reduce_gradient,
        merge_rows,
        heads_gradient,
        input_rows,
        vector_part,
        output_rows,
        wide_gram,
        wide_rows,
    ) = back_pallas(
        attended_full,
        attended_grad,
        query_aux,
        key_aux,
        value_aux,
        first_full,
        full_heads,
        expand_sum,
        reduce_sum,
        merge_sum.reshape(4, data_count, merge_weight.shape[1], group_width),
        layer_base,
        layer_across,
        expand_momentum.T,
        reduce_momentum,
        own_tokens,
        middle_grad,
        vectors,
        vector_sums,
    )
    expand_gradient, merge_gradient = expand_rows.T, merge_rows.T
    expand_new_momentum = momentum_decay * expand_momentum + expand_gradient
    reduce_new_momentum = momentum_decay * reduce_momentum + reduce_gradient
    heads_new_momentum = momentum_decay * heads_momentum + heads_gradient
    merge_new_momentum = momentum_decay * merge_momentum + merge_gradient

    heads_part = heads_new_momentum.reshape(heads_new_momentum.shape[0], head_local * 3, HEAD_DIM)
    merge_part = merge_new_momentum.reshape(head_local, HEAD_DIM, merge_new_momentum.shape[1])
    small_gram = jnp.concatenate(
        [
            jnp.einsum("rmd,rme->mde", heads_part, heads_part, precision=highest),
            jnp.einsum("hdc,hec->hde", merge_part, merge_part, precision=highest),
        ],
        axis=0,
    )
    quarter = small_gram.shape[0] // 4
    small_gram = small_gram.reshape(2, 2, quarter, HEAD_DIM, HEAD_DIM)
    small_gram = jnp.concatenate([small_gram[:, 0], small_gram[:, 1]], axis=3)
    ortho_mine, ortho_other, small_chain, vector_gradient, moved_output, moved_input = last_pallas(
        wide_gram,
        wide_rows,
        small_gram.reshape(2, quarter * HEAD_DIM, 2 * HEAD_DIM),
        vector_part,
        output_rows,
        input_rows.astype(low),
    )
    small_chain = small_chain.reshape(2, quarter, HEAD_DIM, 2, HEAD_DIM)
    small_chain = jnp.transpose(small_chain, (0, 3, 1, 2, 4)).reshape(-1, HEAD_DIM, HEAD_DIM)
    layer_output = jnp.where(at_home, output_rows, moved_output)
    input_gradient = jnp.where(at_home, input_rows, moved_input.astype(jnp.float32))
    vector_new_momentum = momentum_decay * vector_momentum + vector_gradient
    side_count = 3 * head_local
    heads_ortho = jnp.einsum("rmd,mde->rme", heads_part, small_chain[:side_count], precision=highest)
    merge_ortho = jnp.einsum("hde,hec->hdc", small_chain[side_count:], merge_part, precision=highest)

    first_core = core == 0
    expand_ortho = jnp.where(first_core, ortho_mine, ortho_other).T
    reduce_ortho = jnp.where(first_core, ortho_other, ortho_mine)

    keep_factor = 1.0 - muon_rate * weight_decay
    head_step = muon_rate * 0.2 * math.sqrt(max(D, HEAD_DIM))
    wide_step = muon_rate * 0.2 * math.sqrt(max(D, FF))
    heads_new_weight = heads_weight * keep_factor - head_step * heads_ortho.reshape(
        heads_weight.shape
    )
    merge_new_weight = merge_weight * keep_factor - head_step * merge_ortho.reshape(
        merge_weight.shape
    )
    expand_new_weight = expand_weight * keep_factor - wide_step * expand_ortho
    reduce_new_weight = reduce_weight * keep_factor - wide_step * reduce_ortho
    vector_new_value = vectors - vector_rate / math.sqrt(SEQ * data_count) * vector_new_momentum
    heads_new_average = average_decay * heads_average + (1.0 - average_decay) * heads_new_weight
    merge_new_average = average_decay * merge_average + (1.0 - average_decay) * merge_new_weight
    expand_new_average = average_decay * expand_average + (1.0 - average_decay) * expand_new_weight
    reduce_new_average = average_decay * reduce_average + (1.0 - average_decay) * reduce_new_weight
    vector_new_average = average_decay * vector_average + (1.0 - average_decay) * vector_new_value
    return (
        layer_output,
        input_gradient,
        heads_gradient,
        merge_gradient,
        expand_gradient,
        reduce_gradient,
        heads_new_momentum,
        merge_new_momentum,
        expand_new_momentum,
        reduce_new_momentum,
        heads_new_weight,
        merge_new_weight,
        expand_new_weight,
        reduce_new_weight,
        heads_new_average,
        merge_new_average,
        expand_new_average,
        reduce_new_average,
        vector_gradient,
        vector_new_momentum,
        vector_new_value,
        vector_new_average,
    )


def solution(mesh):
    placed = (
        P(("dp", "tensor"), None),
        P("dp"),
        P("dp", None),
        P("dp", "tensor"),
        P("tensor", "dp"),
        P(None, ("tensor", "dp")),
        P(("tensor", "dp"), None),
        P("dp", "tensor"),
        P("tensor", "dp"),
        P(None, ("tensor", "dp")),
        P(("tensor", "dp"), None),
        P("dp", "tensor"),
        P("tensor", "dp"),
        P(None, ("tensor", "dp")),
        P(("tensor", "dp"), None),
        P(),
        P(),
        P(),
    )
    return jax.shard_map(
        per_device,
        mesh=mesh,
        in_specs=placed,
        out_specs=(
            P(("dp", "tensor"), None),
            P(("dp", "tensor"), None),
            P("dp", "tensor"),
            P("tensor", "dp"),
            P(None, ("tensor", "dp")),
            P(("tensor", "dp"), None),
            P("dp", "tensor"),
            P("tensor", "dp"),
            P(None, ("tensor", "dp")),
            P(("tensor", "dp"), None),
            P("dp", "tensor"),
            P("tensor", "dp"),
            P(None, ("tensor", "dp")),
            P(("tensor", "dp"), None),
            P("dp", "tensor"),
            P("tensor", "dp"),
            P(None, ("tensor", "dp")),
            P(("tensor", "dp"), None),
            P(),
            P(),
            P(),
            P(),
        ),
        check_vma=False,
    )
```

```python
import functools
import math

import jax
import jax.numpy as jnp
from jax import lax
from jax.experimental import pallas as pl
from jax.experimental.pallas import tpu as pltpu
from jax.sharding import PartitionSpec as P

D = 768
HEAD_DIM = 64
FF = 3072
SEQ = 2048
NEWTON_STEPS = 5


highest = lax.Precision.HIGHEST
norm_epsilon = 1e-06
newton_epsilon = 1e-07
newton_linear = 3.4445
newton_cubic = -4.775
newton_quintic = 2.0315
momentum_decay = 0.5
average_decay = 0.9
muon_rate = 0.2
weight_decay = 0.1
vector_rate = 0.15
masked_score = -1e30
VMEM_LIMIT = 56 * 2**20


def center_scale(values):
    average = jnp.mean(values, axis=-1, keepdims=True)
    centered = values - average
    inverse = lax.rsqrt(jnp.mean(centered * centered, axis=-1, keepdims=True) + norm_epsilon)
    return (centered * inverse, inverse)


def norm_backward(upstream, normed, inverse, gain):
    scaled = upstream * gain
    mean_one = jnp.mean(scaled, axis=-1, keepdims=True)
    mean_two = jnp.mean(scaled * normed, axis=-1, keepdims=True)
    return inverse * (scaled - mean_one - normed * mean_two)


def gelu_exact(values):
    return jax.nn.gelu(values, approximate=False)


def contract_rows(left_side, right_side):
    return lax.dot_general(
        left_side, right_side, (((0,), (0,)), ((), ())), preferred_element_type=jnp.float32
    )


def contract_cols(left_side, right_side):
    return lax.dot_general(
        left_side, right_side, (((1,), (1,)), ((), ())), preferred_element_type=jnp.float32
    )


KEY_BLOCK = 256
AUX = 128


MESH = pl.DeviceIdType.MESH


def low_rank_bits(data_count):
    return [1 << k for k in range(1, data_count.bit_length() - 1)]


class Wires:
    def __init__(self, send, receive):
        self.send, self.receive, self.used = send, receive, 0

    def number(self):
        self.used += 1
        return self.used - 1

    def start(self, k, source, target, device):
        copy = pltpu.make_async_remote_copy(
            source, target, self.send.at[k], self.receive.at[k], device_id=device, device_id_type=MESH
        )
        copy.start()

    def sent(self, k, source, device):
        pltpu.make_async_remote_copy(
            source, source, self.send.at[k], self.receive.at[k], device_id=device, device_id_type=MESH
        ).wait_send()

    def arrived(self, k, target, device):
        pltpu.make_async_remote_copy(
            target, target, self.send.at[k], self.receive.at[k], device_id=device, device_id_type=MESH
        ).wait_recv()


def greet(devices):
    barrier = pltpu.get_barrier_semaphore()
    for device in devices:
        pl.semaphore_signal(barrier, inc=1, device_id=device, device_id_type=MESH)
    pl.semaphore_wait(barrier, len(devices))


def column_and_plane(data, tensor, data_count, tensor_count):
    found = []
    for core in (0, 1):
        for step in range(tensor_count):
            if core or step:
                found.append((data ^ core, lax.rem(tensor + step, tensor_count)))
    for k in range(1, data_count // 2):
        found.append((data ^ (2 * k), tensor))
    return found


def front_kernel(
    data_count,
    tensor_count,
    gather_heads,
    late,
    tokens,
    heads_wide,
    expand_wide,
    reduce_wide,
    merge_wide,
    vectors,
    segment_column,
    out_grad,
    attended,
    attended_rows,
    query_aux,
    key_aux,
    value_aux,
    first_full,
    own_tokens,
    all_heads,
    all_expand,
    all_reduce,
    merge_full,
    sequence_grad,
    all_merge,
    chunks,
    arrivals,
    heads,
    expand,
    reduce,
    merge,
    send,
    receive,
    local,
):
    low = jnp.bfloat16
    rows, width = tokens.shape
    head_local = query_aux.shape[0]
    group_width = head_local * HEAD_DIM
    data, tensor = lax.axis_index("dp"), lax.axis_index("tensor")
    core, half = data & 1, tensor >> 1
    home = core == half
    group = 2 * (tensor & 1) + core
    wires = Wires(send, receive)
    beside, across, diagonal = (data ^ 1, tensor), (data, tensor ^ 1), (data ^ 1, tensor ^ 1)
    members = [None, beside, across, diagonal]
    away = (data ^ 1, tensor ^ 2)
    pieces = [pl.ds(p * (rows // 4), rows // 4) for p in range(4)]
    pending = []

    def begin(k, source, target, device, when=None):
        if when is None:
            wires.start(k, source, target, device)
        else:

            @pl.when(when)
            def _():
                wires.start(k, source, target, device)

        pending.append((k, source, device, when))

    def await_arrival(k, target, device, when=None):
        if when is None:
            wires.arrived(k, target, device)
        else:

            @pl.when(when)
            def _():
                wires.arrived(k, target, device)

    if gather_heads:
        heads[...] = heads_wide[...].astype(low)
    merge[...] = merge_wide[...].T.astype(low)
    all_merge[data, tensor] = merge[...]
    greet(column_and_plane(data, tensor, data_count, tensor_count))

    pair = (data >> 1) * 2

    def group_send(block, whole):
        numbers = [wires.number() for _ in range(4)]
        for k in (0, 1):
            target = (pair + (tensor & 1), (tensor >> 1) + 2 * k)
            itself = (target[0] == data) & (target[1] == tensor)
            for c in (0, 1):
                begin(
                    numbers[2 * k + c],
                    block,
                    whole.at[data],
                    target,
                    jnp.logical_not(itself) & (core == c),
                )

            @pl.when(itself)
            def _():
                copy = pltpu.make_async_copy(block, whole.at[data], local.at[1])
                copy.start()
                copy.wait()

        return numbers

    def group_wait(numbers, whole):
        for k in (0, 1):
            for c in (0, 1):
                source = (pair + c, group)
                itself = (source[0] == data) & (source[1] == tensor)
                await_arrival(
                    numbers[2 * k + c],
                    whole.at[pair + c],
                    source,
                    jnp.logical_not(itself) & (half == k),
                )

    if gather_heads:
        head_numbers = group_send(heads, all_heads)
    merge_numbers = [wires.number() for _ in range(tensor_count - 1)]
    for k in range(1, tensor_count):
        peer = (data, lax.rem(tensor + k, tensor_count))
        begin(merge_numbers[k - 1], merge, all_merge.at[data, tensor], peer)
    numbers = [wires.number() for _ in range(24)]
    for p, piece in enumerate(pieces):
        begin(numbers[p], tokens.at[piece], chunks.at[2, piece], across, home)
        begin(numbers[4 + p], tokens.at[piece], chunks.at[0, piece], away, jnp.logical_not(home))
        begin(numbers[8 + p], tokens.at[piece], chunks.at[1, piece], beside, home)

    @pl.when(home)
    def _():
        chunks[0] = tokens[...]

    if gather_heads:
        group_wait(head_numbers, all_heads)
        plane = []
        for k in range(1, data_count // 2):
            number = wires.number()
            plane.append((number, k))
            begin(number, all_heads.at[pl.ds(pair, 2)], all_heads.at[pl.ds(pair, 2)], (data ^ (2 * k), tensor))

    def bit_step(plan):
        made = []
        for mat, bit, held, wide in plan:
            for offset in held:
                number = wires.number()
                place = (pair if wide else data) ^ offset
                there = pl.ds(place ^ bit, 2) if wide else place ^ bit
                place = pl.ds(place, 2) if wide else place
                begin(number, mat.at[place], mat.at[place], (data ^ bit, tensor))
                made.append((number, mat, there, bit))
        return made

    def bit_wait(made):
        for number, mat, there, bit in made:
            await_arrival(number, mat.at[there], (data ^ bit, tensor))


    bits = low_rank_bits(data_count)
    schedule = []
    held = [[0], [0], [0]]
    for k in range(len(bits)):
        plan = []
        for m, mat in enumerate((all_expand, all_reduce, all_merge)):
            bit = bits[-1 - k] if m == 1 else bits[k]
            plan.append((mat, bit, list(held[m]), m < 2))
            held[m] = held[m] + [offset ^ bit for offset in held[m]]
        schedule.append(plan)
    schedule.append([(all_merge, 1, list(held[2]), False)])

    for p, piece in enumerate(pieces):
        await_arrival(numbers[4 + p], chunks.at[0, piece], away, jnp.logical_not(home))
        begin(numbers[12 + p], chunks.at[0, piece], chunks.at[2, piece], across, jnp.logical_not(home))
        begin(numbers[16 + p], chunks.at[0, piece], chunks.at[1, piece], beside, jnp.logical_not(home))


    if gather_heads:
        for number, k in plane:
            there = pl.ds(pair ^ (2 * k), 2)
            await_arrival(number, all_heads.at[there], (data ^ (2 * k), tensor))

    block = min(KEY_BLOCK, rows)
    lane = lax.broadcasted_iota(jnp.int32, (block, AUX), 1)
    blank = jnp.zeros((block, AUX - HEAD_DIM), jnp.float32)
    steps = rows // block

    def prepare(member):
        def one(step, carry):
            inside = pl.ds(pl.multiple_of(step * block, block), block)
            at_rows = pl.ds(pl.multiple_of(member * rows + step * block, block), block)
            normed, _ = center_scale(chunks[member, inside, :].astype(jnp.float32))
            first_in = (normed * vectors[0:1, :] + vectors[1:2, :]).astype(low)
            first_full[at_rows, :] = first_in
            weight = all_heads[...].reshape(width, 3 * group_width)
            projected = jnp.dot(first_in, weight, preferred_element_type=jnp.float32)
            projected = projected.astype(low).astype(jnp.float32)
            same = lane - HEAD_DIM == segment_column[at_rows, :]
            segment_lane = (lane >= HEAD_DIM) & (lane < HEAD_DIM + 3)
            query_extra = jnp.where(same & segment_lane, 1.0, 0.0)
            key_extra = jnp.where(
                segment_lane,
                jnp.where(same, 0.0, masked_score),
                jnp.where((lane >= HEAD_DIM + 3) & (lane < HEAD_DIM + 6), -1.0, 0.0),
            )
            value_extra = jnp.where(
                lane == HEAD_DIM,
                1.0,
                jnp.where((lane == HEAD_DIM + 1) | (lane == HEAD_DIM + 2), -1.0, 0.0),
            )
            for head in range(head_local):
                for which, (ref, extra, factor) in enumerate(
                    (
                        (query_aux, query_extra, HEAD_DIM**-0.5),
                        (key_aux, key_extra, 1.0),
                        (value_aux, value_extra, 1.0),
                    )
                ):
                    at = (3 * head + which) * HEAD_DIM
                    part = jnp.concatenate([projected[:, at : at + HEAD_DIM] * factor, blank], axis=1)
                    ref[head, at_rows, :] = jnp.where(lane < HEAD_DIM, part, extra).astype(low)
            return carry

        lax.fori_loop(0, steps, one, 0)

    def attend(member, steps_here):
        def one(step, carry):
            inside = pl.ds(pl.multiple_of(step * block, block), block)
            at_rows = pl.ds(pl.multiple_of(member * rows + step * block, block), block)
            done = []
            for head in range(head_local):
                query = query_aux[head, at_rows, :]
                scores = contract_cols(query, key_aux[head])
                row_max = jnp.max(scores, axis=1, keepdims=True)
                exponent = jnp.exp(scores - row_max).astype(low)
                output = jnp.dot(exponent, value_aux[head], preferred_element_type=jnp.float32)
                totals = output[:, HEAD_DIM : HEAD_DIM + 1]
                done.append(output[:, :HEAD_DIM] / totals)
                logsum = row_max + jnp.log(totals)
                first = logsum.astype(low).astype(jnp.float32)
                second = (logsum - first).astype(low).astype(jnp.float32)
                third = logsum - first - second
                wide = query.astype(jnp.float32)
                wide = jnp.where(lane == HEAD_DIM + 3, first, wide)
                wide = jnp.where(lane == HEAD_DIM + 4, second, wide)
                wide = jnp.where(lane == HEAD_DIM + 5, third, wide)
                query_aux[head, at_rows, :] = wide.astype(low)
            attended[member, inside, :] = jnp.concatenate(done, axis=1).astype(low)
            return carry

        lax.fori_loop(*steps_here, one, 0)

    for k in range(1, tensor_count):
        origin = lax.rem(tensor + tensor_count - k, tensor_count)
        await_arrival(merge_numbers[k - 1], all_merge.at[data, origin], (data, origin))
    merge_made = bit_step(schedule[0][2:])
    expand[...] = expand_wide[...].astype(low)
    reduce[...] = reduce_wide[...].astype(low)
    prepare(0)
    for p, piece in enumerate(pieces):
        await_arrival(numbers[p], chunks.at[2, piece], across, home)
        await_arrival(numbers[12 + p], chunks.at[2, piece], across, jnp.logical_not(home))
        begin(numbers[20 + p], chunks.at[2, piece], chunks.at[3, piece], beside)

    grad_numbers = [wires.number() for _ in range(4)]
    grad_copies = []
    for member in range(4):
        its_core, its_tensor = core ^ (member & 1), tensor ^ (member >> 1)
        chunk = its_tensor ^ (2 * (its_core ^ (its_tensor >> 1)))
        source = out_grad.at[pl.ds(pl.multiple_of(chunk * rows, rows), rows)]
        copy = pltpu.make_async_copy(source, sequence_grad.at[member], local.at[2 + member])
        grad_copies.append(copy)
        pl.when(home)(copy.start)
        begin(grad_numbers[member], source, sequence_grad.at[member ^ 1], beside, home)
    for p, piece in enumerate(pieces):
        await_arrival(numbers[8 + p], chunks.at[1, piece], beside, jnp.logical_not(home))
        await_arrival(numbers[16 + p], chunks.at[1, piece], beside, home)
    expand_numbers = group_send(expand, all_expand)
    reduce_numbers = group_send(reduce, all_reduce)
    for plan in schedule[1:-1]:
        bit_wait(merge_made)
        merge_made = bit_step(plan[2:])
    prepare(1)
    prepare(2)
    for p, piece in enumerate(pieces):
        await_arrival(numbers[20 + p], chunks.at[3, piece], beside)
    prepare(3)
    exchange = {}
    for member in (3, 2, 1, 0):
        attend(member, (0, steps // 2))
        if member == 2:
            group_wait(expand_numbers, all_expand)
            group_wait(reduce_numbers, all_reduce)
            made = bit_step(schedule[0][:2])
        attend(member, (steps // 2, steps))
        if member:
            number = wires.number()
            begin(number, attended.at[member], arrivals.at[group], members[member])
            exchange[member] = number
        else:
            arrivals[group] = attended[0]
        if member == 1:
            bit_wait(merge_made)
            merge_made = bit_step(schedule[-1])
    for plan in schedule[1 : -2 if late else -1]:
        bit_wait(made)
        made = bit_step(plan[:2])
    bit_wait(merge_made)
    strips = []
    for k in range(tensor_count):
        strip = all_merge[:, k].astype(jnp.float32)
        strips.append(strip.reshape(width, group_width))
    merge_full[...] = jnp.concatenate(strips, axis=1).astype(low)
    own_tokens[...] = chunks[0]
    for member, number in exchange.items():
        await_arrival(number, arrivals.at[group ^ member], members[member])
    attended_rows[...] = jnp.concatenate([arrivals[k] for k in range(4)], axis=1)
    bit_wait(made)
    for member in range(4):
        pl.when(home)(grad_copies[member].wait)
        await_arrival(
            grad_numbers[member], sequence_grad.at[member ^ 1], beside, jnp.logical_not(home)
        )
    for k, source, device, when in pending:
        if when is None:
            wires.sent(k, source, device)
        else:

            @pl.when(when)
            def _():
                wires.sent(k, source, device)


def front_pallas(tokens, heads, expand, reduce, merge, vectors, segments, out_grad, gather_heads, late):
    data_count, tensor_count = lax.axis_size("dp"), lax.axis_size("tensor")
    rows, width = tokens.shape
    low = jnp.bfloat16
    head_columns = heads.shape[-1]
    head_local = head_columns // (3 * HEAD_DIM)
    seq_len = segments.shape[0]
    group_width = head_local * HEAD_DIM
    aux = jax.ShapeDtypeStruct((head_local, seq_len, AUX), low)
    inside = pl.BlockSpec(memory_space=pltpu.VMEM)
    anywhere = pl.BlockSpec(memory_space=pl.ANY)
    gathered = [
        jax.ShapeDtypeStruct((data_count,) + reduce.shape, low),
        jax.ShapeDtypeStruct((data_count,) + reduce.shape, low),
        jax.ShapeDtypeStruct((width, width), low),
        jax.ShapeDtypeStruct((4, rows, width), low),
    ]
    hops = 2 * (tensor_count - 1) + 2 * (data_count // 2 - 1) + data_count - 1
    copies = 12 + data_count // 2 + 24 + hops + 4 + 3
    if gather_heads:
        heads_out = jax.ShapeDtypeStruct((data_count,) + heads.shape, low)
    else:
        heads_out = jax.ShapeDtypeStruct(heads.shape, low)

    def kernel(*refs):
        if not gather_heads:
            refs = list(refs)
            refs[15] = refs[1]
        front_kernel(data_count, tensor_count, gather_heads, late, *refs)

    return pl.pallas_call(
        kernel,
        out_shape=(
            jax.ShapeDtypeStruct((4, rows, group_width), low),
            jax.ShapeDtypeStruct((rows, 4 * group_width), low),
            aux,
            aux,
            aux,
            jax.ShapeDtypeStruct((seq_len, width), low),
            jax.ShapeDtypeStruct((rows, width), low),
            heads_out,
            *gathered,
        ),
        in_specs=[inside] * 7 + [anywhere],
        out_specs=(inside,) * 8 + (anywhere,) * 2 + (inside,) * 2,
        scratch_shapes=[
            pltpu.VMEM((data_count, tensor_count) + merge.shape[::-1], low),
            pltpu.VMEM((4, rows, width), low),
            pltpu.VMEM((4, rows, group_width), low),
            pltpu.VMEM(heads.shape, low),
            pltpu.VMEM(reduce.shape, low),
            pltpu.VMEM(reduce.shape, low),
            pltpu.VMEM(merge.shape[::-1], low),
            pltpu.SemaphoreType.DMA((copies,)),
            pltpu.SemaphoreType.DMA((copies,)),
            pltpu.SemaphoreType.DMA((6,)),
        ],
        compiler_params=pltpu.CompilerParams(
            vmem_limit_bytes=VMEM_LIMIT, collective_id=1, has_side_effects=True
        ),
        cost_estimate=pl.CostEstimate(
            flops=4 * head_local * seq_len * seq_len * AUX,
            bytes_accessed=8 * seq_len * width,
            transcendentals=head_local * seq_len * seq_len,
        ),
        name="front",
    )(tokens, heads, expand, reduce, merge, vectors, segments.reshape(seq_len, 1), out_grad)


def dot_rows(left_side, right_side):
    return jnp.dot(left_side, right_side, preferred_element_type=jnp.float32)


def middle_kernel(
    data_count,
    late,
    attended_rows,
    merge,
    tokens,
    vectors,
    expand_in,
    reduce_in,
    sequence_grad,
    layer_base,
    layer_across,
    middle_grad,
    attended_grad,
    expand_sum,
    reduce_sum,
    merge_sum,
    vector_sums,
    second_in,
    middle,
    hidden,
    expand_grad,
    partial,
    reduced,
    from_beside,
    reduced_beside,
    from_across,
    expand_got,
    reduce_got,
    expand_full,
    reduce_full,
    send,
    receive,
    local,
):
    low = jnp.bfloat16
    rows, width = tokens.shape
    group_width = width // 4
    data, tensor = lax.axis_index("dp"), lax.axis_index("tensor")
    wires = Wires(send, receive)
    beside, across = (data ^ 1, tensor), (data, tensor ^ 1)
    part = rows // 2
    pieces = [pl.ds(p * part, part) for p in range(2)]
    pending = []

    def begin(k, source, target, device):
        wires.start(k, source, target, device)
        pending.append((k, source, device))

    bits = low_rank_bits(data_count)
    greet([beside, across] + [(data ^ bit, tensor) for bit in sorted({bits[0], bits[-1]})])
    groups = [
        Group(work, got, None, order, (data, tensor), wires, begin)
        for work, got, order in (
            (expand_sum, expand_got, bits[::-1]),
            (reduce_sum, reduce_got, bits),
        )
    ]
    pair = (data >> 1) * 2
    if late:
        made, copies = [], []
        for m, (source, full, bit) in enumerate(
            ((expand_in, expand_full, bits[-1]), (reduce_in, reduce_full, bits[0]))
        ):
            for offset in [o for o in range(0, data_count, 2) if not o & bit]:
                here = pl.ds(pair ^ offset, 2)
                number = wires.number()
                begin(number, source.at[here], full.at[here], (data ^ bit, tensor))
                made.append((number, full.at[pl.ds(pair ^ offset ^ bit, 2)], (data ^ bit, tensor)))
                copies.append(
                    pltpu.make_async_copy(source.at[here], full.at[here], local.at[len(copies)])
                )
                copies[-1].start()
    units = data_count * expand_full.shape[1]

    def expand():
        return expand_full[...].reshape(units, width) if late else expand_in[...]

    def reduce():
        return reduce_full[...].reshape(units, width) if late else reduce_in[...]

    numbers = [[wires.number() for _ in range(2)] for _ in range(3)]
    for p, piece in enumerate(pieces):
        merged = contract_cols(attended_rows[piece, :], merge[...])
        here = tokens[piece, :].astype(jnp.float32) + merged + vectors[4:5, :]
        middle[piece, :] = here
        normed, _ = center_scale(here)
        second_in[0, piece, :] = (normed * vectors[2:3, :] + vectors[3:4, :]).astype(low)
        begin(numbers[0][p], second_in.at[0, piece], second_in.at[2, piece], across)
        begin(numbers[1][p], second_in.at[0, piece], second_in.at[1, piece], beside)

    def unit(member, p):
        piece = pieces[p]
        expanded = contract_cols(second_in[member, piece, :], expand())
        cdf = 0.5 + 0.5 * lax.erf(expanded * math.sqrt(0.5))
        activated = (expanded * cdf).astype(low)
        hidden[member, piece, :] = activated
        reduced[member, piece, :] = dot_rows(activated, reduce()).astype(low)
        slope = cdf + expanded * (jnp.exp(-0.5 * expanded * expanded) * (1.0 / math.sqrt(2.0 * math.pi)))
        upstream = contract_cols(sequence_grad[member, piece, :], reduce())
        grad = (upstream * slope).astype(low)
        expand_grad[member, piece, :] = grad
        partial[member, piece, :] = dot_rows(grad, expand()).astype(low)

    if late:
        for copy in copies:
            copy.wait()
        for number, there, device in made:
            wires.arrived(number, there, device)
    unit(0, 0)
    unit(0, 1)
    back = [[wires.number() for _ in range(2)] for _ in range(5)]
    for p, piece in enumerate(pieces):
        wires.arrived(numbers[1][p], second_in.at[1, piece], beside)
        unit(1, p)
        begin(back[0][p], partial.at[1, piece], from_beside.at[0, piece], beside)
        begin(back[3][p], reduced.at[1, piece], reduced_beside.at[0, piece], beside)
    for p, piece in enumerate(pieces):
        wires.arrived(numbers[0][p], second_in.at[2, piece], across)
        begin(numbers[2][p], second_in.at[2, piece], second_in.at[3, piece], beside)
    for p, piece in enumerate(pieces):
        wires.arrived(numbers[2][p], second_in.at[3, piece], beside)
        unit(3, p)
        begin(back[1][p], partial.at[3, piece], from_beside.at[1, piece], beside)
        begin(back[4][p], reduced.at[3, piece], reduced_beside.at[1, piece], beside)
        unit(2, p)
        wires.arrived(back[1][p], from_beside.at[1, piece], beside)
        both = partial[2, piece, :].astype(jnp.float32) + from_beside[1, piece, :].astype(jnp.float32)
        partial[2, piece, :] = both.astype(low)
        begin(back[2][p], partial.at[2, piece], from_across.at[piece], across)

    def sum_rows(target, left, right):
        total = None
        for member in range(4):
            term = contract_rows(left[member], right[member])
            total = term if total is None else total + term
        target[...] = total.reshape(target.shape).astype(low)

    sum_rows(reduce_sum, hidden, sequence_grad)
    groups[1].bit_send()
    sum_rows(expand_sum, expand_grad, second_in)
    groups[0].bit_send()
    for p, piece in enumerate(pieces):
        wires.arrived(back[3][p], reduced_beside.at[0, piece], beside)
        wires.arrived(back[4][p], reduced_beside.at[1, piece], beside)
        base = reduced[0, piece, :].astype(jnp.float32) + reduced_beside[0, piece, :].astype(jnp.float32)
        layer_base[piece, :] = base + middle[piece, :] + vectors[5:6, :]
        layer_across[piece, :] = (
            reduced[2, piece, :].astype(jnp.float32)
            + reduced_beside[1, piece, :].astype(jnp.float32)
        ).astype(low)
    sums = [0.0] * 4
    for p, piece in enumerate(pieces):
        wires.arrived(back[0][p], from_beside.at[0, piece], beside)
        wires.arrived(back[2][p], from_across.at[piece], across)
        second_grad = (
            partial[0, piece, :].astype(jnp.float32)
            + from_beside[0, piece, :].astype(jnp.float32)
            + from_across[piece, :].astype(jnp.float32)
        )
        normed, inverse = center_scale(middle[piece, :])
        own = sequence_grad[0, piece, :].astype(jnp.float32)
        total = own + norm_backward(second_grad, normed, inverse, vectors[2:3, :])
        middle_grad[piece, :] = total
        for k, term in enumerate((second_grad * normed, second_grad, total, own)):
            sums[k] = sums[k] + jnp.sum(term, axis=0, keepdims=True)
        into_attended = dot_rows(total.astype(low), merge[...]).astype(low)
        for k in range(4):
            attended_grad[k, piece, :] = into_attended[:, k * group_width : (k + 1) * group_width]
    vector_sums[...] = jnp.concatenate(sums, axis=0)
    into_merge = contract_rows(middle_grad[...].astype(low), attended_rows[...]).astype(low)
    for k in range(4):
        merge_sum[k] = into_merge[:, k * group_width : (k + 1) * group_width]
    for which in groups:
        which.bit_add()
    for k, source, device in pending:
        wires.sent(k, source, device)


def middle_pallas(attended_rows, merge, tokens, vectors, expand, reduce, sequence_grad, late):
    rows, width = tokens.shape
    units = expand.shape[0] * (expand.shape[1] if late else 1)
    data_count = lax.axis_size("dp")
    unit_block = (units // data_count, width)
    first_slots = data_count // 4
    low, wide = jnp.bfloat16, jnp.float32
    inside = pl.BlockSpec(memory_space=pltpu.VMEM)
    shapes = (
        ((rows, width), wide),
        ((rows, width), low),
        ((rows, width), wide),
        ((4, rows, width // 4), low),
        ((data_count,) + unit_block, low),
        ((data_count,) + unit_block, low),
        ((4, width, width // 4), low),
        ((4, width), wide),
    )
    copies = 16 + 4 * first_slots
    return pl.pallas_call(
        functools.partial(middle_kernel, data_count, late),
        out_shape=tuple(jax.ShapeDtypeStruct(*shape) for shape in shapes),
        in_specs=[inside] * 4 + [pl.BlockSpec(memory_space=pl.ANY) if late else inside] * 2 + [inside],
        out_specs=(inside,) * 8,
        scratch_shapes=[
            pltpu.VMEM((4, rows, width), low),
            pltpu.VMEM((rows, width), wide),
            pltpu.VMEM((4, rows, units), low),
            pltpu.VMEM((4, rows, units), low),
            pltpu.VMEM((4, rows, width), low),
            pltpu.VMEM((4, rows, width), low),
            pltpu.VMEM((2, rows, width), low),
            pltpu.VMEM((2, rows, width), low),
            pltpu.VMEM((rows, width), low),
            pltpu.VMEM((first_slots, 2) + unit_block, low),
            pltpu.VMEM((first_slots, 2) + unit_block, low),
            pltpu.VMEM((data_count,) + unit_block, low),
            pltpu.VMEM((data_count,) + unit_block, low),
            pltpu.SemaphoreType.DMA((copies,)),
            pltpu.SemaphoreType.DMA((copies,)),
            pltpu.SemaphoreType.DMA((2 * first_slots,)),
        ],
        compiler_params=pltpu.CompilerParams(
            vmem_limit_bytes=VMEM_LIMIT, collective_id=2, has_side_effects=True
        ),
        cost_estimate=pl.CostEstimate(
            flops=52 * rows * width * units, bytes_accessed=20 * rows * width, transcendentals=rows * units * 8
        ),
        name="middle",
    )(attended_rows, merge, tokens, vectors, expand, reduce, sequence_grad)


class Group:
    def __init__(self, work, arrived, last, order, place, wires, begin, first=0):
        self.work, self.got, self.last, self.order = work, arrived, last, order
        self.data, self.tensor = place
        self.pair = (self.data >> 1) * 2
        self.core, self.half = self.data & 1, self.tensor >> 1
        self.wires, self.begin = wires, begin
        self.left = [
            o for o in range(0, work.shape[0], 2) if not any(o & bit for bit in order[:first])
        ]
        self.slot, self.flight, self.step = 0, [], first

    def bit_send(self):
        bit = self.order[self.step]
        self.flight = []
        for offset in [o for o in self.left if o & bit]:
            number = self.wires.number()
            target = (self.data ^ bit, self.tensor)
            self.begin(number, self.work.at[pl.ds(self.pair ^ offset, 2)], self.got.at[self.slot], target)
            self.flight.append((number, self.slot, offset ^ bit, target))
            self.slot += 1
        self.left = [o for o in self.left if not o & bit]
        self.step += 1

    def bit_add(self):
        for number, slot, offset, target in self.flight:
            self.wires.arrived(number, self.got.at[slot], target)
            here = pl.ds(self.pair ^ offset, 2)
            total = self.work[here].astype(jnp.float32) + self.got[slot].astype(jnp.float32)
            self.work[here] = total.astype(self.work.dtype)

    def own_send(self):
        group = 2 * (self.tensor & 1) + self.core
        self.numbers = [self.wires.number() for _ in range(4)]
        for c in (0, 1):
            owner = (self.pair + c, group)
            itself = (owner[0] == self.data) & (owner[1] == self.tensor)
            for b in (0, 1):
                self.begin(
                    self.numbers[2 * c + b],
                    self.work.at[self.pair + c],
                    self.last.at[b],
                    owner,
                    jnp.logical_not(itself) & (self.half == b),
                )

    def own_sum(self):
        for b in (0, 1):
            source = (self.pair + (self.tensor & 1), (self.tensor >> 1) + 2 * b)
            itself = (source[0] == self.data) & (source[1] == self.tensor)
            for c in (0, 1):

                @pl.when(jnp.logical_not(itself) & (self.core == c))
                def _():
                    self.wires.arrived(self.numbers[2 * c + b], self.last.at[b], source)

            @pl.when(itself)
            def _():
                self.last[b] = self.work[self.data]

        return self.last[0].astype(jnp.float32) + self.last[1].astype(jnp.float32)


class ChipSum:
    def __init__(
        self, array, result, arrived, last, base, size, order, place, tensor_count, wires, begin
    ):
        self.array, self.result, self.got, self.last = array, result, arrived, last
        self.start, self.size, self.order = base, size, order
        self.data, self.tensor = place
        self.count, self.wires, self.begin = tensor_count, wires, begin
        self.slot, self.step, self.trail = 0, 0, []

    def bit_send(self):
        bit = self.order[self.step]
        self.step += 1
        half = self.size // 2
        mine = (self.data & bit) // bit
        keep, give = self.start + mine * half, self.start + (1 - mine) * half
        number = self.wires.number()
        target = (self.data ^ bit, self.tensor)
        there = self.got.at[pl.ds(self.slot, half)]
        self.begin(number, self.array.at[pl.ds(give, half)], there, target)
        self.trail.append((bit, keep, give, half))
        self.flight = (number, self.slot, half, target)
        self.start, self.size = keep, half
        self.slot += half

    def bit_add(self):
        number, slot, half, target = self.flight
        self.wires.arrived(number, self.got.at[pl.ds(slot, half)], target)
        here = pl.ds(self.start, half)
        self.array[here] = self.array[here] + self.got[pl.ds(slot, half)]

    def line_send(self):
        self.spread = self.size % self.count == 0
        self.portion = self.size // self.count if self.spread else self.size
        self.flight = []
        for k in range(1, self.count):
            number = self.wires.number()
            peer = lax.rem(self.tensor + k, self.count)
            at = self.start + peer * self.portion if self.spread else self.start
            source = self.array.at[pl.ds(at, self.portion)]
            self.begin(number, source, self.last.at[k - 1], (self.data, peer))
            origin = lax.rem(self.tensor + self.count - k, self.count)
            self.flight.append((number, k - 1, (self.data, origin)))

    def line_add(self):
        at = self.start + self.tensor * self.portion if self.spread else self.start
        here = pl.ds(at, self.portion)
        for number, slot, origin in self.flight:
            self.wires.arrived(number, self.last.at[slot], origin)
        total = self.array[here]
        for number, slot, origin in self.flight:
            total = total + self.last[slot]
        self.result[here] = total

    def line_back(self):
        self.flight = []
        if self.spread:
            here = pl.ds(self.start + self.tensor * self.portion, self.portion)
            for k in range(1, self.count):
                number = self.wires.number()
                peer = lax.rem(self.tensor + k, self.count)
                self.begin(number, self.result.at[here], self.result.at[here], (self.data, peer))
                origin = lax.rem(self.tensor + self.count - k, self.count)
                there = pl.ds(self.start + origin * self.portion, self.portion)
                self.flight.append((number, there, (self.data, origin)))

    def bit_back(self):
        bit, keep, give, half = self.trail.pop()
        number = self.wires.number()
        target = (self.data ^ bit, self.tensor)
        here = pl.ds(keep, half)
        self.begin(number, self.result.at[here], self.result.at[here], target)
        self.flight = [(number, pl.ds(give, half), target)]
        self.start = jnp.minimum(keep, give)
        self.size = 2 * half

    def back_wait(self):
        for number, there, target in self.flight:
            self.wires.arrived(number, self.result.at[there], target)


def split_low(values):
    high = values.astype(jnp.bfloat16)
    return high, (values - high.astype(jnp.float32)).astype(jnp.bfloat16)


def back_kernel(
    data_count,
    tensor_count,
    attended,
    attended_grad,
    query_aux,
    key_aux,
    value_aux,
    first_full,
    heads_weight,
    expand_sum,
    reduce_sum,
    merge_sum,
    layer_base,
    layer_across,
    expand_momentum,
    reduce_momentum,
    tokens,
    middle_grad,
    vectors,
    vector_sums,
    heads_momentum,
    merge_momentum,
    expand_out,
    reduce_out,
    merge_out,
    heads_out,
    input_rows,
    input_low,
    vector_part,
    output_rows,
    gram,
    both,
    small_gram,
    upstream,
    grad_aux,
    key_turned,
    query_total,
    projected_grad,
    first_parts,
    first_beside,
    first_across,
    layer_got,
    expand_work,
    expand_got,
    expand_last,
    reduce_work,
    reduce_got,
    reduce_last,
    merge_work,
    merge_core,
    merge_line,
    merge_got,
    merge_last,
    heads_work,
    heads_got,
    heads_last,
    side,
    side_got,
    gram_work,
    gram_got,
    gram_last,
    send,
    receive,
    local,
):
    low = jnp.bfloat16
    members, rows, group_width = attended.shape
    head_local = group_width // HEAD_DIM
    seq_len = members * rows
    data, tensor = lax.axis_index("dp"), lax.axis_index("tensor")
    place = (data, tensor)
    core = data & 1
    group = 2 * (tensor & 1) + core
    wires = Wires(send, receive)
    beside, across, diagonal = (data ^ 1, tensor), (data, tensor ^ 1), (data ^ 1, tensor ^ 1)
    peers = [None, beside, across, diagonal]
    pending = []

    def begin(k, source, target, device, when=None):
        if when is None:
            wires.start(k, source, target, device)
        else:

            @pl.when(when)
            def _():
                wires.start(k, source, target, device)

        pending.append((k, source, device, when))

    def finish_sends():
        for k, source, device, when in pending:
            if when is None:
                wires.sent(k, source, device)
            else:

                @pl.when(when)
                def _():
                    wires.sent(k, source, device)

        pending.clear()

    copies = []
    for k, (source, target) in enumerate(
        ((expand_sum, expand_work), (reduce_sum, reduce_work), (merge_sum, merge_work))
    ):
        copies.append(pltpu.make_async_copy(source, target, local.at[k]))
        copies[-1].start()
    greet(column_and_plane(data, tensor, data_count, tensor_count))

    grad_numbers = {}
    for member in (2, 3, 1):
        grad_numbers[member] = wires.number()
        begin(
            grad_numbers[member],
            attended_grad.at[group ^ member],
            upstream.at[member],
            peers[member],
        )
    for copy in copies:
        copy.wait()
    bits = low_rank_bits(data_count)
    own_merge = merge_work.at[group]
    expand_group = Group(expand_work, expand_got, expand_last, bits[::-1], place, wires, begin, 1)
    reduce_group = Group(reduce_work, reduce_got, reduce_last, bits, place, wires, begin, 1)
    merge_group = Group(own_merge, merge_got, merge_last, bits[::-1], place, wires, begin)
    heads_group = Group(heads_work, heads_got, heads_last, bits, place, wires, begin)
    merge_numbers = [wires.number() for _ in range(3)]
    begin(merge_numbers[0], merge_work.at[group ^ 1], merge_core.at[0], beside)
    begin(merge_numbers[1], merge_work.at[group ^ 3], merge_core.at[1], beside)
    if len(bits) > 1:
        expand_group.bit_send()
        reduce_group.bit_send()
    layer_number = wires.number()
    upstream[0] = attended_grad[group]

    block = min(KEY_BLOCK, rows)
    lane = lax.broadcasted_iota(jnp.int32, (block, AUX), 1)
    blank = jnp.zeros((block, AUX - HEAD_DIM), jnp.float32)
    steps = rows // block

    def prepare(member):
        def one(step, carry):
            inside = pl.ds(pl.multiple_of(step * block, block), block)
            at_rows = pl.ds(pl.multiple_of(member * rows + step * block, block), block)
            gradient = upstream[member, inside, :].astype(jnp.float32)
            product = gradient * attended[member, inside, :].astype(jnp.float32)
            for head in range(head_local):
                columns = slice(head * HEAD_DIM, (head + 1) * HEAD_DIM)
                row_dot = jnp.sum(product[:, columns], axis=1, keepdims=True)
                first = row_dot.astype(low).astype(jnp.float32)
                wide = jnp.concatenate([gradient[:, columns], blank], axis=1)
                wide = jnp.where(lane == HEAD_DIM + 1, first, wide)
                wide = jnp.where(lane == HEAD_DIM + 2, row_dot - first, wide)
                grad_aux[head, at_rows, :] = wide.astype(low)
                key_turned[head, :, at_rows] = key_aux[head, at_rows, :].T[:HEAD_DIM]
            return carry

        lax.fori_loop(0, steps, one, 0)

    prepare(0)
    for member in (1, 2, 3):
        wires.arrived(grad_numbers[member], upstream.at[member], peers[member])
        prepare(member)
    query_total[...] = jnp.zeros_like(query_total)

    def back(step, carry):
        at_rows = pl.ds(pl.multiple_of(step * block, block), block)
        for head in range(head_local):
            scores = contract_cols(key_aux[head, at_rows, :], query_aux[head])
            chances = jnp.exp(scores)
            chance_grad = contract_cols(value_aux[head, at_rows, :], grad_aux[head])
            score_grad = (chances * chance_grad).astype(low)
            value_grad = dot_rows(chances.astype(low), grad_aux[head])
            key_grad = dot_rows(score_grad, query_aux[head])
            query_total[head] += dot_rows(key_turned[head, :, at_rows], score_grad)
            at = 3 * head * HEAD_DIM
            two = jnp.concatenate([key_grad[:, :HEAD_DIM], value_grad[:, :HEAD_DIM]], axis=1)
            projected_grad[at_rows, at + HEAD_DIM : at + 3 * HEAD_DIM] = two.astype(low)
        return carry

    eighth = seq_len // block // 8

    def back_eighths(start, stop):
        lax.fori_loop(start * eighth, stop * eighth, back, 0)

    for which in (expand_group, reduce_group):
        for k in range(1, len(bits)):
            which.bit_add()
            if k + 1 < len(bits):
                which.bit_send()
        which.own_send()
    wires.arrived(merge_numbers[0], merge_core.at[0], beside)
    wires.arrived(merge_numbers[1], merge_core.at[1], beside)
    for k in (0, 1):
        here = group ^ (2 * k)
        total = merge_work[here].astype(jnp.float32) + merge_core[k].astype(jnp.float32)
        merge_work[here] = total.astype(low)
    begin(merge_numbers[2], merge_work.at[group ^ 2], merge_line, across)

    back_eighths(0, 3)
    expand_out[...] = expand_group.own_sum()
    reduce_out[...] = reduce_group.own_sum()
    expand_part = momentum_decay * expand_momentum[...] + expand_out[...]
    reduce_part = momentum_decay * reduce_momentum[...] + reduce_out[...]
    first_core = core == 0
    side[0] = jnp.where(first_core, expand_part, reduce_part)
    side[1] = jnp.where(first_core, reduce_part, expand_part)
    side_number = wires.number()
    begin(side_number, side.at[1], side_got, beside)
    wires.arrived(merge_numbers[2], merge_line, across)
    total = merge_work[group].astype(jnp.float32) + merge_line[...].astype(jnp.float32)
    merge_work[group] = total.astype(low)
    merge_group.bit_send()

    back_eighths(3, 4)
    begin(layer_number, layer_across, layer_got, across)
    wires.arrived(side_number, side_got, beside)
    part_rows = side_got.shape[0]
    both[:part_rows, :] = side[0]
    both[part_rows:, :] = side_got[...]
    width = both.shape[1]
    high, rest = split_low(both[...])
    at = 0
    for k in range(0, width, SIDE):
        span = width - k
        part = contract_rows(high[:, k : k + SIDE], high[:, k:])
        part = part + contract_rows(high[:, k : k + SIDE], rest[:, k:])
        part = part + contract_rows(rest[:, k : k + SIDE], high[:, k:])
        gram_work[:, :, at : at + span] = part.reshape(SIDE // 8, 8, span)
        at += span
    slots = SIDE // 16
    halves = [
        ChipSum(
            gram_work,
            gram,
            gram_got.at[h],
            gram_last.at[h],
            h * slots,
            slots,
            order,
            place,
            tensor_count,
            wires,
            begin,
        )
        for h, order in enumerate((bits, bits[::-1]))
    ]
    for half in halves:
        half.bit_send()

    back_eighths(4, 6)
    for half in halves:
        half.bit_add()
        for _ in range(2, len(bits)):
            half.bit_send()
            half.bit_add()
        half.bit_send()
    merge_group.bit_add()
    merge_group.bit_send()

    back_eighths(6, 7)
    for half in halves:
        half.bit_add()
        half.line_send()
    merge_group.bit_add()
    for _ in range(2, len(bits)):
        merge_group.bit_send()
        merge_group.bit_add()
    merge_group.own_send()

    back_eighths(7, 8)

    def finish(step, carry):
        at_rows = pl.ds(pl.multiple_of(step * block, block), block)
        for head in range(head_local):
            query_grad = query_total[head, :, at_rows].T * HEAD_DIM**-0.5
            at = 3 * head * HEAD_DIM
            projected_grad[at_rows, at : at + HEAD_DIM] = query_grad.astype(low)
        return carry

    lax.fori_loop(0, seq_len // block, finish, 0)
    first_numbers = [wires.number() for _ in range(3)]

    def first_part(member):
        at_rows = pl.ds(member * rows, rows)
        part = contract_cols(projected_grad[at_rows, :], heads_weight[...])
        first_parts[member] = part.astype(low)

    heads_work[...] = (
        contract_rows(first_full[...], projected_grad[...]).reshape(heads_work.shape).astype(low)
    )
    heads_group.bit_send()
    for half in halves:
        half.line_add()
        half.line_back()
    for k, member in enumerate((3, 1)):
        first_part(member)
        begin(first_numbers[k], first_parts.at[member], first_beside.at[k], beside)
    first_part(2)
    wires.arrived(first_numbers[0], first_beside.at[0], beside)
    total = first_parts[2].astype(jnp.float32) + first_beside[0].astype(jnp.float32)
    first_parts[2] = total.astype(low)
    for half in halves:
        half.back_wait()
        half.bit_back()
    begin(first_numbers[2], first_parts.at[2], first_across, across)
    heads_group.bit_add()
    for _ in range(2, len(bits)):
        heads_group.bit_send()
        heads_group.bit_add()
    heads_group.bit_send()
    first_part(0)
    for _ in range(1, len(bits)):
        for half in halves:
            half.back_wait()
            half.bit_back()
    heads_group.bit_add()
    heads_group.own_send()
    merge_out[...] = merge_group.own_sum()
    wires.arrived(layer_number, layer_got, across)
    output_rows[...] = (layer_base[...] + layer_got[...].astype(jnp.float32)).astype(low)
    wires.arrived(first_numbers[1], first_beside.at[1], beside)
    wires.arrived(first_numbers[2], first_across, across)
    sums = [0.0, 0.0]
    for p in range(2):
        piece = pl.ds(p * (rows // 2), rows // 2)
        first_grad = (
            first_parts[0, piece, :].astype(jnp.float32)
            + first_beside[1, piece, :].astype(jnp.float32)
            + first_across[piece, :].astype(jnp.float32)
        )
        normed, inverse = center_scale(tokens[piece, :].astype(jnp.float32))
        total = middle_grad[piece, :] + norm_backward(first_grad, normed, inverse, vectors[0:1, :])
        input_rows[piece, :] = total
        input_low[piece, :] = total.astype(low)
        sums[0] = sums[0] + jnp.sum(first_grad * normed, axis=0, keepdims=True)
        sums[1] = sums[1] + jnp.sum(first_grad, axis=0, keepdims=True)
    vector_part[...] = jnp.concatenate(sums + [vector_sums[...]], axis=0)
    heads_out[...] = heads_group.own_sum()
    heads_part = momentum_decay * heads_momentum[...] + heads_out[...]
    merge_part = momentum_decay * merge_momentum[...].T + merge_out[...]
    blocks = [
        side_part[:, k : k + HEAD_DIM]
        for side_part in (heads_part, merge_part)
        for k in range(0, side_part.shape[1], HEAD_DIM)
    ]
    quarter = len(blocks) // 4
    for h in range(2):
        for k in range(quarter):
            first, second = blocks[2 * h * quarter + k], blocks[(2 * h + 1) * quarter + k]
            grams = []
            for block_part in (first, second):
                top, rest = split_low(block_part)
                grams.append(
                    contract_rows(top, top) + (contract_rows(top, rest) + contract_rows(rest, top))
                )
            here = slice(k * HEAD_DIM, (k + 1) * HEAD_DIM)
            small_gram[h, here, :] = jnp.concatenate(grams, axis=1)
    for half in halves:
        half.back_wait()
    finish_sends()


def back_pallas(
    attended,
    attended_grad,
    query_aux,
    key_aux,
    value_aux,
    first_full,
    heads_weight,
    expand_sum,
    reduce_sum,
    merge_sum,
    layer_base,
    layer_across,
    expand_momentum,
    reduce_momentum,
    tokens,
    middle_grad,
    vectors,
    vector_sums,
    heads_momentum,
    merge_momentum,
):
    data_count, tensor_count = lax.axis_size("dp"), lax.axis_size("tensor")
    members, rows, group_width = attended.shape
    head_local = group_width // HEAD_DIM
    seq_len = members * rows
    low, wide = jnp.bfloat16, jnp.float32
    width, columns = heads_weight.shape
    unit_block = expand_sum.shape[1:]
    merge_block = merge_sum.shape[2:]
    heads_block = (width // data_count, columns)
    packed = sum(width - k for k in range(0, width, SIDE))
    inside = pl.BlockSpec(memory_space=pltpu.VMEM)
    outs = (
        (unit_block, wide),
        (unit_block, wide),
        (merge_block, wide),
        (heads_block, wide),
        ((rows, width), wide),
        ((rows, width), low),
        (vectors.shape, wide),
        ((rows, width), low),
        ((SIDE // 8, 8, packed), wide),
        ((2 * unit_block[0], unit_block[1]), wide),
        ((2, head_local * HEAD_DIM, 2 * HEAD_DIM), wide),
    )
    steps = data_count // 2 - 1
    later = max(data_count // 4 - 1, 1)
    slots = SIDE // 16
    left = slots // (data_count // 2)
    portion = left // tensor_count if left % tensor_count == 0 else left
    scratch = []
    for shape, kind in (
        ((members, rows, group_width), low),
        ((head_local, seq_len, AUX), low),
        ((head_local, HEAD_DIM, seq_len), low),
        ((head_local, HEAD_DIM, seq_len), wide),
        ((seq_len, columns), low),
        ((members, rows, width), low),
        ((2, rows, width), low),
        ((rows, width), low),
        ((rows, width), low),
        ((data_count,) + unit_block, low),
        ((later, 2) + unit_block, low),
        ((2,) + unit_block, low),
        ((data_count,) + unit_block, low),
        ((later, 2) + unit_block, low),
        ((2,) + unit_block, low),
        (merge_sum.shape, low),
        ((2, data_count) + merge_block, low),
        ((data_count,) + merge_block, low),
        ((steps, 2) + merge_block, low),
        ((2,) + merge_block, low),
        ((data_count,) + heads_block, low),
        ((steps, 2) + heads_block, low),
        ((2,) + heads_block, low),
        ((2,) + unit_block, wide),
        (unit_block, wide),
        ((SIDE // 8, 8, packed), wide),
        ((2, slots, 8, packed), wide),
        ((2, tensor_count - 1, portion, 8, packed), wide),
    ):
        scratch.append(pltpu.VMEM(shape, kind))
    copies = 3 + 3 + 1 + 4 * (steps + 4) + 1 + 3
    copies += 2 * (2 * (data_count // 2).bit_length() + 2 * tensor_count)
    return pl.pallas_call(
        functools.partial(back_kernel, data_count, tensor_count),
        out_shape=tuple(jax.ShapeDtypeStruct(*out) for out in outs),
        in_specs=[inside] * 7 + [pl.BlockSpec(memory_space=pl.ANY)] * 3 + [inside] * 10,
        out_specs=(inside,) * len(outs),
        scratch_shapes=scratch
        + [
            pltpu.SemaphoreType.DMA((copies,)),
            pltpu.SemaphoreType.DMA((copies,)),
            pltpu.SemaphoreType.DMA((3,)),
        ],
        compiler_params=pltpu.CompilerParams(
            vmem_limit_bytes=VMEM_LIMIT, collective_id=3, has_side_effects=True
        ),
        cost_estimate=pl.CostEstimate(
            flops=10 * head_local * seq_len * seq_len * AUX,
            bytes_accessed=10 * seq_len * width,
            transcendentals=head_local * seq_len * seq_len,
        ),
        name="back",
    )(
        attended,
        attended_grad,
        query_aux,
        key_aux,
        value_aux,
        first_full,
        heads_weight,
        expand_sum,
        reduce_sum,
        merge_sum,
        layer_base,
        layer_across,
        expand_momentum,
        reduce_momentum,
        tokens,
        middle_grad,
        vectors,
        vector_sums,
        heads_momentum,
        merge_momentum,
    )


def three_pass(left, right):
    return dot_rows(left[0], right[0]) + (dot_rows(left[0], right[1]) + dot_rows(left[1], right[0]))


def last_kernel(
    data_count,
    tensor_count,
    gram,
    both,
    small_gram,
    vector_part,
    output_rows,
    input_rows,
    ortho_mine,
    ortho_other,
    small_chain,
    vector_sum,
    moved_output,
    moved_input,
    square,
    gram_high,
    gram_low,
    factor_high,
    factor_low,
    turn_high,
    turn_low,
    part,
    theirs,
    small_got,
    small_sum,
    small_mine,
    vector_got,
    vector_half,
    vector_line,
    send,
    receive,
):
    size = part.shape[1]
    rows = part.shape[0] // 2
    data, tensor = lax.axis_index("dp"), lax.axis_index("tensor")
    beside, away = (data ^ 1, tensor), (data ^ 1, tensor ^ 2)
    moved = jnp.logical_not((data & 1) == (tensor >> 1))
    wires = Wires(send, receive)
    pending = []

    def begin(k, source, target, device, when=None):
        if when is None:
            wires.start(k, source, target, device)
        else:

            @pl.when(when)
            def _():
                wires.start(k, source, target, device)

        pending.append((k, source, device, when))

    greet(column_and_plane(data, tensor, data_count, tensor_count))
    bits = [1] + low_rank_bits(data_count)
    hops = [(wires.number(), wires.number()) for _ in bits]

    core = data & 1

    def hop_send(k):
        peer = (data ^ bits[k], tensor)
        begin(hops[k][0], vector_half.at[k], vector_got.at[k], peer)
        small = small_gram.at[1 - core] if k == 0 else small_sum.at[k]
        begin(hops[k][1], small, small_got.at[k], peer)

    def hop_add(k):
        peer = (data ^ bits[k], tensor)
        wires.arrived(hops[k][0], vector_got.at[k], peer)
        wires.arrived(hops[k][1], small_got.at[k], peer)
        vector_half[k + 1] = vector_half[k] + vector_got[k]
        small = small_gram[core] if k == 0 else small_sum[k]
        small_sum[k + 1] = small + small_got[k]

    vector_half[0] = vector_part[...]
    hop_send(0)
    input_number, output_number = wires.number(), wires.number()
    begin(input_number, input_rows, moved_input, away, moved)
    begin(output_number, output_rows, moved_output, away, moved)

    identity = (
        lax.broadcasted_iota(jnp.int32, (SIDE, SIDE), 0)
        == lax.broadcasted_iota(jnp.int32, (SIDE, SIDE), 1)
    ).astype(jnp.float32)
    blocks = size // SIDE
    trace = 0.0
    at = 0
    for i in range(blocks):
        span = size - i * SIDE
        strip = gram[:, :, at : at + span].reshape(SIDE, span)
        trace = trace + jnp.sum(strip[:, :SIDE] * identity)
        at += span
    factor = 1.0 / (jnp.sqrt(trace) + newton_epsilon)

    def keep(strip, i, high, low):
        top, rest = split_low(strip)
        high[i * SIDE : (i + 1) * SIDE, i * SIDE :] = top
        low[i * SIDE : (i + 1) * SIDE, i * SIDE :] = rest
        for j in range(i + 1, blocks):
            turned = strip[:, (j - i) * SIDE : (j - i + 1) * SIDE].T
            top, rest = split_low(turned)
            high[j * SIDE : (j + 1) * SIDE, i * SIDE : (i + 1) * SIDE] = top
            low[j * SIDE : (j + 1) * SIDE, i * SIDE : (i + 1) * SIDE] = rest

    at = 0
    for i in range(blocks):
        span = size - i * SIDE
        strip = gram[:, :, at : at + span].reshape(SIDE, span) * (factor * factor)
        square[i * SIDE : (i + 1) * SIDE, i * SIDE :] = strip
        keep(strip, i, gram_high, gram_low)
        at += span
    part[...] = both[...] * factor

    def strip_of(left, right, i):
        here = slice(i * SIDE, (i + 1) * SIDE)
        return three_pass(
            (left[0][here, :], left[1][here, :]), (right[0][:, i * SIDE :], right[1][:, i * SIDE :])
        )

    gram_pair, factor_pair = (gram_high, gram_low), (factor_high, factor_low)

    def wide_factor():
        for i in range(blocks):
            here = slice(i * SIDE, (i + 1) * SIDE)
            strip = newton_cubic * square[here, i * SIDE :] + newton_quintic * strip_of(
                gram_pair, gram_pair, i
            )
            first = strip[:, :SIDE] + newton_linear * identity
            strip = first if i == blocks - 1 else jnp.concatenate([first, strip[:, SIDE:]], axis=1)
            keep(strip, i, factor_high, factor_low)

    def wide_part():
        part[...] = three_pass(split_low(part[...]), (factor_high[...], factor_low[...]))

    def wide_gram():
        for i in range(blocks):
            keep(strip_of(gram_pair, factor_pair, i), i, turn_high, turn_low)
        for i in range(blocks):
            strip = strip_of((turn_high, turn_low), factor_pair, i)
            square[i * SIDE : (i + 1) * SIDE, i * SIDE :] = strip
            keep(strip, i, gram_high, gram_low)

    groups, head_size = small_gram.shape[1] // HEAD_DIM, HEAD_DIM
    double = 2 * head_size
    diagonal = identity[:double, :double]
    left = lax.broadcasted_iota(jnp.int32, (head_size, double), 1) < head_size
    small = {}

    def small_start():
        total = small_sum[len(bits)]
        small["gram"], small["chain"], small["scale"] = [], [], []
        for b in range(groups):
            pair = total[b * head_size : (b + 1) * head_size]
            full = jnp.concatenate([jnp.where(left, pair, 0.0), jnp.where(left, 0.0, pair)], axis=0)
            column = jnp.sum(full * diagonal, axis=1, keepdims=True)
            scales = []
            for k in range(2):
                norm = jnp.sqrt(jnp.sum(column[k * head_size : (k + 1) * head_size]))
                scales.append(jnp.full((head_size, 1), 1.0 / (norm + newton_epsilon), jnp.float32))
            scale = jnp.concatenate(scales, axis=0)
            small["gram"].append(full * (scale * scale))
            small["scale"].append(scale)
            small["chain"].append(None)

    def small_step(last):
        for b in range(groups):
            here = split_low(small["gram"][b])
            step = newton_linear * diagonal + newton_cubic * small["gram"][b]
            step = step + newton_quintic * three_pass(here, here)
            step_pair = split_low(step)
            before = small["chain"][b]
            small["chain"][b] = step if before is None else three_pass(split_low(before), step_pair)
            if not last:
                next_gram = three_pass(here, step_pair)
                small["gram"][b] = three_pass(split_low(next_gram), step_pair)

    def small_end():
        for b in range(groups):
            chain = small["chain"][b] * small["scale"][b]
            here = slice(b * head_size, (b + 1) * head_size)
            small_mine[here, :] = jnp.where(left, chain[:head_size], chain[head_size:])
        begin(small_number, small_mine, small_chain.at[core], beside)
        small_chain[core] = small_mine[...]

    small_number = wires.number()
    line_numbers = [wires.number() for _ in range(tensor_count - 1)]
    side_number = wires.number()
    for step in range(NEWTON_STEPS):
        wide_factor()
        if step == 1:
            hop_add(0)
            hop_send(1)
        elif step == 3:
            hop_add(2)
            for k in range(3, len(bits)):
                hop_send(k)
                hop_add(k)
            for k in range(1, tensor_count):
                peer = lax.rem(tensor + k, tensor_count)
                begin(line_numbers[k - 1], vector_half.at[len(bits)], vector_line.at[k - 1], (data, peer))
            small_start()
            small_step(False)
        elif step == 4:
            small_step(False)
        wide_part()
        if step < NEWTON_STEPS - 1:
            wide_gram()
        if step == 1:
            hop_add(1)
            hop_send(2)
        elif step == 3:
            small_step(False)
    small_step(False)
    ortho_mine[...] = part[:rows, :]
    theirs[...] = part[rows:, :]
    begin(side_number, theirs, ortho_other, beside)
    small_step(True)
    small_end()
    total = vector_half[len(bits)]
    for k in range(1, tensor_count):
        origin = lax.rem(tensor + tensor_count - k, tensor_count)
        wires.arrived(line_numbers[k - 1], vector_line.at[k - 1], (data, origin))
        total = total + vector_line[k - 1]
    vector_sum[...] = total

    @pl.when(moved)
    def _():
        wires.arrived(input_number, moved_input, away)
        wires.arrived(output_number, moved_output, away)

    wires.arrived(side_number, ortho_other, beside)
    wires.arrived(small_number, small_chain.at[1 - core], beside)
    for k, source, device, when in pending:
        if when is None:
            wires.sent(k, source, device)
        else:

            @pl.when(when)
            def _():
                wires.sent(k, source, device)


def last_pallas(gram, both, small_gram, vector_part, output_rows, input_rows):
    data_count, tensor_count = lax.axis_size("dp"), lax.axis_size("tensor")
    low, wide = jnp.bfloat16, jnp.float32
    size = both.shape[1]
    rows = both.shape[0] // 2
    hops = data_count.bit_length() - 1
    inside = pl.BlockSpec(memory_space=pltpu.VMEM)
    outs = (
        ((rows, size), wide),
        ((rows, size), wide),
        (small_gram.shape, wide),
        (vector_part.shape, wide),
        (output_rows.shape, low),
        (input_rows.shape, low),
    )
    scratch = [
        pltpu.VMEM(shape, kind)
        for shape, kind in (
            ((size, size), wide),
            ((size, size), low),
            ((size, size), low),
            ((size, size), low),
            ((size, size), low),
            ((size, size), low),
            ((size, size), low),
            (both.shape, wide),
            ((rows, size), wide),
            ((hops,) + small_gram.shape[1:], wide),
            ((hops + 1,) + small_gram.shape[1:], wide),
            (small_gram.shape[1:], wide),
            ((hops,) + vector_part.shape, wide),
            ((hops + 1,) + vector_part.shape, wide),
            ((tensor_count - 1,) + vector_part.shape, wide),
        )
    ]
    copies = 2 * hops + 3 + tensor_count
    return pl.pallas_call(
        functools.partial(last_kernel, data_count, tensor_count),
        out_shape=tuple(jax.ShapeDtypeStruct(*out) for out in outs),
        in_specs=[inside] * 6,
        out_specs=(inside,) * len(outs),
        scratch_shapes=scratch
        + [pltpu.SemaphoreType.DMA((copies,)), pltpu.SemaphoreType.DMA((copies,))],
        compiler_params=pltpu.CompilerParams(
            vmem_limit_bytes=VMEM_LIMIT, collective_id=4, has_side_effects=True
        ),
        cost_estimate=pl.CostEstimate(
            flops=90 * size * size * size, bytes_accessed=20 * size * size, transcendentals=0
        ),
        name="last",
    )(gram, both, small_gram, vector_part, output_rows, input_rows)


SIDE = 256


def swap_bit(values, axis_name, bit):
    count = lax.axis_size(axis_name)
    return lax.ppermute(values, axis_name, [(i, i ^ bit) for i in range(count)])


def data_bits():
    return [1 << k for k in range(1, lax.axis_size("dp").bit_length() - 1)]


def has_bit(index, bit):
    return (index & bit) != 0


def gather_bits_absolute(block, bits):
    index = lax.axis_index("dp")
    for bit in bits:
        other = swap_bit(block, "dp", bit)
        mine = has_bit(index, bit)
        block = jnp.concatenate(
            [jnp.where(mine, other, block), jnp.where(mine, block, other)], axis=0
        )
    return block


def pair_permute(values, where_to):
    data_count, tensor_count = lax.axis_size("dp"), lax.axis_size("tensor")
    moves = []
    for i in range(data_count):
        for j in range(tensor_count):
            target = where_to(i, j)
            if target is not None:
                moves.append((i * tensor_count + j, target[0] * tensor_count + target[1]))
    return lax.ppermute(values, ("dp", "tensor"), moves)


def exchange_home(values):
    return pair_permute(
        values, lambda i, j: (i ^ 1, j ^ 2) if (i & 1) != (j >> 1) else None
    )


def gather_head_group(shard):
    first = []
    for core in (0, 1):
        got = []
        for half in (0, 1):
            got.append(
                pair_permute(
                    shard,
                    lambda i, j: (i - core + (j & 1), (j >> 1) + 2 * half)
                    if (i & 1) == core
                    else None,
                )
            )
        first.append(jnp.where(lax.axis_index("tensor") >= 2, got[1], got[0]))
    return gather_bits_absolute(jnp.concatenate(first, axis=0), data_bits())


def per_device(
    tokens,
    segment_ids,
    out_grad,
    heads_weight,
    merge_weight,
    expand_weight,
    reduce_weight,
    heads_momentum,
    merge_momentum,
    expand_momentum,
    reduce_momentum,
    heads_average,
    merge_average,
    expand_average,
    reduce_average,
    vectors,
    vector_momentum,
    vector_average,
):
    low = jnp.bfloat16
    tensor_count = lax.axis_size("tensor")
    data_count = lax.axis_size("dp")
    tensor_index = lax.axis_index("tensor")
    core = lax.axis_index("dp") & 1
    row_count = tokens.shape[0]
    seq_len = row_count * tensor_count
    head_local = heads_weight.shape[1] // (3 * HEAD_DIM)
    group_width = head_local * HEAD_DIM
    at_home = core == (tensor_index >> 1)
    group = 2 * (tensor_index & 1) + core

    own_segments = jnp.where(at_home, segment_ids, swap_bit(segment_ids, "dp", 1))
    chunk_at = []
    for member in range(4):
        its_core, its_tensor = core ^ (member & 1), tensor_index ^ (member >> 1)
        chunk_at.append(jnp.where(its_core == (its_tensor >> 1), its_tensor, its_tensor ^ 2))
    segments = jnp.take(
        own_segments.reshape(tensor_count, row_count), jnp.stack(chunk_at), axis=0
    ).reshape(seq_len)
    gather_heads = heads_weight.shape[0] % 16 == 0
    late = reduce_weight.shape[0] % 16 == 0
    heads_low = heads_weight
    if not gather_heads:
        heads_low = gather_head_group(heads_weight.astype(low))
    (
        attended_full,
        attended_own,
        query_aux,
        key_aux,
        value_aux,
        first_full,
        own_tokens,
        full_heads,
        full_expand,
        full_reduce,
        full_merge,
        sequence_grad,
    ) = front_pallas(
        tokens,
        heads_low,
        expand_weight.T,
        reduce_weight,
        merge_weight,
        vectors,
        segments,
        out_grad,
        gather_heads,
        late,
    )
    full_heads = full_heads.reshape(D, 3 * group_width) if gather_heads else heads_low
    if not late:
        full_expand, full_reduce = full_expand.reshape(-1, D), full_reduce.reshape(-1, D)
    (
        layer_base,
        layer_across,
        middle_grad,
        attended_grad,
        expand_sum,
        reduce_sum,
        merge_sum,
        vector_sums,
    ) = middle_pallas(
        attended_own, full_merge, own_tokens, vectors, full_expand, full_reduce, sequence_grad, late
    )
    (
        expand_rows,
        reduce_gradient,
        merge_rows,
        heads_gradient,
        input_rows,
        input_low,
        vector_part,
        output_rows,
        wide_gram,
        wide_rows,
        small_gram,
    ) = back_pallas(
        attended_full,
        attended_grad,
        query_aux,
        key_aux,
        value_aux,
        first_full,
        full_heads,
        expand_sum,
        reduce_sum,
        merge_sum.reshape(4, data_count, merge_weight.shape[1], group_width),
        layer_base,
        layer_across,
        expand_momentum.T,
        reduce_momentum,
        own_tokens,
        middle_grad,
        vectors,
        vector_sums,
        heads_momentum,
        merge_momentum,
    )
    expand_gradient, merge_gradient = expand_rows.T, merge_rows.T
    expand_new_momentum = momentum_decay * expand_momentum + expand_gradient
    reduce_new_momentum = momentum_decay * reduce_momentum + reduce_gradient
    heads_new_momentum = momentum_decay * heads_momentum + heads_gradient
    merge_new_momentum = momentum_decay * merge_momentum + merge_gradient

    heads_part = heads_new_momentum.reshape(heads_new_momentum.shape[0], head_local * 3, HEAD_DIM)
    merge_part = merge_new_momentum.reshape(head_local, HEAD_DIM, merge_new_momentum.shape[1])
    quarter = head_local
    ortho_mine, ortho_other, small_chain, vector_gradient, moved_output, moved_input = last_pallas(
        wide_gram,
        wide_rows,
        small_gram,
        vector_part,
        output_rows,
        input_low,
    )
    small_chain = small_chain.reshape(2, quarter, HEAD_DIM, 2, HEAD_DIM)
    small_chain = jnp.transpose(small_chain, (0, 3, 1, 2, 4)).reshape(-1, HEAD_DIM, HEAD_DIM)
    layer_output = jnp.where(at_home, output_rows, moved_output)
    input_gradient = jnp.where(at_home, input_rows, moved_input.astype(jnp.float32))
    vector_new_momentum = momentum_decay * vector_momentum + vector_gradient
    side_count = 3 * head_local
    heads_ortho = jnp.einsum("rmd,mde->rme", heads_part, small_chain[:side_count], precision=highest)
    merge_ortho = jnp.einsum("hde,hec->hdc", small_chain[side_count:], merge_part, precision=highest)

    first_core = core == 0
    expand_ortho = jnp.where(first_core, ortho_mine, ortho_other).T
    reduce_ortho = jnp.where(first_core, ortho_other, ortho_mine)

    keep_factor = 1.0 - muon_rate * weight_decay
    head_step = muon_rate * 0.2 * math.sqrt(max(D, HEAD_DIM))
    wide_step = muon_rate * 0.2 * math.sqrt(max(D, FF))
    heads_new_weight = heads_weight * keep_factor - head_step * heads_ortho.reshape(
        heads_weight.shape
    )
    merge_new_weight = merge_weight * keep_factor - head_step * merge_ortho.reshape(
        merge_weight.shape
    )
    expand_new_weight = expand_weight * keep_factor - wide_step * expand_ortho
    reduce_new_weight = reduce_weight * keep_factor - wide_step * reduce_ortho
    vector_new_value = vectors - vector_rate / math.sqrt(SEQ * data_count) * vector_new_momentum
    heads_new_average = average_decay * heads_average + (1.0 - average_decay) * heads_new_weight
    merge_new_average = average_decay * merge_average + (1.0 - average_decay) * merge_new_weight
    expand_new_average = average_decay * expand_average + (1.0 - average_decay) * expand_new_weight
    reduce_new_average = average_decay * reduce_average + (1.0 - average_decay) * reduce_new_weight
    vector_new_average = average_decay * vector_average + (1.0 - average_decay) * vector_new_value
    return (
        layer_output,
        input_gradient,
        heads_gradient,
        merge_gradient,
        expand_gradient,
        reduce_gradient,
        heads_new_momentum,
        merge_new_momentum,
        expand_new_momentum,
        reduce_new_momentum,
        heads_new_weight,
        merge_new_weight,
        expand_new_weight,
        reduce_new_weight,
        heads_new_average,
        merge_new_average,
        expand_new_average,
        reduce_new_average,
        vector_gradient,
        vector_new_momentum,
        vector_new_value,
        vector_new_average,
    )


def solution(mesh):
    placed = (
        P(("dp", "tensor"), None),
        P("dp"),
        P("dp", None),
        P("dp", "tensor"),
        P("tensor", "dp"),
        P(None, ("tensor", "dp")),
        P(("tensor", "dp"), None),
        P("dp", "tensor"),
        P("tensor", "dp"),
        P(None, ("tensor", "dp")),
        P(("tensor", "dp"), None),
        P("dp", "tensor"),
        P("tensor", "dp"),
        P(None, ("tensor", "dp")),
        P(("tensor", "dp"), None),
        P(),
        P(),
        P(),
    )
    return jax.shard_map(
        per_device,
        mesh=mesh,
        in_specs=placed,
        out_specs=(
            P(("dp", "tensor"), None),
            P(("dp", "tensor"), None),
            P("dp", "tensor"),
            P("tensor", "dp"),
            P(None, ("tensor", "dp")),
            P(("tensor", "dp"), None),
            P("dp", "tensor"),
            P("tensor", "dp"),
            P(None, ("tensor", "dp")),
            P(("tensor", "dp"), None),
            P("dp", "tensor"),
            P("tensor", "dp"),
            P(None, ("tensor", "dp")),
            P(("tensor", "dp"), None),
            P("dp", "tensor"),
            P("tensor", "dp"),
            P(None, ("tensor", "dp")),
            P(("tensor", "dp"), None),
            P(),
            P(),
            P(),
            P(),
        ),
        check_vma=False,
    )
```

```python
import functools
import math

import jax
import jax.numpy as jnp
from jax import lax
from jax.experimental import pallas as pl
from jax.experimental.pallas import tpu as pltpu
from jax.sharding import PartitionSpec as P

D = 768
HEAD_DIM = 64
FF = 3072
SEQ = 2048
NEWTON_STEPS = 5


highest = lax.Precision.HIGHEST
norm_epsilon = 1e-06
newton_epsilon = 1e-07
newton_linear = 3.4445
newton_cubic = -4.775
newton_quintic = 2.0315
momentum_decay = 0.5
average_decay = 0.9
muon_rate = 0.2
weight_decay = 0.1
vector_rate = 0.15
masked_score = -1e30
VMEM_LIMIT = 56 * 2**20


def center_scale(values):
    average = jnp.mean(values, axis=-1, keepdims=True)
    centered = values - average
    inverse = lax.rsqrt(jnp.mean(centered * centered, axis=-1, keepdims=True) + norm_epsilon)
    return (centered * inverse, inverse)


def norm_backward(upstream, normed, inverse, gain):
    scaled = upstream * gain
    mean_one = jnp.mean(scaled, axis=-1, keepdims=True)
    mean_two = jnp.mean(scaled * normed, axis=-1, keepdims=True)
    return inverse * (scaled - mean_one - normed * mean_two)


def gelu_exact(values):
    return jax.nn.gelu(values, approximate=False)


def contract_rows(left_side, right_side):
    return lax.dot_general(
        left_side, right_side, (((0,), (0,)), ((), ())), preferred_element_type=jnp.float32
    )


def contract_cols(left_side, right_side):
    return lax.dot_general(
        left_side, right_side, (((1,), (1,)), ((), ())), preferred_element_type=jnp.float32
    )


KEY_BLOCK = 256
AUX = 128


MESH = pl.DeviceIdType.MESH


def low_rank_bits(data_count):
    return [1 << k for k in range(1, data_count.bit_length() - 1)]


class Wires:
    def __init__(self, send, receive):
        self.send, self.receive, self.used = send, receive, 0

    def number(self):
        self.used += 1
        return self.used - 1

    def start(self, k, source, target, device):
        copy = pltpu.make_async_remote_copy(
            source, target, self.send.at[k], self.receive.at[k], device_id=device, device_id_type=MESH
        )
        copy.start()

    def sent(self, k, source, device):
        pltpu.make_async_remote_copy(
            source, source, self.send.at[k], self.receive.at[k], device_id=device, device_id_type=MESH
        ).wait_send()

    def arrived(self, k, target, device):
        pltpu.make_async_remote_copy(
            target, target, self.send.at[k], self.receive.at[k], device_id=device, device_id_type=MESH
        ).wait_recv()


def greet(devices):
    barrier = pltpu.get_barrier_semaphore()
    for device in devices:
        pl.semaphore_signal(barrier, inc=1, device_id=device, device_id_type=MESH)
    pl.semaphore_wait(barrier, len(devices))


def column_and_plane(data, tensor, data_count, tensor_count):
    found = []
    for core in (0, 1):
        for step in range(tensor_count):
            if core or step:
                found.append((data ^ core, lax.rem(tensor + step, tensor_count)))
    for k in range(1, data_count // 2):
        found.append((data ^ (2 * k), tensor))
    return found


def front_kernel(
    data_count,
    tensor_count,
    gather_heads,
    late,
    tokens,
    heads_wide,
    expand_wide,
    reduce_wide,
    merge_wide,
    vectors,
    segment_rows,
    out_grad,
    attended,
    attended_rows,
    query_aux,
    key_aux,
    value_aux,
    first_full,
    own_tokens,
    all_heads,
    all_expand,
    all_reduce,
    merge_full,
    sequence_grad,
    all_merge,
    chunks,
    arrivals,
    heads,
    expand,
    reduce,
    merge,
    segments,
    send,
    receive,
    local,
):
    low = jnp.bfloat16
    rows, width = tokens.shape
    head_local = query_aux.shape[0]
    group_width = head_local * HEAD_DIM
    data, tensor = lax.axis_index("dp"), lax.axis_index("tensor")
    core, half = data & 1, tensor >> 1
    home = core == half
    group = 2 * (tensor & 1) + core
    wires = Wires(send, receive)
    beside, across, diagonal = (data ^ 1, tensor), (data, tensor ^ 1), (data ^ 1, tensor ^ 1)
    members = [None, beside, across, diagonal]
    away = (data ^ 1, tensor ^ 2)
    pieces = [pl.ds(p * (rows // 4), rows // 4) for p in range(4)]
    pending = []

    def begin(k, source, target, device, when=None):
        if when is None:
            wires.start(k, source, target, device)
        else:

            @pl.when(when)
            def _():
                wires.start(k, source, target, device)

        pending.append((k, source, device, when))

    def await_arrival(k, target, device, when=None):
        if when is None:
            wires.arrived(k, target, device)
        else:

            @pl.when(when)
            def _():
                wires.arrived(k, target, device)

    if gather_heads:
        heads[...] = heads_wide[...].astype(low)
    merge[...] = merge_wide[...].T.astype(low)
    all_merge[data, tensor] = merge[...]
    greet(column_and_plane(data, tensor, data_count, tensor_count))

    pair = (data >> 1) * 2

    def group_send(block, whole):
        numbers = [wires.number() for _ in range(4)]
        for k in (0, 1):
            target = (pair + (tensor & 1), (tensor >> 1) + 2 * k)
            itself = (target[0] == data) & (target[1] == tensor)
            for c in (0, 1):
                begin(
                    numbers[2 * k + c],
                    block,
                    whole.at[data],
                    target,
                    jnp.logical_not(itself) & (core == c),
                )

            @pl.when(itself)
            def _():
                copy = pltpu.make_async_copy(block, whole.at[data], local.at[1])
                copy.start()
                copy.wait()

        return numbers

    def group_wait(numbers, whole):
        for k in (0, 1):
            for c in (0, 1):
                source = (pair + c, group)
                itself = (source[0] == data) & (source[1] == tensor)
                await_arrival(
                    numbers[2 * k + c],
                    whole.at[pair + c],
                    source,
                    jnp.logical_not(itself) & (half == k),
                )

    if gather_heads:
        head_numbers = group_send(heads, all_heads)
    merge_numbers = [wires.number() for _ in range(tensor_count - 1)]
    for k in range(1, tensor_count):
        peer = (data, lax.rem(tensor + k, tensor_count))
        begin(merge_numbers[k - 1], merge, all_merge.at[data, tensor], peer)
    segment_number = wires.number()
    begin(segment_number, segment_rows, segments, beside, home)

    @pl.when(home)
    def _():
        segments[...] = segment_rows[...]

    numbers = [wires.number() for _ in range(24)]
    for p, piece in enumerate(pieces):
        begin(numbers[p], tokens.at[piece], chunks.at[2, piece], across, home)
        begin(numbers[4 + p], tokens.at[piece], chunks.at[0, piece], away, jnp.logical_not(home))
        begin(numbers[8 + p], tokens.at[piece], chunks.at[1, piece], beside, home)

    @pl.when(home)
    def _():
        chunks[0] = tokens[...]

    if gather_heads:
        group_wait(head_numbers, all_heads)
        plane = []
        for k in range(1, data_count // 2):
            number = wires.number()
            plane.append((number, k))
            begin(number, all_heads.at[pl.ds(pair, 2)], all_heads.at[pl.ds(pair, 2)], (data ^ (2 * k), tensor))

    def bit_step(plan):
        made = []
        for mat, bit, held, wide in plan:
            for offset in held:
                number = wires.number()
                place = (pair if wide else data) ^ offset
                there = pl.ds(place ^ bit, 2) if wide else place ^ bit
                place = pl.ds(place, 2) if wide else place
                begin(number, mat.at[place], mat.at[place], (data ^ bit, tensor))
                made.append((number, mat, there, bit))
        return made

    def bit_wait(made):
        for number, mat, there, bit in made:
            await_arrival(number, mat.at[there], (data ^ bit, tensor))


    bits = low_rank_bits(data_count)
    schedule = []
    held = [[0], [0], [0]]
    for k in range(len(bits)):
        plan = []
        for m, mat in enumerate((all_expand, all_reduce, all_merge)):
            bit = bits[-1 - k] if m == 1 else bits[k]
            plan.append((mat, bit, list(held[m]), m < 2))
            held[m] = held[m] + [offset ^ bit for offset in held[m]]
        schedule.append(plan)
    schedule.append([(all_merge, 1, list(held[2]), False)])

    for p, piece in enumerate(pieces):
        await_arrival(numbers[4 + p], chunks.at[0, piece], away, jnp.logical_not(home))
        begin(numbers[12 + p], chunks.at[0, piece], chunks.at[2, piece], across, jnp.logical_not(home))
        begin(numbers[16 + p], chunks.at[0, piece], chunks.at[1, piece], beside, jnp.logical_not(home))


    if gather_heads:
        for number, k in plane:
            there = pl.ds(pair ^ (2 * k), 2)
            await_arrival(number, all_heads.at[there], (data ^ (2 * k), tensor))

    block = min(KEY_BLOCK, rows)
    lane = lax.broadcasted_iota(jnp.int32, (block, AUX), 1)
    blank = jnp.zeros((block, AUX - HEAD_DIM), jnp.float32)
    steps = rows // block

    def chunk_at(member):
        its_core, its_tensor = core ^ (member & 1), tensor ^ (member >> 1)
        return its_tensor ^ (2 * (its_core ^ (its_tensor >> 1)))

    def prepare(member):
        def one(step, carry):
            inside = pl.ds(pl.multiple_of(step * block, block), block)
            at_rows = pl.ds(pl.multiple_of(member * rows + step * block, block), block)
            normed, _ = center_scale(chunks[member, inside, :].astype(jnp.float32))
            first_in = (normed * vectors[0:1, :] + vectors[1:2, :]).astype(low)
            first_full[at_rows, :] = first_in
            weight = all_heads[...].reshape(width, 3 * group_width)
            projected = jnp.dot(first_in, weight, preferred_element_type=jnp.float32)
            projected = projected.astype(low).astype(jnp.float32)
            here = segments[pl.ds(chunk_at(member), 1), inside].astype(jnp.float32)
            here = jnp.broadcast_to(here, (AUX, block)).T
            same = (lane - HEAD_DIM).astype(jnp.float32) == here
            segment_lane = (lane >= HEAD_DIM) & (lane < HEAD_DIM + 3)
            query_extra = jnp.where(same & segment_lane, 1.0, 0.0)
            key_extra = jnp.where(
                segment_lane,
                jnp.where(same, 0.0, masked_score),
                jnp.where((lane >= HEAD_DIM + 3) & (lane < HEAD_DIM + 6), -1.0, 0.0),
            )
            value_extra = jnp.where(
                lane == HEAD_DIM,
                1.0,
                jnp.where((lane == HEAD_DIM + 1) | (lane == HEAD_DIM + 2), -1.0, 0.0),
            )
            for head in range(head_local):
                for which, (ref, extra, factor) in enumerate(
                    (
                        (query_aux, query_extra, HEAD_DIM**-0.5),
                        (key_aux, key_extra, 1.0),
                        (value_aux, value_extra, 1.0),
                    )
                ):
                    at = (3 * head + which) * HEAD_DIM
                    part = jnp.concatenate([projected[:, at : at + HEAD_DIM] * factor, blank], axis=1)
                    ref[head, at_rows, :] = jnp.where(lane < HEAD_DIM, part, extra).astype(low)
            return carry

        lax.fori_loop(0, steps, one, 0)

    def attend(member, steps_here):
        def one(step, carry):
            inside = pl.ds(pl.multiple_of(step * block, block), block)
            at_rows = pl.ds(pl.multiple_of(member * rows + step * block, block), block)
            done = []
            for head in range(head_local):
                query = query_aux[head, at_rows, :]
                scores = contract_cols(query, key_aux[head])
                row_max = jnp.max(scores, axis=1, keepdims=True)
                exponent = jnp.exp(scores - row_max).astype(low)
                output = jnp.dot(exponent, value_aux[head], preferred_element_type=jnp.float32)
                totals = output[:, HEAD_DIM : HEAD_DIM + 1]
                done.append(output[:, :HEAD_DIM] / totals)
                logsum = row_max + jnp.log(totals)
                first = logsum.astype(low).astype(jnp.float32)
                second = (logsum - first).astype(low).astype(jnp.float32)
                third = logsum - first - second
                wide = query.astype(jnp.float32)
                wide = jnp.where(lane == HEAD_DIM + 3, first, wide)
                wide = jnp.where(lane == HEAD_DIM + 4, second, wide)
                wide = jnp.where(lane == HEAD_DIM + 5, third, wide)
                query_aux[head, at_rows, :] = wide.astype(low)
            attended[member, inside, :] = jnp.concatenate(done, axis=1).astype(low)
            return carry

        lax.fori_loop(*steps_here, one, 0)

    for k in range(1, tensor_count):
        origin = lax.rem(tensor + tensor_count - k, tensor_count)
        await_arrival(merge_numbers[k - 1], all_merge.at[data, origin], (data, origin))
    merge_made = bit_step(schedule[0][2:])
    await_arrival(segment_number, segments, beside, jnp.logical_not(home))
    expand[...] = expand_wide[...].astype(low)
    reduce[...] = reduce_wide[...].astype(low)
    prepare(0)
    for p, piece in enumerate(pieces):
        await_arrival(numbers[p], chunks.at[2, piece], across, home)
        await_arrival(numbers[12 + p], chunks.at[2, piece], across, jnp.logical_not(home))
        begin(numbers[20 + p], chunks.at[2, piece], chunks.at[3, piece], beside)

    grad_numbers = [wires.number() for _ in range(4)]
    grad_copies = []
    for member in range(4):
        chunk = chunk_at(member)
        source = out_grad.at[pl.ds(pl.multiple_of(chunk * rows, rows), rows)]
        copy = pltpu.make_async_copy(source, sequence_grad.at[member], local.at[2 + member])
        grad_copies.append(copy)
        pl.when(home)(copy.start)
        begin(grad_numbers[member], source, sequence_grad.at[member ^ 1], beside, home)
    for p, piece in enumerate(pieces):
        await_arrival(numbers[8 + p], chunks.at[1, piece], beside, jnp.logical_not(home))
        await_arrival(numbers[16 + p], chunks.at[1, piece], beside, home)
    expand_numbers = group_send(expand, all_expand)
    reduce_numbers = group_send(reduce, all_reduce)
    for plan in schedule[1:-1]:
        bit_wait(merge_made)
        merge_made = bit_step(plan[2:])
    prepare(1)
    prepare(2)
    for p, piece in enumerate(pieces):
        await_arrival(numbers[20 + p], chunks.at[3, piece], beside)
    prepare(3)
    exchange = {}
    for member in (3, 2, 1, 0):
        attend(member, (0, steps // 2))
        if member == 2:
            group_wait(expand_numbers, all_expand)
            group_wait(reduce_numbers, all_reduce)
            made = bit_step(schedule[0][:2])
        attend(member, (steps // 2, steps))
        if member:
            number = wires.number()
            begin(number, attended.at[member], arrivals.at[group], members[member])
            exchange[member] = number
        else:
            arrivals[group] = attended[0]
        if member == 1:
            bit_wait(merge_made)
            merge_made = bit_step(schedule[-1])
    for plan in schedule[1 : -2 if late else -1]:
        bit_wait(made)
        made = bit_step(plan[:2])
    bit_wait(merge_made)
    strips = []
    for k in range(tensor_count):
        strip = all_merge[:, k].astype(jnp.float32)
        strips.append(strip.reshape(width, group_width))
    merge_full[...] = jnp.concatenate(strips, axis=1).astype(low)
    own_tokens[...] = chunks[0]
    for member, number in exchange.items():
        await_arrival(number, arrivals.at[group ^ member], members[member])
    attended_rows[...] = jnp.concatenate([arrivals[k] for k in range(4)], axis=1)
    bit_wait(made)
    for member in range(4):
        pl.when(home)(grad_copies[member].wait)
        await_arrival(
            grad_numbers[member], sequence_grad.at[member ^ 1], beside, jnp.logical_not(home)
        )
    for k, source, device, when in pending:
        if when is None:
            wires.sent(k, source, device)
        else:

            @pl.when(when)
            def _():
                wires.sent(k, source, device)


def front_pallas(tokens, heads, expand, reduce, merge, vectors, segments, out_grad, gather_heads, late):
    data_count, tensor_count = lax.axis_size("dp"), lax.axis_size("tensor")
    rows, width = tokens.shape
    low = jnp.bfloat16
    head_columns = heads.shape[-1]
    head_local = head_columns // (3 * HEAD_DIM)
    seq_len = segments.shape[0] * segments.shape[1]
    group_width = head_local * HEAD_DIM
    aux = jax.ShapeDtypeStruct((head_local, seq_len, AUX), low)
    inside = pl.BlockSpec(memory_space=pltpu.VMEM)
    anywhere = pl.BlockSpec(memory_space=pl.ANY)
    gathered = [
        jax.ShapeDtypeStruct((data_count,) + reduce.shape, low),
        jax.ShapeDtypeStruct((data_count,) + reduce.shape, low),
        jax.ShapeDtypeStruct((width, width), low),
        jax.ShapeDtypeStruct((4, rows, width), low),
    ]
    hops = 2 * (tensor_count - 1) + 2 * (data_count // 2 - 1) + data_count - 1
    copies = 13 + data_count // 2 + 24 + hops + 4 + 3
    if gather_heads:
        heads_out = jax.ShapeDtypeStruct((data_count,) + heads.shape, low)
    else:
        heads_out = jax.ShapeDtypeStruct(heads.shape, low)

    def kernel(*refs):
        if not gather_heads:
            refs = list(refs)
            refs[15] = refs[1]
        front_kernel(data_count, tensor_count, gather_heads, late, *refs)

    return pl.pallas_call(
        kernel,
        out_shape=(
            jax.ShapeDtypeStruct((4, rows, group_width), low),
            jax.ShapeDtypeStruct((rows, 4 * group_width), low),
            aux,
            aux,
            aux,
            jax.ShapeDtypeStruct((seq_len, width), low),
            jax.ShapeDtypeStruct((rows, width), low),
            heads_out,
            *gathered,
        ),
        in_specs=[inside] * 7 + [anywhere],
        out_specs=(inside,) * 8 + (anywhere,) * 2 + (inside,) * 2,
        scratch_shapes=[
            pltpu.VMEM((data_count, tensor_count) + merge.shape[::-1], low),
            pltpu.VMEM((4, rows, width), low),
            pltpu.VMEM((4, rows, group_width), low),
            pltpu.VMEM(heads.shape, low),
            pltpu.VMEM(reduce.shape, low),
            pltpu.VMEM(reduce.shape, low),
            pltpu.VMEM(merge.shape[::-1], low),
            pltpu.VMEM(segments.shape, jnp.int32),
            pltpu.SemaphoreType.DMA((copies,)),
            pltpu.SemaphoreType.DMA((copies,)),
            pltpu.SemaphoreType.DMA((6,)),
        ],
        compiler_params=pltpu.CompilerParams(
            vmem_limit_bytes=VMEM_LIMIT, collective_id=1, has_side_effects=True
        ),
        cost_estimate=pl.CostEstimate(
            flops=4 * head_local * seq_len * seq_len * AUX,
            bytes_accessed=8 * seq_len * width,
            transcendentals=head_local * seq_len * seq_len,
        ),
        name="front",
    )(tokens, heads, expand, reduce, merge, vectors, segments, out_grad)


def dot_rows(left_side, right_side):
    return jnp.dot(left_side, right_side, preferred_element_type=jnp.float32)


def middle_kernel(
    data_count,
    late,
    attended_rows,
    merge,
    tokens,
    vectors,
    expand_in,
    reduce_in,
    sequence_grad,
    layer_base,
    layer_across,
    middle_grad,
    attended_grad,
    expand_sum,
    reduce_sum,
    merge_sum,
    vector_sums,
    second_in,
    middle,
    hidden,
    expand_grad,
    partial,
    reduced,
    from_beside,
    reduced_beside,
    from_across,
    expand_got,
    reduce_got,
    expand_full,
    reduce_full,
    send,
    receive,
    local,
):
    low = jnp.bfloat16
    rows, width = tokens.shape
    group_width = width // 4
    data, tensor = lax.axis_index("dp"), lax.axis_index("tensor")
    wires = Wires(send, receive)
    beside, across = (data ^ 1, tensor), (data, tensor ^ 1)
    part = rows // 2
    pieces = [pl.ds(p * part, part) for p in range(2)]
    pending = []

    def begin(k, source, target, device):
        wires.start(k, source, target, device)
        pending.append((k, source, device))

    bits = low_rank_bits(data_count)
    greet([beside, across] + [(data ^ bit, tensor) for bit in sorted({bits[0], bits[-1]})])
    groups = [
        Group(work, got, None, order, (data, tensor), wires, begin)
        for work, got, order in (
            (expand_sum, expand_got, bits[::-1]),
            (reduce_sum, reduce_got, bits),
        )
    ]
    pair = (data >> 1) * 2
    if late:
        made, copies = [], []
        for m, (source, full, bit) in enumerate(
            ((expand_in, expand_full, bits[-1]), (reduce_in, reduce_full, bits[0]))
        ):
            for offset in [o for o in range(0, data_count, 2) if not o & bit]:
                here = pl.ds(pair ^ offset, 2)
                number = wires.number()
                begin(number, source.at[here], full.at[here], (data ^ bit, tensor))
                made.append((number, full.at[pl.ds(pair ^ offset ^ bit, 2)], (data ^ bit, tensor)))
                copies.append(
                    pltpu.make_async_copy(source.at[here], full.at[here], local.at[len(copies)])
                )
                copies[-1].start()
    units = data_count * expand_full.shape[1]

    def expand():
        return expand_full[...].reshape(units, width) if late else expand_in[...]

    def reduce():
        return reduce_full[...].reshape(units, width) if late else reduce_in[...]

    numbers = [[wires.number() for _ in range(2)] for _ in range(3)]
    for p, piece in enumerate(pieces):
        merged = contract_cols(attended_rows[piece, :], merge[...])
        here = tokens[piece, :].astype(jnp.float32) + merged + vectors[4:5, :]
        middle[piece, :] = here
        normed, _ = center_scale(here)
        second_in[0, piece, :] = (normed * vectors[2:3, :] + vectors[3:4, :]).astype(low)
        begin(numbers[0][p], second_in.at[0, piece], second_in.at[2, piece], across)
        begin(numbers[1][p], second_in.at[0, piece], second_in.at[1, piece], beside)

    def unit(member, p):
        piece = pieces[p]
        expanded = contract_cols(second_in[member, piece, :], expand())
        cdf = 0.5 + 0.5 * lax.erf(expanded * math.sqrt(0.5))
        activated = (expanded * cdf).astype(low)
        hidden[member, piece, :] = activated
        reduced[member, piece, :] = dot_rows(activated, reduce()).astype(low)
        slope = cdf + expanded * (jnp.exp(-0.5 * expanded * expanded) * (1.0 / math.sqrt(2.0 * math.pi)))
        upstream = contract_cols(sequence_grad[member, piece, :], reduce())
        grad = (upstream * slope).astype(low)
        expand_grad[member, piece, :] = grad
        partial[member, piece, :] = dot_rows(grad, expand()).astype(low)

    if late:
        for copy in copies:
            copy.wait()
        for number, there, device in made:
            wires.arrived(number, there, device)
    unit(0, 0)
    unit(0, 1)
    back = [[wires.number() for _ in range(2)] for _ in range(5)]
    for p, piece in enumerate(pieces):
        wires.arrived(numbers[1][p], second_in.at[1, piece], beside)
        unit(1, p)
        begin(back[0][p], partial.at[1, piece], from_beside.at[0, piece], beside)
        begin(back[3][p], reduced.at[1, piece], reduced_beside.at[0, piece], beside)
    for p, piece in enumerate(pieces):
        wires.arrived(numbers[0][p], second_in.at[2, piece], across)
        begin(numbers[2][p], second_in.at[2, piece], second_in.at[3, piece], beside)
    for p, piece in enumerate(pieces):
        wires.arrived(numbers[2][p], second_in.at[3, piece], beside)
        unit(3, p)
        begin(back[1][p], partial.at[3, piece], from_beside.at[1, piece], beside)
        begin(back[4][p], reduced.at[3, piece], reduced_beside.at[1, piece], beside)
        unit(2, p)
        wires.arrived(back[1][p], from_beside.at[1, piece], beside)
        both = partial[2, piece, :].astype(jnp.float32) + from_beside[1, piece, :].astype(jnp.float32)
        partial[2, piece, :] = both.astype(low)
        begin(back[2][p], partial.at[2, piece], from_across.at[piece], across)

    def sum_rows(target, left, right):
        total = None
        for member in range(4):
            term = contract_rows(left[member], right[member])
            total = term if total is None else total + term
        target[...] = total.reshape(target.shape).astype(low)

    sum_rows(reduce_sum, hidden, sequence_grad)
    groups[1].bit_send()
    sum_rows(expand_sum, expand_grad, second_in)
    groups[0].bit_send()
    for p, piece in enumerate(pieces):
        wires.arrived(back[3][p], reduced_beside.at[0, piece], beside)
        wires.arrived(back[4][p], reduced_beside.at[1, piece], beside)
        base = reduced[0, piece, :].astype(jnp.float32) + reduced_beside[0, piece, :].astype(jnp.float32)
        layer_base[piece, :] = base + middle[piece, :] + vectors[5:6, :]
        layer_across[piece, :] = (
            reduced[2, piece, :].astype(jnp.float32)
            + reduced_beside[1, piece, :].astype(jnp.float32)
        ).astype(low)
    sums = [0.0] * 4
    for p, piece in enumerate(pieces):
        wires.arrived(back[0][p], from_beside.at[0, piece], beside)
        wires.arrived(back[2][p], from_across.at[piece], across)
        second_grad = (
            partial[0, piece, :].astype(jnp.float32)
            + from_beside[0, piece, :].astype(jnp.float32)
            + from_across[piece, :].astype(jnp.float32)
        )
        normed, inverse = center_scale(middle[piece, :])
        own = sequence_grad[0, piece, :].astype(jnp.float32)
        total = own + norm_backward(second_grad, normed, inverse, vectors[2:3, :])
        middle_grad[piece, :] = total
        for k, term in enumerate((second_grad * normed, second_grad, total, own)):
            sums[k] = sums[k] + jnp.sum(term, axis=0, keepdims=True)
        into_attended = dot_rows(total.astype(low), merge[...]).astype(low)
        for k in range(4):
            attended_grad[k, piece, :] = into_attended[:, k * group_width : (k + 1) * group_width]
    vector_sums[...] = jnp.concatenate(sums, axis=0)
    into_merge = contract_rows(middle_grad[...].astype(low), attended_rows[...]).astype(low)
    for k in range(4):
        merge_sum[k] = into_merge[:, k * group_width : (k + 1) * group_width]
    for which in groups:
        which.bit_add()
    for k, source, device in pending:
        wires.sent(k, source, device)


def middle_pallas(attended_rows, merge, tokens, vectors, expand, reduce, sequence_grad, late):
    rows, width = tokens.shape
    units = expand.shape[0] * (expand.shape[1] if late else 1)
    data_count = lax.axis_size("dp")
    unit_block = (units // data_count, width)
    first_slots = data_count // 4
    low, wide = jnp.bfloat16, jnp.float32
    inside = pl.BlockSpec(memory_space=pltpu.VMEM)
    shapes = (
        ((rows, width), wide),
        ((rows, width), low),
        ((rows, width), wide),
        ((4, rows, width // 4), low),
        ((data_count,) + unit_block, low),
        ((data_count,) + unit_block, low),
        ((4, width, width // 4), low),
        ((4, width), wide),
    )
    copies = 16 + 4 * first_slots
    return pl.pallas_call(
        functools.partial(middle_kernel, data_count, late),
        out_shape=tuple(jax.ShapeDtypeStruct(*shape) for shape in shapes),
        in_specs=[inside] * 4 + [pl.BlockSpec(memory_space=pl.ANY) if late else inside] * 2 + [inside],
        out_specs=(inside,) * 8,
        scratch_shapes=[
            pltpu.VMEM((4, rows, width), low),
            pltpu.VMEM((rows, width), wide),
            pltpu.VMEM((4, rows, units), low),
            pltpu.VMEM((4, rows, units), low),
            pltpu.VMEM((4, rows, width), low),
            pltpu.VMEM((4, rows, width), low),
            pltpu.VMEM((2, rows, width), low),
            pltpu.VMEM((2, rows, width), low),
            pltpu.VMEM((rows, width), low),
            pltpu.VMEM((first_slots, 2) + unit_block, low),
            pltpu.VMEM((first_slots, 2) + unit_block, low),
            pltpu.VMEM((data_count,) + unit_block, low),
            pltpu.VMEM((data_count,) + unit_block, low),
            pltpu.SemaphoreType.DMA((copies,)),
            pltpu.SemaphoreType.DMA((copies,)),
            pltpu.SemaphoreType.DMA((2 * first_slots,)),
        ],
        compiler_params=pltpu.CompilerParams(
            vmem_limit_bytes=VMEM_LIMIT, collective_id=2, has_side_effects=True
        ),
        cost_estimate=pl.CostEstimate(
            flops=52 * rows * width * units, bytes_accessed=20 * rows * width, transcendentals=rows * units * 8
        ),
        name="middle",
    )(attended_rows, merge, tokens, vectors, expand, reduce, sequence_grad)


class Group:
    def __init__(self, work, arrived, last, order, place, wires, begin, first=0):
        self.work, self.got, self.last, self.order = work, arrived, last, order
        self.data, self.tensor = place
        self.pair = (self.data >> 1) * 2
        self.core, self.half = self.data & 1, self.tensor >> 1
        self.wires, self.begin = wires, begin
        self.left = [
            o for o in range(0, work.shape[0], 2) if not any(o & bit for bit in order[:first])
        ]
        self.slot, self.flight, self.step = 0, [], first

    def bit_send(self):
        bit = self.order[self.step]
        self.flight = []
        for offset in [o for o in self.left if o & bit]:
            number = self.wires.number()
            target = (self.data ^ bit, self.tensor)
            self.begin(number, self.work.at[pl.ds(self.pair ^ offset, 2)], self.got.at[self.slot], target)
            self.flight.append((number, self.slot, offset ^ bit, target))
            self.slot += 1
        self.left = [o for o in self.left if not o & bit]
        self.step += 1

    def bit_add(self):
        for number, slot, offset, target in self.flight:
            self.wires.arrived(number, self.got.at[slot], target)
            here = pl.ds(self.pair ^ offset, 2)
            total = self.work[here].astype(jnp.float32) + self.got[slot].astype(jnp.float32)
            self.work[here] = total.astype(self.work.dtype)

    def own_send(self):
        group = 2 * (self.tensor & 1) + self.core
        self.numbers = [self.wires.number() for _ in range(4)]
        for c in (0, 1):
            owner = (self.pair + c, group)
            itself = (owner[0] == self.data) & (owner[1] == self.tensor)
            for b in (0, 1):
                self.begin(
                    self.numbers[2 * c + b],
                    self.work.at[self.pair + c],
                    self.last.at[b],
                    owner,
                    jnp.logical_not(itself) & (self.half == b),
                )

    def own_sum(self):
        for b in (0, 1):
            source = (self.pair + (self.tensor & 1), (self.tensor >> 1) + 2 * b)
            itself = (source[0] == self.data) & (source[1] == self.tensor)
            for c in (0, 1):

                @pl.when(jnp.logical_not(itself) & (self.core == c))
                def _():
                    self.wires.arrived(self.numbers[2 * c + b], self.last.at[b], source)

            @pl.when(itself)
            def _():
                self.last[b] = self.work[self.data]

        return self.last[0].astype(jnp.float32) + self.last[1].astype(jnp.float32)


class ChipSum:
    def __init__(
        self, array, result, arrived, last, base, size, order, place, tensor_count, wires, begin
    ):
        self.array, self.result, self.got, self.last = array, result, arrived, last
        self.start, self.size, self.order = base, size, order
        self.data, self.tensor = place
        self.count, self.wires, self.begin = tensor_count, wires, begin
        self.slot, self.step, self.trail = 0, 0, []

    def bit_send(self):
        bit = self.order[self.step]
        self.step += 1
        half = self.size // 2
        mine = (self.data & bit) // bit
        keep, give = self.start + mine * half, self.start + (1 - mine) * half
        number = self.wires.number()
        target = (self.data ^ bit, self.tensor)
        there = self.got.at[pl.ds(self.slot, half)]
        self.begin(number, self.array.at[pl.ds(give, half)], there, target)
        self.trail.append((bit, keep, give, half))
        self.flight = (number, self.slot, half, target)
        self.start, self.size = keep, half
        self.slot += half

    def bit_add(self):
        number, slot, half, target = self.flight
        self.wires.arrived(number, self.got.at[pl.ds(slot, half)], target)
        here = pl.ds(self.start, half)
        self.array[here] = self.array[here] + self.got[pl.ds(slot, half)]

    def line_send(self):
        self.spread = self.size % self.count == 0
        self.portion = self.size // self.count if self.spread else self.size
        self.flight = []
        for k in range(1, self.count):
            number = self.wires.number()
            peer = lax.rem(self.tensor + k, self.count)
            at = self.start + peer * self.portion if self.spread else self.start
            source = self.array.at[pl.ds(at, self.portion)]
            self.begin(number, source, self.last.at[k - 1], (self.data, peer))
            origin = lax.rem(self.tensor + self.count - k, self.count)
            self.flight.append((number, k - 1, (self.data, origin)))

    def line_add(self):
        at = self.start + self.tensor * self.portion if self.spread else self.start
        here = pl.ds(at, self.portion)
        for number, slot, origin in self.flight:
            self.wires.arrived(number, self.last.at[slot], origin)
        total = self.array[here]
        for number, slot, origin in self.flight:
            total = total + self.last[slot]
        self.result[here] = total

    def line_back(self):
        self.flight = []
        if self.spread:
            here = pl.ds(self.start + self.tensor * self.portion, self.portion)
            for k in range(1, self.count):
                number = self.wires.number()
                peer = lax.rem(self.tensor + k, self.count)
                self.begin(number, self.result.at[here], self.result.at[here], (self.data, peer))
                origin = lax.rem(self.tensor + self.count - k, self.count)
                there = pl.ds(self.start + origin * self.portion, self.portion)
                self.flight.append((number, there, (self.data, origin)))

    def bit_back(self):
        bit, keep, give, half = self.trail.pop()
        number = self.wires.number()
        target = (self.data ^ bit, self.tensor)
        here = pl.ds(keep, half)
        self.begin(number, self.result.at[here], self.result.at[here], target)
        self.flight = [(number, pl.ds(give, half), target)]
        self.start = jnp.minimum(keep, give)
        self.size = 2 * half

    def back_wait(self):
        for number, there, target in self.flight:
            self.wires.arrived(number, self.result.at[there], target)


def split_low(values):
    high = values.astype(jnp.bfloat16)
    return high, (values - high.astype(jnp.float32)).astype(jnp.bfloat16)


def back_kernel(
    data_count,
    tensor_count,
    attended,
    attended_grad,
    query_aux,
    key_aux,
    value_aux,
    first_full,
    heads_weight,
    expand_sum,
    reduce_sum,
    merge_sum,
    layer_base,
    layer_across,
    expand_momentum,
    reduce_momentum,
    tokens,
    middle_grad,
    vectors,
    vector_sums,
    heads_momentum,
    merge_momentum,
    expand_out,
    reduce_out,
    merge_out,
    heads_out,
    input_rows,
    input_low,
    vector_part,
    output_rows,
    gram,
    both,
    small_gram,
    upstream,
    grad_aux,
    key_turned,
    query_total,
    projected_grad,
    first_parts,
    first_beside,
    first_across,
    layer_got,
    expand_work,
    expand_got,
    expand_last,
    reduce_work,
    reduce_got,
    reduce_last,
    merge_work,
    merge_core,
    merge_line,
    merge_got,
    merge_last,
    heads_work,
    heads_got,
    heads_last,
    side,
    side_got,
    gram_work,
    gram_got,
    gram_last,
    send,
    receive,
    local,
):
    low = jnp.bfloat16
    members, rows, group_width = attended.shape
    head_local = group_width // HEAD_DIM
    seq_len = members * rows
    data, tensor = lax.axis_index("dp"), lax.axis_index("tensor")
    place = (data, tensor)
    core = data & 1
    group = 2 * (tensor & 1) + core
    wires = Wires(send, receive)
    beside, across, diagonal = (data ^ 1, tensor), (data, tensor ^ 1), (data ^ 1, tensor ^ 1)
    peers = [None, beside, across, diagonal]
    pending = []

    def begin(k, source, target, device, when=None):
        if when is None:
            wires.start(k, source, target, device)
        else:

            @pl.when(when)
            def _():
                wires.start(k, source, target, device)

        pending.append((k, source, device, when))

    def finish_sends():
        for k, source, device, when in pending:
            if when is None:
                wires.sent(k, source, device)
            else:

                @pl.when(when)
                def _():
                    wires.sent(k, source, device)

        pending.clear()

    copies = []
    for k, (source, target) in enumerate(
        ((expand_sum, expand_work), (reduce_sum, reduce_work), (merge_sum, merge_work))
    ):
        copies.append(pltpu.make_async_copy(source, target, local.at[k]))
        copies[-1].start()
    greet(column_and_plane(data, tensor, data_count, tensor_count))

    grad_numbers = {}
    for member in (2, 3, 1):
        grad_numbers[member] = wires.number()
        begin(
            grad_numbers[member],
            attended_grad.at[group ^ member],
            upstream.at[member],
            peers[member],
        )
    for copy in copies:
        copy.wait()
    bits = low_rank_bits(data_count)
    own_merge = merge_work.at[group]
    expand_group = Group(expand_work, expand_got, expand_last, bits[::-1], place, wires, begin, 1)
    reduce_group = Group(reduce_work, reduce_got, reduce_last, bits, place, wires, begin, 1)
    merge_group = Group(own_merge, merge_got, merge_last, bits[::-1], place, wires, begin)
    heads_group = Group(heads_work, heads_got, heads_last, bits, place, wires, begin)
    merge_numbers = [wires.number() for _ in range(3)]
    begin(merge_numbers[0], merge_work.at[group ^ 1], merge_core.at[0], beside)
    begin(merge_numbers[1], merge_work.at[group ^ 3], merge_core.at[1], beside)
    if len(bits) > 1:
        expand_group.bit_send()
        reduce_group.bit_send()
    layer_number = wires.number()
    upstream[0] = attended_grad[group]

    block = min(KEY_BLOCK, rows)
    lane = lax.broadcasted_iota(jnp.int32, (block, AUX), 1)
    blank = jnp.zeros((block, AUX - HEAD_DIM), jnp.float32)
    steps = rows // block

    def prepare(member):
        def one(step, carry):
            inside = pl.ds(pl.multiple_of(step * block, block), block)
            at_rows = pl.ds(pl.multiple_of(member * rows + step * block, block), block)
            gradient = upstream[member, inside, :].astype(jnp.float32)
            product = gradient * attended[member, inside, :].astype(jnp.float32)
            for head in range(head_local):
                columns = slice(head * HEAD_DIM, (head + 1) * HEAD_DIM)
                row_dot = jnp.sum(product[:, columns], axis=1, keepdims=True)
                first = row_dot.astype(low).astype(jnp.float32)
                wide = jnp.concatenate([gradient[:, columns], blank], axis=1)
                wide = jnp.where(lane == HEAD_DIM + 1, first, wide)
                wide = jnp.where(lane == HEAD_DIM + 2, row_dot - first, wide)
                grad_aux[head, at_rows, :] = wide.astype(low)
                key_turned[head, :, at_rows] = key_aux[head, at_rows, :].T[:HEAD_DIM]
            return carry

        lax.fori_loop(0, steps, one, 0)

    prepare(0)
    for member in (1, 2, 3):
        wires.arrived(grad_numbers[member], upstream.at[member], peers[member])
        prepare(member)
    query_total[...] = jnp.zeros_like(query_total)

    def back(step, carry):
        at_rows = pl.ds(pl.multiple_of(step * block, block), block)
        for head in range(head_local):
            scores = contract_cols(key_aux[head, at_rows, :], query_aux[head])
            chances = jnp.exp(scores)
            chance_grad = contract_cols(value_aux[head, at_rows, :], grad_aux[head])
            score_grad = (chances * chance_grad).astype(low)
            value_grad = dot_rows(chances.astype(low), grad_aux[head])
            key_grad = dot_rows(score_grad, query_aux[head])
            query_total[head] += dot_rows(key_turned[head, :, at_rows], score_grad)
            at = 3 * head * HEAD_DIM
            two = jnp.concatenate([key_grad[:, :HEAD_DIM], value_grad[:, :HEAD_DIM]], axis=1)
            projected_grad[at_rows, at + HEAD_DIM : at + 3 * HEAD_DIM] = two.astype(low)
        return carry

    eighth = seq_len // block // 8

    def back_eighths(start, stop):
        lax.fori_loop(start * eighth, stop * eighth, back, 0)

    for which in (expand_group, reduce_group):
        for k in range(1, len(bits)):
            which.bit_add()
            if k + 1 < len(bits):
                which.bit_send()
        which.own_send()
    wires.arrived(merge_numbers[0], merge_core.at[0], beside)
    wires.arrived(merge_numbers[1], merge_core.at[1], beside)
    for k in (0, 1):
        here = group ^ (2 * k)
        total = merge_work[here].astype(jnp.float32) + merge_core[k].astype(jnp.float32)
        merge_work[here] = total.astype(low)
    begin(merge_numbers[2], merge_work.at[group ^ 2], merge_line, across)

    back_eighths(0, 3)
    expand_out[...] = expand_group.own_sum()
    reduce_out[...] = reduce_group.own_sum()
    expand_part = momentum_decay * expand_momentum[...] + expand_out[...]
    reduce_part = momentum_decay * reduce_momentum[...] + reduce_out[...]
    first_core = core == 0
    side[0] = jnp.where(first_core, expand_part, reduce_part)
    side[1] = jnp.where(first_core, reduce_part, expand_part)
    side_number = wires.number()
    begin(side_number, side.at[1], side_got, beside)
    wires.arrived(merge_numbers[2], merge_line, across)
    total = merge_work[group].astype(jnp.float32) + merge_line[...].astype(jnp.float32)
    merge_work[group] = total.astype(low)
    merge_group.bit_send()

    wires.arrived(side_number, side_got, beside)
    part_rows = side_got.shape[0]
    both[:part_rows, :] = side[0]
    both[part_rows:, :] = side_got[...]
    width = both.shape[1]
    high, rest = split_low(both[...])
    at = 0
    for k in range(0, width, SIDE):
        span = width - k
        part = contract_rows(high[:, k : k + SIDE], high[:, k:])
        part = part + contract_rows(high[:, k : k + SIDE], rest[:, k:])
        part = part + contract_rows(rest[:, k : k + SIDE], high[:, k:])
        gram_work[:, :, at : at + span] = part.reshape(SIDE // 8, 8, span)
        at += span
    slots = SIDE // 16
    halves = [
        ChipSum(
            gram_work,
            gram,
            gram_got.at[h],
            gram_last.at[h],
            h * slots,
            slots,
            order,
            place,
            tensor_count,
            wires,
            begin,
        )
        for h, order in enumerate((bits, bits[::-1]))
    ]
    for half in halves:
        half.bit_send()
    begin(layer_number, layer_across, layer_got, across)

    back_eighths(3, 5)
    for half in halves:
        half.bit_add()
        for _ in range(2, len(bits)):
            half.bit_send()
            half.bit_add()
        half.bit_send()
    merge_group.bit_add()
    merge_group.bit_send()

    back_eighths(5, 6)
    for half in halves:
        half.bit_add()
        half.line_send()
    merge_group.bit_add()
    for _ in range(2, len(bits)):
        merge_group.bit_send()
        merge_group.bit_add()
    merge_group.own_send()

    back_eighths(6, 8)
    for half in halves:
        half.line_add()
        half.line_back()

    def finish(step, carry):
        at_rows = pl.ds(pl.multiple_of(step * block, block), block)
        for head in range(head_local):
            query_grad = query_total[head, :, at_rows].T * HEAD_DIM**-0.5
            at = 3 * head * HEAD_DIM
            projected_grad[at_rows, at : at + HEAD_DIM] = query_grad.astype(low)
        return carry

    lax.fori_loop(0, seq_len // block, finish, 0)
    first_numbers = [wires.number() for _ in range(3)]

    def first_part(member):
        at_rows = pl.ds(member * rows, rows)
        part = contract_cols(projected_grad[at_rows, :], heads_weight[...])
        first_parts[member] = part.astype(low)

    heads_work[...] = (
        contract_rows(first_full[...], projected_grad[...]).reshape(heads_work.shape).astype(low)
    )
    heads_group.bit_send()
    for k, member in enumerate((3, 1)):
        first_part(member)
        begin(first_numbers[k], first_parts.at[member], first_beside.at[k], beside)
    first_part(2)
    wires.arrived(first_numbers[0], first_beside.at[0], beside)
    total = first_parts[2].astype(jnp.float32) + first_beside[0].astype(jnp.float32)
    first_parts[2] = total.astype(low)
    for half in halves:
        half.back_wait()
        half.bit_back()
    begin(first_numbers[2], first_parts.at[2], first_across, across)
    heads_group.bit_add()
    for _ in range(2, len(bits)):
        heads_group.bit_send()
        heads_group.bit_add()
    heads_group.bit_send()
    first_part(0)
    for _ in range(1, len(bits)):
        for half in halves:
            half.back_wait()
            half.bit_back()
    heads_group.bit_add()
    heads_group.own_send()
    merge_out[...] = merge_group.own_sum()
    wires.arrived(layer_number, layer_got, across)
    output_rows[...] = (layer_base[...] + layer_got[...].astype(jnp.float32)).astype(low)
    wires.arrived(first_numbers[1], first_beside.at[1], beside)
    wires.arrived(first_numbers[2], first_across, across)
    sums = [0.0, 0.0]
    for p in range(2):
        piece = pl.ds(p * (rows // 2), rows // 2)
        first_grad = (
            first_parts[0, piece, :].astype(jnp.float32)
            + first_beside[1, piece, :].astype(jnp.float32)
            + first_across[piece, :].astype(jnp.float32)
        )
        normed, inverse = center_scale(tokens[piece, :].astype(jnp.float32))
        total = middle_grad[piece, :] + norm_backward(first_grad, normed, inverse, vectors[0:1, :])
        input_rows[piece, :] = total
        input_low[piece, :] = total.astype(low)
        sums[0] = sums[0] + jnp.sum(first_grad * normed, axis=0, keepdims=True)
        sums[1] = sums[1] + jnp.sum(first_grad, axis=0, keepdims=True)
    vector_part[...] = jnp.concatenate(sums + [vector_sums[...]], axis=0)
    heads_out[...] = heads_group.own_sum()
    heads_part = momentum_decay * heads_momentum[...] + heads_out[...]
    merge_part = momentum_decay * merge_momentum[...].T + merge_out[...]
    blocks = [
        side_part[:, k : k + HEAD_DIM]
        for side_part in (heads_part, merge_part)
        for k in range(0, side_part.shape[1], HEAD_DIM)
    ]
    quarter = len(blocks) // 4
    for h in range(2):
        for k in range(quarter):
            first, second = blocks[2 * h * quarter + k], blocks[(2 * h + 1) * quarter + k]
            grams = []
            for block_part in (first, second):
                top, rest = split_low(block_part)
                grams.append(
                    contract_rows(top, top) + (contract_rows(top, rest) + contract_rows(rest, top))
                )
            here = slice(k * HEAD_DIM, (k + 1) * HEAD_DIM)
            small_gram[h, here, :] = jnp.concatenate(grams, axis=1)
    for half in halves:
        half.back_wait()
    finish_sends()


def back_pallas(
    attended,
    attended_grad,
    query_aux,
    key_aux,
    value_aux,
    first_full,
    heads_weight,
    expand_sum,
    reduce_sum,
    merge_sum,
    layer_base,
    layer_across,
    expand_momentum,
    reduce_momentum,
    tokens,
    middle_grad,
    vectors,
    vector_sums,
    heads_momentum,
    merge_momentum,
):
    data_count, tensor_count = lax.axis_size("dp"), lax.axis_size("tensor")
    members, rows, group_width = attended.shape
    head_local = group_width // HEAD_DIM
    seq_len = members * rows
    low, wide = jnp.bfloat16, jnp.float32
    width, columns = heads_weight.shape
    unit_block = expand_sum.shape[1:]
    merge_block = merge_sum.shape[2:]
    heads_block = (width // data_count, columns)
    packed = sum(width - k for k in range(0, width, SIDE))
    inside = pl.BlockSpec(memory_space=pltpu.VMEM)
    outs = (
        (unit_block, wide),
        (unit_block, wide),
        (merge_block, wide),
        (heads_block, wide),
        ((rows, width), wide),
        ((rows, width), low),
        (vectors.shape, wide),
        ((rows, width), low),
        ((SIDE // 8, 8, packed), wide),
        ((2 * unit_block[0], unit_block[1]), wide),
        ((2, head_local * HEAD_DIM, 2 * HEAD_DIM), wide),
    )
    steps = data_count // 2 - 1
    later = max(data_count // 4 - 1, 1)
    slots = SIDE // 16
    left = slots // (data_count // 2)
    portion = left // tensor_count if left % tensor_count == 0 else left
    scratch = []
    for shape, kind in (
        ((members, rows, group_width), low),
        ((head_local, seq_len, AUX), low),
        ((head_local, HEAD_DIM, seq_len), low),
        ((head_local, HEAD_DIM, seq_len), wide),
        ((seq_len, columns), low),
        ((members, rows, width), low),
        ((2, rows, width), low),
        ((rows, width), low),
        ((rows, width), low),
        ((data_count,) + unit_block, low),
        ((later, 2) + unit_block, low),
        ((2,) + unit_block, low),
        ((data_count,) + unit_block, low),
        ((later, 2) + unit_block, low),
        ((2,) + unit_block, low),
        (merge_sum.shape, low),
        ((2, data_count) + merge_block, low),
        ((data_count,) + merge_block, low),
        ((steps, 2) + merge_block, low),
        ((2,) + merge_block, low),
        ((data_count,) + heads_block, low),
        ((steps, 2) + heads_block, low),
        ((2,) + heads_block, low),
        ((2,) + unit_block, wide),
        (unit_block, wide),
        ((SIDE // 8, 8, packed), wide),
        ((2, slots, 8, packed), wide),
        ((2, tensor_count - 1, portion, 8, packed), wide),
    ):
        scratch.append(pltpu.VMEM(shape, kind))
    copies = 3 + 3 + 1 + 4 * (steps + 4) + 1 + 3
    copies += 2 * (2 * (data_count // 2).bit_length() + 2 * tensor_count)
    return pl.pallas_call(
        functools.partial(back_kernel, data_count, tensor_count),
        out_shape=tuple(jax.ShapeDtypeStruct(*out) for out in outs),
        in_specs=[inside] * 7 + [pl.BlockSpec(memory_space=pl.ANY)] * 3 + [inside] * 10,
        out_specs=(inside,) * len(outs),
        scratch_shapes=scratch
        + [
            pltpu.SemaphoreType.DMA((copies,)),
            pltpu.SemaphoreType.DMA((copies,)),
            pltpu.SemaphoreType.DMA((3,)),
        ],
        compiler_params=pltpu.CompilerParams(
            vmem_limit_bytes=VMEM_LIMIT, collective_id=3, has_side_effects=True
        ),
        cost_estimate=pl.CostEstimate(
            flops=10 * head_local * seq_len * seq_len * AUX,
            bytes_accessed=10 * seq_len * width,
            transcendentals=head_local * seq_len * seq_len,
        ),
        name="back",
    )(
        attended,
        attended_grad,
        query_aux,
        key_aux,
        value_aux,
        first_full,
        heads_weight,
        expand_sum,
        reduce_sum,
        merge_sum,
        layer_base,
        layer_across,
        expand_momentum,
        reduce_momentum,
        tokens,
        middle_grad,
        vectors,
        vector_sums,
        heads_momentum,
        merge_momentum,
    )


def three_pass(left, right):
    return dot_rows(left[0], right[0]) + (dot_rows(left[0], right[1]) + dot_rows(left[1], right[0]))


def last_kernel(
    data_count,
    tensor_count,
    gram,
    both,
    small_gram,
    vector_part,
    output_rows,
    input_rows,
    ortho_mine,
    ortho_other,
    small_chain,
    vector_sum,
    moved_output,
    moved_input,
    square,
    gram_high,
    gram_low,
    factor_high,
    factor_low,
    turn_high,
    turn_low,
    part,
    theirs,
    small_got,
    small_sum,
    small_mine,
    vector_got,
    vector_half,
    vector_line,
    send,
    receive,
):
    size = part.shape[1]
    rows = part.shape[0] // 2
    data, tensor = lax.axis_index("dp"), lax.axis_index("tensor")
    beside, away = (data ^ 1, tensor), (data ^ 1, tensor ^ 2)
    moved = jnp.logical_not((data & 1) == (tensor >> 1))
    wires = Wires(send, receive)
    pending = []

    def begin(k, source, target, device, when=None):
        if when is None:
            wires.start(k, source, target, device)
        else:

            @pl.when(when)
            def _():
                wires.start(k, source, target, device)

        pending.append((k, source, device, when))

    greet(column_and_plane(data, tensor, data_count, tensor_count))
    bits = [1] + low_rank_bits(data_count)
    hops = [(wires.number(), wires.number()) for _ in bits]

    core = data & 1

    def hop_send(k):
        peer = (data ^ bits[k], tensor)
        begin(hops[k][0], vector_half.at[k], vector_got.at[k], peer)
        small = small_gram.at[1 - core] if k == 0 else small_sum.at[k]
        begin(hops[k][1], small, small_got.at[k], peer)

    def hop_add(k):
        peer = (data ^ bits[k], tensor)
        wires.arrived(hops[k][0], vector_got.at[k], peer)
        wires.arrived(hops[k][1], small_got.at[k], peer)
        vector_half[k + 1] = vector_half[k] + vector_got[k]
        small = small_gram[core] if k == 0 else small_sum[k]
        small_sum[k + 1] = small + small_got[k]

    vector_half[0] = vector_part[...]
    hop_send(0)
    input_number, output_number = wires.number(), wires.number()
    begin(input_number, input_rows, moved_input, away, moved)
    begin(output_number, output_rows, moved_output, away, moved)

    identity = (
        lax.broadcasted_iota(jnp.int32, (SIDE, SIDE), 0)
        == lax.broadcasted_iota(jnp.int32, (SIDE, SIDE), 1)
    ).astype(jnp.float32)
    blocks = size // SIDE
    trace = 0.0
    at = 0
    for i in range(blocks):
        span = size - i * SIDE
        strip = gram[:, :, at : at + span].reshape(SIDE, span)
        trace = trace + jnp.sum(strip[:, :SIDE] * identity)
        at += span
    factor = 1.0 / (jnp.sqrt(trace) + newton_epsilon)

    def keep(strip, i, high, low):
        top, rest = split_low(strip)
        high[i * SIDE : (i + 1) * SIDE, i * SIDE :] = top
        low[i * SIDE : (i + 1) * SIDE, i * SIDE :] = rest
        for j in range(i + 1, blocks):
            turned = strip[:, (j - i) * SIDE : (j - i + 1) * SIDE].T
            top, rest = split_low(turned)
            high[j * SIDE : (j + 1) * SIDE, i * SIDE : (i + 1) * SIDE] = top
            low[j * SIDE : (j + 1) * SIDE, i * SIDE : (i + 1) * SIDE] = rest

    at = 0
    for i in range(blocks):
        span = size - i * SIDE
        strip = gram[:, :, at : at + span].reshape(SIDE, span) * (factor * factor)
        square[i * SIDE : (i + 1) * SIDE, i * SIDE :] = strip
        keep(strip, i, gram_high, gram_low)
        at += span
    part[...] = both[...] * factor

    def strip_of(left, right, i):
        here = slice(i * SIDE, (i + 1) * SIDE)
        return three_pass(
            (left[0][here, :], left[1][here, :]), (right[0][:, i * SIDE :], right[1][:, i * SIDE :])
        )

    gram_pair, factor_pair = (gram_high, gram_low), (factor_high, factor_low)

    def wide_factor():
        for i in range(blocks):
            here = slice(i * SIDE, (i + 1) * SIDE)
            strip = newton_cubic * square[here, i * SIDE :] + newton_quintic * strip_of(
                gram_pair, gram_pair, i
            )
            first = strip[:, :SIDE] + newton_linear * identity
            strip = first if i == blocks - 1 else jnp.concatenate([first, strip[:, SIDE:]], axis=1)
            keep(strip, i, factor_high, factor_low)

    def wide_part():
        part[...] = three_pass(split_low(part[...]), (factor_high[...], factor_low[...]))

    def wide_gram():
        for i in range(blocks):
            keep(strip_of(gram_pair, factor_pair, i), i, turn_high, turn_low)
        for i in range(blocks):
            strip = strip_of((turn_high, turn_low), factor_pair, i)
            square[i * SIDE : (i + 1) * SIDE, i * SIDE :] = strip
            keep(strip, i, gram_high, gram_low)

    groups, head_size = small_gram.shape[1] // HEAD_DIM, HEAD_DIM
    double = 2 * head_size
    diagonal = identity[:double, :double]
    left = lax.broadcasted_iota(jnp.int32, (head_size, double), 1) < head_size
    small = {}

    def small_start():
        total = small_sum[len(bits)]
        small["gram"], small["chain"], small["scale"] = [], [], []
        for b in range(groups):
            pair = total[b * head_size : (b + 1) * head_size]
            full = jnp.concatenate([jnp.where(left, pair, 0.0), jnp.where(left, 0.0, pair)], axis=0)
            column = jnp.sum(full * diagonal, axis=1, keepdims=True)
            scales = []
            for k in range(2):
                norm = jnp.sqrt(jnp.sum(column[k * head_size : (k + 1) * head_size]))
                scales.append(jnp.full((head_size, 1), 1.0 / (norm + newton_epsilon), jnp.float32))
            scale = jnp.concatenate(scales, axis=0)
            small["gram"].append(full * (scale * scale))
            small["scale"].append(scale)
            small["chain"].append(None)

    def small_step(last):
        for b in range(groups):
            here = split_low(small["gram"][b])
            step = newton_linear * diagonal + newton_cubic * small["gram"][b]
            step = step + newton_quintic * three_pass(here, here)
            step_pair = split_low(step)
            before = small["chain"][b]
            small["chain"][b] = step if before is None else three_pass(split_low(before), step_pair)
            if not last:
                next_gram = three_pass(here, step_pair)
                small["gram"][b] = three_pass(split_low(next_gram), step_pair)

    def small_end():
        for b in range(groups):
            chain = small["chain"][b] * small["scale"][b]
            here = slice(b * head_size, (b + 1) * head_size)
            small_mine[here, :] = jnp.where(left, chain[:head_size], chain[head_size:])
        begin(small_number, small_mine, small_chain.at[core], beside)
        small_chain[core] = small_mine[...]

    small_number = wires.number()
    line_numbers = [wires.number() for _ in range(tensor_count - 1)]
    side_number = wires.number()
    for step in range(NEWTON_STEPS):
        wide_factor()
        if step == 1:
            hop_add(0)
            hop_send(1)
        elif step == 3:
            hop_add(2)
            for k in range(3, len(bits)):
                hop_send(k)
                hop_add(k)
            for k in range(1, tensor_count):
                peer = lax.rem(tensor + k, tensor_count)
                begin(line_numbers[k - 1], vector_half.at[len(bits)], vector_line.at[k - 1], (data, peer))
            small_start()
            small_step(False)
        elif step == 4:
            small_step(False)
        wide_part()
        if step < NEWTON_STEPS - 1:
            wide_gram()
        if step == 1:
            hop_add(1)
            hop_send(2)
        elif step == 3:
            small_step(False)
    small_step(False)
    ortho_mine[...] = part[:rows, :]
    theirs[...] = part[rows:, :]
    begin(side_number, theirs, ortho_other, beside)
    small_step(True)
    small_end()
    total = vector_half[len(bits)]
    for k in range(1, tensor_count):
        origin = lax.rem(tensor + tensor_count - k, tensor_count)
        wires.arrived(line_numbers[k - 1], vector_line.at[k - 1], (data, origin))
        total = total + vector_line[k - 1]
    vector_sum[...] = total

    @pl.when(moved)
    def _():
        wires.arrived(input_number, moved_input, away)
        wires.arrived(output_number, moved_output, away)

    wires.arrived(side_number, ortho_other, beside)
    wires.arrived(small_number, small_chain.at[1 - core], beside)
    for k, source, device, when in pending:
        if when is None:
            wires.sent(k, source, device)
        else:

            @pl.when(when)
            def _():
                wires.sent(k, source, device)


def last_pallas(gram, both, small_gram, vector_part, output_rows, input_rows):
    data_count, tensor_count = lax.axis_size("dp"), lax.axis_size("tensor")
    low, wide = jnp.bfloat16, jnp.float32
    size = both.shape[1]
    rows = both.shape[0] // 2
    hops = data_count.bit_length() - 1
    inside = pl.BlockSpec(memory_space=pltpu.VMEM)
    outs = (
        ((rows, size), wide),
        ((rows, size), wide),
        (small_gram.shape, wide),
        (vector_part.shape, wide),
        (output_rows.shape, low),
        (input_rows.shape, low),
    )
    scratch = [
        pltpu.VMEM(shape, kind)
        for shape, kind in (
            ((size, size), wide),
            ((size, size), low),
            ((size, size), low),
            ((size, size), low),
            ((size, size), low),
            ((size, size), low),
            ((size, size), low),
            (both.shape, wide),
            ((rows, size), wide),
            ((hops,) + small_gram.shape[1:], wide),
            ((hops + 1,) + small_gram.shape[1:], wide),
            (small_gram.shape[1:], wide),
            ((hops,) + vector_part.shape, wide),
            ((hops + 1,) + vector_part.shape, wide),
            ((tensor_count - 1,) + vector_part.shape, wide),
        )
    ]
    copies = 2 * hops + 3 + tensor_count
    return pl.pallas_call(
        functools.partial(last_kernel, data_count, tensor_count),
        out_shape=tuple(jax.ShapeDtypeStruct(*out) for out in outs),
        in_specs=[inside] * 6,
        out_specs=(inside,) * len(outs),
        scratch_shapes=scratch
        + [pltpu.SemaphoreType.DMA((copies,)), pltpu.SemaphoreType.DMA((copies,))],
        compiler_params=pltpu.CompilerParams(
            vmem_limit_bytes=VMEM_LIMIT, collective_id=4, has_side_effects=True
        ),
        cost_estimate=pl.CostEstimate(
            flops=90 * size * size * size, bytes_accessed=20 * size * size, transcendentals=0
        ),
        name="last",
    )(gram, both, small_gram, vector_part, output_rows, input_rows)


SIDE = 256


def swap_bit(values, axis_name, bit):
    count = lax.axis_size(axis_name)
    return lax.ppermute(values, axis_name, [(i, i ^ bit) for i in range(count)])


def data_bits():
    return [1 << k for k in range(1, lax.axis_size("dp").bit_length() - 1)]


def has_bit(index, bit):
    return (index & bit) != 0


def gather_bits_absolute(block, bits):
    index = lax.axis_index("dp")
    for bit in bits:
        other = swap_bit(block, "dp", bit)
        mine = has_bit(index, bit)
        block = jnp.concatenate(
            [jnp.where(mine, other, block), jnp.where(mine, block, other)], axis=0
        )
    return block


def pair_permute(values, where_to):
    data_count, tensor_count = lax.axis_size("dp"), lax.axis_size("tensor")
    moves = []
    for i in range(data_count):
        for j in range(tensor_count):
            target = where_to(i, j)
            if target is not None:
                moves.append((i * tensor_count + j, target[0] * tensor_count + target[1]))
    return lax.ppermute(values, ("dp", "tensor"), moves)


def exchange_home(values):
    return pair_permute(
        values, lambda i, j: (i ^ 1, j ^ 2) if (i & 1) != (j >> 1) else None
    )


def gather_head_group(shard):
    first = []
    for core in (0, 1):
        got = []
        for half in (0, 1):
            got.append(
                pair_permute(
                    shard,
                    lambda i, j: (i - core + (j & 1), (j >> 1) + 2 * half)
                    if (i & 1) == core
                    else None,
                )
            )
        first.append(jnp.where(lax.axis_index("tensor") >= 2, got[1], got[0]))
    return gather_bits_absolute(jnp.concatenate(first, axis=0), data_bits())


def per_device(
    tokens,
    segment_ids,
    out_grad,
    heads_weight,
    merge_weight,
    expand_weight,
    reduce_weight,
    heads_momentum,
    merge_momentum,
    expand_momentum,
    reduce_momentum,
    heads_average,
    merge_average,
    expand_average,
    reduce_average,
    vectors,
    vector_momentum,
    vector_average,
):
    low = jnp.bfloat16
    tensor_count = lax.axis_size("tensor")
    data_count = lax.axis_size("dp")
    tensor_index = lax.axis_index("tensor")
    core = lax.axis_index("dp") & 1
    row_count = tokens.shape[0]
    seq_len = row_count * tensor_count
    head_local = heads_weight.shape[1] // (3 * HEAD_DIM)
    group_width = head_local * HEAD_DIM
    at_home = core == (tensor_index >> 1)
    group = 2 * (tensor_index & 1) + core

    gather_heads = heads_weight.shape[0] % 16 == 0
    late = reduce_weight.shape[0] % 16 == 0
    heads_low = heads_weight
    if not gather_heads:
        heads_low = gather_head_group(heads_weight.astype(low))
    (
        attended_full,
        attended_own,
        query_aux,
        key_aux,
        value_aux,
        first_full,
        own_tokens,
        full_heads,
        full_expand,
        full_reduce,
        full_merge,
        sequence_grad,
    ) = front_pallas(
        tokens,
        heads_low,
        expand_weight.T,
        reduce_weight,
        merge_weight,
        vectors,
        segment_ids.reshape(tensor_count, row_count),
        out_grad,
        gather_heads,
        late,
    )
    full_heads = full_heads.reshape(D, 3 * group_width) if gather_heads else heads_low
    if not late:
        full_expand, full_reduce = full_expand.reshape(-1, D), full_reduce.reshape(-1, D)
    (
        layer_base,
        layer_across,
        middle_grad,
        attended_grad,
        expand_sum,
        reduce_sum,
        merge_sum,
        vector_sums,
    ) = middle_pallas(
        attended_own, full_merge, own_tokens, vectors, full_expand, full_reduce, sequence_grad, late
    )
    (
        expand_rows,
        reduce_gradient,
        merge_rows,
        heads_gradient,
        input_rows,
        input_low,
        vector_part,
        output_rows,
        wide_gram,
        wide_rows,
        small_gram,
    ) = back_pallas(
        attended_full,
        attended_grad,
        query_aux,
        key_aux,
        value_aux,
        first_full,
        full_heads,
        expand_sum,
        reduce_sum,
        merge_sum.reshape(4, data_count, merge_weight.shape[1], group_width),
        layer_base,
        layer_across,
        expand_momentum.T,
        reduce_momentum,
        own_tokens,
        middle_grad,
        vectors,
        vector_sums,
        heads_momentum,
        merge_momentum,
    )
    expand_gradient, merge_gradient = expand_rows.T, merge_rows.T
    expand_new_momentum = momentum_decay * expand_momentum + expand_gradient
    reduce_new_momentum = momentum_decay * reduce_momentum + reduce_gradient
    heads_new_momentum = momentum_decay * heads_momentum + heads_gradient
    merge_new_momentum = momentum_decay * merge_momentum + merge_gradient

    heads_part = heads_new_momentum.reshape(heads_new_momentum.shape[0], head_local * 3, HEAD_DIM)
    merge_part = merge_new_momentum.reshape(head_local, HEAD_DIM, merge_new_momentum.shape[1])
    quarter = head_local
    ortho_mine, ortho_other, small_chain, vector_gradient, moved_output, moved_input = last_pallas(
        wide_gram,
        wide_rows,
        small_gram,
        vector_part,
        output_rows,
        input_low,
    )
    small_chain = small_chain.reshape(2, quarter, HEAD_DIM, 2, HEAD_DIM)
    small_chain = jnp.transpose(small_chain, (0, 3, 1, 2, 4)).reshape(-1, HEAD_DIM, HEAD_DIM)
    layer_output = jnp.where(at_home, output_rows, moved_output)
    input_gradient = jnp.where(at_home, input_rows, moved_input.astype(jnp.float32))
    vector_new_momentum = momentum_decay * vector_momentum + vector_gradient
    side_count = 3 * head_local
    heads_ortho = jnp.einsum("rmd,mde->rme", heads_part, small_chain[:side_count], precision=highest)
    merge_ortho = jnp.einsum("hde,hec->hdc", small_chain[side_count:], merge_part, precision=highest)

    first_core = core == 0
    expand_ortho = jnp.where(first_core, ortho_mine, ortho_other).T
    reduce_ortho = jnp.where(first_core, ortho_other, ortho_mine)

    keep_factor = 1.0 - muon_rate * weight_decay
    head_step = muon_rate * 0.2 * math.sqrt(max(D, HEAD_DIM))
    wide_step = muon_rate * 0.2 * math.sqrt(max(D, FF))
    heads_new_weight = heads_weight * keep_factor - head_step * heads_ortho.reshape(
        heads_weight.shape
    )
    merge_new_weight = merge_weight * keep_factor - head_step * merge_ortho.reshape(
        merge_weight.shape
    )
    expand_new_weight = expand_weight * keep_factor - wide_step * expand_ortho
    reduce_new_weight = reduce_weight * keep_factor - wide_step * reduce_ortho
    vector_new_value = vectors - vector_rate / math.sqrt(SEQ * data_count) * vector_new_momentum
    heads_new_average = average_decay * heads_average + (1.0 - average_decay) * heads_new_weight
    merge_new_average = average_decay * merge_average + (1.0 - average_decay) * merge_new_weight
    expand_new_average = average_decay * expand_average + (1.0 - average_decay) * expand_new_weight
    reduce_new_average = average_decay * reduce_average + (1.0 - average_decay) * reduce_new_weight
    vector_new_average = average_decay * vector_average + (1.0 - average_decay) * vector_new_value
    return (
        layer_output,
        input_gradient,
        heads_gradient,
        merge_gradient,
        expand_gradient,
        reduce_gradient,
        heads_new_momentum,
        merge_new_momentum,
        expand_new_momentum,
        reduce_new_momentum,
        heads_new_weight,
        merge_new_weight,
        expand_new_weight,
        reduce_new_weight,
        heads_new_average,
        merge_new_average,
        expand_new_average,
        reduce_new_average,
        vector_gradient,
        vector_new_momentum,
        vector_new_value,
        vector_new_average,
    )


def solution(mesh):
    placed = (
        P(("dp", "tensor"), None),
        P("dp"),
        P("dp", None),
        P("dp", "tensor"),
        P("tensor", "dp"),
        P(None, ("tensor", "dp")),
        P(("tensor", "dp"), None),
        P("dp", "tensor"),
        P("tensor", "dp"),
        P(None, ("tensor", "dp")),
        P(("tensor", "dp"), None),
        P("dp", "tensor"),
        P("tensor", "dp"),
        P(None, ("tensor", "dp")),
        P(("tensor", "dp"), None),
        P(),
        P(),
        P(),
    )
    return jax.shard_map(
        per_device,
        mesh=mesh,
        in_specs=placed,
        out_specs=(
            P(("dp", "tensor"), None),
            P(("dp", "tensor"), None),
            P("dp", "tensor"),
            P("tensor", "dp"),
            P(None, ("tensor", "dp")),
            P(("tensor", "dp"), None),
            P("dp", "tensor"),
            P("tensor", "dp"),
            P(None, ("tensor", "dp")),
            P(("tensor", "dp"), None),
            P("dp", "tensor"),
            P("tensor", "dp"),
            P(None, ("tensor", "dp")),
            P(("tensor", "dp"), None),
            P("dp", "tensor"),
            P("tensor", "dp"),
            P(None, ("tensor", "dp")),
            P(("tensor", "dp"), None),
            P(),
            P(),
            P(),
            P(),
        ),
        check_vma=False,
    )
```
